32 devices in a mesh: dp: 4 (over y, core), seq: 8 (over z, x).
Axes of the slice: x: 2, y: 2, z: 4, core: 2. Of those that a mesh axis runs over, the one named last changes fastest.
Arguments:
- queries: bfloat16 [4, 4096, 1024], P('dp', 'seq'), may hold values from -6 to 6
- keys: bfloat16 [4, 4096, 1024], P('dp', 'seq'), may hold values from -6 to 6
- values: bfloat16 [4, 4096, 1024], P('dp', 'seq'), may hold values from -6 to 6
- out_grad: bfloat16 [4, 4096, 2048], P('dp', 'seq'), may hold values from -6 to 6
- out_weight: bfloat16 [1024, 2048], P(('dp', 'seq')), may hold values from -0.125 to 0.125
- gain: float32 [1024], replicated, may hold values from 0.1 to 1.9
Outputs:
- query_grad: bfloat16 [4, 4096, 1024], P('dp', 'seq')
- key_grad: bfloat16 [4, 4096, 1024], P('dp', 'seq')
- value_grad: bfloat16 [4, 4096, 1024], P('dp', 'seq')
- weight_grad: float32 [1024, 2048], P(('dp', 'seq'))
- gain_grad: float32 [1024], replicated
The draws below stay inside these ranges and needn't reach their ends.
All inputs are finite; a program needn't handle non-finite values.
Results may differ from the reference program's by a relative error of at most 0.015.
Values may be sent and summed in bfloat16 or wider, within the bound.
No kernel may reach another device: no remote copies, remote signals or barrier semaphores. Data moves between devices by JAX's collectives and lax.ppermute only.
A program may use at most 128 MiB of HBM per device.

```python
import jax
import jax.numpy as jnp
from jax import lax

D = 2048
HEADS = 8
HEAD_DIM = 128
BLOCK = 512
HD = 1024
LENGTH = 4096
BATCH = 4
ALLTOK = 16384


def steps_of(stream_key, shape, cuts, low, largest):
    level = 1.0
    for position, shards_of in cuts:
        steps = jax.random.uniform(jax.random.fold_in(jax.random.fold_in(stream_key, 6), position), (shards_of,), jnp.float32, low / len(cuts), largest / len(cuts))
        level = level * jnp.repeat(jnp.exp(steps), shape[position] // shards_of).reshape((-1,) + (1,) * (len(shape) - 1 - position))
    return level


def bell_draw(stream_key, extent, scale, bound, split=(), kind=jnp.bfloat16):
    result = scale * jax.random.normal(stream_key, extent, jnp.float32)
    if split:
        result = result * steps_of(stream_key, extent, split, -0.22, 0.18)
    return jnp.clip(result, -bound, bound).astype(kind)


def setup_inputs(seed: int = 0) -> dict:
    streams_of = jax.random.split(jax.random.key(seed), 7)
    queries = bell_draw(streams_of[0], (BATCH, LENGTH, HD), 1.0, 6.0, ((0, 4), (1, 8)))
    keys = bell_draw(streams_of[1], (BATCH, LENGTH, HD), 1.0, 6.0, ((0, 4), (1, 8)))
    values = bell_draw(streams_of[2], (BATCH, LENGTH, HD), 1.0, 6.0, ((0, 4), (1, 8)))
    out_grad = bell_draw(streams_of[3], (BATCH, LENGTH, D), 1.0, 6.0, ((0, 4), (1, 8)))
    out_weight = bell_draw(streams_of[4], (HD, D), D ** -0.5, 0.125, ((0, 32),))
    gain = jnp.clip(1.0 + 0.18 * jax.random.normal(streams_of[5], (HD,), jnp.float32), 0.1, 1.9)
    return {"queries": queries, "keys": keys, "values": values, "out_grad": out_grad, "out_weight": out_weight, "gain": gain}


norm_eps = 1e-06

def as_float(array):
    return array.astype(jnp.float32)

def causal_mask():
    places = jnp.arange(BLOCK, dtype=jnp.int32)
    return (places[None, :] <= places[:, None]).astype(jnp.float32)

def reference(queries, keys, values, out_grad, out_weight, gain):
    causal = causal_mask()
    gain_heads = gain.reshape(HEADS, HEAD_DIM)
    blocks = LENGTH // BLOCK
    block_shape = (blocks, BLOCK, HEADS, HEAD_DIM)

    def one_sequence(items):
        seq_q, seq_k, seq_v, seq_g = items
        query_blk = seq_q.reshape(block_shape)
        key_blk = seq_k.reshape(block_shape)
        value_blk = seq_v.reshape(block_shape)
        grad_blk = seq_g.reshape(blocks, BLOCK, D)

        def forward_step(carry, inputs):
            state, weight_acc, gain_acc = carry
            qx, kx, vx, gx = inputs
            state_bf = state.astype(jnp.bfloat16)
            attn_bf = (jnp.einsum('thd,shd->hts', as_float(qx), as_float(kx)) * causal[None]).astype(jnp.bfloat16)
            outputs = jnp.einsum('hts,shd->thd', as_float(attn_bf), as_float(vx)) + jnp.einsum('thd,hde->the', as_float(qx), as_float(state_bf))
            rms = jnp.sqrt(lax.optimization_barrier(jnp.mean(outputs * outputs, axis=-1, keepdims=True)) + norm_eps)
            normed = outputs / rms
            unit_bf = (normed * gain_heads[None]).astype(jnp.bfloat16)
            unit_grad = jnp.dot(gx, out_weight.T, preferred_element_type=jnp.float32).reshape(BLOCK, HEADS, HEAD_DIM)
            gain_acc = gain_acc + lax.optimization_barrier(jnp.sum(unit_grad * normed, axis=0))
            scaled = unit_grad * gain_heads[None]
            middle = lax.optimization_barrier(jnp.mean(scaled * normed, axis=-1, keepdims=True))
            attn_grad = ((scaled - normed * middle) / rms).astype(jnp.bfloat16)
            weight_acc = weight_acc + jnp.dot(unit_bf.reshape(BLOCK, HD).T, gx, preferred_element_type=jnp.float32)
            state = state + jnp.einsum('shd,she->hde', as_float(kx), as_float(vx))
            return ((state, weight_acc, gain_acc), (attn_grad, state_bf))
        start_carry = (jnp.zeros((HEADS, HEAD_DIM, HEAD_DIM), jnp.float32), jnp.zeros((HD, D), jnp.float32), jnp.zeros((HEADS, HEAD_DIM), jnp.float32))
        (state_end, weight_acc, gain_acc), (attn_grads, states_bf) = lax.scan(forward_step, start_carry, (query_blk, key_blk, value_blk, grad_blk))

        def backward_step(rev, inputs):
            qx, kx, vx, ag, sbf = inputs
            rev_bf = rev.astype(jnp.bfloat16)
            attn_bf = (jnp.einsum('thd,shd->hts', as_float(qx), as_float(kx)) * causal[None]).astype(jnp.bfloat16)
            score_grad = (jnp.einsum('the,she->hts', as_float(ag), as_float(vx)) * causal[None]).astype(jnp.bfloat16)
            query_g = jnp.einsum('hts,shd->thd', as_float(score_grad), as_float(kx)) + jnp.einsum('the,hde->thd', as_float(ag), as_float(sbf))
            key_g = jnp.einsum('hts,thd->shd', as_float(score_grad), as_float(qx)) + jnp.einsum('she,hde->shd', as_float(vx), as_float(rev_bf))
            value_g = jnp.einsum('hts,the->she', as_float(attn_bf), as_float(ag)) + jnp.einsum('shd,hde->she', as_float(kx), as_float(rev_bf))
            rev = rev + jnp.einsum('thd,the->hde', as_float(qx), as_float(ag))
            return (rev, (query_g.astype(jnp.bfloat16), key_g.astype(jnp.bfloat16), value_g.astype(jnp.bfloat16)))
        rev_zero = jnp.zeros((HEADS, HEAD_DIM, HEAD_DIM), jnp.float32)
        rev_end, (query_g, key_g, value_g) = lax.scan(backward_step, rev_zero, (query_blk, key_blk, value_blk, attn_grads, states_bf), reverse=True)
        return (query_g.reshape(LENGTH, HD), key_g.reshape(LENGTH, HD), value_g.reshape(LENGTH, HD), weight_acc, gain_acc.reshape(HD))
    query_grad, key_grad, value_grad, weight_parts, gain_parts = lax.map(one_sequence, (queries, keys, values, out_grad))
    factor = 1.0 / jnp.sqrt(jnp.float32(ALLTOK))
    weight_grad = lax.optimization_barrier(jnp.sum(weight_parts, axis=0)) * factor
    gain_grad = lax.optimization_barrier(jnp.sum(gain_parts, axis=0)) * factor
    return (query_grad, key_grad, value_grad, weight_grad, gain_grad)
```

```python
import jax
import jax.numpy as jnp
from jax import lax
from jax.sharding import PartitionSpec as P

HEADS = 8
HEAD_DIM = 128
BLOCK = 512
HD = 1024


norm_eps = 1e-06


def flip(axis, bit):
    return [(i, i ^ bit) for i in range(lax.axis_size(axis))]


def bits_of(axis):
    size = lax.axis_size(axis)
    assert size & (size - 1) == 0
    return [1 << k for k in range(size.bit_length() - 1)]


def has(axis, bit):
    return (lax.axis_index(axis) // bit) % 2


def gather_rows(x, order):
    for axis, bit in order:
        x = jnp.concatenate([x, lax.ppermute(x, axis, flip(axis, bit))], axis=0)
    return x


def in_place(x, axis):
    size = lax.axis_size(axis)
    pieces = x.reshape((size, -1) + x.shape[1:])
    here = lax.axis_index(axis)
    order = jnp.arange(size, dtype=jnp.int32) ^ here
    return jnp.take(pieces, order, axis=0).reshape(x.shape)


def scatter_sum(x, order):
    for axis, bit in order:
        mine = has(axis, bit)
        keep = lax.dynamic_index_in_dim(x, mine, axis=0, keepdims=False)
        send = lax.dynamic_index_in_dim(x, 1 - mine, axis=0, keepdims=False)
        got = lax.ppermute(send.astype(jnp.bfloat16), axis, flip(axis, bit))
        x = keep.astype(jnp.float32) + got.astype(jnp.float32)
    return x


def shift_perm(size, s):
    return [(i, (i + s) % size) for i in range(size)]


def prefix_owned(x, axis, reverse):
    size, here = lax.axis_size(axis), lax.axis_index(axis)
    rows = x.reshape((size, -1, x.shape[-1])).astype(jnp.bfloat16)
    own = lax.dynamic_index_in_dim(rows, here, 0, keepdims=False)
    parts = [own]
    for s in range(1, size):
        to = (here + s) % size
        parts.append(
            lax.ppermute(lax.dynamic_index_in_dim(rows, to, 0, keepdims=False), axis, shift_perm(size, s))
        )
    stacked = jnp.stack(parts).astype(jnp.float32)
    places = (here - jnp.arange(size, dtype=jnp.int32)) % size

    def sum_for(place):
        use = (places > place) if reverse else (places < place)
        return jnp.sum(jnp.where(use[:, None, None], stacked, 0.0), axis=0).astype(jnp.bfloat16)

    result = jnp.zeros((size,) + own.shape, jnp.bfloat16)
    result = lax.dynamic_update_index_in_dim(result, sum_for(here), here, 0)
    for s in range(1, size):
        got = lax.ppermute(sum_for((here + s) % size), axis, shift_perm(size, s))
        result = lax.dynamic_update_index_in_dim(result, got, (here - s) % size, 0)
    return result.reshape(x.shape)


def prefix_scan(x, axis, reverse):
    total = x
    before = jnp.zeros_like(x)
    for bit in bits_of(axis):
        other = lax.ppermute(total.astype(jnp.bfloat16), axis, flip(axis, bit)).astype(jnp.float32)
        wanted = has(axis, bit) == (0 if reverse else 1)
        before = before + jnp.where(wanted, other, 0.0)
        total = total + other
    return before


def total_of(x):
    for axis in ("seq", "dp"):
        for bit in bits_of(axis):
            x = x + lax.ppermute(x, axis, flip(axis, bit))
    return x


def causal_mask():
    places = jnp.arange(BLOCK, dtype=jnp.int32)
    return (places[None, :] <= places[:, None]).astype(jnp.float32)


def before_each(block_terms):
    running = jnp.cumsum(block_terms, axis=0)
    return jnp.concatenate([jnp.zeros_like(block_terms), running[:-1]], axis=0)


def after_each(block_terms):
    running = jnp.cumsum(block_terms[::-1], axis=0)[::-1]
    return jnp.concatenate([running[1:], jnp.zeros_like(block_terms)], axis=0)


def shards(queries, keys, values, out_grad, out_weight, gain):
    tok_count = queries.shape[1]
    blocks = tok_count // BLOCK
    block_shape = (blocks, BLOCK, HEADS, HEAD_DIM)
    query_blk = queries.reshape(block_shape)
    key_blk = keys.reshape(block_shape)
    value_blk = values.reshape(block_shape)
    grad_rows = out_grad[0]
    gain_heads = gain.reshape(HEADS, HEAD_DIM)
    causal = causal_mask()
    seq_order = [("seq", bit) for bit in bits_of("seq")]
    dp_order = [("dp", bit) for bit in bits_of("dp")[::-1]]
    block_kv = jnp.einsum("nshd,nshe->nhde", key_blk, value_blk, preferred_element_type=jnp.float32)
    within = before_each(block_kv)
    local_total = jnp.sum(block_kv, axis=0)
    weight_seq = in_place(gather_rows(out_weight, seq_order), "seq")
    before = prefix_owned(local_total, "seq", False)
    weight = weight_seq
    for bit in bits_of("dp"):
        weight = jnp.concatenate([weight, lax.ppermute(weight, "dp", flip("dp", bit))], axis=0)
    weight = in_place(weight, "dp")
    state_bf = (before.astype(jnp.float32)[None] + within).astype(jnp.bfloat16)
    scores = jnp.einsum("nthd,nshd->nhts", query_blk, key_blk, preferred_element_type=jnp.float32)
    attn_bf = (scores * causal[None, None]).astype(jnp.bfloat16)
    outputs = jnp.einsum("nhts,nshd->nthd", attn_bf, value_blk, preferred_element_type=jnp.float32)
    outputs = outputs + jnp.einsum(
        "nthd,nhde->nthe", query_blk, state_bf, preferred_element_type=jnp.float32
    )
    rms = jnp.sqrt(jnp.mean(outputs * outputs, axis=-1, keepdims=True) + norm_eps)
    normed = outputs / rms
    unit_bf = (normed * gain_heads[None, None]).astype(jnp.bfloat16)
    unit_flat = unit_bf.reshape(tok_count, HD)
    partial = lax.dot_general(
        unit_flat, grad_rows, (((0,), (0,)), ((), ())), preferred_element_type=jnp.float32
    ).astype(jnp.bfloat16)
    scatter_order = [("dp", bit) for bit in bits_of("dp")[::-1]] + [("seq", bit) for bit in bits_of("seq")[::-1]]
    rows = HD // (lax.axis_size("dp") * lax.axis_size("seq"))
    weight_sum = scatter_sum(
        partial.reshape((2,) * len(scatter_order) + (rows, partial.shape[1])), scatter_order
    )
    unit_grad = lax.dot_general(
        grad_rows, weight, (((1,), (1,)), ((), ())), preferred_element_type=jnp.float32
    ).reshape(block_shape)
    gain_part = jnp.sum(unit_grad * normed, axis=(0, 1)).reshape(-1)
    scaled = unit_grad * gain_heads[None, None]
    middle = jnp.mean(scaled * normed, axis=-1, keepdims=True)
    attn_grad = ((scaled - normed * middle) / rms).astype(jnp.bfloat16)
    block_qg = jnp.einsum(
        "nthd,nthe->nhde", query_blk, attn_grad, preferred_element_type=jnp.float32
    )
    later_inside = after_each(block_qg)
    local_qg = jnp.sum(block_qg, axis=0)
    after = prefix_scan(local_qg, "seq", True)
    gain_total = total_of(gain_part)
    rev_bf = (after[None] + later_inside).astype(jnp.bfloat16)
    score_grad = (
        jnp.einsum("nthe,nshe->nhts", attn_grad, value_blk, preferred_element_type=jnp.float32)
        * causal[None, None]
    ).astype(jnp.bfloat16)
    query_g = jnp.einsum("nhts,nshd->nthd", score_grad, key_blk, preferred_element_type=jnp.float32)
    query_g = query_g + jnp.einsum(
        "nthe,nhde->nthd", attn_grad, state_bf, preferred_element_type=jnp.float32
    )
    key_g = jnp.einsum("nhts,nthd->nshd", score_grad, query_blk, preferred_element_type=jnp.float32)
    key_g = key_g + jnp.einsum(
        "nshe,nhde->nshd", value_blk, rev_bf, preferred_element_type=jnp.float32
    )
    value_g = jnp.einsum("nhts,nthe->nshe", attn_bf, attn_grad, preferred_element_type=jnp.float32)
    value_g = value_g + jnp.einsum(
        "nshd,nhde->nshe", key_blk, rev_bf, preferred_element_type=jnp.float32
    )
    factor = 1.0 / jnp.sqrt(jnp.float32(tok_count * lax.axis_size("dp") * lax.axis_size("seq")))
    out_shape = (1, tok_count, HD)
    return (
        query_g.astype(jnp.bfloat16).reshape(out_shape),
        key_g.astype(jnp.bfloat16).reshape(out_shape),
        value_g.astype(jnp.bfloat16).reshape(out_shape),
        weight_sum * factor,
        gain_total * factor,
    )


def solution(mesh):
    placed = (
        P("dp", "seq", None),
        P("dp", "seq", None),
        P("dp", "seq", None),
        P("dp", "seq", None),
        P(("dp", "seq"), None),
        P(),
    )
    return jax.shard_map(
        shards,
        mesh=mesh,
        in_specs=placed,
        out_specs=(
            P("dp", "seq", None),
            P("dp", "seq", None),
            P("dp", "seq", None),
            P(("dp", "seq"), None),
            P(),
        ),
        check_vma=False,
    )
```

```python
import functools

import jax
import jax.numpy as jnp
from jax import lax
from jax.experimental import pallas as pl
from jax.experimental.pallas import tpu as pltpu
from jax.sharding import PartitionSpec as P

HEAD_DIM = 128
BLOCK = 512
MIB = 1 << 20

norm_eps = 1e-06

F32 = jnp.float32
BF16 = jnp.bfloat16


def dot(a, b, contract):
    return lax.dot_general(a, b, (contract, ((), ())), preferred_element_type=F32)


def flip(axis, bit):
    return [(i, i ^ bit) for i in range(lax.axis_size(axis))]


def bits_of(axis):
    size = lax.axis_size(axis)
    assert size & (size - 1) == 0
    return [1 << k for k in range(size.bit_length() - 1)]


def has(axis, bit):
    return (lax.axis_index(axis) // bit) % 2


def params(mib, dims=1):
    return pltpu.CompilerParams(
        vmem_limit_bytes=mib * MIB, dimension_semantics=("arbitrary",) * dims
    )


def head(ref, i):
    return ref[:, i * HEAD_DIM : (i + 1) * HEAD_DIM]


def kv_kernel(k_ref, v_ref, o_ref):
    for i in range(o_ref.shape[0]):
        o_ref[i] = dot(head(k_ref, i), head(v_ref, i), ((0,), (0,))).astype(BF16)


def key_value_sums(keys, values, pair):
    tokens, channels = keys.shape
    width = pair * HEAD_DIM
    heads = channels // HEAD_DIM
    spec = pl.BlockSpec((tokens, width), lambda b: (0, b))
    return pl.pallas_call(
        kv_kernel,
        grid=(heads // pair,),
        in_specs=[spec, spec],
        out_specs=pl.BlockSpec((pair, HEAD_DIM, HEAD_DIM), lambda b: (b, 0, 0)),
        out_shape=jax.ShapeDtypeStruct((heads, HEAD_DIM, HEAD_DIM), BF16),
        compiler_params=params(16),
        cost_estimate=pl.CostEstimate(
            flops=2 * tokens * channels * HEAD_DIM, bytes_accessed=4 * tokens * channels, transcendentals=0
        ),
        name="key_value_sums",
    )(keys, values)


def lower(x):
    rows = lax.broadcasted_iota(jnp.int32, x.shape, 0)
    cols = lax.broadcasted_iota(jnp.int32, x.shape, 1)
    return jnp.where(cols <= rows, x, 0.0).astype(BF16)


def intra_kernel(q_ref, k_ref, v_ref, o_ref):
    half = q_ref.shape[0] // 2
    for i in range(o_ref.shape[1] // HEAD_DIM):
        q, k, v = head(q_ref, i), head(k_ref, i), head(v_ref, i)
        here = slice(i * HEAD_DIM, (i + 1) * HEAD_DIM)
        top = lower(dot(q[:half], k[:half], ((1,), (1,))))
        o_ref[:half, here] = dot(top, v[:half], ((1,), (0,)))
        left = dot(q[half:], k[:half], ((1,), (1,))).astype(BF16)
        right = lower(dot(q[half:], k[half:], ((1,), (1,))))
        o_ref[half:, here] = dot(left, v[:half], ((1,), (0,))) + dot(right, v[half:], ((1,), (0,)))


def intra_outputs(queries, keys, values, pair):
    tokens, channels = keys.shape
    spec = pl.BlockSpec((tokens, pair * HEAD_DIM), lambda b: (0, b))
    return pl.pallas_call(
        intra_kernel,
        grid=(channels // (pair * HEAD_DIM),),
        in_specs=[spec] * 3,
        out_specs=spec,
        out_shape=jax.ShapeDtypeStruct((tokens, channels), F32),
        compiler_params=params(24),
        cost_estimate=pl.CostEstimate(
            flops=4 * tokens * tokens * channels, bytes_accessed=10 * tokens * channels, transcendentals=0
        ),
        name="intra_outputs",
    )(queries, keys, values)


def rms_inverse(x):
    return lax.rsqrt(jnp.mean(x * x, axis=-1, keepdims=True) + norm_eps)


def unit_kernel(pos_ref, q_ref, s_ref, intra_ref, gain_ref, og_ref, out_ref, send_ref, keep_ref):
    units = []
    for i in range(s_ref.shape[0]):
        x = head(intra_ref, i) + dot(head(q_ref, i), s_ref[i], ((1,), (0,)))
        out_ref[:, i * HEAD_DIM : (i + 1) * HEAD_DIM] = x
        units.append((x * rms_inverse(x) * head(gain_ref, i)).astype(BF16))
    unit = jnp.concatenate(units, axis=1) if len(units) > 1 else units[0]
    part = dot(unit, og_ref[...], ((0,), (0,))).astype(BF16)

    @pl.when(pl.program_id(0) == 0)
    def _():
        send_ref[0] = part

    @pl.when(pl.program_id(0) == 1)
    def _():
        keep_ref[0] = part


def weight_parts(pos, queries, state, intra, gain, out_grad, pair):
    tokens, channels = queries.shape
    width = pair * HEAD_DIM
    count = channels // width // 2
    wide = out_grad.shape[1]

    def block(c, y, pos_ref):
        return 2 * y + lax.rem(pos_ref[0] + 1 + c, 2)

    cols = pl.BlockSpec((tokens, width), lambda c, y, pos_ref: (0, block(c, y, pos_ref)))
    part = jax.ShapeDtypeStruct((count, width, wide), BF16)
    return pl.pallas_call(
        unit_kernel,
        grid_spec=pltpu.PrefetchScalarGridSpec(
            num_scalar_prefetch=1,
            grid=(2, count),
            in_specs=[
                cols,
                pl.BlockSpec((pair, HEAD_DIM, HEAD_DIM), lambda c, y, p: (block(c, y, p), 0, 0)),
                cols,
                pl.BlockSpec((1, width), lambda c, y, p: (0, block(c, y, p))),
                pl.BlockSpec((tokens, wide), lambda c, y, p: (0, 0)),
            ],
            out_specs=[
                cols,
                pl.BlockSpec((1, width, wide), lambda c, y, p: (jnp.where(c == 0, y, count - 1), 0, 0)),
                pl.BlockSpec((1, width, wide), lambda c, y, p: (jnp.where(c == 0, 0, y), 0, 0)),
            ],
        ),
        out_shape=[jax.ShapeDtypeStruct((tokens, channels), F32), part, part],
        compiler_params=params(32, 2),
        cost_estimate=pl.CostEstimate(
            flops=2 * tokens * channels * wide,
            bytes_accessed=10 * tokens * channels + 2 * tokens * wide + 2 * channels * wide,
            transcendentals=0,
        ),
        name="weight_parts",
    )(pos, queries, state, intra, gain, out_grad)


def attn_grad_kernel(groups, pos_ref, q_ref, o_ref, gain_ref, og_ref, *refs):
    mine, other = refs[:groups], refs[groups : 2 * groups]
    ag_ref, gg_ref, qg_ref, ug_ref = refs[2 * groups :]

    def project(parts):
        start, total = 0, None
        for part in parts:
            stop = start + part.shape[-1]
            term = dot(og_ref[:, start:stop], part[0], ((1,), (1,)))
            total = term if total is None else total + term
            start = stop
        ug_ref[...] = total

    @pl.when(pl.program_id(0) == 0)
    def _():
        project(mine)

    @pl.when(pl.program_id(0) == 1)
    def _():
        project(other)

    for i in range(qg_ref.shape[0]):
        here = slice(i * HEAD_DIM, (i + 1) * HEAD_DIM)
        x = head(o_ref, i)
        inverse = rms_inverse(x)
        normed = x * inverse
        ug = head(ug_ref, i)
        gg_ref[:, here] = jnp.sum(ug * normed, axis=0, keepdims=True)
        scaled = ug * head(gain_ref, i)
        middle = jnp.mean(scaled * normed, axis=-1, keepdims=True)
        ag = ((scaled - normed * middle) * inverse).astype(BF16)
        ag_ref[:, here] = ag
        qg_ref[i] = dot(head(q_ref, i), ag, ((0,), (0,))).astype(BF16)


def attn_grads(pos, queries, outputs, gain, out_grad, mine, other, pair):
    tokens, channels = queries.shape
    width = pair * HEAD_DIM
    count = channels // width // 2
    wide = out_grad.shape[1]
    heads = channels // HEAD_DIM

    def block(c, y, pos_ref):
        return 2 * y + lax.rem(pos_ref[0] + c, 2)

    cols = pl.BlockSpec((tokens, width), lambda c, y, p: (0, block(c, y, p)))
    row = pl.BlockSpec((1, width), lambda c, y, p: (0, block(c, y, p)))
    states = pl.BlockSpec((pair, HEAD_DIM, HEAD_DIM), lambda c, y, p: (block(c, y, p), 0, 0))
    weights = [
        pl.BlockSpec((1, width, w.shape[-1]), lambda c, y, p: (jnp.where(c == 0, y, count - 1), 0, 0))
        for w in mine
    ] + [
        pl.BlockSpec((1, width, w.shape[-1]), lambda c, y, p: (jnp.where(c == 0, 0, y), 0, 0))
        for w in other
    ]
    return pl.pallas_call(
        functools.partial(attn_grad_kernel, len(mine)),
        grid_spec=pltpu.PrefetchScalarGridSpec(
            num_scalar_prefetch=1,
            grid=(2, count),
            in_specs=[cols, cols, row, pl.BlockSpec((tokens, wide), lambda c, y, p: (0, 0))] + weights,
            out_specs=[cols, row, states],
            scratch_shapes=[pltpu.VMEM((tokens, width), F32)],
        ),
        out_shape=[
            jax.ShapeDtypeStruct((tokens, channels), BF16),
            jax.ShapeDtypeStruct((1, channels), F32),
            jax.ShapeDtypeStruct((heads, HEAD_DIM, HEAD_DIM), BF16),
        ],
        compiler_params=params(32, 2),
        cost_estimate=pl.CostEstimate(
            flops=2 * tokens * channels * wide,
            bytes_accessed=8 * tokens * channels + 2 * tokens * wide + 2 * channels * wide,
            transcendentals=0,
        ),
        name="attn_grads",
    )(pos, queries, outputs, gain, out_grad, *mine, *other)


def inner_grad_kernel(q_ref, k_ref, v_ref, ag_ref, s_ref, qg_ref, kg_ref, vg_ref):
    half = q_ref.shape[0] // 2
    top, low = slice(0, half), slice(half, 2 * half)
    for i in range(s_ref.shape[0]):
        q, k, v, ag = head(q_ref, i), head(k_ref, i), head(v_ref, i), head(ag_ref, i)
        here = slice(i * HEAD_DIM, (i + 1) * HEAD_DIM)
        nt, nn, tn = ((1,), (1,)), ((1,), (0,)), ((0,), (0,))
        from_state = dot(ag, s_ref[i], nt)
        g00 = lower(dot(ag[top], v[top], nt))
        g10 = dot(ag[low], v[top], nt).astype(BF16)
        g11 = lower(dot(ag[low], v[low], nt))
        qg_ref[top, here] = (dot(g00, k[top], nn) + from_state[top]).astype(BF16)
        qg_ref[low, here] = (dot(g10, k[top], nn) + dot(g11, k[low], nn) + from_state[low]).astype(BF16)
        kg_ref[top, here] = dot(g00, q[top], tn) + dot(g10, q[low], tn)
        kg_ref[low, here] = dot(g11, q[low], tn)
        a00 = lower(dot(q[top], k[top], nt))
        a10 = dot(q[low], k[top], nt).astype(BF16)
        a11 = lower(dot(q[low], k[low], nt))
        vg_ref[top, here] = dot(a00, ag[top], tn) + dot(a10, ag[low], tn)
        vg_ref[low, here] = dot(a11, ag[low], tn)


def inner_grads(queries, keys, values, attn_grad, state, pair):
    tokens, channels = queries.shape
    spec = pl.BlockSpec((tokens, pair * HEAD_DIM), lambda b: (0, b))
    return pl.pallas_call(
        inner_grad_kernel,
        grid=(channels // (pair * HEAD_DIM),),
        in_specs=[spec] * 4 + [pl.BlockSpec((pair, HEAD_DIM, HEAD_DIM), lambda b: (b, 0, 0))],
        out_specs=[spec] * 3,
        out_shape=[jax.ShapeDtypeStruct((tokens, channels), t) for t in (BF16, F32, F32)],
        compiler_params=params(32),
        cost_estimate=pl.CostEstimate(
            flops=8 * tokens * tokens * channels, bytes_accessed=18 * tokens * channels, transcendentals=0
        ),
        name="inner_grads",
    )(queries, keys, values, attn_grad, state)


def outer_grad_kernel(k_ref, v_ref, r_ref, kin_ref, vin_ref, kg_ref, vg_ref):
    for i in range(r_ref.shape[0]):
        here = slice(i * HEAD_DIM, (i + 1) * HEAD_DIM)
        rev = r_ref[i]
        kg_ref[:, here] = (head(kin_ref, i) + dot(head(v_ref, i), rev, ((1,), (1,)))).astype(BF16)
        vg_ref[:, here] = (head(vin_ref, i) + dot(head(k_ref, i), rev, ((1,), (0,)))).astype(BF16)


def outer_grads(keys, values, rev, key_in, value_in, pair):
    tokens, channels = keys.shape
    spec = pl.BlockSpec((tokens, pair * HEAD_DIM), lambda b: (0, b))
    return pl.pallas_call(
        outer_grad_kernel,
        grid=(channels // (pair * HEAD_DIM),),
        in_specs=[spec] * 2 + [pl.BlockSpec((pair, HEAD_DIM, HEAD_DIM), lambda b: (b, 0, 0))] + [spec] * 2,
        out_specs=[spec] * 2,
        out_shape=[jax.ShapeDtypeStruct((tokens, channels), BF16)] * 2,
        compiler_params=params(24),
        cost_estimate=pl.CostEstimate(
            flops=4 * tokens * channels * HEAD_DIM, bytes_accessed=16 * tokens * channels, transcendentals=0
        ),
        name="outer_grads",
    )(keys, values, rev, key_in, value_in)


def running_kernel(reverse, x_ref, o_ref):
    count = x_ref.shape[0]
    total = jnp.zeros(x_ref.shape[1:], F32)
    for place in range(count)[:: -1 if reverse else 1]:
        o_ref[place] = total.astype(BF16)
        total = total + x_ref[place].astype(F32)


def sums_ahead(x, axis, reverse):
    size = lax.axis_size(axis)
    rows = x.reshape((size, -1, x.shape[-1]))
    rows = lax.all_to_all(rows, axis, 0, 0, tiled=True)
    rows = pl.pallas_call(
        functools.partial(running_kernel, reverse),
        out_shape=jax.ShapeDtypeStruct(rows.shape, BF16),
        name="running_sums",
    )(rows)
    return lax.all_to_all(rows, axis, 0, 0, tiled=True).reshape(x.shape)


def merge_kernel(groups, axis, bit, mine_ref, theirs_ref, *refs):
    outs, sems = refs[:-1], refs[-1]
    place = (lax.axis_index(axis) // bit) % 2
    copies = []
    for g, (start, stop) in enumerate(groups):
        for side, source in ((place, mine_ref), (1 - place, theirs_ref)):
            copies.append(
                pltpu.make_async_copy(
                    source.at[:, :, start:stop], outs[g].at[:, side], sems.at[len(copies)]
                )
            )
    for copy in copies:
        copy.start()
    for copy in copies:
        copy.wait()


def merge(mine, theirs, axis, bit, groups=None):
    groups = groups or [(0, mine.shape[-1])]
    shape = mine.shape
    outs = pl.pallas_call(
        functools.partial(merge_kernel, groups, axis, bit),
        in_specs=[pl.BlockSpec(memory_space=pl.ANY)] * 2,
        out_specs=[pl.BlockSpec(memory_space=pl.ANY)] * len(groups),
        out_shape=[
            jax.ShapeDtypeStruct((shape[0], 2, shape[1], stop - start), mine.dtype) for start, stop in groups
        ],
        scratch_shapes=[pltpu.SemaphoreType.DMA((2 * len(groups),))],
        cost_estimate=pl.CostEstimate(
            flops=0, bytes_accessed=8 * mine.size, transcendentals=0
        ),
        name="merge",
    )(mine, theirs)
    return outs


def column_groups(wide):
    tiles = wide // 128
    cuts = [0, (tiles + 2) // 3, (tiles + 2) // 3 + (tiles + 1) // 3, tiles]
    return [(128 * a, 128 * b) for a, b in zip(cuts, cuts[1:])]


def bit_orders():
    seq, dp = bits_of("seq"), bits_of("dp")
    rest = [("seq", bit) for bit in seq[:-1]] + [("dp", bit) for bit in dp[1:]]
    return ("seq", seq[-1]), [rest[k:] + rest[:k] for k in range(3)]


def canonical():
    return [("dp", bit) for bit in bits_of("dp")[:0:-1]] + [("seq", bit) for bit in bits_of("seq")[::-1]]


def gathered_projection(weight):
    dp_count, seq_count = lax.axis_size("dp"), lax.axis_size("seq")
    rows, wide = weight.shape
    if rows % 16:
        whole = lax.all_gather(weight, ("dp", "seq"), axis=0, tiled=True)
        whole = whole.reshape(dp_count // 2, 2, rows * seq_count, wide)
        core = has("dp", 1)
        return (
            [lax.dynamic_index_in_dim(whole, core, 1, keepdims=False)],
            [lax.dynamic_index_in_dim(whole, 1 - core, 1, keepdims=False)],
        )
    far, orders = bit_orders()
    places = canonical()
    theirs = lax.ppermute(weight, far[0], flip(*far))
    parts = list(merge(weight[None], theirs[None], *far, column_groups(wide)))
    done = [[far] for _ in parts]
    for stage in range(len(orders[0])):
        for g, order in enumerate(orders):
            bit = order[::-1][stage]
            before = [b for b in done[g] if places.index(b) < places.index(bit)]
            mine = parts[g].reshape((1 << len(before), -1, parts[g].shape[-1]))
            theirs = lax.ppermute(mine, bit[0], flip(*bit))
            (parts[g],) = merge(mine, theirs, *bit)
            done[g].append(bit)
    parts = [p.reshape(dp_count // 2, rows * seq_count, p.shape[-1]) for p in parts]
    others = [lax.ppermute(p, "dp", flip("dp", 1)) for p in parts]
    return parts, others


def added(keep, got):
    return (keep.astype(F32) + got.astype(F32)).astype(BF16)


def halves(x, places, bit):
    at = places.index(bit)
    mine = has(*bit)
    keep = lax.dynamic_index_in_dim(x, mine, at, keepdims=False)
    send = lax.dynamic_index_in_dim(x, 1 - mine, at, keepdims=False)
    return keep, send, [b for b in places if b != bit]


def scattered(send, keep, rows):
    wide = send.shape[-1]
    got = lax.ppermute(send, "dp", flip("dp", 1))
    far, orders = bit_orders()
    places = canonical()
    split = (2,) * len(places) + (rows, wide)
    keep, got = keep.reshape(split), got.reshape(split)
    last_keep, last_send = [], []
    xs = [(added(keep[..., a:b], got[..., a:b]), places) for a, b in column_groups(wide)]
    for stage in range(len(orders[0])):
        nexts = []
        for (x, left), order in zip(xs, orders):
            bit = order[stage]
            mine, theirs, left = halves(x, left, bit)
            nexts.append((added(mine, lax.ppermute(theirs, bit[0], flip(*bit))), left))
        xs = nexts
    for x, left in xs:
        mine, theirs, _ = halves(x, left, far)
        last_keep.append(mine)
        last_send.append(theirs)
    got = lax.ppermute(jnp.concatenate(last_send, axis=-1), far[0], flip(*far))
    return jnp.concatenate(last_keep, axis=-1).astype(F32) + got.astype(F32)


def total_of(x):
    for axis in ("seq", "dp"):
        for bit in bits_of(axis):
            x = x + lax.ppermute(x, axis, flip(axis, bit))
    return x


def shards(queries, keys, values, out_grad, out_weight, gain):
    tokens, channels = queries.shape[1:]
    assert tokens == BLOCK
    dp_count, seq_count = lax.axis_size("dp"), lax.axis_size("seq")
    pair = channels // dp_count // HEAD_DIM
    q, k, v, og = queries[0], keys[0], values[0], out_grad[0]
    gain_row = gain.reshape(1, channels)
    pos = jnp.stack([lax.axis_index("dp"), lax.axis_index("seq")]).astype(jnp.int32)
    kv = key_value_sums(k, v, pair)
    state = sums_ahead(kv, "seq", False)
    mine, other = gathered_projection(out_weight)
    intra = intra_outputs(q, k, v, pair)
    outputs, send, keep = weight_parts(pos, q, state, intra, gain_row, og, pair)
    weight_sum = scattered(send, keep, out_weight.shape[0])
    attn_grad, gain_part, qg = attn_grads(pos, q, outputs, gain_row, og, mine, other, pair)
    rev = sums_ahead(qg, "seq", True)
    query_g, key_in, value_in = inner_grads(q, k, v, attn_grad, state, pair)
    gain_total = total_of(gain_part.reshape(channels))
    key_g, value_g = outer_grads(k, v, rev, key_in, value_in, pair)
    factor = 1.0 / jnp.sqrt(jnp.float32(tokens * dp_count * seq_count))
    out_shape = (1, tokens, channels)
    return (
        query_g.reshape(out_shape),
        key_g.reshape(out_shape),
        value_g.reshape(out_shape),
        weight_sum * factor,
        gain_total * factor,
    )


def solution(mesh):
    placed = (
        P("dp", "seq", None),
        P("dp", "seq", None),
        P("dp", "seq", None),
        P("dp", "seq", None),
        P(("dp", "seq"), None),
        P(),
    )
    return jax.shard_map(
        shards,
        mesh=mesh,
        in_specs=placed,
        out_specs=(
            P("dp", "seq", None),
            P("dp", "seq", None),
            P("dp", "seq", None),
            P(("dp", "seq"), None),
            P(),
        ),
        check_vma=False,
    )
```

```python
import functools

import jax
import jax.numpy as jnp
from jax import lax
from jax.experimental import pallas as pl
from jax.experimental.pallas import tpu as pltpu
from jax.sharding import PartitionSpec as P

HEAD_DIM = 128
BLOCK = 512
MIB = 1 << 20

norm_eps = 1e-06

F32 = jnp.float32
BF16 = jnp.bfloat16


def dot(a, b, contract):
    return lax.dot_general(a, b, (contract, ((), ())), preferred_element_type=F32)


def flip(axis, bit):
    return [(i, i ^ bit) for i in range(lax.axis_size(axis))]


def bits_of(axis):
    size = lax.axis_size(axis)
    assert size & (size - 1) == 0
    return [1 << k for k in range(size.bit_length() - 1)]


def has(axis, bit):
    return (lax.axis_index(axis) // bit) % 2


def params(mib, dims=1):
    return pltpu.CompilerParams(
        vmem_limit_bytes=mib * MIB, dimension_semantics=("arbitrary",) * dims
    )


def head(ref, i):
    return ref[:, i * HEAD_DIM : (i + 1) * HEAD_DIM]


def kv_kernel(k_ref, v_ref, o_ref):
    for i in range(o_ref.shape[0]):
        o_ref[i] = dot(head(k_ref, i), head(v_ref, i), ((0,), (0,))).astype(BF16)


def key_value_sums(keys, values, pair):
    tokens, channels = keys.shape
    width = pair * HEAD_DIM
    heads = channels // HEAD_DIM
    spec = pl.BlockSpec((tokens, width), lambda b: (0, b))
    return pl.pallas_call(
        kv_kernel,
        grid=(heads // pair,),
        in_specs=[spec, spec],
        out_specs=pl.BlockSpec((pair, HEAD_DIM, HEAD_DIM), lambda b: (b, 0, 0)),
        out_shape=jax.ShapeDtypeStruct((heads, HEAD_DIM, HEAD_DIM), BF16),
        compiler_params=params(56),
        cost_estimate=pl.CostEstimate(
            flops=2 * tokens * channels * HEAD_DIM, bytes_accessed=4 * tokens * channels, transcendentals=0
        ),
        name="key_value_sums",
    )(keys, values)


def lower(x):
    rows = lax.broadcasted_iota(jnp.int32, x.shape, 0)
    cols = lax.broadcasted_iota(jnp.int32, x.shape, 1)
    return jnp.where(cols <= rows, x, 0.0).astype(BF16)


def intra_kernel(q_ref, k_ref, v_ref, o_ref):
    half = q_ref.shape[0] // 2
    for i in range(o_ref.shape[1] // HEAD_DIM):
        q, k, v = head(q_ref, i), head(k_ref, i), head(v_ref, i)
        here = slice(i * HEAD_DIM, (i + 1) * HEAD_DIM)
        top = lower(dot(q[:half], k[:half], ((1,), (1,))))
        o_ref[:half, here] = dot(top, v[:half], ((1,), (0,)))
        left = dot(q[half:], k[:half], ((1,), (1,))).astype(BF16)
        right = lower(dot(q[half:], k[half:], ((1,), (1,))))
        o_ref[half:, here] = dot(left, v[:half], ((1,), (0,))) + dot(right, v[half:], ((1,), (0,)))


def intra_outputs(queries, keys, values, pair):
    tokens, channels = keys.shape
    spec = pl.BlockSpec((tokens, pair * HEAD_DIM), lambda b: (0, b))
    return pl.pallas_call(
        intra_kernel,
        grid=(channels // (pair * HEAD_DIM),),
        in_specs=[spec] * 3,
        out_specs=spec,
        out_shape=jax.ShapeDtypeStruct((tokens, channels), F32),
        compiler_params=params(56),
        cost_estimate=pl.CostEstimate(
            flops=4 * tokens * tokens * channels, bytes_accessed=10 * tokens * channels, transcendentals=0
        ),
        name="intra_outputs",
    )(queries, keys, values)


def rms_inverse(x):
    return lax.rsqrt(jnp.mean(x * x, axis=-1, keepdims=True) + norm_eps)


def unit_kernel(pos_ref, q_ref, s_ref, intra_ref, gain_ref, og_ref, out_ref, send_ref, keep_ref):
    units = []
    for i in range(s_ref.shape[0]):
        x = head(intra_ref, i) + dot(head(q_ref, i), s_ref[i], ((1,), (0,)))
        out_ref[:, i * HEAD_DIM : (i + 1) * HEAD_DIM] = x
        units.append((x * rms_inverse(x) * head(gain_ref, i)).astype(BF16))
    unit = jnp.concatenate(units, axis=1) if len(units) > 1 else units[0]
    part = dot(unit, og_ref[...], ((0,), (0,))).astype(BF16)

    @pl.when(pl.program_id(0) == 0)
    def _():
        send_ref[0] = part

    @pl.when(pl.program_id(0) == 1)
    def _():
        keep_ref[0] = part


def weight_parts(pos, queries, state, intra, gain, out_grad, pair):
    tokens, channels = queries.shape
    width = pair * HEAD_DIM
    count = channels // width // 2
    wide = out_grad.shape[1]

    def block(c, y, pos_ref):
        return 2 * y + lax.rem(pos_ref[0] + 1 + c, 2)

    cols = pl.BlockSpec((tokens, width), lambda c, y, pos_ref: (0, block(c, y, pos_ref)))
    part = jax.ShapeDtypeStruct((count, width, wide), BF16)
    return pl.pallas_call(
        unit_kernel,
        grid_spec=pltpu.PrefetchScalarGridSpec(
            num_scalar_prefetch=1,
            grid=(2, count),
            in_specs=[
                cols,
                pl.BlockSpec((pair, HEAD_DIM, HEAD_DIM), lambda c, y, p: (block(c, y, p), 0, 0)),
                cols,
                pl.BlockSpec((1, width), lambda c, y, p: (0, block(c, y, p))),
                pl.BlockSpec((tokens, wide), lambda c, y, p: (0, 0)),
            ],
            out_specs=[
                cols,
                pl.BlockSpec((1, width, wide), lambda c, y, p: (jnp.where(c == 0, y, count - 1), 0, 0)),
                pl.BlockSpec((1, width, wide), lambda c, y, p: (jnp.where(c == 0, 0, y), 0, 0)),
            ],
        ),
        out_shape=[jax.ShapeDtypeStruct((tokens, channels), F32), part, part],
        compiler_params=params(56, 2),
        cost_estimate=pl.CostEstimate(
            flops=2 * tokens * channels * wide,
            bytes_accessed=10 * tokens * channels + 2 * tokens * wide + 2 * channels * wide,
            transcendentals=0,
        ),
        name="weight_parts",
    )(pos, queries, state, intra, gain, out_grad)


def attn_grad_kernel(groups, pos_ref, q_ref, o_ref, gain_ref, og_ref, *refs):
    mine, other = refs[:groups], refs[groups : 2 * groups]
    ag_ref, gg_ref, qg_ref, ug_ref = refs[2 * groups :]

    def project(parts):
        start, total = 0, None
        for part in parts:
            stop = start + part.shape[-1]
            term = dot(og_ref[:, start:stop], part[0], ((1,), (1,)))
            total = term if total is None else total + term
            start = stop
        ug_ref[...] = total

    @pl.when(pl.program_id(0) == 0)
    def _():
        project(mine)

    @pl.when(pl.program_id(0) == 1)
    def _():
        project(other)

    for i in range(qg_ref.shape[0]):
        here = slice(i * HEAD_DIM, (i + 1) * HEAD_DIM)
        x = head(o_ref, i)
        inverse = rms_inverse(x)
        normed = x * inverse
        ug = head(ug_ref, i)
        gg_ref[:, here] = jnp.sum(ug * normed, axis=0, keepdims=True)
        scaled = ug * head(gain_ref, i)
        middle = jnp.mean(scaled * normed, axis=-1, keepdims=True)
        ag = ((scaled - normed * middle) * inverse).astype(BF16)
        ag_ref[:, here] = ag
        qg_ref[i] = dot(head(q_ref, i), ag, ((0,), (0,))).astype(BF16)


def attn_grads(pos, queries, outputs, gain, out_grad, mine, other, pair):
    tokens, channels = queries.shape
    width = pair * HEAD_DIM
    count = channels // width // 2
    wide = out_grad.shape[1]
    heads = channels // HEAD_DIM

    def block(c, y, pos_ref):
        return 2 * y + lax.rem(pos_ref[0] + c, 2)

    cols = pl.BlockSpec((tokens, width), lambda c, y, p: (0, block(c, y, p)))
    row = pl.BlockSpec((1, width), lambda c, y, p: (0, block(c, y, p)))
    states = pl.BlockSpec((pair, HEAD_DIM, HEAD_DIM), lambda c, y, p: (block(c, y, p), 0, 0))
    weights = [
        pl.BlockSpec((1, width, w.shape[-1]), lambda c, y, p: (jnp.where(c == 0, y, count - 1), 0, 0))
        for w in mine
    ] + [
        pl.BlockSpec((1, width, w.shape[-1]), lambda c, y, p: (jnp.where(c == 0, 0, y), 0, 0))
        for w in other
    ]
    return pl.pallas_call(
        functools.partial(attn_grad_kernel, len(mine)),
        grid_spec=pltpu.PrefetchScalarGridSpec(
            num_scalar_prefetch=1,
            grid=(2, count),
            in_specs=[cols, cols, row, pl.BlockSpec((tokens, wide), lambda c, y, p: (0, 0))] + weights,
            out_specs=[cols, row, states],
            scratch_shapes=[pltpu.VMEM((tokens, width), F32)],
        ),
        out_shape=[
            jax.ShapeDtypeStruct((tokens, channels), BF16),
            jax.ShapeDtypeStruct((1, channels), F32),
            jax.ShapeDtypeStruct((heads, HEAD_DIM, HEAD_DIM), BF16),
        ],
        compiler_params=params(56, 2),
        cost_estimate=pl.CostEstimate(
            flops=2 * tokens * channels * wide,
            bytes_accessed=8 * tokens * channels + 2 * tokens * wide + 2 * channels * wide,
            transcendentals=0,
        ),
        name="attn_grads",
    )(pos, queries, outputs, gain, out_grad, *mine, *other)


def inner_grad_kernel(q_ref, k_ref, v_ref, ag_ref, s_ref, qg_ref, kg_ref, vg_ref):
    half = q_ref.shape[0] // 2
    top, low = slice(0, half), slice(half, 2 * half)
    for i in range(s_ref.shape[0]):
        q, k, v, ag = head(q_ref, i), head(k_ref, i), head(v_ref, i), head(ag_ref, i)
        here = slice(i * HEAD_DIM, (i + 1) * HEAD_DIM)
        nt, nn, tn = ((1,), (1,)), ((1,), (0,)), ((0,), (0,))
        from_state = dot(ag, s_ref[i], nt)
        g00 = lower(dot(ag[top], v[top], nt))
        g10 = dot(ag[low], v[top], nt).astype(BF16)
        g11 = lower(dot(ag[low], v[low], nt))
        qg_ref[top, here] = (dot(g00, k[top], nn) + from_state[top]).astype(BF16)
        qg_ref[low, here] = (dot(g10, k[top], nn) + dot(g11, k[low], nn) + from_state[low]).astype(BF16)
        kg_ref[top, here] = dot(g00, q[top], tn) + dot(g10, q[low], tn)
        kg_ref[low, here] = dot(g11, q[low], tn)
        a00 = lower(dot(q[top], k[top], nt))
        a10 = dot(q[low], k[top], nt).astype(BF16)
        a11 = lower(dot(q[low], k[low], nt))
        vg_ref[top, here] = dot(a00, ag[top], tn) + dot(a10, ag[low], tn)
        vg_ref[low, here] = dot(a11, ag[low], tn)


def inner_grads(queries, keys, values, attn_grad, state, pair):
    tokens, channels = queries.shape
    spec = pl.BlockSpec((tokens, pair * HEAD_DIM), lambda b: (0, b))
    return pl.pallas_call(
        inner_grad_kernel,
        grid=(channels // (pair * HEAD_DIM),),
        in_specs=[spec] * 4 + [pl.BlockSpec((pair, HEAD_DIM, HEAD_DIM), lambda b: (b, 0, 0))],
        out_specs=[spec] * 3,
        out_shape=[jax.ShapeDtypeStruct((tokens, channels), t) for t in (BF16, F32, F32)],
        compiler_params=params(56),
        cost_estimate=pl.CostEstimate(
            flops=8 * tokens * tokens * channels, bytes_accessed=18 * tokens * channels, transcendentals=0
        ),
        name="inner_grads",
    )(queries, keys, values, attn_grad, state)


def outer_grad_kernel(k_ref, v_ref, r_ref, kin_ref, vin_ref, kg_ref, vg_ref):
    for i in range(r_ref.shape[0]):
        here = slice(i * HEAD_DIM, (i + 1) * HEAD_DIM)
        rev = r_ref[i]
        kg_ref[:, here] = (head(kin_ref, i) + dot(head(v_ref, i), rev, ((1,), (1,)))).astype(BF16)
        vg_ref[:, here] = (head(vin_ref, i) + dot(head(k_ref, i), rev, ((1,), (0,)))).astype(BF16)


def outer_grads(keys, values, rev, key_in, value_in, pair):
    tokens, channels = keys.shape
    spec = pl.BlockSpec((tokens, pair * HEAD_DIM), lambda b: (0, b))
    return pl.pallas_call(
        outer_grad_kernel,
        grid=(channels // (pair * HEAD_DIM),),
        in_specs=[spec] * 2 + [pl.BlockSpec((pair, HEAD_DIM, HEAD_DIM), lambda b: (b, 0, 0))] + [spec] * 2,
        out_specs=[spec] * 2,
        out_shape=[jax.ShapeDtypeStruct((tokens, channels), BF16)] * 2,
        compiler_params=params(56),
        cost_estimate=pl.CostEstimate(
            flops=4 * tokens * channels * HEAD_DIM, bytes_accessed=16 * tokens * channels, transcendentals=0
        ),
        name="outer_grads",
    )(keys, values, rev, key_in, value_in)


def running_kernel(reverse, x_ref, o_ref):
    count = x_ref.shape[0]
    total = jnp.zeros(x_ref.shape[1:], F32)
    for place in range(count)[:: -1 if reverse else 1]:
        o_ref[place] = total.astype(BF16)
        total = total + x_ref[place].astype(F32)


def running(rows, reverse):
    return pl.pallas_call(
        functools.partial(running_kernel, reverse),
        out_shape=jax.ShapeDtypeStruct(rows.shape, BF16),
        name="running_sums",
    )(rows)


def merge_kernel(turns, *refs):
    count = len(turns)
    for (axis, bit, start, stop, at), out_ref in zip(turns, refs[-count:]):
        place = (lax.axis_index(axis) // bit) % 2
        out_ref[:, pl.ds(place, 1)] = refs[2 * at][:, :, start:stop][:, None]
        out_ref[:, pl.ds(1 - place, 1)] = refs[2 * at + 1][:, :, start:stop][:, None]


def merge(turns, *pairs):
    shapes = [pairs[2 * at].shape for *_, at in turns]
    return pl.pallas_call(
        functools.partial(merge_kernel, turns),
        out_shape=[
            jax.ShapeDtypeStruct((shape[0], 2, shape[1], stop - start), BF16)
            for shape, (_, _, start, stop, _) in zip(shapes, turns)
        ],
        compiler_params=pltpu.CompilerParams(vmem_limit_bytes=24 * MIB),
        cost_estimate=pl.CostEstimate(
            flops=0, bytes_accessed=4 * sum(p.size for p in pairs), transcendentals=0
        ),
        name="merge",
    )(*pairs)


def column_groups(wide):
    tiles = wide // 128
    cuts = [0, (tiles + 2) // 3, (tiles + 2) // 3 + (tiles + 1) // 3, tiles]
    return [(128 * a, 128 * b) for a, b in zip(cuts, cuts[1:])]


def bit_orders():
    seq, dp = bits_of("seq"), bits_of("dp")
    rest = [("seq", bit) for bit in seq[:-1]] + [("dp", bit) for bit in dp[1:]]
    return ("seq", seq[-1]), [rest[k:] + rest[:k] for k in range(3)]


def canonical():
    return [("dp", bit) for bit in bits_of("dp")[:0:-1]] + [("seq", bit) for bit in bits_of("seq")[::-1]]


def whole_projection(weight):
    dp_count, seq_count = lax.axis_size("dp"), lax.axis_size("seq")
    rows, wide = weight.shape
    whole = lax.all_gather(weight, ("dp", "seq"), axis=0, tiled=True)
    whole = whole.reshape(dp_count // 2, 2, rows * seq_count, wide)
    core = has("dp", 1)
    return (
        [lax.dynamic_index_in_dim(whole, core, 1, keepdims=False)],
        [lax.dynamic_index_in_dim(whole, 1 - core, 1, keepdims=False)],
    )


def gather_send(parts, done, stage):
    _, orders = bit_orders()
    places = canonical()
    mines, theirs, turns = [], [], []
    for g, order in enumerate(orders):
        axis, bit = order[::-1][stage]
        before = [b for b in done[g] if places.index(b) < places.index((axis, bit))]
        wide = parts[g].shape[-1]
        mine = parts[g].reshape((1 << len(before), -1, wide))
        mines.append(mine)
        theirs.append(lax.ppermute(mine, axis, flip(axis, bit)))
        turns.append((axis, bit, 0, wide, g))
        done[g].append((axis, bit))
    return turns, mines, theirs


def gather_merge(turns, mines, theirs):
    pairs = [x for pair in zip(mines, theirs) for x in pair]
    return list(merge(turns, *pairs))


def added(keep, got):
    return (keep.astype(F32) + got.astype(F32)).astype(BF16)


def halves(x, places, bit):
    at = places.index(bit)
    mine = has(*bit)
    keep = lax.dynamic_index_in_dim(x, mine, at, keepdims=False)
    send = lax.dynamic_index_in_dim(x, 1 - mine, at, keepdims=False)
    return keep, send, [b for b in places if b != bit]


def scatter_first(keep, got, rows):
    places = canonical()
    wide = keep.shape[-1]
    split = (2,) * len(places) + (rows, wide)
    keep, got = keep.reshape(split), got.reshape(split)
    return [(added(keep[..., a:b], got[..., a:b]), places) for a, b in column_groups(wide)]


def scatter_send(xs, stage):
    mines, gots, lefts = [], [], []
    for (x, places), order in zip(xs, bit_orders()[1]):
        axis, bit = order[stage]
        mine, theirs, left = halves(x, places, (axis, bit))
        mines.append(mine)
        gots.append(lax.ppermute(theirs, axis, flip(axis, bit)))
        lefts.append(left)
    return mines, gots, lefts


def scatter_last(xs):
    far, _ = bit_orders()
    ends = [halves(x, places, far) for x, places in xs]
    got = lax.ppermute(jnp.concatenate([e[1] for e in ends], axis=-1), far[0], flip(*far))
    return jnp.concatenate([e[0] for e in ends], axis=-1), got


def total_of(x):
    count = lax.axis_size(("dp", "seq"))
    terms = jnp.broadcast_to(x[None], (count,) + x.shape)
    return jnp.sum(lax.all_to_all(terms, ("dp", "seq"), 0, 0, tiled=True), axis=0)


def together(*xs):
    return lax.optimization_barrier(xs)


def exchange(x, axis):
    rows = x.reshape((lax.axis_size(axis), -1, x.shape[-1]))
    return lax.all_to_all(rows, axis, 0, 0, tiled=True)


def shards(queries, keys, values, out_grad, out_weight, gain):
    tokens, channels = queries.shape[1:]
    assert tokens == BLOCK
    dp_count, seq_count = lax.axis_size("dp"), lax.axis_size("seq")
    pair = channels // dp_count // HEAD_DIM
    q, k, v, og = queries[0], keys[0], values[0], out_grad[0]
    gain_row = gain.reshape(1, channels)
    pos = jnp.stack([lax.axis_index("dp"), lax.axis_index("seq")]).astype(jnp.int32)
    rows, wide = out_weight.shape
    far, orders = bit_orders()
    stages = len(orders[0])
    by_bits = rows % 16 == 0

    kv = key_value_sums(k, v, pair)
    if by_bits:
        theirs = lax.ppermute(out_weight, far[0], flip(*far))
        kv, theirs = together(kv, theirs)
        turns = [(*far, start, stop, 0) for start, stop in column_groups(wide)]
        done = [[far] for _ in turns]
        parts = list(merge(turns, out_weight[None], theirs[None]))
    chain = [
        lambda: exchange(kv, "seq"),
        lambda: exchange(running(chained[0], False), "seq"),
        lambda: intra_outputs(q, k, v, pair),
    ]
    chained = []
    for stage in range(max(stages, len(chain)) if by_bits else len(chain)):
        sent = by_bits and stage < stages
        if sent:
            turns, mines, theirs = gather_send(parts, done, stage)
        if stage < len(chain):
            chained.append(chain[stage]())
        if sent:
            chained[-1], theirs = together(chained[-1], theirs)
            parts = gather_merge(turns, mines, theirs)
    _, state, intra = chained
    state = state.reshape(kv.shape)
    if by_bits:
        mine = [p.reshape(dp_count // 2, rows * seq_count, p.shape[-1]) for p in parts]
        other = [lax.ppermute(p, "dp", flip("dp", 1)) for p in mine]
    else:
        mine, other = whole_projection(out_weight)
    outputs, send, keep = weight_parts(pos, q, state, intra, gain_row, og, pair)
    send, other = together(send, other)

    got = lax.ppermute(send, "dp", flip("dp", 1))
    attn_grad, gain_part, qg = attn_grads(pos, q, outputs, gain_row, og, mine, other, pair)
    qg, got = together(qg, got)
    xs = scatter_first(keep, got, rows)
    work = [
        lambda: exchange(qg, "seq"),
        lambda: exchange(running(results[0], True), "seq"),
        lambda: inner_grads(q, k, v, attn_grad, state, pair),
    ]
    results = []
    for stage in range(max(stages, len(work))):
        if stage < stages:
            mines, gots, lefts = scatter_send(xs, stage)
        if stage < len(work):
            results.append(work[stage]())
        if stage < stages:
            results[-1], gots = together(results[-1], gots)
            xs = [(added(m, g), left) for m, g, left in zip(mines, gots, lefts)]
    _, rev, (query_g, key_in, value_in) = results
    last, got = scatter_last(xs)
    gain_total = total_of(gain_part.reshape(channels))
    key_g, value_g = outer_grads(k, v, rev.reshape(kv.shape), key_in, value_in, pair)
    factor = 1.0 / jnp.sqrt(jnp.float32(tokens * dp_count * seq_count))
    out_shape = (1, tokens, channels)
    return (
        query_g.reshape(out_shape),
        key_g.reshape(out_shape),
        value_g.reshape(out_shape),
        (last.astype(F32) + got.astype(F32)) * factor,
        gain_total * factor,
    )


def solution(mesh):
    placed = (
        P("dp", "seq", None),
        P("dp", "seq", None),
        P("dp", "seq", None),
        P("dp", "seq", None),
        P(("dp", "seq"), None),
        P(),
    )
    return jax.shard_map(
        shards,
        mesh=mesh,
        in_specs=placed,
        out_specs=(
            P("dp", "seq", None),
            P("dp", "seq", None),
            P("dp", "seq", None),
            P(("dp", "seq"), None),
            P(),
        ),
        check_vma=False,
    )
```

```python
import functools

import jax
import jax.numpy as jnp
from jax import lax
from jax.experimental import pallas as pl
from jax.experimental.pallas import tpu as pltpu
from jax.sharding import Mesh
from jax.sharding import PartitionSpec as P

HEAD_DIM = 128
BLOCK = 512
MIB = 1 << 20

norm_eps = 1e-06

F32 = jnp.float32
BF16 = jnp.bfloat16


def dot(a, b, contract):
    return lax.dot_general(a, b, (contract, ((), ())), preferred_element_type=F32)


def params(mib, dims=1):
    return pltpu.CompilerParams(
        vmem_limit_bytes=mib * MIB, dimension_semantics=("arbitrary",) * dims
    )


def head(ref, i):
    return ref[:, i * HEAD_DIM : (i + 1) * HEAD_DIM]


def kv_kernel(k_ref, v_ref, o_ref):
    for i in range(o_ref.shape[0]):
        o_ref[i] = dot(head(k_ref, i), head(v_ref, i), ((0,), (0,))).astype(BF16)


def key_value_sums(keys, values, pair):
    tokens, channels = keys.shape
    width = pair * HEAD_DIM
    heads = channels // HEAD_DIM
    spec = pl.BlockSpec((tokens, width), lambda b: (0, b))
    return pl.pallas_call(
        kv_kernel,
        grid=(heads // pair,),
        in_specs=[spec, spec],
        out_specs=pl.BlockSpec((pair, HEAD_DIM, HEAD_DIM), lambda b: (b, 0, 0)),
        out_shape=jax.ShapeDtypeStruct((heads, HEAD_DIM, HEAD_DIM), BF16),
        compiler_params=params(20),
        cost_estimate=pl.CostEstimate(
            flops=2 * tokens * channels * HEAD_DIM, bytes_accessed=4 * tokens * channels, transcendentals=0
        ),
        name="key_value_sums",
    )(keys, values)


def lower(x):
    rows = lax.broadcasted_iota(jnp.int32, x.shape, 0)
    cols = lax.broadcasted_iota(jnp.int32, x.shape, 1)
    return jnp.where(cols <= rows, x, 0.0).astype(BF16)


def intra_kernel(q_ref, k_ref, v_ref, o_ref):
    half = q_ref.shape[0] // 2
    for i in range(o_ref.shape[1] // HEAD_DIM):
        q, k, v = head(q_ref, i), head(k_ref, i), head(v_ref, i)
        here = slice(i * HEAD_DIM, (i + 1) * HEAD_DIM)
        top = lower(dot(q[:half], k[:half], ((1,), (1,))))
        o_ref[:half, here] = dot(top, v[:half], ((1,), (0,)))
        left = dot(q[half:], k[:half], ((1,), (1,))).astype(BF16)
        right = lower(dot(q[half:], k[half:], ((1,), (1,))))
        o_ref[half:, here] = dot(left, v[:half], ((1,), (0,))) + dot(right, v[half:], ((1,), (0,)))


def intra_outputs(queries, keys, values, pair):
    tokens, channels = keys.shape
    spec = pl.BlockSpec((tokens, pair * HEAD_DIM), lambda b: (0, b))
    return pl.pallas_call(
        intra_kernel,
        grid=(channels // (pair * HEAD_DIM),),
        in_specs=[spec] * 3,
        out_specs=spec,
        out_shape=jax.ShapeDtypeStruct((tokens, channels), F32),
        compiler_params=params(20),
        cost_estimate=pl.CostEstimate(
            flops=4 * tokens * tokens * channels, bytes_accessed=10 * tokens * channels, transcendentals=0
        ),
        name="intra_outputs",
    )(queries, keys, values)


def rms_inverse(x):
    return lax.rsqrt(jnp.mean(x * x, axis=-1, keepdims=True) + norm_eps)


def unit_kernel(pos_ref, q_ref, s_ref, intra_ref, gain_ref, og_ref, out_ref, send_ref, keep_ref):
    units = []
    for i in range(s_ref.shape[0]):
        x = head(intra_ref, i) + dot(head(q_ref, i), s_ref[i], ((1,), (0,)))
        out_ref[:, i * HEAD_DIM : (i + 1) * HEAD_DIM] = x
        units.append((x * rms_inverse(x) * head(gain_ref, i)).astype(BF16))
    unit = jnp.concatenate(units, axis=1) if len(units) > 1 else units[0]
    part = dot(unit, og_ref[...], ((0,), (0,))).astype(BF16)

    @pl.when(pl.program_id(0) == 0)
    def _():
        send_ref[0] = part

    @pl.when(pl.program_id(0) == 1)
    def _():
        keep_ref[0] = part


def weight_parts(pos, queries, state, intra, gain, out_grad, pair):
    tokens, channels = queries.shape
    width = pair * HEAD_DIM
    count = channels // width // 2
    wide = out_grad.shape[1]

    def block(c, y, pos_ref):
        return 2 * y + lax.rem(pos_ref[0] + 1 + c, 2)

    cols = pl.BlockSpec((tokens, width), lambda c, y, pos_ref: (0, block(c, y, pos_ref)))
    part = jax.ShapeDtypeStruct((count, width, wide), BF16)
    return pl.pallas_call(
        unit_kernel,
        grid_spec=pltpu.PrefetchScalarGridSpec(
            num_scalar_prefetch=1,
            grid=(2, count),
            in_specs=[
                cols,
                pl.BlockSpec((pair, HEAD_DIM, HEAD_DIM), lambda c, y, p: (block(c, y, p), 0, 0)),
                cols,
                pl.BlockSpec((1, width), lambda c, y, p: (0, block(c, y, p))),
                pl.BlockSpec((tokens, wide), lambda c, y, p: (0, 0)),
            ],
            out_specs=[
                cols,
                pl.BlockSpec((1, width, wide), lambda c, y, p: (jnp.where(c == 0, y, count - 1), 0, 0)),
                pl.BlockSpec((1, width, wide), lambda c, y, p: (jnp.where(c == 0, 0, y), 0, 0)),
            ],
        ),
        out_shape=[jax.ShapeDtypeStruct((tokens, channels), F32), part, part],
        compiler_params=params(20, 2),
        cost_estimate=pl.CostEstimate(
            flops=2 * tokens * channels * wide,
            bytes_accessed=10 * tokens * channels + 2 * tokens * wide + 2 * channels * wide,
            transcendentals=0,
        ),
        name="weight_parts",
    )(pos, queries, state, intra, gain, out_grad)


def attn_grad_kernel(pos_ref, q_ref, o_ref, gain_ref, og_ref, mine_ref, other_ref, ag_ref, gg_ref, qg_ref, ug_ref):
    def project(ref):
        weight = jnp.concatenate(
            [ref[0, x, z] for z in range(ref.shape[2]) for x in range(ref.shape[1])], axis=0
        )
        ug_ref[...] = dot(og_ref[...], weight, ((1,), (1,)))

    @pl.when(pl.program_id(0) == 0)
    def _():
        project(mine_ref)

    @pl.when(pl.program_id(0) == 1)
    def _():
        project(other_ref)

    for i in range(qg_ref.shape[0]):
        here = slice(i * HEAD_DIM, (i + 1) * HEAD_DIM)
        x = head(o_ref, i)
        inverse = rms_inverse(x)
        normed = x * inverse
        ug = head(ug_ref, i)
        gg_ref[:, here] = jnp.sum(ug * normed, axis=0, keepdims=True)
        scaled = ug * head(gain_ref, i)
        middle = jnp.mean(scaled * normed, axis=-1, keepdims=True)
        ag = ((scaled - normed * middle) * inverse).astype(BF16)
        ag_ref[:, here] = ag
        qg_ref[i] = dot(head(q_ref, i), ag, ((0,), (0,))).astype(BF16)


def attn_grads(pos, queries, outputs, gain, out_grad, mine, other, pair):
    tokens, channels = queries.shape
    width = pair * HEAD_DIM
    count = channels // width // 2
    wide = out_grad.shape[1]
    heads = channels // HEAD_DIM

    def block(c, y, pos_ref):
        return 2 * y + lax.rem(pos_ref[0] + c, 2)

    cols = pl.BlockSpec((tokens, width), lambda c, y, p: (0, block(c, y, p)))
    row = pl.BlockSpec((1, width), lambda c, y, p: (0, block(c, y, p)))
    states = pl.BlockSpec((pair, HEAD_DIM, HEAD_DIM), lambda c, y, p: (block(c, y, p), 0, 0))
    piece = (1,) + mine.shape[1:]
    return pl.pallas_call(
        attn_grad_kernel,
        grid_spec=pltpu.PrefetchScalarGridSpec(
            num_scalar_prefetch=1,
            grid=(2, count),
            in_specs=[
                cols,
                cols,
                row,
                pl.BlockSpec((tokens, wide), lambda c, y, p: (0, 0)),
                pl.BlockSpec(piece, lambda c, y, p: (jnp.where(c == 0, y, count - 1), 0, 0, 0, 0)),
                pl.BlockSpec(piece, lambda c, y, p: (jnp.where(c == 0, 0, y), 0, 0, 0, 0)),
            ],
            out_specs=[cols, row, states],
            scratch_shapes=[pltpu.VMEM((tokens, width), F32)],
        ),
        out_shape=[
            jax.ShapeDtypeStruct((tokens, channels), BF16),
            jax.ShapeDtypeStruct((1, channels), F32),
            jax.ShapeDtypeStruct((heads, HEAD_DIM, HEAD_DIM), BF16),
        ],
        compiler_params=params(20, 2),
        cost_estimate=pl.CostEstimate(
            flops=2 * tokens * channels * wide,
            bytes_accessed=8 * tokens * channels + 2 * tokens * wide + 2 * channels * wide,
            transcendentals=0,
        ),
        name="attn_grads",
    )(pos, queries, outputs, gain, out_grad, mine, other)


def inner_grad_kernel(q_ref, k_ref, v_ref, ag_ref, s_ref, qg_ref, kg_ref, vg_ref):
    half = q_ref.shape[0] // 2
    top, low = slice(0, half), slice(half, 2 * half)
    for i in range(s_ref.shape[0]):
        q, k, v, ag = head(q_ref, i), head(k_ref, i), head(v_ref, i), head(ag_ref, i)
        here = slice(i * HEAD_DIM, (i + 1) * HEAD_DIM)
        nt, nn, tn = ((1,), (1,)), ((1,), (0,)), ((0,), (0,))
        from_state = dot(ag, s_ref[i], nt)
        g00 = lower(dot(ag[top], v[top], nt))
        g10 = dot(ag[low], v[top], nt).astype(BF16)
        g11 = lower(dot(ag[low], v[low], nt))
        qg_ref[top, here] = (dot(g00, k[top], nn) + from_state[top]).astype(BF16)
        qg_ref[low, here] = (dot(g10, k[top], nn) + dot(g11, k[low], nn) + from_state[low]).astype(BF16)
        kg_ref[top, here] = dot(g00, q[top], tn) + dot(g10, q[low], tn)
        kg_ref[low, here] = dot(g11, q[low], tn)
        a00 = lower(dot(q[top], k[top], nt))
        a10 = dot(q[low], k[top], nt).astype(BF16)
        a11 = lower(dot(q[low], k[low], nt))
        vg_ref[top, here] = dot(a00, ag[top], tn) + dot(a10, ag[low], tn)
        vg_ref[low, here] = dot(a11, ag[low], tn)


def inner_grads(queries, keys, values, attn_grad, state, pair):
    tokens, channels = queries.shape
    spec = pl.BlockSpec((tokens, pair * HEAD_DIM), lambda b: (0, b))
    return pl.pallas_call(
        inner_grad_kernel,
        grid=(channels // (pair * HEAD_DIM),),
        in_specs=[spec] * 4 + [pl.BlockSpec((pair, HEAD_DIM, HEAD_DIM), lambda b: (b, 0, 0))],
        out_specs=[spec] * 3,
        out_shape=[jax.ShapeDtypeStruct((tokens, channels), t) for t in (BF16, F32, F32)],
        compiler_params=params(20),
        cost_estimate=pl.CostEstimate(
            flops=8 * tokens * tokens * channels, bytes_accessed=18 * tokens * channels, transcendentals=0
        ),
        name="inner_grads",
    )(queries, keys, values, attn_grad, state)


def outer_grad_kernel(k_ref, v_ref, r_ref, kin_ref, vin_ref, kg_ref, vg_ref):
    for i in range(r_ref.shape[0]):
        here = slice(i * HEAD_DIM, (i + 1) * HEAD_DIM)
        rev = r_ref[i]
        kg_ref[:, here] = (head(kin_ref, i) + dot(head(v_ref, i), rev, ((1,), (1,)))).astype(BF16)
        vg_ref[:, here] = (head(vin_ref, i) + dot(head(k_ref, i), rev, ((1,), (0,)))).astype(BF16)


def outer_grads(keys, values, rev, key_in, value_in, pair):
    tokens, channels = keys.shape
    spec = pl.BlockSpec((tokens, pair * HEAD_DIM), lambda b: (0, b))
    return pl.pallas_call(
        outer_grad_kernel,
        grid=(channels // (pair * HEAD_DIM),),
        in_specs=[spec] * 2 + [pl.BlockSpec((pair, HEAD_DIM, HEAD_DIM), lambda b: (b, 0, 0))] + [spec] * 2,
        out_specs=[spec] * 2,
        out_shape=[jax.ShapeDtypeStruct((tokens, channels), BF16)] * 2,
        compiler_params=params(20),
        cost_estimate=pl.CostEstimate(
            flops=4 * tokens * channels * HEAD_DIM, bytes_accessed=16 * tokens * channels, transcendentals=0
        ),
        name="outer_grads",
    )(keys, values, rev, key_in, value_in)


def running_kernel(reverse, x_ref, o_ref):
    count = x_ref.shape[0]
    total = jnp.zeros(x_ref.shape[1:], F32)
    for place in range(count)[:: -1 if reverse else 1]:
        o_ref[place] = total.astype(BF16)
        total = total + x_ref[place].astype(F32)


def running(rows, reverse):
    return pl.pallas_call(
        functools.partial(running_kernel, reverse),
        out_shape=jax.ShapeDtypeStruct(rows.shape, BF16),
        name="running_sums",
    )(rows)


ALL = ("y", "core", "z", "x")
SEQ = ("z", "x")
PLANE = ("y", "x")


def other_core(x):
    return lax.ppermute(x, "core", [(0, 1), (1, 0)])


def exchange(x, axis):
    rows = x.reshape((lax.axis_size(axis), -1) + x.shape[-1:])
    return lax.all_to_all(rows, axis, 0, 0, tiled=True)


def everyones(x, axis):
    return lax.all_to_all(jnp.broadcast_to(x[None], (lax.axis_size(axis),) + x.shape), axis, 0, 0, tiled=True)


def by_plane(weight, sizes):
    rows, wide = weight.shape[-2:]
    weight = weight.reshape((sizes["y"], sizes["x"], sizes["z"], rows, wide))
    if rows % 16:
        weight = weight.transpose(0, 2, 1, 3, 4).reshape(sizes["y"], 1, 1, -1, wide)
    return weight


def added(*terms):
    total = terms[0].astype(F32)
    for term in terms[1:]:
        total = total + term.astype(F32)
    return total


def together(*xs):
    return lax.optimization_barrier(xs)


def shards(queries, keys, values, out_grad, out_weight, gain):
    tokens, channels = queries.shape[1:]
    assert tokens == BLOCK
    sizes = {name: lax.axis_size(name) for name in ALL}
    devices = lax.axis_size(ALL)
    dp_index = lax.axis_index(("y", "core"))
    pair = channels // (sizes["y"] * sizes["core"]) // HEAD_DIM
    q, k, v, og = queries[0], keys[0], values[0], out_grad[0]
    gain_row = gain.reshape(1, channels)
    pos = dp_index.reshape(1).astype(jnp.int32)
    rows, wide = out_weight.shape

    weight_z = everyones(out_weight, "z")
    kv = key_value_sums(k, v, pair)
    sent = exchange(kv, SEQ)
    intra = intra_outputs(q, k, v, pair)
    sums, weight_z = together(running(sent, False), weight_z)
    state = exchange(sums, SEQ).reshape(kv.shape)
    weight = everyones(weight_z, PLANE)
    outputs, send, keep = weight_parts(pos, q, state, intra, gain_row, og, pair)
    got = other_core(send)
    mine = by_plane(weight, sizes)
    part = added(keep, got).astype(BF16)
    part = part.reshape(sizes["y"], sizes["z"], sizes["x"], rows, wide).transpose(0, 2, 1, 3, 4)
    part = part.reshape(sizes["y"] * sizes["x"], sizes["z"], rows, wide)
    part, mine = together(part, mine)
    other = other_core(mine)
    attn_grad, gain_part, qg = attn_grads(pos, q, outputs, gain_row, og, mine, other, pair)
    part = lax.all_to_all(part, PLANE, 0, 0, tiled=True)
    sent = exchange(qg, SEQ)
    query_g, key_in, value_in = inner_grads(q, k, v, attn_grad, state, pair)
    rev = exchange(running(sent, True), SEQ).reshape(kv.shape)
    part = added(*[part[i] for i in range(part.shape[0])]).astype(BF16)
    part = lax.all_to_all(part, "z", 0, 0, tiled=True)
    gain_parts = everyones(gain_part.reshape(channels), ALL)
    key_g, value_g = outer_grads(k, v, rev, key_in, value_in, pair)
    factor = 1.0 / jnp.sqrt(jnp.float32(tokens * devices))
    out_shape = (1, tokens, channels)
    return (
        query_g.reshape(out_shape),
        key_g.reshape(out_shape),
        value_g.reshape(out_shape),
        added(*[part[i] for i in range(part.shape[0])]) * factor,
        jnp.sum(gain_parts, axis=0) * factor,
    )


def solution(mesh):
    dp_count, seq_count = mesh.shape["dp"], mesh.shape["seq"]
    finer = Mesh(mesh.devices.reshape(dp_count // 2, 2, seq_count // 2, 2), ALL)
    tokens = P(("y", "core"), ("z", "x"), None)
    rows = P(ALL, None)
    return jax.shard_map(
        shards,
        mesh=finer,
        in_specs=(tokens, tokens, tokens, tokens, rows, P()),
        out_specs=(tokens, tokens, tokens, rows, P()),
        check_vma=False,
    )
```

```python
import functools

import jax
import jax.numpy as jnp
from jax import lax
from jax.experimental import pallas as pl
from jax.experimental.pallas import tpu as pltpu
from jax.sharding import Mesh
from jax.sharding import PartitionSpec as P

HEAD_DIM = 128
BLOCK = 512
MIB = 1 << 20

norm_eps = 1e-06

F32 = jnp.float32
BF16 = jnp.bfloat16


def dot(a, b, contract):
    return lax.dot_general(a, b, (contract, ((), ())), preferred_element_type=F32)


def params(mib, dims=1):
    return pltpu.CompilerParams(
        vmem_limit_bytes=mib * MIB, dimension_semantics=("arbitrary",) * dims
    )


ROW_BLOCKS = 4


def row_blocks(tokens, wide):
    return [
        pl.BlockSpec((tokens // ROW_BLOCKS, wide), lambda c, y, p, r=r: (r, 0)) for r in range(ROW_BLOCKS)
    ]


def head(ref, i):
    return ref[:, i * HEAD_DIM : (i + 1) * HEAD_DIM]


def kv_kernel(k_ref, v_ref, o_ref):
    for i in range(o_ref.shape[0]):
        o_ref[i] = dot(head(k_ref, i), head(v_ref, i), ((0,), (0,))).astype(BF16)


def key_value_sums(keys, values, pair):
    tokens, channels = keys.shape
    width = pair * HEAD_DIM
    heads = channels // HEAD_DIM
    spec = pl.BlockSpec((tokens, width), lambda b: (0, b))
    return pl.pallas_call(
        kv_kernel,
        grid=(heads // pair,),
        in_specs=[spec, spec],
        out_specs=pl.BlockSpec((pair, HEAD_DIM, HEAD_DIM), lambda b: (b, 0, 0)),
        out_shape=jax.ShapeDtypeStruct((heads, HEAD_DIM, HEAD_DIM), BF16),
        compiler_params=params(56),
        cost_estimate=pl.CostEstimate(
            flops=2 * tokens * channels * HEAD_DIM, bytes_accessed=4 * tokens * channels, transcendentals=0
        ),
        name="key_value_sums",
    )(keys, values)


def lower(x):
    rows = lax.broadcasted_iota(jnp.int32, x.shape, 0)
    cols = lax.broadcasted_iota(jnp.int32, x.shape, 1)
    return jnp.where(cols <= rows, x, 0.0).astype(BF16)


def intra_kernel(q_ref, k_ref, v_ref, o_ref):
    half = q_ref.shape[0] // 2
    for i in range(o_ref.shape[1] // HEAD_DIM):
        q, k, v = head(q_ref, i), head(k_ref, i), head(v_ref, i)
        here = slice(i * HEAD_DIM, (i + 1) * HEAD_DIM)
        top = lower(dot(q[:half], k[:half], ((1,), (1,))))
        o_ref[:half, here] = dot(top, v[:half], ((1,), (0,)))
        left = dot(q[half:], k[:half], ((1,), (1,))).astype(BF16)
        right = lower(dot(q[half:], k[half:], ((1,), (1,))))
        o_ref[half:, here] = dot(left, v[:half], ((1,), (0,))) + dot(right, v[half:], ((1,), (0,)))


def intra_outputs(queries, keys, values, pair):
    tokens, channels = keys.shape
    spec = pl.BlockSpec((tokens, pair * HEAD_DIM), lambda b: (0, b))
    return pl.pallas_call(
        intra_kernel,
        grid=(channels // (pair * HEAD_DIM),),
        in_specs=[spec] * 3,
        out_specs=spec,
        out_shape=jax.ShapeDtypeStruct((tokens, channels), F32),
        compiler_params=params(56),
        cost_estimate=pl.CostEstimate(
            flops=4 * tokens * tokens * channels, bytes_accessed=10 * tokens * channels, transcendentals=0
        ),
        name="intra_outputs",
    )(queries, keys, values)


def rms_inverse(x):
    return lax.rsqrt(jnp.mean(x * x, axis=-1, keepdims=True) + norm_eps)


def unit_kernel(pos_ref, q_ref, s_ref, intra_ref, gain_ref, *refs):
    *og_refs, out_ref, send_ref, keep_ref = refs
    units = []
    for i in range(s_ref.shape[0]):
        x = head(intra_ref, i) + dot(head(q_ref, i), s_ref[i], ((1,), (0,)))
        out_ref[:, i * HEAD_DIM : (i + 1) * HEAD_DIM] = x
        units.append((x * rms_inverse(x) * head(gain_ref, i)).astype(BF16))
    unit = jnp.concatenate(units, axis=1) if len(units) > 1 else units[0]
    og = jnp.concatenate([og_ref[...] for og_ref in og_refs], axis=0)
    part = dot(unit, og, ((0,), (0,))).astype(BF16)

    @pl.when(pl.program_id(0) == 0)
    def _():
        send_ref[0] = part

    @pl.when(pl.program_id(0) == 1)
    def _():
        keep_ref[0] = part


def weight_parts(pos, queries, state, intra, gain, out_grad, pair):
    tokens, channels = queries.shape
    width = pair * HEAD_DIM
    count = channels // width // 2
    wide = out_grad.shape[1]

    def block(c, y, pos_ref):
        return 2 * y + lax.rem(pos_ref[0] + 1 + c, 2)

    cols = pl.BlockSpec((tokens, width), lambda c, y, pos_ref: (0, block(c, y, pos_ref)))
    part = jax.ShapeDtypeStruct((count, width, wide), BF16)
    return pl.pallas_call(
        unit_kernel,
        grid_spec=pltpu.PrefetchScalarGridSpec(
            num_scalar_prefetch=1,
            grid=(2, count),
            in_specs=[
                cols,
                pl.BlockSpec((pair, HEAD_DIM, HEAD_DIM), lambda c, y, p: (block(c, y, p), 0, 0)),
                cols,
                pl.BlockSpec((1, width), lambda c, y, p: (0, block(c, y, p))),
            ]
            + row_blocks(tokens, wide),
            out_specs=[
                cols,
                pl.BlockSpec((1, width, wide), lambda c, y, p: (jnp.where(c == 0, y, count - 1), 0, 0)),
                pl.BlockSpec((1, width, wide), lambda c, y, p: (jnp.where(c == 0, 0, y), 0, 0)),
            ],
        ),
        out_shape=[jax.ShapeDtypeStruct((tokens, channels), F32), part, part],
        compiler_params=params(56, 2),
        cost_estimate=pl.CostEstimate(
            flops=2 * tokens * channels * wide,
            bytes_accessed=10 * tokens * channels + 2 * tokens * wide + 2 * channels * wide,
            transcendentals=0,
        ),
        name="weight_parts",
    )(pos, queries, state, intra, gain, *[out_grad] * ROW_BLOCKS)


def attn_grad_kernel(pos_ref, q_ref, o_ref, gain_ref, *refs):
    *og_refs, mine_ref, other_ref, ag_ref, gg_ref, qg_ref, ug_ref = refs

    def project(ref):
        start = 0
        for og_ref in og_refs:
            stop = start + og_ref.shape[0]
            ug_ref[start:stop] = dot(og_ref[...], ref[0], ((1,), (1,)))
            start = stop

    @pl.when(pl.program_id(0) == 0)
    def _():
        project(mine_ref)

    @pl.when(pl.program_id(0) == 1)
    def _():
        project(other_ref)

    for i in range(qg_ref.shape[0]):
        here = slice(i * HEAD_DIM, (i + 1) * HEAD_DIM)
        x = head(o_ref, i)
        inverse = rms_inverse(x)
        normed = x * inverse
        ug = head(ug_ref, i)
        gg_ref[:, here] = jnp.sum(ug * normed, axis=0, keepdims=True)
        scaled = ug * head(gain_ref, i)
        middle = jnp.mean(scaled * normed, axis=-1, keepdims=True)
        ag = ((scaled - normed * middle) * inverse).astype(BF16)
        ag_ref[:, here] = ag
        qg_ref[i] = dot(head(q_ref, i), ag, ((0,), (0,))).astype(BF16)


def attn_grads(pos, queries, outputs, gain, out_grad, mine, other, pair):
    tokens, channels = queries.shape
    width = pair * HEAD_DIM
    count = channels // width // 2
    wide = out_grad.shape[1]
    heads = channels // HEAD_DIM

    def block(c, y, pos_ref):
        return 2 * y + lax.rem(pos_ref[0] + c, 2)

    cols = pl.BlockSpec((tokens, width), lambda c, y, p: (0, block(c, y, p)))
    row = pl.BlockSpec((1, width), lambda c, y, p: (0, block(c, y, p)))
    states = pl.BlockSpec((pair, HEAD_DIM, HEAD_DIM), lambda c, y, p: (block(c, y, p), 0, 0))
    piece = (1,) + mine.shape[1:]
    return pl.pallas_call(
        attn_grad_kernel,
        grid_spec=pltpu.PrefetchScalarGridSpec(
            num_scalar_prefetch=1,
            grid=(2, count),
            in_specs=[
                cols,
                cols,
                row,
            ]
            + row_blocks(tokens, wide)
            + [
                pl.BlockSpec(piece, lambda c, y, p: (jnp.where(c == 0, y, count - 1), 0, 0)),
                pl.BlockSpec(piece, lambda c, y, p: (jnp.where(c == 0, 0, y), 0, 0)),
            ],
            out_specs=[cols, row, states],
            scratch_shapes=[pltpu.VMEM((tokens, width), F32)],
        ),
        out_shape=[
            jax.ShapeDtypeStruct((tokens, channels), BF16),
            jax.ShapeDtypeStruct((1, channels), F32),
            jax.ShapeDtypeStruct((heads, HEAD_DIM, HEAD_DIM), BF16),
        ],
        compiler_params=params(56, 2),
        cost_estimate=pl.CostEstimate(
            flops=2 * tokens * channels * wide,
            bytes_accessed=8 * tokens * channels + 2 * tokens * wide + 2 * channels * wide,
            transcendentals=0,
        ),
        name="attn_grads",
    )(pos, queries, outputs, gain, *[out_grad] * ROW_BLOCKS, mine, other)


NT, NN, TN = ((1,), (1,)), ((1,), (0,)), ((0,), (0,))


def query_grad_kernel(q_ref, k_ref, v_ref, ag_ref, s_ref, qg_ref, kg_ref):
    half = q_ref.shape[0] // 2
    top, low = slice(0, half), slice(half, 2 * half)
    for i in range(s_ref.shape[0]):
        q, k, v, ag = head(q_ref, i), head(k_ref, i), head(v_ref, i), head(ag_ref, i)
        here = slice(i * HEAD_DIM, (i + 1) * HEAD_DIM)
        from_state = dot(ag, s_ref[i], NT)
        g00 = lower(dot(ag[top], v[top], NT))
        g10 = dot(ag[low], v[top], NT).astype(BF16)
        g11 = lower(dot(ag[low], v[low], NT))
        qg_ref[top, here] = (dot(g00, k[top], NN) + from_state[top]).astype(BF16)
        qg_ref[low, here] = (dot(g10, k[top], NN) + dot(g11, k[low], NN) + from_state[low]).astype(BF16)
        kg_ref[top, here] = dot(g00, q[top], TN) + dot(g10, q[low], TN)
        kg_ref[low, here] = dot(g11, q[low], TN)


def query_grads(queries, keys, values, attn_grad, state, pair):
    tokens, channels = queries.shape
    spec = pl.BlockSpec((tokens, pair * HEAD_DIM), lambda b: (0, b))
    return pl.pallas_call(
        query_grad_kernel,
        grid=(channels // (pair * HEAD_DIM),),
        in_specs=[spec] * 4 + [pl.BlockSpec((pair, HEAD_DIM, HEAD_DIM), lambda b: (b, 0, 0))],
        out_specs=[spec] * 2,
        out_shape=[jax.ShapeDtypeStruct((tokens, channels), t) for t in (BF16, F32)],
        compiler_params=params(56),
        cost_estimate=pl.CostEstimate(
            flops=6 * tokens * tokens * channels, bytes_accessed=14 * tokens * channels, transcendentals=0
        ),
        name="query_grads",
    )(queries, keys, values, attn_grad, state)


def key_value_grad_kernel(q_ref, k_ref, v_ref, ag_ref, r_ref, kin_ref, kg_ref, vg_ref):
    half = q_ref.shape[0] // 2
    top, low = slice(0, half), slice(half, 2 * half)
    for i in range(r_ref.shape[0]):
        q, k, v, ag = head(q_ref, i), head(k_ref, i), head(v_ref, i), head(ag_ref, i)
        here = slice(i * HEAD_DIM, (i + 1) * HEAD_DIM)
        rev = r_ref[i]
        kg_ref[:, here] = (head(kin_ref, i) + dot(v, rev, NT)).astype(BF16)
        a00 = lower(dot(q[top], k[top], NT))
        a10 = dot(q[low], k[top], NT).astype(BF16)
        a11 = lower(dot(q[low], k[low], NT))
        from_rev = dot(k, rev, NN)
        vg_ref[top, here] = (dot(a00, ag[top], TN) + dot(a10, ag[low], TN) + from_rev[top]).astype(BF16)
        vg_ref[low, here] = (dot(a11, ag[low], TN) + from_rev[low]).astype(BF16)


def key_value_grads(queries, keys, values, attn_grad, rev, key_in, pair):
    tokens, channels = keys.shape
    spec = pl.BlockSpec((tokens, pair * HEAD_DIM), lambda b: (0, b))
    return pl.pallas_call(
        key_value_grad_kernel,
        grid=(channels // (pair * HEAD_DIM),),
        in_specs=[spec] * 4 + [pl.BlockSpec((pair, HEAD_DIM, HEAD_DIM), lambda b: (b, 0, 0)), spec],
        out_specs=[spec] * 2,
        out_shape=[jax.ShapeDtypeStruct((tokens, channels), BF16)] * 2,
        compiler_params=params(56),
        cost_estimate=pl.CostEstimate(
            flops=5 * tokens * tokens * channels, bytes_accessed=16 * tokens * channels, transcendentals=0
        ),
        name="key_value_grads",
    )(queries, keys, values, attn_grad, rev, key_in)


def running_kernel(reverse, x_ref, o_ref):
    count = x_ref.shape[0]
    total = jnp.zeros(x_ref.shape[1:], F32)
    for place in range(count)[:: -1 if reverse else 1]:
        o_ref[place] = total.astype(BF16)
        total = total + x_ref[place].astype(F32)


def running(rows, reverse):
    return pl.pallas_call(
        functools.partial(running_kernel, reverse),
        out_shape=jax.ShapeDtypeStruct(rows.shape, BF16),
        name="running_sums",
    )(rows)


ALL = ("y", "core", "z", "x")
SEQ = ("z", "x")
PLANE = ("y", "x")


def exchange(x, axis):
    rows = x.reshape((lax.axis_size(axis), -1) + x.shape[-1:])
    return lax.all_to_all(rows, axis, 0, 0, tiled=True)


def everyones(x, axis):
    return lax.all_to_all(jnp.broadcast_to(x[None], (lax.axis_size(axis),) + x.shape), axis, 0, 0, tiled=True)


def flipped(x, axis, bit=1):
    return lax.ppermute(x, axis, [(i, i ^ bit) for i in range(lax.axis_size(axis))])


def added(*terms):
    total = terms[0].astype(F32)
    for term in terms[1:]:
        total = total + term.astype(F32)
    return total


def together(*xs):
    return lax.optimization_barrier(xs)


def small_call(kernel, out_shapes, *args):
    return pl.pallas_call(
        kernel,
        out_shape=[jax.ShapeDtypeStruct(shape, BF16) for shape in out_shapes],
        compiler_params=pltpu.CompilerParams(vmem_limit_bytes=24 * MIB),
        cost_estimate=pl.CostEstimate(
            flops=0, bytes_accessed=4 * sum(x.size for x in args), transcendentals=0
        ),
        name=kernel.__name__,
    )(*args)


def one(i):
    return pl.ds(i, 1)


def place(axis, bit=1):
    here = (lax.axis_index(axis) // bit) % 2
    return here, 1 - here


def merge_far(mine_ref, theirs_ref, out_ref):
    here, there = place("z", 2)
    out_ref[one(here)] = mine_ref[...][None]
    out_ref[one(there)] = theirs_ref[...][None]


def merge_near(mine_ref, theirs_ref, left_ref, right_ref):
    here, there = place("z")
    half = left_ref.shape[-1]
    for at, ref in ((here, mine_ref), (there, theirs_ref)):
        left_ref[:, one(at)] = ref[:, :, :half][:, None]
        right_ref[:, one(at)] = ref[:, :, half:][:, None]


def merge_sides(left_ref, left_got_ref, right_ref, right_got_ref, left_out_ref, right_out_ref):
    here, there = place("x")
    left_out_ref[:, one(here)] = left_ref[...][:, None]
    left_out_ref[:, one(there)] = left_got_ref[...][:, None]
    here, there = place("y")
    right_out_ref[one(here)] = right_ref[...][None]
    right_out_ref[one(there)] = right_got_ref[...][None]


def merge_all(left_ref, left_got_ref, right_ref, right_got_ref, out_ref):
    half = left_ref.shape[-1]
    here, there = place("y")
    out_ref[one(here), :, :, :, :half] = left_ref[...][None]
    out_ref[one(there), :, :, :, :half] = left_got_ref[...][None]
    here, there = place("x")
    out_ref[:, :, one(here), :, half:] = right_ref[...][:, :, None]
    out_ref[:, :, one(there), :, half:] = right_got_ref[...][:, :, None]


def total(a_ref, b_ref, *index):
    return (a_ref[index].astype(F32) + b_ref[index].astype(F32)).astype(BF16)


def split_first(keep_ref, got_ref, left_ref, right_ref, left_keep_ref, right_keep_ref):
    half = left_ref.shape[-1]
    here, there = place("y")
    every = slice(None)
    for at, ref in ((there, left_ref), (here, left_keep_ref)):
        ref[...] = total(keep_ref, got_ref, one(at), every, every, every, slice(0, half))[0]
    here, there = place("x")
    for at, ref in ((there, right_ref), (here, right_keep_ref)):
        ref[...] = total(keep_ref, got_ref, every, every, one(at), every, slice(half, 2 * half))[:, :, 0]


def split_second(left_ref, left_got_ref, right_ref, right_got_ref, left_out, right_out, left_keep, right_keep):
    here, there = place("x")
    for at, ref in ((there, left_out), (here, left_keep)):
        ref[...] = total(left_ref, left_got_ref, slice(None), one(at))[:, 0]
    here, there = place("y")
    for at, ref in ((there, right_out), (here, right_keep)):
        ref[...] = total(right_ref, right_got_ref, one(at))[0]


def join_sides(left_ref, left_got_ref, right_ref, right_got_ref, out_ref):
    half = left_ref.shape[-1]
    out_ref[:, :, :half] = total(left_ref, left_got_ref, slice(None))
    out_ref[:, :, half:] = total(right_ref, right_got_ref, slice(None))


def by_halves(sizes, rows, q, k, v, og, out_weight, gain_row, pos, pair):
    tokens, channels = q.shape
    wide = out_weight.shape[1]
    y, z, x, half = sizes["y"], sizes["z"], sizes["x"], wide // 2

    got = flipped(out_weight, "z", 2)
    kv = key_value_sums(k, v, pair)
    kv, got = together(kv, got)
    (weight,) = small_call(merge_far, [(2, rows, wide)], out_weight, got)

    got = flipped(weight, "z", 1)
    sent = exchange(kv, SEQ)
    intra = intra_outputs(q, k, v, pair)
    sent, intra, got = together(sent, intra, got)
    left, right = small_call(merge_near, [(2, 2, rows, half)] * 2, weight, got)
    left, right = left.reshape(z, rows, half), right.reshape(z, rows, half)

    left_got, right_got = flipped(left, "x"), flipped(right, "y")
    state = exchange(running(sent, False), SEQ).reshape(kv.shape)
    state, left_got, right_got = together(state, left_got, right_got)
    left, right = small_call(
        merge_sides, [(z, x, rows, half), (y, z, rows, half)], left, left_got, right, right_got
    )

    left_got, right_got = flipped(left, "y"), flipped(right, "x")
    outputs, send, keep = weight_parts(pos, q, state, intra, gain_row, og, pair)
    send, left_got, right_got = together(send, left_got, right_got)
    got = flipped(send, "core")
    (mine,) = small_call(merge_all, [(y, z, x, rows, wide)], left, left_got, right, right_got)
    mine = mine.reshape(y, -1, wide)
    other = flipped(mine, "core")

    split = (y, z, x, rows, wide)
    left, right, left_keep, right_keep = small_call(
        split_first,
        [(z, x, rows, half), (y, z, rows, half)] * 2,
        keep.reshape(split),
        got.reshape(split),
    )
    other, left, right = together(other, left, right)
    left_got, right_got = flipped(left, "y"), flipped(right, "x")
    attn_grad, gain_part, qg = attn_grads(pos, q, outputs, gain_row, og, mine, other, pair)
    qg, left_got, right_got = together(qg, left_got, right_got)

    sent = exchange(qg, SEQ)
    left, right, left_keep, right_keep = small_call(
        split_second, [(z, rows, half)] * 4, left_keep, left_got, right_keep, right_got
    )
    left_got, right_got = flipped(left, "x"), flipped(right, "y")
    query_g, key_in = query_grads(q, k, v, attn_grad, state, pair)
    sent, key_in, left_got, right_got = together(sent, key_in, left_got, right_got)

    (part,) = small_call(join_sides, [(z, rows, wide)], left_keep, left_got, right_keep, right_got)
    sums, gain_part, part = together(running(sent, True), gain_part, part)
    rev = exchange(sums, SEQ).reshape(kv.shape)
    part = lax.all_to_all(part, "z", 0, 0, tiled=True)
    gain_parts = everyones(gain_part.reshape(channels), ALL)
    key_g, value_g = key_value_grads(q, k, v, attn_grad, rev, key_in, pair)
    return query_g, key_g, value_g, part, gain_parts


def by_planes(sizes, rows, q, k, v, og, out_weight, gain_row, pos, pair):
    tokens, channels = q.shape
    wide = out_weight.shape[1]
    y, z, x = sizes["y"], sizes["z"], sizes["x"]
    weight = everyones(everyones(out_weight, "z"), PLANE)
    weight = weight.reshape(y, x, z, rows, wide).transpose(0, 2, 1, 3, 4).reshape(y, -1, wide)
    kv = key_value_sums(k, v, pair)
    intra = intra_outputs(q, k, v, pair)
    state = exchange(running(exchange(kv, SEQ), False), SEQ).reshape(kv.shape)
    outputs, send, keep = weight_parts(pos, q, state, intra, gain_row, og, pair)
    part = added(keep, flipped(send, "core")).astype(BF16)
    part = part.reshape(y, z, x, rows, wide).transpose(0, 2, 1, 3, 4).reshape(y * x, z, rows, wide)
    part = lax.all_to_all(part, PLANE, 0, 0, tiled=True)
    part = added(*[part[i] for i in range(y * x)]).astype(BF16)
    part = lax.all_to_all(part, "z", 0, 0, tiled=True)
    attn_grad, gain_part, qg = attn_grads(
        pos, q, outputs, gain_row, og, weight, flipped(weight, "core"), pair
    )
    rev = exchange(running(exchange(qg, SEQ), True), SEQ).reshape(kv.shape)
    query_g, key_in = query_grads(q, k, v, attn_grad, state, pair)
    key_g, value_g = key_value_grads(q, k, v, attn_grad, rev, key_in, pair)
    return query_g, key_g, value_g, part, everyones(gain_part.reshape(channels), ALL)


def shards(queries, keys, values, out_grad, out_weight, gain):
    tokens, channels = queries.shape[1:]
    assert tokens == BLOCK
    sizes = {name: lax.axis_size(name) for name in ALL}
    devices = lax.axis_size(ALL)
    rows = out_weight.shape[0]
    pair = channels // (sizes["y"] * sizes["core"]) // HEAD_DIM
    pos = lax.axis_index(("y", "core")).reshape(1).astype(jnp.int32)
    halves = (sizes["y"], sizes["z"], sizes["x"]) == (2, 4, 2) and rows % 16 == 0
    query_g, key_g, value_g, part, gain_parts = (by_halves if halves else by_planes)(
        sizes,
        rows,
        queries[0],
        keys[0],
        values[0],
        out_grad[0],
        out_weight,
        gain.reshape(1, channels),
        pos,
        pair,
    )
    factor = 1.0 / jnp.sqrt(jnp.float32(tokens * devices))
    out_shape = (1, tokens, channels)
    return (
        query_g.reshape(out_shape),
        key_g.reshape(out_shape),
        value_g.reshape(out_shape),
        added(*[part[i] for i in range(part.shape[0])]) * factor,
        jnp.sum(gain_parts, axis=0) * factor,
    )


def solution(mesh):
    dp_count, seq_count = mesh.shape["dp"], mesh.shape["seq"]
    finer = Mesh(mesh.devices.reshape(dp_count // 2, 2, seq_count // 2, 2), ALL)
    tokens = P(("y", "core"), ("z", "x"), None)
    rows = P(ALL, None)
    return jax.shard_map(
        shards,
        mesh=finer,
        in_specs=(tokens, tokens, tokens, tokens, rows, P()),
        out_specs=(tokens, tokens, tokens, rows, P()),
        check_vma=False,
    )
```

```python
import functools

import jax
import jax.numpy as jnp
from jax import lax
from jax.experimental import pallas as pl
from jax.experimental.pallas import tpu as pltpu
from jax.sharding import Mesh
from jax.sharding import PartitionSpec as P

HEAD_DIM = 128
BLOCK = 512
MIB = 1 << 20

norm_eps = 1e-06

F32 = jnp.float32
BF16 = jnp.bfloat16


def dot(a, b, contract):
    return lax.dot_general(a, b, (contract, ((), ())), preferred_element_type=F32)


def params(mib, dims=1):
    return pltpu.CompilerParams(
        vmem_limit_bytes=mib * MIB, dimension_semantics=("arbitrary",) * dims
    )


ROW_BLOCKS = 4


def row_blocks(tokens, wide):
    return [
        pl.BlockSpec((tokens // ROW_BLOCKS, wide), lambda c, y, p, r=r: (r, 0)) for r in range(ROW_BLOCKS)
    ]


def head(ref, i):
    return ref[:, i * HEAD_DIM : (i + 1) * HEAD_DIM]


def kv_kernel(k_ref, v_ref, o_ref, k_out_ref, v_out_ref):
    k_out_ref[...] = k_ref[...]
    v_out_ref[...] = v_ref[...]
    for i in range(o_ref.shape[0]):
        o_ref[i] = dot(head(k_ref, i), head(v_ref, i), ((0,), (0,))).astype(BF16)


def key_value_sums(keys, values, pair):
    tokens, channels = keys.shape
    width = pair * HEAD_DIM
    heads = channels // HEAD_DIM
    spec = pl.BlockSpec((tokens, width), lambda b: (0, b))
    return pl.pallas_call(
        kv_kernel,
        grid=(heads // pair,),
        in_specs=[spec, spec],
        out_specs=[pl.BlockSpec((pair, HEAD_DIM, HEAD_DIM), lambda b: (b, 0, 0)), spec, spec],
        out_shape=[
            jax.ShapeDtypeStruct((heads, HEAD_DIM, HEAD_DIM), BF16),
            jax.ShapeDtypeStruct(keys.shape, BF16),
            jax.ShapeDtypeStruct(keys.shape, BF16),
        ],
        compiler_params=params(56),
        cost_estimate=pl.CostEstimate(
            flops=2 * tokens * channels * HEAD_DIM, bytes_accessed=4 * tokens * channels, transcendentals=0
        ),
        name="key_value_sums",
    )(keys, values)


def lower(x):
    rows = lax.broadcasted_iota(jnp.int32, x.shape, 0)
    cols = lax.broadcasted_iota(jnp.int32, x.shape, 1)
    return jnp.where(cols <= rows, x, 0.0).astype(BF16)


def intra_kernel(q_ref, k_ref, v_ref, o_ref, q_out_ref):
    q_out_ref[...] = q_ref[...]
    half = q_ref.shape[0] // 2
    for i in range(o_ref.shape[1] // HEAD_DIM):
        q, k, v = head(q_ref, i), head(k_ref, i), head(v_ref, i)
        here = slice(i * HEAD_DIM, (i + 1) * HEAD_DIM)
        top = lower(dot(q[:half], k[:half], ((1,), (1,))))
        o_ref[:half, here] = dot(top, v[:half], ((1,), (0,)))
        left = dot(q[half:], k[:half], ((1,), (1,))).astype(BF16)
        right = lower(dot(q[half:], k[half:], ((1,), (1,))))
        o_ref[half:, here] = dot(left, v[:half], ((1,), (0,))) + dot(right, v[half:], ((1,), (0,)))


def intra_outputs(queries, keys, values, pair):
    tokens, channels = keys.shape
    spec = pl.BlockSpec((tokens, pair * HEAD_DIM), lambda b: (0, b))
    return pl.pallas_call(
        intra_kernel,
        grid=(channels // (pair * HEAD_DIM),),
        in_specs=[spec] * 3,
        out_specs=[spec, spec],
        out_shape=[jax.ShapeDtypeStruct((tokens, channels), t) for t in (F32, BF16)],
        compiler_params=params(52),
        cost_estimate=pl.CostEstimate(
            flops=4 * tokens * tokens * channels, bytes_accessed=10 * tokens * channels, transcendentals=0
        ),
        name="intra_outputs",
    )(queries, keys, values)


def rms_inverse(x):
    return lax.rsqrt(jnp.mean(x * x, axis=-1, keepdims=True) + norm_eps)


def unit_kernel(pos_ref, q_ref, s_ref, intra_ref, gain_ref, *refs):
    *og_refs, out_ref, send_ref, keep_ref, og_out_ref = refs
    units = []
    for i in range(s_ref.shape[0]):
        x = head(intra_ref, i) + dot(head(q_ref, i), s_ref[i], ((1,), (0,)))
        out_ref[:, i * HEAD_DIM : (i + 1) * HEAD_DIM] = x
        units.append((x * rms_inverse(x) * head(gain_ref, i)).astype(BF16))
    unit = jnp.concatenate(units, axis=1) if len(units) > 1 else units[0]
    og = jnp.concatenate([og_ref[...] for og_ref in og_refs], axis=0)
    part = dot(unit, og, ((0,), (0,))).astype(BF16)

    @pl.when((pl.program_id(0) == 0) & (pl.program_id(1) == 0))
    def _():
        og_out_ref[...] = og

    @pl.when(pl.program_id(0) == 0)
    def _():
        send_ref[0] = part

    @pl.when(pl.program_id(0) == 1)
    def _():
        keep_ref[0] = part


def weight_parts(pos, queries, state, intra, gain, out_grad, pair):
    tokens, channels = queries.shape
    width = pair * HEAD_DIM
    count = channels // width // 2
    wide = out_grad.shape[1]

    def block(c, y, pos_ref):
        return 2 * y + lax.rem(pos_ref[0] + 1 + c, 2)

    cols = pl.BlockSpec((tokens, width), lambda c, y, pos_ref: (0, block(c, y, pos_ref)))
    part = jax.ShapeDtypeStruct((count, width, wide), BF16)
    return pl.pallas_call(
        unit_kernel,
        grid_spec=pltpu.PrefetchScalarGridSpec(
            num_scalar_prefetch=1,
            grid=(2, count),
            in_specs=[
                cols,
                pl.BlockSpec((pair, HEAD_DIM, HEAD_DIM), lambda c, y, p: (block(c, y, p), 0, 0)),
                cols,
                pl.BlockSpec((1, width), lambda c, y, p: (0, block(c, y, p))),
            ]
            + row_blocks(tokens, wide),
            out_specs=[
                cols,
                pl.BlockSpec((1, width, wide), lambda c, y, p: (jnp.where(c == 0, y, count - 1), 0, 0)),
                pl.BlockSpec((1, width, wide), lambda c, y, p: (jnp.where(c == 0, 0, y), 0, 0)),
                pl.BlockSpec((tokens, wide), lambda c, y, p: (0, 0)),
            ],
        ),
        out_shape=[
            jax.ShapeDtypeStruct((tokens, channels), F32),
            part,
            part,
            jax.ShapeDtypeStruct((tokens, wide), BF16),
        ],
        compiler_params=params(26, 2),
        cost_estimate=pl.CostEstimate(
            flops=2 * tokens * channels * wide,
            bytes_accessed=10 * tokens * channels + 2 * tokens * wide + 2 * channels * wide,
            transcendentals=0,
        ),
        name="weight_parts",
    )(pos, queries, state, intra, gain, *[out_grad] * ROW_BLOCKS)


def attn_grad_kernel(pos_ref, q_ref, o_ref, gain_ref, *refs):
    *og_refs, w_ref, ag_ref, gg_ref, qg_ref, ug_ref = refs
    start = 0
    for og_ref in og_refs:
        stop = start + og_ref.shape[0]
        ug_ref[start:stop] = dot(og_ref[...], w_ref[0], ((1,), (1,)))
        start = stop
    for i in range(qg_ref.shape[0]):
        here = slice(i * HEAD_DIM, (i + 1) * HEAD_DIM)
        x = head(o_ref, i)
        inverse = rms_inverse(x)
        normed = x * inverse
        ug = head(ug_ref, i)
        gg_ref[:, here] = jnp.sum(ug * normed, axis=0, keepdims=True)
        scaled = ug * head(gain_ref, i)
        middle = jnp.mean(scaled * normed, axis=-1, keepdims=True)
        ag = ((scaled - normed * middle) * inverse).astype(BF16)
        ag_ref[:, here] = ag
        qg_ref[i] = dot(head(q_ref, i), ag, ((0,), (0,))).astype(BF16)


def more_attn_grad_kernel(pos_ref, q_ref, o_ref, gain_ref, *refs):
    ins, outs = refs[: ROW_BLOCKS + 1], refs[ROW_BLOCKS + 4 :]
    attn_grad_kernel(pos_ref, q_ref, o_ref, gain_ref, *ins, *outs)


def attn_grads(pos, side, queries, outputs, gain, out_grad, weight, pair, begun=()):
    tokens, channels = queries.shape
    width = pair * HEAD_DIM
    count = channels // width // 2
    wide = out_grad.shape[1]
    heads = channels // HEAD_DIM

    def block(y, pos_ref):
        return 2 * y + lax.rem(pos_ref[0] + side, 2)

    cols = pl.BlockSpec((tokens, width), lambda y, p: (0, block(y, p)))
    row = pl.BlockSpec((1, width), lambda y, p: (0, block(y, p)))
    states = pl.BlockSpec((pair, HEAD_DIM, HEAD_DIM), lambda y, p: (block(y, p), 0, 0))
    chunk = tokens // ROW_BLOCKS
    og_specs = [pl.BlockSpec((chunk, wide), lambda y, p, r=r: (r, 0)) for r in range(ROW_BLOCKS)]
    before = 5 + ROW_BLOCKS
    return pl.pallas_call(
        more_attn_grad_kernel if begun else attn_grad_kernel,
        grid_spec=pltpu.PrefetchScalarGridSpec(
            num_scalar_prefetch=1,
            grid=(count,),
            in_specs=[cols, cols, row]
            + og_specs
            + [pl.BlockSpec((1,) + weight.shape[1:], lambda y, p: (y, 0, 0))]
            + [pl.BlockSpec(memory_space=pl.ANY)] * len(begun),
            out_specs=[cols, row, states],
            scratch_shapes=[pltpu.VMEM((tokens, width), F32)],
        ),
        out_shape=[
            jax.ShapeDtypeStruct((tokens, channels), BF16),
            jax.ShapeDtypeStruct((1, channels), F32),
            jax.ShapeDtypeStruct((heads, HEAD_DIM, HEAD_DIM), BF16),
        ],
        input_output_aliases={before + i: i for i in range(len(begun))},
        compiler_params=params(24),
        cost_estimate=pl.CostEstimate(
            flops=tokens * channels * wide,
            bytes_accessed=4 * tokens * channels + 2 * tokens * wide + channels * wide,
            transcendentals=0,
        ),
        name="attn_grads",
    )(pos, queries, outputs, gain, *[out_grad] * ROW_BLOCKS, weight, *begun)


NT, NN, TN = ((1,), (1,)), ((1,), (0,)), ((0,), (0,))


def query_grad_kernel(q_ref, k_ref, v_ref, ag_ref, s_ref, qg_ref, kg_ref):
    half = q_ref.shape[0] // 2
    top, low = slice(0, half), slice(half, 2 * half)
    for i in range(s_ref.shape[0]):
        q, k, v, ag = head(q_ref, i), head(k_ref, i), head(v_ref, i), head(ag_ref, i)
        here = slice(i * HEAD_DIM, (i + 1) * HEAD_DIM)
        from_state = dot(ag, s_ref[i], NT)
        g00 = lower(dot(ag[top], v[top], NT))
        g10 = dot(ag[low], v[top], NT).astype(BF16)
        g11 = lower(dot(ag[low], v[low], NT))
        qg_ref[top, here] = (dot(g00, k[top], NN) + from_state[top]).astype(BF16)
        qg_ref[low, here] = (dot(g10, k[top], NN) + dot(g11, k[low], NN) + from_state[low]).astype(BF16)
        kg_ref[top, here] = dot(g00, q[top], TN) + dot(g10, q[low], TN)
        kg_ref[low, here] = dot(g11, q[low], TN)


def query_grads(queries, keys, values, attn_grad, state, pair):
    tokens, channels = queries.shape
    spec = pl.BlockSpec((tokens, pair * HEAD_DIM), lambda b: (0, b))
    return pl.pallas_call(
        query_grad_kernel,
        grid=(channels // (pair * HEAD_DIM),),
        in_specs=[spec] * 4 + [pl.BlockSpec((pair, HEAD_DIM, HEAD_DIM), lambda b: (b, 0, 0))],
        out_specs=[spec] * 2,
        out_shape=[jax.ShapeDtypeStruct((tokens, channels), t) for t in (BF16, F32)],
        compiler_params=params(24),
        cost_estimate=pl.CostEstimate(
            flops=6 * tokens * tokens * channels, bytes_accessed=14 * tokens * channels, transcendentals=0
        ),
        name="query_grads",
    )(queries, keys, values, attn_grad, state)


def key_value_grad_kernel(q_ref, k_ref, v_ref, ag_ref, r_ref, kin_ref, kg_ref, vg_ref):
    half = q_ref.shape[0] // 2
    top, low = slice(0, half), slice(half, 2 * half)
    for i in range(r_ref.shape[0]):
        q, k, v, ag = head(q_ref, i), head(k_ref, i), head(v_ref, i), head(ag_ref, i)
        here = slice(i * HEAD_DIM, (i + 1) * HEAD_DIM)
        rev = r_ref[i]
        kg_ref[:, here] = (head(kin_ref, i) + dot(v, rev, NT)).astype(BF16)
        a00 = lower(dot(q[top], k[top], NT))
        a10 = dot(q[low], k[top], NT).astype(BF16)
        a11 = lower(dot(q[low], k[low], NT))
        from_rev = dot(k, rev, NN)
        vg_ref[top, here] = (dot(a00, ag[top], TN) + dot(a10, ag[low], TN) + from_rev[top]).astype(BF16)
        vg_ref[low, here] = (dot(a11, ag[low], TN) + from_rev[low]).astype(BF16)


def key_value_grads(queries, keys, values, attn_grad, rev, key_in, pair):
    tokens, channels = keys.shape
    spec = pl.BlockSpec((tokens, pair * HEAD_DIM), lambda b: (0, b))
    return pl.pallas_call(
        key_value_grad_kernel,
        grid=(channels // (pair * HEAD_DIM),),
        in_specs=[spec] * 4 + [pl.BlockSpec((pair, HEAD_DIM, HEAD_DIM), lambda b: (b, 0, 0)), spec],
        out_specs=[spec] * 2,
        out_shape=[jax.ShapeDtypeStruct((tokens, channels), BF16)] * 2,
        compiler_params=params(24),
        cost_estimate=pl.CostEstimate(
            flops=5 * tokens * tokens * channels, bytes_accessed=16 * tokens * channels, transcendentals=0
        ),
        name="key_value_grads",
    )(queries, keys, values, attn_grad, rev, key_in)


def running_kernel(reverse, x_ref, o_ref):
    count = x_ref.shape[0]
    total = jnp.zeros(x_ref.shape[1:], F32)
    for place in range(count)[:: -1 if reverse else 1]:
        o_ref[place] = total.astype(BF16)
        total = total + x_ref[place].astype(F32)


def running(rows, reverse):
    return pl.pallas_call(
        functools.partial(running_kernel, reverse),
        out_shape=jax.ShapeDtypeStruct(rows.shape, BF16),
        name="running_sums",
    )(rows)


ALL = ("y", "core", "z", "x")
SEQ = ("z", "x")
PLANE = ("y", "x")


def exchange(x, axis):
    rows = x.reshape((lax.axis_size(axis), -1) + x.shape[-1:])
    return lax.all_to_all(rows, axis, 0, 0, tiled=True)


def everyones(x, axis):
    return lax.all_to_all(jnp.broadcast_to(x[None], (lax.axis_size(axis),) + x.shape), axis, 0, 0, tiled=True)


def flipped(x, axis, bit=1):
    return lax.ppermute(x, axis, [(i, i ^ bit) for i in range(lax.axis_size(axis))])


def added(*terms):
    total = terms[0].astype(F32)
    for term in terms[1:]:
        total = total + term.astype(F32)
    return total


def together(*xs):
    return lax.optimization_barrier(xs)


def small_call(kernel, out_shapes, *args, after=()):
    def call(*refs):
        kernel(*refs[: len(args)], *refs[len(args) + len(after) :])

    return pl.pallas_call(
        call,
        in_specs=[pl.BlockSpec(memory_space=pltpu.VMEM)] * len(args)
        + [pl.BlockSpec(memory_space=pl.ANY)] * len(after),
        out_shape=[jax.ShapeDtypeStruct(shape, BF16) for shape in out_shapes],
        compiler_params=pltpu.CompilerParams(vmem_limit_bytes=24 * MIB),
        cost_estimate=pl.CostEstimate(
            flops=0, bytes_accessed=4 * sum(x.size for x in args), transcendentals=0
        ),
        name=kernel.__name__,
    )(*args, *after)


def one(i):
    return pl.ds(i, 1)


def place(axis, bit=1):
    here = (lax.axis_index(axis) // bit) % 2
    return here, 1 - here


def merge_far(mine_ref, theirs_ref, out_ref):
    here, there = place("z", 2)
    out_ref[one(here)] = mine_ref[...][None]
    out_ref[one(there)] = theirs_ref[...][None]


def merge_near(mine_ref, theirs_ref, left_ref, right_ref):
    here, there = place("z")
    half = left_ref.shape[-1]
    for at, ref in ((here, mine_ref), (there, theirs_ref)):
        left_ref[:, one(at)] = ref[:, :, :half][:, None]
        right_ref[:, one(at)] = ref[:, :, half:][:, None]


def merge_sides(left_ref, left_got_ref, right_ref, right_got_ref, left_out_ref, right_out_ref):
    here, there = place("x")
    left_out_ref[:, one(here)] = left_ref[...][:, None]
    left_out_ref[:, one(there)] = left_got_ref[...][:, None]
    here, there = place("y")
    right_out_ref[one(here)] = right_ref[...][None]
    right_out_ref[one(there)] = right_got_ref[...][None]


def merge_all(left_ref, left_got_ref, right_ref, right_got_ref, out_ref):
    half = left_ref.shape[-1]
    here, there = place("y")
    out_ref[one(here), :, :, :, :half] = left_ref[...][None]
    out_ref[one(there), :, :, :, :half] = left_got_ref[...][None]
    here, there = place("x")
    out_ref[:, :, one(here), :, half:] = right_ref[...][:, :, None]
    out_ref[:, :, one(there), :, half:] = right_got_ref[...][:, :, None]


def total(a_ref, b_ref, *index):
    return (a_ref[index].astype(F32) + b_ref[index].astype(F32)).astype(BF16)


def split_first(keep_ref, got_ref, left_ref, right_ref, left_keep_ref, right_keep_ref):
    half = left_ref.shape[-1]
    here, there = place("y")
    every = slice(None)
    for at, ref in ((there, left_ref), (here, left_keep_ref)):
        ref[...] = total(keep_ref, got_ref, one(at), every, every, every, slice(0, half))[0]
    here, there = place("x")
    for at, ref in ((there, right_ref), (here, right_keep_ref)):
        ref[...] = total(keep_ref, got_ref, every, every, one(at), every, slice(half, 2 * half))[:, :, 0]


def split_second(left_ref, left_got_ref, right_ref, right_got_ref, left_out, right_out, left_keep, right_keep):
    here, there = place("x")
    for at, ref in ((there, left_out), (here, left_keep)):
        ref[...] = total(left_ref, left_got_ref, slice(None), one(at))[:, 0]
    here, there = place("y")
    for at, ref in ((there, right_out), (here, right_keep)):
        ref[...] = total(right_ref, right_got_ref, one(at))[0]


def join_sides(left_ref, left_got_ref, right_ref, right_got_ref, out_ref):
    half = left_ref.shape[-1]
    out_ref[:, :, :half] = total(left_ref, left_got_ref, slice(None))
    out_ref[:, :, half:] = total(right_ref, right_got_ref, slice(None))


def by_halves(sizes, rows, q, k, v, og, out_weight, gain_row, pos, pair):
    tokens, channels = q.shape
    wide = out_weight.shape[1]
    y, z, x, half = sizes["y"], sizes["z"], sizes["x"], wide // 2

    got = flipped(out_weight, "z", 2)
    kv, k, v = key_value_sums(k, v, pair)
    kv, got = together(kv, got)
    (weight,) = small_call(merge_far, [(2, rows, wide)], out_weight, got)

    got = flipped(weight, "z", 1)
    sent = exchange(kv, SEQ)
    intra, q = intra_outputs(q, k, v, pair)
    sums = running(sent, False)
    state = exchange(sums, SEQ).reshape(kv.shape)
    left, right = small_call(merge_near, [(2, 2, rows, half)] * 2, weight, got, after=(sums,))
    left, right = left.reshape(z, rows, half), right.reshape(z, rows, half)

    left_got, right_got = flipped(left, "x"), flipped(right, "y")
    state, left_got, right_got = together(state, left_got, right_got)
    left, right = small_call(
        merge_sides, [(z, x, rows, half), (y, z, rows, half)], left, left_got, right, right_got
    )

    state, left, right = together(state, left, right)
    left_got, right_got = flipped(left, "y"), flipped(right, "x")
    outputs, send, keep, og = weight_parts(pos, q, state, intra, gain_row, og, pair)
    send, left_got, right_got = together(send, left_got, right_got)
    got = flipped(send, "core")
    (mine,) = small_call(merge_all, [(y, z, x, rows, wide)], left, left_got, right, right_got)
    mine = mine.reshape(y, -1, wide)
    other = flipped(mine, "core")
    begun = attn_grads(pos, 0, q, outputs, gain_row, og, mine, pair)

    split = (y, z, x, rows, wide)
    left, right, left_keep, right_keep = small_call(
        split_first,
        [(z, x, rows, half), (y, z, rows, half)] * 2,
        keep.reshape(split),
        got.reshape(split),
        after=(begun[1],),
    )
    other, left, right = together(other, left, right)
    left_got, right_got = flipped(left, "y"), flipped(right, "x")
    attn_grad, gain_part, qg = attn_grads(pos, 1, q, outputs, gain_row, og, other, pair, begun)
    qg, left_got, right_got = together(qg, left_got, right_got)

    sent = exchange(qg, SEQ)
    left, right, left_keep, right_keep = small_call(
        split_second, [(z, rows, half)] * 4, left_keep, left_got, right_keep, right_got
    )
    left_got, right_got = flipped(left, "x"), flipped(right, "y")
    query_g, key_in = query_grads(q, k, v, attn_grad, state, pair)
    sent, key_in, left_got, right_got = together(sent, key_in, left_got, right_got)

    sums = running(sent, True)
    rev = exchange(sums, SEQ).reshape(kv.shape)
    (part,) = small_call(
        join_sides, [(z, rows, wide)], left_keep, left_got, right_keep, right_got, after=(sums,)
    )
    gain_part, part = together(gain_part, part)
    part = lax.all_to_all(part, "z", 0, 0, tiled=True)
    gain_parts = everyones(gain_part.reshape(channels), ALL)
    key_g, value_g = key_value_grads(q, k, v, attn_grad, rev, key_in, pair)
    return query_g, key_g, value_g, part, gain_parts


def by_planes(sizes, rows, q, k, v, og, out_weight, gain_row, pos, pair):
    tokens, channels = q.shape
    wide = out_weight.shape[1]
    y, z, x = sizes["y"], sizes["z"], sizes["x"]
    weight = everyones(everyones(out_weight, "z"), PLANE)
    weight = weight.reshape(y, x, z, rows, wide).transpose(0, 2, 1, 3, 4).reshape(y, -1, wide)
    kv, k, v = key_value_sums(k, v, pair)
    intra, q = intra_outputs(q, k, v, pair)
    state = exchange(running(exchange(kv, SEQ), False), SEQ).reshape(kv.shape)
    outputs, send, keep, og = weight_parts(pos, q, state, intra, gain_row, og, pair)
    part = added(keep, flipped(send, "core")).astype(BF16)
    part = part.reshape(y, z, x, rows, wide).transpose(0, 2, 1, 3, 4).reshape(y * x, z, rows, wide)
    part = lax.all_to_all(part, PLANE, 0, 0, tiled=True)
    part = added(*[part[i] for i in range(y * x)]).astype(BF16)
    part = lax.all_to_all(part, "z", 0, 0, tiled=True)
    begun = attn_grads(pos, 0, q, outputs, gain_row, og, weight, pair)
    attn_grad, gain_part, qg = attn_grads(
        pos, 1, q, outputs, gain_row, og, flipped(weight, "core"), pair, begun
    )
    rev = exchange(running(exchange(qg, SEQ), True), SEQ).reshape(kv.shape)
    query_g, key_in = query_grads(q, k, v, attn_grad, state, pair)
    key_g, value_g = key_value_grads(q, k, v, attn_grad, rev, key_in, pair)
    return query_g, key_g, value_g, part, everyones(gain_part.reshape(channels), ALL)


def shards(queries, keys, values, out_grad, out_weight, gain):
    tokens, channels = queries.shape[1:]
    assert tokens == BLOCK
    sizes = {name: lax.axis_size(name) for name in ALL}
    devices = lax.axis_size(ALL)
    rows = out_weight.shape[0]
    pair = channels // (sizes["y"] * sizes["core"]) // HEAD_DIM
    pos = lax.axis_index(("y", "core")).reshape(1).astype(jnp.int32)
    halves = (sizes["y"], sizes["z"], sizes["x"]) == (2, 4, 2) and rows % 16 == 0
    query_g, key_g, value_g, part, gain_parts = (by_halves if halves else by_planes)(
        sizes,
        rows,
        queries[0],
        keys[0],
        values[0],
        out_grad[0],
        out_weight,
        gain.reshape(1, channels),
        pos,
        pair,
    )
    factor = 1.0 / jnp.sqrt(jnp.float32(tokens * devices))
    out_shape = (1, tokens, channels)
    return (
        query_g.reshape(out_shape),
        key_g.reshape(out_shape),
        value_g.reshape(out_shape),
        added(*[part[i] for i in range(part.shape[0])]) * factor,
        jnp.sum(gain_parts, axis=0) * factor,
    )


def solution(mesh):
    dp_count, seq_count = mesh.shape["dp"], mesh.shape["seq"]
    finer = Mesh(mesh.devices.reshape(dp_count // 2, 2, seq_count // 2, 2), ALL)
    tokens = P(("y", "core"), ("z", "x"), None)
    rows = P(ALL, None)
    return jax.shard_map(
        shards,
        mesh=finer,
        in_specs=(tokens, tokens, tokens, tokens, rows, P()),
        out_specs=(tokens, tokens, tokens, rows, P()),
        check_vma=False,
    )
```

```python
import functools

import jax
import jax.numpy as jnp
from jax import lax
from jax.experimental import pallas as pl
from jax.experimental.pallas import tpu as pltpu
from jax.sharding import Mesh
from jax.sharding import PartitionSpec as P

HEAD_DIM = 128
BLOCK = 512
MIB = 1 << 20

norm_eps = 1e-06

END = (8, 128)

F32 = jnp.float32
BF16 = jnp.bfloat16


def dot(a, b, contract):
    return lax.dot_general(a, b, (contract, ((), ())), preferred_element_type=F32)


def params(mib, dims=1):
    return pltpu.CompilerParams(
        vmem_limit_bytes=mib * MIB, dimension_semantics=("arbitrary",) * dims
    )


ROW_BLOCKS = 4


def row_blocks(tokens, wide):
    return [
        pl.BlockSpec((tokens // ROW_BLOCKS, wide), lambda c, y, p, r=r: (r, 0)) for r in range(ROW_BLOCKS)
    ]


def head(ref, i):
    return ref[:, i * HEAD_DIM : (i + 1) * HEAD_DIM]


def kv_kernel(k_ref, v_ref, o_ref, k_out_ref, v_out_ref):
    k_out_ref[...] = k_ref[...]
    v_out_ref[...] = v_ref[...]
    for i in range(o_ref.shape[0]):
        o_ref[i] = dot(head(k_ref, i), head(v_ref, i), ((0,), (0,))).astype(BF16)


def key_value_sums(keys, values, pair):
    tokens, channels = keys.shape
    width = pair * HEAD_DIM
    heads = channels // HEAD_DIM
    spec = pl.BlockSpec((tokens, width), lambda b: (0, b))
    return pl.pallas_call(
        kv_kernel,
        grid=(heads // pair,),
        in_specs=[spec, spec],
        out_specs=[pl.BlockSpec((pair, HEAD_DIM, HEAD_DIM), lambda b: (b, 0, 0)), spec, spec],
        out_shape=[
            jax.ShapeDtypeStruct((heads, HEAD_DIM, HEAD_DIM), BF16),
            jax.ShapeDtypeStruct(keys.shape, BF16),
            jax.ShapeDtypeStruct(keys.shape, BF16),
        ],
        compiler_params=params(56),
        cost_estimate=pl.CostEstimate(
            flops=2 * tokens * channels * HEAD_DIM, bytes_accessed=4 * tokens * channels, transcendentals=0
        ),
        name="key_value_sums",
    )(keys, values)


def lower(x):
    rows = lax.broadcasted_iota(jnp.int32, x.shape, 0)
    cols = lax.broadcasted_iota(jnp.int32, x.shape, 1)
    return jnp.where(cols <= rows, x, 0.0).astype(BF16)


def intra_kernel(q_ref, k_ref, v_ref, o_ref, q_out_ref, end_ref):
    q_out_ref[...] = q_ref[...]
    end_ref[...] = jnp.zeros_like(end_ref)
    half = q_ref.shape[0] // 2
    for i in range(o_ref.shape[1] // HEAD_DIM):
        q, k, v = head(q_ref, i), head(k_ref, i), head(v_ref, i)
        here = slice(i * HEAD_DIM, (i + 1) * HEAD_DIM)
        top = lower(dot(q[:half], k[:half], ((1,), (1,))))
        o_ref[:half, here] = dot(top, v[:half], ((1,), (0,)))
        left = dot(q[half:], k[:half], ((1,), (1,))).astype(BF16)
        right = lower(dot(q[half:], k[half:], ((1,), (1,))))
        o_ref[half:, here] = dot(left, v[:half], ((1,), (0,))) + dot(right, v[half:], ((1,), (0,)))


def intra_outputs(queries, keys, values, pair):
    tokens, channels = keys.shape
    spec = pl.BlockSpec((tokens, pair * HEAD_DIM), lambda b: (0, b))
    return pl.pallas_call(
        intra_kernel,
        grid=(channels // (pair * HEAD_DIM),),
        in_specs=[spec] * 3,
        out_specs=[spec, spec, pl.BlockSpec(END, lambda b: (0, 0))],
        out_shape=[jax.ShapeDtypeStruct((tokens, channels), t) for t in (F32, BF16)]
        + [jax.ShapeDtypeStruct(END, F32)],
        compiler_params=params(52),
        cost_estimate=pl.CostEstimate(
            flops=4 * tokens * tokens * channels, bytes_accessed=10 * tokens * channels, transcendentals=0
        ),
        name="intra_outputs",
    )(queries, keys, values)


def rms_inverse(x):
    return lax.rsqrt(jnp.mean(x * x, axis=-1, keepdims=True) + norm_eps)


def unit_kernel(pos_ref, q_ref, s_ref, intra_ref, gain_ref, *refs):
    *og_refs, out_ref, send_ref, keep_ref, og_out_ref = refs
    units = []
    for i in range(s_ref.shape[0]):
        x = head(intra_ref, i) + dot(head(q_ref, i), s_ref[i], ((1,), (0,)))
        out_ref[:, i * HEAD_DIM : (i + 1) * HEAD_DIM] = x
        units.append((x * rms_inverse(x) * head(gain_ref, i)).astype(BF16))
    unit = jnp.concatenate(units, axis=1) if len(units) > 1 else units[0]
    og = jnp.concatenate([og_ref[...] for og_ref in og_refs], axis=0)
    part = dot(unit, og, ((0,), (0,))).astype(BF16)

    @pl.when((pl.program_id(0) == 0) & (pl.program_id(1) == 0))
    def _():
        og_out_ref[...] = og

    @pl.when(pl.program_id(0) == 0)
    def _():
        send_ref[0] = part

    @pl.when(pl.program_id(0) == 1)
    def _():
        keep_ref[0] = part


def weight_parts(pos, queries, state, intra, gain, out_grad, pair):
    tokens, channels = queries.shape
    width = pair * HEAD_DIM
    count = channels // width // 2
    wide = out_grad.shape[1]

    def block(c, y, pos_ref):
        return 2 * y + lax.rem(pos_ref[0] + 1 + c, 2)

    cols = pl.BlockSpec((tokens, width), lambda c, y, pos_ref: (0, block(c, y, pos_ref)))
    part = jax.ShapeDtypeStruct((count, width, wide), BF16)
    return pl.pallas_call(
        unit_kernel,
        grid_spec=pltpu.PrefetchScalarGridSpec(
            num_scalar_prefetch=1,
            grid=(2, count),
            in_specs=[
                cols,
                pl.BlockSpec((pair, HEAD_DIM, HEAD_DIM), lambda c, y, p: (block(c, y, p), 0, 0)),
                cols,
                pl.BlockSpec((1, width), lambda c, y, p: (0, block(c, y, p))),
            ]
            + row_blocks(tokens, wide),
            out_specs=[
                cols,
                pl.BlockSpec((1, width, wide), lambda c, y, p: (jnp.where(c == 0, y, count - 1), 0, 0)),
                pl.BlockSpec((1, width, wide), lambda c, y, p: (jnp.where(c == 0, 0, y), 0, 0)),
                pl.BlockSpec((tokens, wide), lambda c, y, p: (0, 0)),
            ],
        ),
        out_shape=[
            jax.ShapeDtypeStruct((tokens, channels), F32),
            part,
            part,
            jax.ShapeDtypeStruct((tokens, wide), BF16),
        ],
        compiler_params=params(26, 2),
        cost_estimate=pl.CostEstimate(
            flops=2 * tokens * channels * wide,
            bytes_accessed=10 * tokens * channels + 2 * tokens * wide + 2 * channels * wide,
            transcendentals=0,
        ),
        name="weight_parts",
    )(pos, queries, state, intra, gain, *[out_grad] * ROW_BLOCKS)


def attn_grad_kernel(pos_ref, q_ref, o_ref, gain_ref, *refs):
    *og_refs, w_ref, ag_ref, gg_ref, qg_ref, ug_ref = refs
    start = 0
    for og_ref in og_refs:
        stop = start + og_ref.shape[0]
        ug_ref[start:stop] = dot(og_ref[...], w_ref[0], ((1,), (1,)))
        start = stop
    for i in range(qg_ref.shape[0]):
        here = slice(i * HEAD_DIM, (i + 1) * HEAD_DIM)
        x = head(o_ref, i)
        inverse = rms_inverse(x)
        normed = x * inverse
        ug = head(ug_ref, i)
        gg_ref[:, here] = jnp.sum(ug * normed, axis=0, keepdims=True)
        scaled = ug * head(gain_ref, i)
        middle = jnp.mean(scaled * normed, axis=-1, keepdims=True)
        ag = ((scaled - normed * middle) * inverse).astype(BF16)
        ag_ref[:, here] = ag
        qg_ref[i] = dot(head(q_ref, i), ag, ((0,), (0,))).astype(BF16)


def more_attn_grad_kernel(pos_ref, q_ref, o_ref, gain_ref, *refs):
    ins, outs = refs[: ROW_BLOCKS + 1], refs[ROW_BLOCKS + 4 :]
    attn_grad_kernel(pos_ref, q_ref, o_ref, gain_ref, *ins, *outs)


def attn_grads(pos, side, queries, outputs, gain, out_grad, weight, pair, begun=()):
    tokens, channels = queries.shape
    width = pair * HEAD_DIM
    count = channels // width // 2
    wide = out_grad.shape[1]
    heads = channels // HEAD_DIM

    def block(y, pos_ref):
        return 2 * y + lax.rem(pos_ref[0] + side, 2)

    cols = pl.BlockSpec((tokens, width), lambda y, p: (0, block(y, p)))
    row = pl.BlockSpec((1, width), lambda y, p: (0, block(y, p)))
    states = pl.BlockSpec((pair, HEAD_DIM, HEAD_DIM), lambda y, p: (block(y, p), 0, 0))
    chunk = tokens // ROW_BLOCKS
    og_specs = [pl.BlockSpec((chunk, wide), lambda y, p, r=r: (r, 0)) for r in range(ROW_BLOCKS)]
    before = 5 + ROW_BLOCKS
    return pl.pallas_call(
        more_attn_grad_kernel if begun else attn_grad_kernel,
        grid_spec=pltpu.PrefetchScalarGridSpec(
            num_scalar_prefetch=1,
            grid=(count,),
            in_specs=[cols, cols, row]
            + og_specs
            + [pl.BlockSpec((1,) + weight.shape[1:], lambda y, p: (y, 0, 0))]
            + [pl.BlockSpec(memory_space=pl.ANY)] * len(begun),
            out_specs=[cols, row, states],
            scratch_shapes=[pltpu.VMEM((tokens, width), F32)],
        ),
        out_shape=[
            jax.ShapeDtypeStruct((tokens, channels), BF16),
            jax.ShapeDtypeStruct((1, channels), F32),
            jax.ShapeDtypeStruct((heads, HEAD_DIM, HEAD_DIM), BF16),
        ],
        input_output_aliases={before + i: i for i in range(len(begun))},
        compiler_params=params(24),
        cost_estimate=pl.CostEstimate(
            flops=tokens * channels * wide,
            bytes_accessed=4 * tokens * channels + 2 * tokens * wide + channels * wide,
            transcendentals=0,
        ),
        name="attn_grads",
    )(pos, queries, outputs, gain, *[out_grad] * ROW_BLOCKS, weight, *begun)


NT, NN, TN = ((1,), (1,)), ((1,), (0,)), ((0,), (0,))


def query_grad_kernel(q_ref, k_ref, v_ref, ag_ref, s_ref, *refs):
    qg_ref, kg_ref = refs[-2:]
    half = q_ref.shape[0] // 2
    top, low = slice(0, half), slice(half, 2 * half)
    for i in range(s_ref.shape[0]):
        q, k, v, ag = head(q_ref, i), head(k_ref, i), head(v_ref, i), head(ag_ref, i)
        here = slice(i * HEAD_DIM, (i + 1) * HEAD_DIM)
        from_state = dot(ag, s_ref[i], NT)
        g00 = lower(dot(ag[top], v[top], NT))
        g10 = dot(ag[low], v[top], NT).astype(BF16)
        g11 = lower(dot(ag[low], v[low], NT))
        qg_ref[top, here] = (dot(g00, k[top], NN) + from_state[top]).astype(BF16)
        qg_ref[low, here] = (dot(g10, k[top], NN) + dot(g11, k[low], NN) + from_state[low]).astype(BF16)
        kg_ref[top, here] = dot(g00, q[top], TN) + dot(g10, q[low], TN)
        kg_ref[low, here] = dot(g11, q[low], TN)


def query_grads(queries, keys, values, attn_grad, state, pair, after=()):
    tokens, channels = queries.shape
    spec = pl.BlockSpec((tokens, pair * HEAD_DIM), lambda b: (0, b))
    return pl.pallas_call(
        query_grad_kernel,
        grid=(channels // (pair * HEAD_DIM),),
        in_specs=[spec] * 4
        + [pl.BlockSpec((pair, HEAD_DIM, HEAD_DIM), lambda b: (b, 0, 0))]
        + [pl.BlockSpec(memory_space=pl.ANY)] * len(after),
        out_specs=[spec] * 2,
        out_shape=[jax.ShapeDtypeStruct((tokens, channels), t) for t in (BF16, F32)],
        compiler_params=params(24),
        cost_estimate=pl.CostEstimate(
            flops=6 * tokens * tokens * channels, bytes_accessed=14 * tokens * channels, transcendentals=0
        ),
        name="query_grads",
    )(queries, keys, values, attn_grad, state, *after)


def key_value_grad_kernel(q_ref, k_ref, v_ref, ag_ref, r_ref, kin_ref, *refs):
    kg_ref, vg_ref = refs[-2:]
    half = q_ref.shape[0] // 2
    top, low = slice(0, half), slice(half, 2 * half)
    for i in range(r_ref.shape[0]):
        q, k, v, ag = head(q_ref, i), head(k_ref, i), head(v_ref, i), head(ag_ref, i)
        here = slice(i * HEAD_DIM, (i + 1) * HEAD_DIM)
        rev = r_ref[i]
        kg_ref[:, here] = (head(kin_ref, i) + dot(v, rev, NT)).astype(BF16)
        a00 = lower(dot(q[top], k[top], NT))
        a10 = dot(q[low], k[top], NT).astype(BF16)
        a11 = lower(dot(q[low], k[low], NT))
        from_rev = dot(k, rev, NN)
        vg_ref[top, here] = (dot(a00, ag[top], TN) + dot(a10, ag[low], TN) + from_rev[top]).astype(BF16)
        vg_ref[low, here] = (dot(a11, ag[low], TN) + from_rev[low]).astype(BF16)


def key_value_grads(queries, keys, values, attn_grad, rev, key_in, pair, after=()):
    tokens, channels = keys.shape
    spec = pl.BlockSpec((tokens, pair * HEAD_DIM), lambda b: (0, b))
    return pl.pallas_call(
        key_value_grad_kernel,
        grid=(channels // (pair * HEAD_DIM),),
        in_specs=[spec] * 4
        + [pl.BlockSpec((pair, HEAD_DIM, HEAD_DIM), lambda b: (b, 0, 0)), spec]
        + [pl.BlockSpec(memory_space=pl.ANY)] * len(after),
        out_specs=[spec] * 2,
        out_shape=[jax.ShapeDtypeStruct((tokens, channels), BF16)] * 2,
        compiler_params=params(24),
        cost_estimate=pl.CostEstimate(
            flops=5 * tokens * tokens * channels, bytes_accessed=16 * tokens * channels, transcendentals=0
        ),
        name="key_value_grads",
    )(queries, keys, values, attn_grad, rev, key_in, *after)


def running_kernel(reverse, after, x_ref, *refs):
    refs = refs[after:]
    o_ref = refs[-1]
    count, rows = x_ref.shape[:2]
    total = jnp.zeros(x_ref.shape[1:], F32)
    for place in range(count)[:: -1 if reverse else 1]:
        o_ref[place, :rows] = total.astype(BF16)
        total = total + x_ref[place].astype(F32)
    if len(refs) > 1:
        parts = in_parts(refs[0][...])
        width = x_ref.shape[-1]
        extra = [part[:, i : i + width] for part in parts for i in range(0, part.shape[1], width)]
        extra = extra + [jnp.zeros((1, width), F32)] * (o_ref.shape[1] - rows - len(extra))
        extra = jnp.concatenate(extra, axis=0).astype(BF16)
        for place in range(count):
            o_ref[place, rows:] = extra


def in_parts(x):
    high = x.astype(BF16).astype(F32)
    middle = (x - high).astype(BF16).astype(F32)
    return high, middle, (x - high - middle).astype(BF16).astype(F32)


def running(rows, reverse, row=None, after=()):
    count, height, width = rows.shape
    more = 0 if row is None else -(-3 * row.shape[1] // width // 16) * 16
    args = [rows, *after] + ([] if row is None else [row])
    return pl.pallas_call(
        functools.partial(running_kernel, reverse, len(after)),
        in_specs=[pl.BlockSpec()]
        + [pl.BlockSpec(memory_space=pl.ANY)] * len(after)
        + ([] if row is None else [pl.BlockSpec()]),
        out_shape=jax.ShapeDtypeStruct((count, height + more, width), BF16),
        name="running_sums",
    )(*args)


def row_total(arrived, height, channels):
    count, _, width = arrived.shape
    parts = arrived[:, height : height + 3 * channels // width].astype(F32)
    return jnp.sum(parts.reshape(count, 3, channels // width, width), axis=(0, 1)).reshape(channels)


ALL = ("y", "core", "z", "x")
SEQ = ("z", "x")
PLANE = ("y", "x")


def exchange(x, axis):
    rows = x.reshape((lax.axis_size(axis), -1) + x.shape[-1:])
    return lax.all_to_all(rows, axis, 0, 0, tiled=True)


def everyones(x, axis):
    return lax.all_to_all(jnp.broadcast_to(x[None], (lax.axis_size(axis),) + x.shape), axis, 0, 0, tiled=True)


def flipped(x, axis, bit=1):
    return lax.ppermute(x, axis, [(i, i ^ bit) for i in range(lax.axis_size(axis))])


def added(*terms):
    total = terms[0].astype(F32)
    for term in terms[1:]:
        total = total + term.astype(F32)
    return total


def together(*xs):
    return lax.optimization_barrier(xs)


def small_call(kernel, out_shapes, *args, after=()):
    def call(*refs):
        kernel(*refs[: len(args)], *refs[len(args) + len(after) :])

    return pl.pallas_call(
        call,
        in_specs=[pl.BlockSpec()] * len(args)
        + [pl.BlockSpec(memory_space=pl.ANY)] * len(after),
        out_shape=[jax.ShapeDtypeStruct(shape, F32 if shape == END else BF16) for shape in out_shapes],
        compiler_params=pltpu.CompilerParams(vmem_limit_bytes=24 * MIB),
        cost_estimate=pl.CostEstimate(
            flops=0, bytes_accessed=4 * sum(x.size for x in args), transcendentals=0
        ),
        name=kernel.__name__,
    )(*args, *after)


def one(i):
    return pl.ds(i, 1)


def place(axis, bit=1):
    here = (lax.axis_index(axis) // bit) % 2
    return here, 1 - here


def merge_far(mine_ref, theirs_ref, out_ref):
    here, there = place("z", 2)
    out_ref[one(here)] = mine_ref[...][None]
    out_ref[one(there)] = theirs_ref[...][None]


def merge_near(mine_ref, theirs_ref, left_ref, right_ref, end_ref):
    end_ref[...] = jnp.zeros_like(end_ref)
    here, there = place("z")
    half = left_ref.shape[-1]
    for at, ref in ((here, mine_ref), (there, theirs_ref)):
        left_ref[:, one(at)] = ref[:, :, :half][:, None]
        right_ref[:, one(at)] = ref[:, :, half:][:, None]


def merge_sides(left_ref, left_got_ref, right_ref, right_got_ref, left_out_ref, right_out_ref):
    here, there = place("x")
    left_out_ref[:, one(here)] = left_ref[...][:, None]
    left_out_ref[:, one(there)] = left_got_ref[...][:, None]
    here, there = place("y")
    right_out_ref[one(here)] = right_ref[...][None]
    right_out_ref[one(there)] = right_got_ref[...][None]


def merge_all(left_ref, left_got_ref, right_ref, right_got_ref, out_ref):
    half = left_ref.shape[-1]
    here, there = place("y")
    out_ref[one(here), :, :, :, :half] = left_ref[...][None]
    out_ref[one(there), :, :, :, :half] = left_got_ref[...][None]
    here, there = place("x")
    out_ref[:, :, one(here), :, half:] = right_ref[...][:, :, None]
    out_ref[:, :, one(there), :, half:] = right_got_ref[...][:, :, None]


def total(a_ref, b_ref, *index):
    return (a_ref[index].astype(F32) + b_ref[index].astype(F32)).astype(BF16)


def split_first(keep_ref, got_ref, left_ref, right_ref, left_keep_ref, right_keep_ref):
    half = left_ref.shape[-1]
    here, there = place("y")
    every = slice(None)
    for at, ref in ((there, left_ref), (here, left_keep_ref)):
        ref[...] = total(keep_ref, got_ref, one(at), every, every, every, slice(0, half))[0]
    here, there = place("x")
    for at, ref in ((there, right_ref), (here, right_keep_ref)):
        ref[...] = total(keep_ref, got_ref, every, every, one(at), every, slice(half, 2 * half))[:, :, 0]


def split_second(
    left_ref, left_got_ref, right_ref, right_got_ref, left_out, right_out, left_keep, right_keep, end_ref
):
    end_ref[...] = jnp.zeros_like(end_ref)
    here, there = place("x")
    for at, ref in ((there, left_out), (here, left_keep)):
        ref[...] = total(left_ref, left_got_ref, slice(None), one(at))[:, 0]
    here, there = place("y")
    for at, ref in ((there, right_out), (here, right_keep)):
        ref[...] = total(right_ref, right_got_ref, one(at))[0]


def join_sides(left_ref, left_got_ref, right_ref, right_got_ref, out_ref, end_ref):
    end_ref[...] = jnp.zeros_like(end_ref)
    half = left_ref.shape[-1]
    out_ref[:, :, :half] = total(left_ref, left_got_ref, slice(None))
    out_ref[:, :, half:] = total(right_ref, right_got_ref, slice(None))


def by_halves(sizes, rows, q, k, v, og, out_weight, gain_row, pos, pair):
    tokens, channels = q.shape
    wide = out_weight.shape[1]
    y, z, x, half = sizes["y"], sizes["z"], sizes["x"], wide // 2

    got = flipped(out_weight, "z", 2)
    kv, k, v = key_value_sums(k, v, pair)
    (weight,) = small_call(merge_far, [(2, rows, wide)], out_weight, got)

    got = flipped(weight, "z", 1)
    sent = exchange(kv, SEQ)
    intra, q, intra_end = intra_outputs(q, k, v, pair)
    left, right, end = small_call(
        merge_near, [(2, 2, rows, half)] * 2 + [END], weight, got, after=(intra_end,)
    )
    left, right = left.reshape(z, rows, half), right.reshape(z, rows, half)
    left_got, right_got = flipped(left, "x"), flipped(right, "y")
    state = exchange(running(sent, False, after=(end,)), SEQ).reshape(kv.shape)
    state, left_got, right_got = together(state, left_got, right_got)
    left, right = small_call(
        merge_sides, [(z, x, rows, half), (y, z, rows, half)], left, left_got, right, right_got
    )

    state, left, right = together(state, left, right)
    left_got, right_got = flipped(left, "y"), flipped(right, "x")
    outputs, send, keep, og = weight_parts(pos, q, state, intra, gain_row, og, pair)
    send, left_got, right_got = together(send, left_got, right_got)
    got = flipped(send, "core")
    (mine,) = small_call(merge_all, [(y, z, x, rows, wide)], left, left_got, right, right_got)
    mine = mine.reshape(y, -1, wide)
    other = flipped(mine, "core")
    begun = attn_grads(pos, 0, q, outputs, gain_row, og, mine, pair)

    split = (y, z, x, rows, wide)
    left, right, left_keep, right_keep = small_call(
        split_first,
        [(z, x, rows, half), (y, z, rows, half)] * 2,
        keep.reshape(split),
        got.reshape(split),
        after=(begun[1],),
    )
    other, left, right = together(other, left, right)
    left_got, right_got = flipped(left, "y"), flipped(right, "x")
    attn_grad, gain_part, qg = attn_grads(pos, 1, q, outputs, gain_row, og, other, pair, begun)

    sent = exchange(qg, SEQ)
    gain_part = gain_part + flipped(gain_part, "core")
    gain_part = gain_part + flipped(gain_part, "y")
    left, right, left_keep, right_keep, end = small_call(
        split_second, [(z, rows, half)] * 4 + [END], left_keep, left_got, right_keep, right_got
    )
    left_got, right_got = flipped(left, "x"), flipped(right, "y")
    sums = running(sent, True, gain_part)
    arrived = exchange(sums, SEQ)
    query_g, key_in = query_grads(q, k, v, attn_grad, state, pair, after=(sums, end))
    part, end = small_call(
        join_sides, [(z, rows, wide), END], left_keep, left_got, right_keep, right_got, after=(sums,)
    )
    part = lax.all_to_all(part, "z", 0, 0, tiled=True)
    key_g, value_g = key_value_grads(q, k, v, attn_grad, arrived, key_in, pair, after=(end,))
    return query_g, key_g, value_g, part, row_total(arrived, sent.shape[1], channels)


def by_planes(sizes, rows, q, k, v, og, out_weight, gain_row, pos, pair):
    tokens, channels = q.shape
    wide = out_weight.shape[1]
    y, z, x = sizes["y"], sizes["z"], sizes["x"]
    weight = everyones(everyones(out_weight, "z"), PLANE)
    weight = weight.reshape(y, x, z, rows, wide).transpose(0, 2, 1, 3, 4).reshape(y, -1, wide)
    kv, k, v = key_value_sums(k, v, pair)
    intra, q, _ = intra_outputs(q, k, v, pair)
    state = exchange(running(exchange(kv, SEQ), False), SEQ).reshape(kv.shape)
    outputs, send, keep, og = weight_parts(pos, q, state, intra, gain_row, og, pair)
    part = added(keep, flipped(send, "core")).astype(BF16)
    part = part.reshape(y, z, x, rows, wide).transpose(0, 2, 1, 3, 4).reshape(y * x, z, rows, wide)
    part = lax.all_to_all(part, PLANE, 0, 0, tiled=True)
    part = added(*[part[i] for i in range(y * x)]).astype(BF16)
    part = lax.all_to_all(part, "z", 0, 0, tiled=True)
    begun = attn_grads(pos, 0, q, outputs, gain_row, og, weight, pair)
    attn_grad, gain_part, qg = attn_grads(
        pos, 1, q, outputs, gain_row, og, flipped(weight, "core"), pair, begun
    )
    rev = exchange(running(exchange(qg, SEQ), True), SEQ).reshape(kv.shape)
    query_g, key_in = query_grads(q, k, v, attn_grad, state, pair)
    key_g, value_g = key_value_grads(q, k, v, attn_grad, rev, key_in, pair)
    gain_sum = jnp.sum(everyones(gain_part.reshape(channels), ALL), axis=0)
    return query_g, key_g, value_g, part, gain_sum


def shards(queries, keys, values, out_grad, out_weight, gain):
    tokens, channels = queries.shape[1:]
    assert tokens == BLOCK
    sizes = {name: lax.axis_size(name) for name in ALL}
    devices = lax.axis_size(ALL)
    rows = out_weight.shape[0]
    pair = channels // (sizes["y"] * sizes["core"]) // HEAD_DIM
    pos = lax.axis_index(("y", "core")).reshape(1).astype(jnp.int32)
    halves = (sizes["y"], sizes["z"], sizes["x"]) == (2, 4, 2) and rows % 16 == 0
    query_g, key_g, value_g, part, gain_sum = (by_halves if halves else by_planes)(
        sizes,
        rows,
        queries[0],
        keys[0],
        values[0],
        out_grad[0],
        out_weight,
        gain.reshape(1, channels),
        pos,
        pair,
    )
    factor = 1.0 / jnp.sqrt(jnp.float32(tokens * devices))
    out_shape = (1, tokens, channels)
    return (
        query_g.reshape(out_shape),
        key_g.reshape(out_shape),
        value_g.reshape(out_shape),
        added(*[part[i] for i in range(part.shape[0])]) * factor,
        gain_sum * factor,
    )


def solution(mesh):
    dp_count, seq_count = mesh.shape["dp"], mesh.shape["seq"]
    finer = Mesh(mesh.devices.reshape(dp_count // 2, 2, seq_count // 2, 2), ALL)
    tokens = P(("y", "core"), ("z", "x"), None)
    rows = P(ALL, None)
    return jax.shard_map(
        shards,
        mesh=finer,
        in_specs=(tokens, tokens, tokens, tokens, rows, P()),
        out_specs=(tokens, tokens, tokens, rows, P()),
        check_vma=False,
    )
```

```python
import functools

import jax
import jax.numpy as jnp
from jax import lax
from jax.experimental import pallas as pl
from jax.experimental.pallas import tpu as pltpu
from jax.sharding import Mesh
from jax.sharding import PartitionSpec as P

HEAD_DIM = 128
BLOCK = 512
MIB = 1 << 20

norm_eps = 1e-06

END = (8, 128)

F32 = jnp.float32
BF16 = jnp.bfloat16


def dot(a, b, contract):
    return lax.dot_general(a, b, (contract, ((), ())), preferred_element_type=F32)


def params(mib, dims=1):
    return pltpu.CompilerParams(
        vmem_limit_bytes=mib * MIB, dimension_semantics=("arbitrary",) * dims
    )


ROW_BLOCKS = 4


def row_blocks(tokens, wide):
    return [
        pl.BlockSpec((tokens // ROW_BLOCKS, wide), lambda y, p, r=r: (r, 0)) for r in range(ROW_BLOCKS)
    ]


def head(ref, i):
    return ref[:, i * HEAD_DIM : (i + 1) * HEAD_DIM]


def kv_kernel(k_ref, v_ref, o_ref, k_out_ref, v_out_ref):
    k_out_ref[...] = k_ref[...]
    v_out_ref[...] = v_ref[...]
    for i in range(o_ref.shape[0]):
        o_ref[i] = dot(head(k_ref, i), head(v_ref, i), ((0,), (0,))).astype(BF16)


def key_value_sums(keys, values, pair):
    tokens, channels = keys.shape
    width = pair * HEAD_DIM
    heads = channels // HEAD_DIM
    spec = pl.BlockSpec((tokens, width), lambda b: (0, b))
    return pl.pallas_call(
        kv_kernel,
        grid=(heads // pair,),
        in_specs=[spec, spec],
        out_specs=[pl.BlockSpec((pair, HEAD_DIM, HEAD_DIM), lambda b: (b, 0, 0)), spec, spec],
        out_shape=[
            jax.ShapeDtypeStruct((heads, HEAD_DIM, HEAD_DIM), BF16),
            jax.ShapeDtypeStruct(keys.shape, BF16),
            jax.ShapeDtypeStruct(keys.shape, BF16),
        ],
        compiler_params=params(40),
        cost_estimate=pl.CostEstimate(
            flops=2 * tokens * channels * HEAD_DIM, bytes_accessed=4 * tokens * channels, transcendentals=0
        ),
        name="key_value_sums",
    )(keys, values)


def lower(x):
    rows = lax.broadcasted_iota(jnp.int32, x.shape, 0)
    cols = lax.broadcasted_iota(jnp.int32, x.shape, 1)
    return jnp.where(cols <= rows, x, 0.0).astype(BF16)


def intra_kernel(q_ref, k_ref, v_ref, o_ref, q_out_ref, end_ref):
    q_out_ref[...] = q_ref[...]
    end_ref[...] = jnp.zeros_like(end_ref)
    half = q_ref.shape[0] // 2
    for i in range(o_ref.shape[1] // HEAD_DIM):
        q, k, v = head(q_ref, i), head(k_ref, i), head(v_ref, i)
        here = slice(i * HEAD_DIM, (i + 1) * HEAD_DIM)
        top = lower(dot(q[:half], k[:half], ((1,), (1,))))
        o_ref[:half, here] = dot(top, v[:half], ((1,), (0,)))
        left = dot(q[half:], k[:half], ((1,), (1,))).astype(BF16)
        right = lower(dot(q[half:], k[half:], ((1,), (1,))))
        o_ref[half:, here] = dot(left, v[:half], ((1,), (0,))) + dot(right, v[half:], ((1,), (0,)))


def intra_outputs(queries, keys, values, pair):
    tokens, channels = keys.shape
    spec = pl.BlockSpec((tokens, pair * HEAD_DIM), lambda b: (0, b))
    return pl.pallas_call(
        intra_kernel,
        grid=(channels // (pair * HEAD_DIM),),
        in_specs=[spec] * 3,
        out_specs=[spec, spec, pl.BlockSpec(END, lambda b: (0, 0))],
        out_shape=[jax.ShapeDtypeStruct((tokens, channels), t) for t in (F32, BF16)]
        + [jax.ShapeDtypeStruct(END, F32)],
        compiler_params=params(24),
        cost_estimate=pl.CostEstimate(
            flops=4 * tokens * tokens * channels, bytes_accessed=10 * tokens * channels, transcendentals=0
        ),
        name="intra_outputs",
    )(queries, keys, values)


def rms_inverse(x):
    return lax.rsqrt(jnp.mean(x * x, axis=-1, keepdims=True) + norm_eps)


def unit_kernel(begun, pos_ref, q_ref, s_ref, intra_ref, gain_ref, *refs):
    og_refs, refs = refs[:ROW_BLOCKS], refs[ROW_BLOCKS + begun :]
    out_ref, part_ref = refs[:2]
    units = []
    for i in range(s_ref.shape[0]):
        x = head(intra_ref, i) + dot(head(q_ref, i), s_ref[i], ((1,), (0,)))
        out_ref[:, i * HEAD_DIM : (i + 1) * HEAD_DIM] = x
        units.append((x * rms_inverse(x) * head(gain_ref, i)).astype(BF16))
    unit = jnp.concatenate(units, axis=1) if len(units) > 1 else units[0]
    og = jnp.concatenate([og_ref[...] for og_ref in og_refs], axis=0)
    part_ref[0] = dot(unit, og, ((0,), (0,))).astype(BF16)

    if len(refs) > 2:

        @pl.when(pl.program_id(0) == 0)
        def _():
            refs[2][...] = og


def weight_parts(pos, side, queries, state, intra, gain, out_grad, pair, begun=()):
    tokens, channels = queries.shape
    width = pair * HEAD_DIM
    count = channels // width // 2
    wide = out_grad.shape[1]

    def block(y, pos_ref):
        return 2 * y + lax.rem(pos_ref[0] + side, 2)

    cols = pl.BlockSpec((tokens, width), lambda y, p: (0, block(y, p)))
    whole = pl.BlockSpec((tokens, wide), lambda y, p: (0, 0))
    more = [] if begun else [(whole, jax.ShapeDtypeStruct((tokens, wide), BF16))]
    return pl.pallas_call(
        functools.partial(unit_kernel, len(begun)),
        grid_spec=pltpu.PrefetchScalarGridSpec(
            num_scalar_prefetch=1,
            grid=(count,),
            in_specs=[
                cols,
                pl.BlockSpec((pair, HEAD_DIM, HEAD_DIM), lambda y, p: (block(y, p), 0, 0)),
                cols,
                pl.BlockSpec((1, width), lambda y, p: (0, block(y, p))),
            ]
            + row_blocks(tokens, wide)
            + [pl.BlockSpec(memory_space=pl.ANY)] * len(begun),
            out_specs=[cols, pl.BlockSpec((1, width, wide), lambda y, p: (y, 0, 0))] + [m[0] for m in more],
        ),
        out_shape=[
            jax.ShapeDtypeStruct((tokens, channels), F32),
            jax.ShapeDtypeStruct((count, width, wide), BF16),
        ]
        + [m[1] for m in more],
        input_output_aliases={5 + ROW_BLOCKS: 0} if begun else {},
        compiler_params=params(24),
        cost_estimate=pl.CostEstimate(
            flops=tokens * channels * wide,
            bytes_accessed=5 * tokens * channels + 2 * tokens * wide + channels * wide,
            transcendentals=0,
        ),
        name="weight_parts",
    )(pos, queries, state, intra, gain, *[out_grad] * ROW_BLOCKS, *begun)


def attn_grad_kernel(pos_ref, q_ref, o_ref, gain_ref, *refs):
    *og_refs, mine_ref, other_ref, ag_ref, gg_ref, qg_ref, ug_ref = refs

    def project(ref):
        start = 0
        for og_ref in og_refs:
            stop = start + og_ref.shape[0]
            ug_ref[start:stop] = dot(og_ref[...], ref[0], ((1,), (1,)))
            start = stop

    count = pl.num_programs(0) // 2

    @pl.when(pl.program_id(0) < count)
    def _():
        project(mine_ref)

    @pl.when(pl.program_id(0) >= count)
    def _():
        project(other_ref)

    for i in range(qg_ref.shape[0]):
        here = slice(i * HEAD_DIM, (i + 1) * HEAD_DIM)
        x = head(o_ref, i)
        inverse = rms_inverse(x)
        normed = x * inverse
        ug = head(ug_ref, i)
        gg_ref[:, here] = jnp.sum(ug * normed, axis=0, keepdims=True)
        scaled = ug * head(gain_ref, i)
        middle = jnp.mean(scaled * normed, axis=-1, keepdims=True)
        ag = ((scaled - normed * middle) * inverse).astype(BF16)
        ag_ref[:, here] = ag
        qg_ref[i] = dot(head(q_ref, i), ag, ((0,), (0,))).astype(BF16)


def attn_grads(pos, queries, outputs, gain, out_grad, mine, other, pair):
    tokens, channels = queries.shape
    width = pair * HEAD_DIM
    count = channels // width // 2
    wide = out_grad.shape[1]
    heads = channels // HEAD_DIM

    def block(s, pos_ref):
        return 2 * lax.rem(s, count) + lax.rem(pos_ref[0] + s // count, 2)

    cols = pl.BlockSpec((tokens, width), lambda s, p: (0, block(s, p)))
    row = pl.BlockSpec((1, width), lambda s, p: (0, block(s, p)))
    states = pl.BlockSpec((pair, HEAD_DIM, HEAD_DIM), lambda s, p: (block(s, p), 0, 0))
    piece = (1,) + mine.shape[1:]
    return pl.pallas_call(
        attn_grad_kernel,
        grid_spec=pltpu.PrefetchScalarGridSpec(
            num_scalar_prefetch=1,
            grid=(2 * count,),
            in_specs=[cols, cols, row]
            + row_blocks(tokens, wide)
            + [
                pl.BlockSpec(piece, lambda s, p: (jnp.minimum(s, count - 1), 0, 0)),
                pl.BlockSpec(piece, lambda s, p: (jnp.maximum(s - count, 0), 0, 0)),
            ],
            out_specs=[cols, row, states],
            scratch_shapes=[pltpu.VMEM((tokens, width), F32)],
        ),
        out_shape=[
            jax.ShapeDtypeStruct((tokens, channels), BF16),
            jax.ShapeDtypeStruct((1, channels), F32),
            jax.ShapeDtypeStruct((heads, HEAD_DIM, HEAD_DIM), BF16),
        ],
        compiler_params=params(24),
        cost_estimate=pl.CostEstimate(
            flops=2 * tokens * channels * wide,
            bytes_accessed=8 * tokens * channels + 2 * tokens * wide + 2 * channels * wide,
            transcendentals=0,
        ),
        name="attn_grads",
    )(pos, queries, outputs, gain, *[out_grad] * ROW_BLOCKS, mine, other)


NT, NN, TN = ((1,), (1,)), ((1,), (0,)), ((0,), (0,))


def query_grad_kernel(q_ref, k_ref, v_ref, ag_ref, s_ref, *refs):
    qg_ref, kg_ref = refs[-2:]
    half = q_ref.shape[0] // 2
    top, low = slice(0, half), slice(half, 2 * half)
    for i in range(s_ref.shape[0]):
        q, k, v, ag = head(q_ref, i), head(k_ref, i), head(v_ref, i), head(ag_ref, i)
        here = slice(i * HEAD_DIM, (i + 1) * HEAD_DIM)
        from_state = dot(ag, s_ref[i], NT)
        g00 = lower(dot(ag[top], v[top], NT))
        g10 = dot(ag[low], v[top], NT).astype(BF16)
        g11 = lower(dot(ag[low], v[low], NT))
        qg_ref[top, here] = (dot(g00, k[top], NN) + from_state[top]).astype(BF16)
        qg_ref[low, here] = (dot(g10, k[top], NN) + dot(g11, k[low], NN) + from_state[low]).astype(BF16)
        kg_ref[top, here] = dot(g00, q[top], TN) + dot(g10, q[low], TN)
        kg_ref[low, here] = dot(g11, q[low], TN)


def query_grads(queries, keys, values, attn_grad, state, pair, after=()):
    tokens, channels = queries.shape
    spec = pl.BlockSpec((tokens, pair * HEAD_DIM), lambda b: (0, b))
    return pl.pallas_call(
        query_grad_kernel,
        grid=(channels // (pair * HEAD_DIM),),
        in_specs=[spec] * 4
        + [pl.BlockSpec((pair, HEAD_DIM, HEAD_DIM), lambda b: (b, 0, 0))]
        + [pl.BlockSpec(memory_space=pl.ANY)] * len(after),
        out_specs=[spec] * 2,
        out_shape=[jax.ShapeDtypeStruct((tokens, channels), t) for t in (BF16, F32)],
        compiler_params=params(24),
        cost_estimate=pl.CostEstimate(
            flops=6 * tokens * tokens * channels, bytes_accessed=14 * tokens * channels, transcendentals=0
        ),
        name="query_grads",
    )(queries, keys, values, attn_grad, state, *after)


def key_value_grad_kernel(q_ref, k_ref, v_ref, ag_ref, r_ref, kin_ref, *refs):
    kg_ref, vg_ref = refs[-2:]
    half = q_ref.shape[0] // 2
    top, low = slice(0, half), slice(half, 2 * half)
    for i in range(r_ref.shape[0]):
        q, k, v, ag = head(q_ref, i), head(k_ref, i), head(v_ref, i), head(ag_ref, i)
        here = slice(i * HEAD_DIM, (i + 1) * HEAD_DIM)
        rev = r_ref[i]
        kg_ref[:, here] = (head(kin_ref, i) + dot(v, rev, NT)).astype(BF16)
        a00 = lower(dot(q[top], k[top], NT))
        a10 = dot(q[low], k[top], NT).astype(BF16)
        a11 = lower(dot(q[low], k[low], NT))
        from_rev = dot(k, rev, NN)
        vg_ref[top, here] = (dot(a00, ag[top], TN) + dot(a10, ag[low], TN) + from_rev[top]).astype(BF16)
        vg_ref[low, here] = (dot(a11, ag[low], TN) + from_rev[low]).astype(BF16)


def key_value_grads(queries, keys, values, attn_grad, rev, key_in, pair, after=()):
    tokens, channels = keys.shape
    spec = pl.BlockSpec((tokens, pair * HEAD_DIM), lambda b: (0, b))
    return pl.pallas_call(
        key_value_grad_kernel,
        grid=(channels // (pair * HEAD_DIM),),
        in_specs=[spec] * 4
        + [pl.BlockSpec((pair, HEAD_DIM, HEAD_DIM), lambda b: (b, 0, 0)), spec]
        + [pl.BlockSpec(memory_space=pl.ANY)] * len(after),
        out_specs=[spec] * 2,
        out_shape=[jax.ShapeDtypeStruct((tokens, channels), BF16)] * 2,
        compiler_params=params(24),
        cost_estimate=pl.CostEstimate(
            flops=5 * tokens * tokens * channels, bytes_accessed=16 * tokens * channels, transcendentals=0
        ),
        name="key_value_grads",
    )(queries, keys, values, attn_grad, rev, key_in, *after)


def running_kernel(reverse, after, x_ref, *refs):
    refs = refs[after:]
    o_ref = refs[-1]
    count, rows = x_ref.shape[:2]
    total = jnp.zeros(x_ref.shape[1:], F32)
    for place in range(count)[:: -1 if reverse else 1]:
        o_ref[place, :rows] = total.astype(BF16)
        total = total + x_ref[place].astype(F32)
    if len(refs) > 1:
        parts = in_parts(refs[0][...])
        width = x_ref.shape[-1]
        extra = [part[:, i : i + width] for part in parts for i in range(0, part.shape[1], width)]
        extra = extra + [jnp.zeros((1, width), F32)] * (o_ref.shape[1] - rows - len(extra))
        extra = jnp.concatenate(extra, axis=0).astype(BF16)
        for place in range(count):
            o_ref[place, rows:] = extra


def in_parts(x):
    high = x.astype(BF16).astype(F32)
    middle = (x - high).astype(BF16).astype(F32)
    return high, middle, (x - high - middle).astype(BF16).astype(F32)


def running(rows, reverse, row=None, after=()):
    count, height, width = rows.shape
    more = 0 if row is None else -(-3 * row.shape[1] // width // 16) * 16
    args = [rows, *after] + ([] if row is None else [row])
    return pl.pallas_call(
        functools.partial(running_kernel, reverse, len(after)),
        in_specs=[pl.BlockSpec()]
        + [pl.BlockSpec(memory_space=pl.ANY)] * len(after)
        + ([] if row is None else [pl.BlockSpec()]),
        out_shape=jax.ShapeDtypeStruct((count, height + more, width), BF16),
        compiler_params=pltpu.CompilerParams(vmem_limit_bytes=8 * MIB),
        name="running_sums",
    )(*args)


def row_total(arrived, height, channels):
    count, _, width = arrived.shape
    parts = arrived[:, height : height + 3 * channels // width].astype(F32)
    return jnp.sum(parts.reshape(count, 3, channels // width, width), axis=(0, 1)).reshape(channels)


ALL = ("y", "core", "z", "x")
SEQ = ("z", "x")
PLANE = ("y", "x")


def exchange(x, axis):
    rows = x.reshape((lax.axis_size(axis), -1) + x.shape[-1:])
    return lax.all_to_all(rows, axis, 0, 0, tiled=True)


def everyones(x, axis):
    return lax.all_to_all(jnp.broadcast_to(x[None], (lax.axis_size(axis),) + x.shape), axis, 0, 0, tiled=True)


def flipped(x, axis, bit=1):
    return lax.ppermute(x, axis, [(i, i ^ bit) for i in range(lax.axis_size(axis))])


def added(*terms):
    total = terms[0].astype(F32)
    for term in terms[1:]:
        total = total + term.astype(F32)
    return total


def together(*xs):
    return lax.optimization_barrier(xs)


def small_call(kernel, out_shapes, *args, after=()):
    def call(*refs):
        kernel(*refs[: len(args)], *refs[len(args) + len(after) :])

    return pl.pallas_call(
        call,
        in_specs=[pl.BlockSpec()] * len(args)
        + [pl.BlockSpec(memory_space=pl.ANY)] * len(after),
        out_shape=[jax.ShapeDtypeStruct(shape, F32 if shape == END else BF16) for shape in out_shapes],
        compiler_params=pltpu.CompilerParams(vmem_limit_bytes=20 * MIB),
        cost_estimate=pl.CostEstimate(
            flops=0, bytes_accessed=4 * sum(x.size for x in args), transcendentals=0
        ),
        name=kernel.__name__,
    )(*args, *after)


def one(i):
    return pl.ds(i, 1)


def place(axis, bit=1):
    here = (lax.axis_index(axis) // bit) % 2
    return here, 1 - here


def merge_far(mine_ref, theirs_ref, out_ref):
    here, there = place("z", 2)
    out_ref[one(here)] = mine_ref[...][None]
    out_ref[one(there)] = theirs_ref[...][None]


def merge_near(mine_ref, theirs_ref, left_ref, right_ref, end_ref):
    end_ref[...] = jnp.zeros_like(end_ref)
    here, there = place("z")
    half = left_ref.shape[-1]
    for at, ref in ((here, mine_ref), (there, theirs_ref)):
        left_ref[:, one(at)] = ref[:, :, :half][:, None]
        right_ref[:, one(at)] = ref[:, :, half:][:, None]


def merge_sides(left_ref, left_got_ref, right_ref, right_got_ref, left_out_ref, right_out_ref):
    here, there = place("x")
    left_out_ref[:, one(here)] = left_ref[...][:, None]
    left_out_ref[:, one(there)] = left_got_ref[...][:, None]
    here, there = place("y")
    right_out_ref[one(here)] = right_ref[...][None]
    right_out_ref[one(there)] = right_got_ref[...][None]


def merge_all(left_ref, left_got_ref, right_ref, right_got_ref, out_ref):
    half = left_ref.shape[-1]
    here, there = place("y")
    out_ref[one(here), :, :, :, :half] = left_ref[...][None]
    out_ref[one(there), :, :, :, :half] = left_got_ref[...][None]
    here, there = place("x")
    out_ref[:, :, one(here), :, half:] = right_ref[...][:, :, None]
    out_ref[:, :, one(there), :, half:] = right_got_ref[...][:, :, None]


def total(a_ref, b_ref, *index):
    return (a_ref[index].astype(F32) + b_ref[index].astype(F32)).astype(BF16)


def split_first(keep_ref, got_ref, left_ref, right_ref, left_keep_ref, right_keep_ref):
    half = left_ref.shape[-1]
    here, there = place("y")
    every = slice(None)
    for at, ref in ((there, left_ref), (here, left_keep_ref)):
        ref[...] = total(keep_ref, got_ref, one(at), every, every, every, slice(0, half))[0]
    here, there = place("x")
    for at, ref in ((there, right_ref), (here, right_keep_ref)):
        ref[...] = total(keep_ref, got_ref, every, every, one(at), every, slice(half, 2 * half))[:, :, 0]


def split_second(
    left_ref, left_got_ref, right_ref, right_got_ref, left_out, right_out, left_keep, right_keep, end_ref
):
    end_ref[...] = jnp.zeros_like(end_ref)
    here, there = place("x")
    for at, ref in ((there, left_out), (here, left_keep)):
        ref[...] = total(left_ref, left_got_ref, slice(None), one(at))[:, 0]
    here, there = place("y")
    for at, ref in ((there, right_out), (here, right_keep)):
        ref[...] = total(right_ref, right_got_ref, one(at))[0]


def join_sides(left_ref, left_got_ref, right_ref, right_got_ref, out_ref, end_ref):
    end_ref[...] = jnp.zeros_like(end_ref)
    half = left_ref.shape[-1]
    out_ref[:, :, :half] = total(left_ref, left_got_ref, slice(None))
    out_ref[:, :, half:] = total(right_ref, right_got_ref, slice(None))


def by_halves(sizes, rows, q, k, v, og, out_weight, gain_row, pos, pair):
    tokens, channels = q.shape
    wide = out_weight.shape[1]
    y, z, x, half = sizes["y"], sizes["z"], sizes["x"], wide // 2

    got = flipped(out_weight, "z", 2)
    kv, k, v = key_value_sums(k, v, pair)
    kv, got = together(kv, got)
    (weight,) = small_call(merge_far, [(2, rows, wide)], out_weight, got)

    got = flipped(weight, "z", 1)
    sent = exchange(kv, SEQ)
    intra, q, intra_end = intra_outputs(q, k, v, pair)
    left, right, end = small_call(
        merge_near, [(2, 2, rows, half)] * 2 + [END], weight, got, after=(intra_end,)
    )
    left, right = left.reshape(z, rows, half), right.reshape(z, rows, half)
    left_got, right_got = flipped(left, "x"), flipped(right, "y")
    state = exchange(running(sent, False, after=(end,)), SEQ).reshape(kv.shape)
    state, left_got, right_got = together(state, left_got, right_got)
    left, right = small_call(
        merge_sides, [(z, x, rows, half), (y, z, rows, half)], left, left_got, right, right_got
    )

    state, left, right = together(state, left, right)
    left_got, right_got = flipped(left, "y"), flipped(right, "x")
    outputs, send, og = weight_parts(pos, 1, q, state, intra, gain_row, og, pair)
    send, left_got, right_got = together(send, left_got, right_got)
    got = flipped(send, "core")
    (mine,) = small_call(merge_all, [(y, z, x, rows, wide)], left, left_got, right, right_got)
    mine = mine.reshape(y, -1, wide)
    other = flipped(mine, "core")
    outputs, keep = weight_parts(pos, 0, q, state, intra, gain_row, og, pair, (outputs,))

    split = (y, z, x, rows, wide)
    left, right, left_keep, right_keep = small_call(
        split_first,
        [(z, x, rows, half), (y, z, rows, half)] * 2,
        keep.reshape(split),
        got.reshape(split),
    )
    other, left, right = together(other, left, right)
    left_got, right_got = flipped(left, "y"), flipped(right, "x")
    attn_grad, gain_part, qg = attn_grads(pos, q, outputs, gain_row, og, mine, other, pair)
    qg, left_got, right_got = together(qg, left_got, right_got)

    sent = exchange(qg, SEQ)
    gain_part = gain_part + flipped(gain_part, "core")
    left, right, left_keep, right_keep, end = small_call(
        split_second, [(z, rows, half)] * 4 + [END], left_keep, left_got, right_keep, right_got
    )
    left_got, right_got = flipped(left, "x"), flipped(right, "y")
    sums = running(sent, True, gain_part, after=(end,))
    arrived = exchange(sums, SEQ)
    query_g, key_in = query_grads(q, k, v, attn_grad, state, pair, after=(sums,))
    part, end = small_call(
        join_sides, [(z, rows, wide), END], left_keep, left_got, right_keep, right_got, after=(sums,)
    )
    part = lax.all_to_all(part, "z", 0, 0, tiled=True)
    key_g, value_g = key_value_grads(q, k, v, attn_grad, arrived, key_in, pair, after=(end,))
    gain_sum = row_total(arrived, sent.shape[1], channels)
    return query_g, key_g, value_g, part, gain_sum + flipped(gain_sum, "y")


def by_planes(sizes, rows, q, k, v, og, out_weight, gain_row, pos, pair):
    tokens, channels = q.shape
    wide = out_weight.shape[1]
    y, z, x = sizes["y"], sizes["z"], sizes["x"]
    weight = everyones(everyones(out_weight, "z"), PLANE)
    weight = weight.reshape(y, x, z, rows, wide).transpose(0, 2, 1, 3, 4).reshape(y, -1, wide)
    kv, k, v = key_value_sums(k, v, pair)
    intra, q, _ = intra_outputs(q, k, v, pair)
    state = exchange(running(exchange(kv, SEQ), False), SEQ).reshape(kv.shape)
    outputs, send, og = weight_parts(pos, 1, q, state, intra, gain_row, og, pair)
    outputs, keep = weight_parts(pos, 0, q, state, intra, gain_row, og, pair, (outputs,))
    part = added(keep, flipped(send, "core")).astype(BF16)
    part = part.reshape(y, z, x, rows, wide).transpose(0, 2, 1, 3, 4).reshape(y * x, z, rows, wide)
    part = lax.all_to_all(part, PLANE, 0, 0, tiled=True)
    part = added(*[part[i] for i in range(y * x)]).astype(BF16)
    part = lax.all_to_all(part, "z", 0, 0, tiled=True)
    attn_grad, gain_part, qg = attn_grads(
        pos, q, outputs, gain_row, og, weight, flipped(weight, "core"), pair
    )
    rev = exchange(running(exchange(qg, SEQ), True), SEQ).reshape(kv.shape)
    query_g, key_in = query_grads(q, k, v, attn_grad, state, pair)
    key_g, value_g = key_value_grads(q, k, v, attn_grad, rev, key_in, pair)
    gain_sum = jnp.sum(everyones(gain_part.reshape(channels), ALL), axis=0)
    return query_g, key_g, value_g, part, gain_sum


def shards(queries, keys, values, out_grad, out_weight, gain):
    tokens, channels = queries.shape[1:]
    assert tokens == BLOCK
    sizes = {name: lax.axis_size(name) for name in ALL}
    devices = lax.axis_size(ALL)
    rows = out_weight.shape[0]
    pair = channels // (sizes["y"] * sizes["core"]) // HEAD_DIM
    pos = lax.axis_index(("y", "core")).reshape(1).astype(jnp.int32)
    halves = (sizes["y"], sizes["z"], sizes["x"]) == (2, 4, 2) and rows % 16 == 0
    query_g, key_g, value_g, part, gain_sum = (by_halves if halves else by_planes)(
        sizes,
        rows,
        queries[0],
        keys[0],
        values[0],
        out_grad[0],
        out_weight,
        gain.reshape(1, channels),
        pos,
        pair,
    )
    factor = 1.0 / jnp.sqrt(jnp.float32(tokens * devices))
    out_shape = (1, tokens, channels)
    return (
        query_g.reshape(out_shape),
        key_g.reshape(out_shape),
        value_g.reshape(out_shape),
        added(*[part[i] for i in range(part.shape[0])]) * factor,
        gain_sum * factor,
    )


def solution(mesh):
    dp_count, seq_count = mesh.shape["dp"], mesh.shape["seq"]
    finer = Mesh(mesh.devices.reshape(dp_count // 2, 2, seq_count // 2, 2), ALL)
    tokens = P(("y", "core"), ("z", "x"), None)
    rows = P(ALL, None)
    return jax.shard_map(
        shards,
        mesh=finer,
        in_specs=(tokens, tokens, tokens, tokens, rows, P()),
        out_specs=(tokens, tokens, tokens, rows, P()),
        check_vma=False,
    )
```

```python
import functools

import jax
import jax.numpy as jnp
from jax import lax
from jax.experimental import pallas as pl
from jax.experimental.pallas import tpu as pltpu
from jax.sharding import Mesh
from jax.sharding import PartitionSpec as P

HEAD_DIM = 128
BLOCK = 512
MIB = 1 << 20

norm_eps = 1e-06

END = (8, 128)

F32 = jnp.float32
BF16 = jnp.bfloat16


def dot(a, b, contract):
    return lax.dot_general(a, b, (contract, ((), ())), preferred_element_type=F32)


def params(mib, dims=1):
    return pltpu.CompilerParams(
        vmem_limit_bytes=mib * MIB, dimension_semantics=("arbitrary",) * dims
    )


ROW_BLOCKS = 4


def row_blocks(tokens, wide):
    return [
        pl.BlockSpec((tokens // ROW_BLOCKS, wide), lambda y, p, r=r: (r, 0)) for r in range(ROW_BLOCKS)
    ]


def head(ref, i):
    return ref[:, i * HEAD_DIM : (i + 1) * HEAD_DIM]


def kv_kernel(k_ref, v_ref, o_ref):
    for i in range(o_ref.shape[0]):
        o_ref[i] = dot(head(k_ref, i), head(v_ref, i), ((0,), (0,))).astype(BF16)


def key_value_sums(keys, values, pair):
    tokens, channels = keys.shape
    width = pair * HEAD_DIM
    heads = channels // HEAD_DIM
    spec = pl.BlockSpec((tokens, width), lambda b: (0, b))
    return pl.pallas_call(
        kv_kernel,
        grid=(heads // pair,),
        in_specs=[spec, spec],
        out_specs=pl.BlockSpec((pair, HEAD_DIM, HEAD_DIM), lambda b: (b, 0, 0)),
        out_shape=jax.ShapeDtypeStruct((heads, HEAD_DIM, HEAD_DIM), BF16),
        compiler_params=params(56),
        cost_estimate=pl.CostEstimate(
            flops=2 * tokens * channels * HEAD_DIM, bytes_accessed=4 * tokens * channels, transcendentals=0
        ),
        name="key_value_sums",
    )(keys, values)


def lower(x):
    rows = lax.broadcasted_iota(jnp.int32, x.shape, 0)
    cols = lax.broadcasted_iota(jnp.int32, x.shape, 1)
    return jnp.where(cols <= rows, x, 0.0).astype(BF16)


def intra_kernel(q_ref, k_ref, v_ref, o_ref, end_ref):
    end_ref[...] = jnp.zeros_like(end_ref)
    half = q_ref.shape[0] // 2
    for i in range(o_ref.shape[1] // HEAD_DIM):
        q, k, v = head(q_ref, i), head(k_ref, i), head(v_ref, i)
        here = slice(i * HEAD_DIM, (i + 1) * HEAD_DIM)
        top = lower(dot(q[:half], k[:half], ((1,), (1,))))
        o_ref[:half, here] = dot(top, v[:half], ((1,), (0,)))
        left = dot(q[half:], k[:half], ((1,), (1,))).astype(BF16)
        right = lower(dot(q[half:], k[half:], ((1,), (1,))))
        o_ref[half:, here] = dot(left, v[:half], ((1,), (0,))) + dot(right, v[half:], ((1,), (0,)))


def intra_outputs(queries, keys, values, pair):
    tokens, channels = keys.shape
    spec = pl.BlockSpec((tokens, pair * HEAD_DIM), lambda b: (0, b))
    return pl.pallas_call(
        intra_kernel,
        grid=(channels // (pair * HEAD_DIM),),
        in_specs=[spec] * 3,
        out_specs=[spec, pl.BlockSpec(END, lambda b: (0, 0))],
        out_shape=[jax.ShapeDtypeStruct((tokens, channels), F32), jax.ShapeDtypeStruct(END, F32)],
        compiler_params=params(56),
        cost_estimate=pl.CostEstimate(
            flops=4 * tokens * tokens * channels, bytes_accessed=10 * tokens * channels, transcendentals=0
        ),
        name="intra_outputs",
    )(queries, keys, values)


def rms_inverse(x):
    return lax.rsqrt(jnp.mean(x * x, axis=-1, keepdims=True) + norm_eps)


def unit_kernel(begun, pos_ref, q_ref, s_ref, intra_ref, gain_ref, *refs):
    og_refs, refs = refs[:ROW_BLOCKS], refs[ROW_BLOCKS + begun :]
    out_ref, part_ref = refs[:2]
    units = []
    for i in range(s_ref.shape[0]):
        x = head(intra_ref, i) + dot(head(q_ref, i), s_ref[i], ((1,), (0,)))
        out_ref[:, i * HEAD_DIM : (i + 1) * HEAD_DIM] = x
        units.append((x * rms_inverse(x) * head(gain_ref, i)).astype(BF16))
    unit = jnp.concatenate(units, axis=1) if len(units) > 1 else units[0]
    og = jnp.concatenate([og_ref[...] for og_ref in og_refs], axis=0)
    part_ref[0] = dot(unit, og, ((0,), (0,))).astype(BF16)

    if len(refs) > 2:

        @pl.when(pl.program_id(0) == 0)
        def _():
            refs[2][...] = og


def weight_parts(pos, side, queries, state, intra, gain, out_grad, pair, begun=()):
    tokens, channels = queries.shape
    width = pair * HEAD_DIM
    count = channels // width // 2
    wide = out_grad.shape[1]

    def block(y, pos_ref):
        return 2 * y + lax.rem(pos_ref[0] + side, 2)

    cols = pl.BlockSpec((tokens, width), lambda y, p: (0, block(y, p)))
    whole = pl.BlockSpec((tokens, wide), lambda y, p: (0, 0))
    more = [] if begun else [(whole, jax.ShapeDtypeStruct((tokens, wide), BF16))]
    return pl.pallas_call(
        functools.partial(unit_kernel, len(begun)),
        grid_spec=pltpu.PrefetchScalarGridSpec(
            num_scalar_prefetch=1,
            grid=(count,),
            in_specs=[
                cols,
                pl.BlockSpec((pair, HEAD_DIM, HEAD_DIM), lambda y, p: (block(y, p), 0, 0)),
                cols,
                pl.BlockSpec((1, width), lambda y, p: (0, block(y, p))),
            ]
            + row_blocks(tokens, wide)
            + [pl.BlockSpec(memory_space=pl.ANY)] * len(begun),
            out_specs=[cols, pl.BlockSpec((1, width, wide), lambda y, p: (y, 0, 0))] + [m[0] for m in more],
        ),
        out_shape=[
            jax.ShapeDtypeStruct((tokens, channels), F32),
            jax.ShapeDtypeStruct((count, width, wide), BF16),
        ]
        + [m[1] for m in more],
        input_output_aliases={5 + ROW_BLOCKS: 0} if begun else {},
        compiler_params=params(30 if begun else 44),
        cost_estimate=pl.CostEstimate(
            flops=tokens * channels * wide,
            bytes_accessed=5 * tokens * channels + 2 * tokens * wide + channels * wide,
            transcendentals=0,
        ),
        name="weight_parts",
    )(pos, queries, state, intra, gain, *[out_grad] * ROW_BLOCKS, *begun)


def attn_grad_kernel(pos_ref, q_ref, o_ref, gain_ref, *refs):
    *og_refs, mine_ref, other_ref, ag_ref, gg_ref, qg_ref, ug_ref = refs

    def project(ref):
        start = 0
        for og_ref in og_refs:
            stop = start + og_ref.shape[0]
            ug_ref[start:stop] = dot(og_ref[...], ref[0], ((1,), (1,)))
            start = stop

    count = pl.num_programs(0) // 2

    @pl.when(pl.program_id(0) < count)
    def _():
        project(mine_ref)

    @pl.when(pl.program_id(0) >= count)
    def _():
        project(other_ref)

    for i in range(qg_ref.shape[0]):
        here = slice(i * HEAD_DIM, (i + 1) * HEAD_DIM)
        x = head(o_ref, i)
        inverse = rms_inverse(x)
        normed = x * inverse
        ug = head(ug_ref, i)
        gg_ref[:, here] = jnp.sum(ug * normed, axis=0, keepdims=True)
        scaled = ug * head(gain_ref, i)
        middle = jnp.mean(scaled * normed, axis=-1, keepdims=True)
        ag = ((scaled - normed * middle) * inverse).astype(BF16)
        ag_ref[:, here] = ag
        qg_ref[i] = dot(head(q_ref, i), ag, ((0,), (0,))).astype(BF16)


def attn_grads(pos, queries, outputs, gain, out_grad, mine, other, pair):
    tokens, channels = queries.shape
    width = pair * HEAD_DIM
    count = channels // width // 2
    wide = out_grad.shape[1]
    heads = channels // HEAD_DIM

    def block(s, pos_ref):
        return 2 * lax.rem(s, count) + lax.rem(pos_ref[0] + s // count, 2)

    cols = pl.BlockSpec((tokens, width), lambda s, p: (0, block(s, p)))
    row = pl.BlockSpec((1, width), lambda s, p: (0, block(s, p)))
    states = pl.BlockSpec((pair, HEAD_DIM, HEAD_DIM), lambda s, p: (block(s, p), 0, 0))
    piece = (1,) + mine.shape[1:]
    return pl.pallas_call(
        attn_grad_kernel,
        grid_spec=pltpu.PrefetchScalarGridSpec(
            num_scalar_prefetch=1,
            grid=(2 * count,),
            in_specs=[cols, cols, row]
            + row_blocks(tokens, wide)
            + [
                pl.BlockSpec(piece, lambda s, p: (jnp.minimum(s, count - 1), 0, 0)),
                pl.BlockSpec(piece, lambda s, p: (jnp.maximum(s - count, 0), 0, 0)),
            ],
            out_specs=[cols, row, states],
            scratch_shapes=[pltpu.VMEM((tokens, width), F32)],
        ),
        out_shape=[
            jax.ShapeDtypeStruct((tokens, channels), BF16),
            jax.ShapeDtypeStruct((1, channels), F32),
            jax.ShapeDtypeStruct((heads, HEAD_DIM, HEAD_DIM), BF16),
        ],
        compiler_params=params(30),
        cost_estimate=pl.CostEstimate(
            flops=2 * tokens * channels * wide,
            bytes_accessed=8 * tokens * channels + 2 * tokens * wide + 2 * channels * wide,
            transcendentals=0,
        ),
        name="attn_grads",
    )(pos, queries, outputs, gain, *[out_grad] * ROW_BLOCKS, mine, other)


NT, NN, TN = ((1,), (1,)), ((1,), (0,)), ((0,), (0,))


def query_grad_kernel(q_ref, k_ref, v_ref, ag_ref, s_ref, *refs):
    qg_ref, kg_ref, end_ref = refs[-3:]
    end_ref[...] = jnp.zeros_like(end_ref)
    half = q_ref.shape[0] // 2
    top, low = slice(0, half), slice(half, 2 * half)
    for i in range(s_ref.shape[0]):
        q, k, v, ag = head(q_ref, i), head(k_ref, i), head(v_ref, i), head(ag_ref, i)
        here = slice(i * HEAD_DIM, (i + 1) * HEAD_DIM)
        from_state = dot(ag, s_ref[i], NT)
        g00 = lower(dot(ag[top], v[top], NT))
        g10 = dot(ag[low], v[top], NT).astype(BF16)
        g11 = lower(dot(ag[low], v[low], NT))
        qg_ref[top, here] = (dot(g00, k[top], NN) + from_state[top]).astype(BF16)
        qg_ref[low, here] = (dot(g10, k[top], NN) + dot(g11, k[low], NN) + from_state[low]).astype(BF16)
        kg_ref[top, here] = dot(g00, q[top], TN) + dot(g10, q[low], TN)
        kg_ref[low, here] = dot(g11, q[low], TN)


def query_grads(queries, keys, values, attn_grad, state, pair, after=()):
    tokens, channels = queries.shape
    spec = pl.BlockSpec((tokens, pair * HEAD_DIM), lambda b: (0, b))
    return pl.pallas_call(
        query_grad_kernel,
        grid=(channels // (pair * HEAD_DIM),),
        in_specs=[spec] * 4
        + [pl.BlockSpec((pair, HEAD_DIM, HEAD_DIM), lambda b: (b, 0, 0))]
        + [pl.BlockSpec(memory_space=pl.ANY)] * len(after),
        out_specs=[spec, spec, pl.BlockSpec(END, lambda b: (0, 0))],
        out_shape=[jax.ShapeDtypeStruct((tokens, channels), t) for t in (BF16, F32)]
        + [jax.ShapeDtypeStruct(END, F32)],
        compiler_params=params(56),
        cost_estimate=pl.CostEstimate(
            flops=6 * tokens * tokens * channels, bytes_accessed=14 * tokens * channels, transcendentals=0
        ),
        name="query_grads",
    )(queries, keys, values, attn_grad, state, *after)


def key_value_grad_kernel(q_ref, k_ref, v_ref, ag_ref, r_ref, kin_ref, *refs):
    kg_ref, vg_ref = refs[-2:]
    half = q_ref.shape[0] // 2
    top, low = slice(0, half), slice(half, 2 * half)
    for i in range(r_ref.shape[0]):
        q, k, v, ag = head(q_ref, i), head(k_ref, i), head(v_ref, i), head(ag_ref, i)
        here = slice(i * HEAD_DIM, (i + 1) * HEAD_DIM)
        rev = r_ref[i]
        kg_ref[:, here] = (head(kin_ref, i) + dot(v, rev, NT)).astype(BF16)
        a00 = lower(dot(q[top], k[top], NT))
        a10 = dot(q[low], k[top], NT).astype(BF16)
        a11 = lower(dot(q[low], k[low], NT))
        from_rev = dot(k, rev, NN)
        vg_ref[top, here] = (dot(a00, ag[top], TN) + dot(a10, ag[low], TN) + from_rev[top]).astype(BF16)
        vg_ref[low, here] = (dot(a11, ag[low], TN) + from_rev[low]).astype(BF16)


def key_value_grads(queries, keys, values, attn_grad, rev, key_in, pair, after=()):
    tokens, channels = keys.shape
    spec = pl.BlockSpec((tokens, pair * HEAD_DIM), lambda b: (0, b))
    return pl.pallas_call(
        key_value_grad_kernel,
        grid=(channels // (pair * HEAD_DIM),),
        in_specs=[spec] * 4
        + [pl.BlockSpec((pair, HEAD_DIM, HEAD_DIM), lambda b: (b, 0, 0)), spec]
        + [pl.BlockSpec(memory_space=pl.ANY)] * len(after),
        out_specs=[spec] * 2,
        out_shape=[jax.ShapeDtypeStruct((tokens, channels), BF16)] * 2,
        compiler_params=params(56),
        cost_estimate=pl.CostEstimate(
            flops=5 * tokens * tokens * channels, bytes_accessed=16 * tokens * channels, transcendentals=0
        ),
        name="key_value_grads",
    )(queries, keys, values, attn_grad, rev, key_in, *after)


def running_kernel(reverse, after, x_ref, *refs):
    refs = refs[after:]
    o_ref = refs[-1]
    count, rows = x_ref.shape[:2]
    total = jnp.zeros(x_ref.shape[1:], F32)
    for place in range(count)[:: -1 if reverse else 1]:
        o_ref[place, :rows] = total.astype(BF16)
        total = total + x_ref[place].astype(F32)
    if len(refs) > 1:
        parts = in_parts(refs[0][...])
        width = x_ref.shape[-1]
        extra = [part[:, i : i + width] for part in parts for i in range(0, part.shape[1], width)]
        extra = extra + [jnp.zeros((1, width), F32)] * (o_ref.shape[1] - rows - len(extra))
        extra = jnp.concatenate(extra, axis=0).astype(BF16)
        for place in range(count):
            o_ref[place, rows:] = extra


def in_parts(x):
    high = x.astype(BF16).astype(F32)
    middle = (x - high).astype(BF16).astype(F32)
    return high, middle, (x - high - middle).astype(BF16).astype(F32)


def running(rows, reverse, row=None, after=()):
    count, height, width = rows.shape
    more = 0 if row is None else -(-3 * row.shape[1] // width // 16) * 16
    args = [rows, *after] + ([] if row is None else [row])
    return pl.pallas_call(
        functools.partial(running_kernel, reverse, len(after)),
        in_specs=[pl.BlockSpec()]
        + [pl.BlockSpec(memory_space=pl.ANY)] * len(after)
        + ([] if row is None else [pl.BlockSpec()]),
        out_shape=jax.ShapeDtypeStruct((count, height + more, width), BF16),
        compiler_params=pltpu.CompilerParams(vmem_limit_bytes=8 * MIB),
        name="running_sums",
    )(*args)


def row_total(arrived, height, channels):
    count, _, width = arrived.shape
    parts = arrived[:, height : height + 3 * channels // width].astype(F32)
    return jnp.sum(parts.reshape(count, 3, channels // width, width), axis=(0, 1)).reshape(channels)


ALL = ("y", "core", "z", "x")
SEQ = ("z", "x")
PLANE = ("y", "x")


def exchange(x, axis):
    rows = x.reshape((lax.axis_size(axis), -1) + x.shape[-1:])
    return lax.all_to_all(rows, axis, 0, 0, tiled=True)


def everyones(x, axis):
    return lax.all_to_all(jnp.broadcast_to(x[None], (lax.axis_size(axis),) + x.shape), axis, 0, 0, tiled=True)


def flipped(x, axis, bit=1):
    return lax.ppermute(x, axis, [(i, i ^ bit) for i in range(lax.axis_size(axis))])


def added(*terms):
    total = terms[0].astype(F32)
    for term in terms[1:]:
        total = total + term.astype(F32)
    return total


def together(*xs):
    return lax.optimization_barrier(xs)


def small_call(kernel, out_shapes, *args, after=(), mib=56):
    def call(*refs):
        kernel(*refs[: len(args)], *refs[len(args) + len(after) :])

    return pl.pallas_call(
        call,
        in_specs=[pl.BlockSpec()] * len(args)
        + [pl.BlockSpec(memory_space=pl.ANY)] * len(after),
        out_shape=[jax.ShapeDtypeStruct(shape, F32 if shape == END else BF16) for shape in out_shapes],
        compiler_params=pltpu.CompilerParams(vmem_limit_bytes=mib * MIB),
        cost_estimate=pl.CostEstimate(
            flops=0, bytes_accessed=4 * sum(x.size for x in args), transcendentals=0
        ),
        name=kernel.__name__,
    )(*args, *after)


def one(i):
    return pl.ds(i, 1)


def place(axis, bit=1):
    here = (lax.axis_index(axis) // bit) % 2
    return here, 1 - here


def merge_far(mine_ref, theirs_ref, out_ref):
    here, there = place("z", 2)
    out_ref[one(here)] = mine_ref[...][None]
    out_ref[one(there)] = theirs_ref[...][None]


def merge_near(mine_ref, theirs_ref, left_ref, right_ref, end_ref):
    end_ref[...] = jnp.zeros_like(end_ref)
    here, there = place("z")
    half = left_ref.shape[-1]
    for at, ref in ((here, mine_ref), (there, theirs_ref)):
        left_ref[:, one(at)] = ref[:, :, :half][:, None]
        right_ref[:, one(at)] = ref[:, :, half:][:, None]


def merge_sides(left_ref, left_got_ref, right_ref, right_got_ref, left_out_ref, right_out_ref):
    here, there = place("x")
    left_out_ref[:, one(here)] = left_ref[...][:, None]
    left_out_ref[:, one(there)] = left_got_ref[...][:, None]
    here, there = place("y")
    right_out_ref[one(here)] = right_ref[...][None]
    right_out_ref[one(there)] = right_got_ref[...][None]


def merge_all(left_ref, left_got_ref, right_ref, right_got_ref, out_ref):
    half = left_ref.shape[-1]
    here, there = place("y")
    out_ref[one(here), :, :, :, :half] = left_ref[...][None]
    out_ref[one(there), :, :, :, :half] = left_got_ref[...][None]
    here, there = place("x")
    out_ref[:, :, one(here), :, half:] = right_ref[...][:, :, None]
    out_ref[:, :, one(there), :, half:] = right_got_ref[...][:, :, None]


def total(a_ref, b_ref, *index):
    return (a_ref[index].astype(F32) + b_ref[index].astype(F32)).astype(BF16)


def split_first(keep_ref, got_ref, left_ref, right_ref, left_keep_ref, right_keep_ref):
    half = left_ref.shape[-1]
    here, there = place("y")
    every = slice(None)
    for at, ref in ((there, left_ref), (here, left_keep_ref)):
        ref[...] = total(keep_ref, got_ref, one(at), every, every, every, slice(0, half))[0]
    here, there = place("x")
    for at, ref in ((there, right_ref), (here, right_keep_ref)):
        ref[...] = total(keep_ref, got_ref, every, every, one(at), every, slice(half, 2 * half))[:, :, 0]


def split_second(
    left_ref, left_got_ref, right_ref, right_got_ref, left_out, right_out, left_keep, right_keep, end_ref
):
    end_ref[...] = jnp.zeros_like(end_ref)
    here, there = place("x")
    for at, ref in ((there, left_out), (here, left_keep)):
        ref[...] = total(left_ref, left_got_ref, slice(None), one(at))[:, 0]
    here, there = place("y")
    for at, ref in ((there, right_out), (here, right_keep)):
        ref[...] = total(right_ref, right_got_ref, one(at))[0]


def join_sides(left_ref, left_got_ref, right_ref, right_got_ref, out_ref, end_ref):
    end_ref[...] = jnp.zeros_like(end_ref)
    half = left_ref.shape[-1]
    out_ref[:, :, :half] = total(left_ref, left_got_ref, slice(None))
    out_ref[:, :, half:] = total(right_ref, right_got_ref, slice(None))


def by_halves(sizes, rows, q, k, v, og, out_weight, gain_row, pos, pair):
    tokens, channels = q.shape
    wide = out_weight.shape[1]
    y, z, x, half = sizes["y"], sizes["z"], sizes["x"], wide // 2

    got = flipped(out_weight, "z", 2)
    kv = key_value_sums(k, v, pair)
    kv, got = together(kv, got)
    (weight,) = small_call(merge_far, [(2, rows, wide)], out_weight, got)

    got = flipped(weight, "z", 1)
    sent = exchange(kv, SEQ)
    intra, intra_end = intra_outputs(q, k, v, pair)
    left, right, end = small_call(
        merge_near, [(2, 2, rows, half)] * 2 + [END], weight, got, after=(intra_end,)
    )
    left, right = left.reshape(z, rows, half), right.reshape(z, rows, half)
    left_got, right_got = flipped(left, "x"), flipped(right, "y")
    state = exchange(running(sent, False, after=(end,)), SEQ).reshape(kv.shape)
    state, left_got, right_got = together(state, left_got, right_got)
    left, right = small_call(
        merge_sides, [(z, x, rows, half), (y, z, rows, half)], left, left_got, right, right_got
    )

    state, left, right = together(state, left, right)
    left_got, right_got = flipped(left, "y"), flipped(right, "x")
    outputs, send, og = weight_parts(pos, 1, q, state, intra, gain_row, og, pair)
    send, left_got, right_got = together(send, left_got, right_got)
    got = flipped(send, "core")
    (mine,) = small_call(merge_all, [(y, z, x, rows, wide)], left, left_got, right, right_got, mib=20)
    mine = mine.reshape(y, -1, wide)
    other = flipped(mine, "core")
    outputs, keep = weight_parts(pos, 0, q, state, intra, gain_row, og, pair, (outputs,))

    split = (y, z, x, rows, wide)
    left, right, left_keep, right_keep = small_call(
        split_first,
        [(z, x, rows, half), (y, z, rows, half)] * 2,
        keep.reshape(split),
        got.reshape(split),
        mib=20,
    )
    other, left, right = together(other, left, right)
    left_got, right_got = flipped(left, "y"), flipped(right, "x")
    attn_grad, gain_part, qg = attn_grads(pos, q, outputs, gain_row, og, mine, other, pair)
    qg, left_got, right_got = together(qg, left_got, right_got)

    sent = exchange(qg, SEQ)
    gain_part = gain_part + flipped(gain_part, "core")
    left, right, left_keep, right_keep, end = small_call(
        split_second, [(z, rows, half)] * 4 + [END], left_keep, left_got, right_keep, right_got
    )
    left_got, right_got = flipped(left, "x"), flipped(right, "y")
    sums = running(sent, True, gain_part, after=(end,))
    arrived = exchange(sums, SEQ)
    query_g, key_in, end = query_grads(q, k, v, attn_grad, state, pair, after=(sums,))
    part, end = small_call(
        join_sides, [(z, rows, wide), END], left_keep, left_got, right_keep, right_got, after=(end,)
    )
    part = lax.all_to_all(part, "z", 0, 0, tiled=True)
    key_g, value_g = key_value_grads(q, k, v, attn_grad, arrived, key_in, pair, after=(end,))
    gain_sum = row_total(arrived, sent.shape[1], channels)
    return query_g, key_g, value_g, part, gain_sum + flipped(gain_sum, "y")


def by_planes(sizes, rows, q, k, v, og, out_weight, gain_row, pos, pair):
    tokens, channels = q.shape
    wide = out_weight.shape[1]
    y, z, x = sizes["y"], sizes["z"], sizes["x"]
    weight = everyones(everyones(out_weight, "z"), PLANE)
    weight = weight.reshape(y, x, z, rows, wide).transpose(0, 2, 1, 3, 4).reshape(y, -1, wide)
    kv = key_value_sums(k, v, pair)
    intra, _ = intra_outputs(q, k, v, pair)
    state = exchange(running(exchange(kv, SEQ), False), SEQ).reshape(kv.shape)
    outputs, send, og = weight_parts(pos, 1, q, state, intra, gain_row, og, pair)
    outputs, keep = weight_parts(pos, 0, q, state, intra, gain_row, og, pair, (outputs,))
    part = added(keep, flipped(send, "core")).astype(BF16)
    part = part.reshape(y, z, x, rows, wide).transpose(0, 2, 1, 3, 4).reshape(y * x, z, rows, wide)
    part = lax.all_to_all(part, PLANE, 0, 0, tiled=True)
    part = added(*[part[i] for i in range(y * x)]).astype(BF16)
    part = lax.all_to_all(part, "z", 0, 0, tiled=True)
    attn_grad, gain_part, qg = attn_grads(
        pos, q, outputs, gain_row, og, weight, flipped(weight, "core"), pair
    )
    rev = exchange(running(exchange(qg, SEQ), True), SEQ).reshape(kv.shape)
    query_g, key_in, _ = query_grads(q, k, v, attn_grad, state, pair)
    key_g, value_g = key_value_grads(q, k, v, attn_grad, rev, key_in, pair)
    gain_sum = jnp.sum(everyones(gain_part.reshape(channels), ALL), axis=0)
    return query_g, key_g, value_g, part, gain_sum


def shards(queries, keys, values, out_grad, out_weight, gain):
    tokens, channels = queries.shape[1:]
    assert tokens == BLOCK
    sizes = {name: lax.axis_size(name) for name in ALL}
    devices = lax.axis_size(ALL)
    rows = out_weight.shape[0]
    pair = channels // (sizes["y"] * sizes["core"]) // HEAD_DIM
    pos = lax.axis_index(("y", "core")).reshape(1).astype(jnp.int32)
    halves = (sizes["y"], sizes["z"], sizes["x"]) == (2, 4, 2) and rows % 16 == 0
    query_g, key_g, value_g, part, gain_sum = (by_halves if halves else by_planes)(
        sizes,
        rows,
        queries[0],
        keys[0],
        values[0],
        out_grad[0],
        out_weight,
        gain.reshape(1, channels),
        pos,
        pair,
    )
    factor = 1.0 / jnp.sqrt(jnp.float32(tokens * devices))
    out_shape = (1, tokens, channels)
    return (
        query_g.reshape(out_shape),
        key_g.reshape(out_shape),
        value_g.reshape(out_shape),
        added(*[part[i] for i in range(part.shape[0])]) * factor,
        gain_sum * factor,
    )


def solution(mesh):
    dp_count, seq_count = mesh.shape["dp"], mesh.shape["seq"]
    finer = Mesh(mesh.devices.reshape(dp_count // 2, 2, seq_count // 2, 2), ALL)
    tokens = P(("y", "core"), ("z", "x"), None)
    rows = P(ALL, None)
    return jax.shard_map(
        shards,
        mesh=finer,
        in_specs=(tokens, tokens, tokens, tokens, rows, P()),
        out_specs=(tokens, tokens, tokens, rows, P()),
        check_vma=False,
    )
```

```python
import functools

import jax
import jax.numpy as jnp
from jax import lax
from jax.experimental import pallas as pl
from jax.experimental.pallas import tpu as pltpu
from jax.sharding import Mesh
from jax.sharding import PartitionSpec as P

HEAD_DIM = 128
BLOCK = 512
MIB = 1 << 20

norm_eps = 1e-06

END = (8, 128)

F32 = jnp.float32
BF16 = jnp.bfloat16


def dot(a, b, contract):
    return lax.dot_general(a, b, (contract, ((), ())), preferred_element_type=F32)


def params(mib, dims=1):
    return pltpu.CompilerParams(
        vmem_limit_bytes=mib * MIB, dimension_semantics=("arbitrary",) * dims
    )


ROW_BLOCKS = 4


def row_blocks(tokens, wide):
    return [
        pl.BlockSpec((tokens // ROW_BLOCKS, wide), lambda y, p, r=r: (r, 0)) for r in range(ROW_BLOCKS)
    ]


def head(ref, i):
    return ref[:, i * HEAD_DIM : (i + 1) * HEAD_DIM]


def kv_kernel(k_ref, v_ref, o_ref):
    for i in range(o_ref.shape[0]):
        o_ref[i] = dot(head(k_ref, i), head(v_ref, i), ((0,), (0,))).astype(BF16)


def key_value_sums(keys, values, pair):
    tokens, channels = keys.shape
    width = pair * HEAD_DIM
    heads = channels // HEAD_DIM
    spec = pl.BlockSpec((tokens, width), lambda b: (0, b))
    return pl.pallas_call(
        kv_kernel,
        grid=(heads // pair,),
        in_specs=[spec, spec],
        out_specs=pl.BlockSpec((pair, HEAD_DIM, HEAD_DIM), lambda b: (b, 0, 0)),
        out_shape=jax.ShapeDtypeStruct((heads, HEAD_DIM, HEAD_DIM), BF16),
        compiler_params=params(56),
        cost_estimate=pl.CostEstimate(
            flops=2 * tokens * channels * HEAD_DIM, bytes_accessed=4 * tokens * channels, transcendentals=0
        ),
        name="key_value_sums",
    )(keys, values)


def lower(x):
    rows = lax.broadcasted_iota(jnp.int32, x.shape, 0)
    cols = lax.broadcasted_iota(jnp.int32, x.shape, 1)
    return jnp.where(cols <= rows, x, 0.0).astype(BF16)


def intra_kernel(q_ref, k_ref, v_ref, o_ref, end_ref):
    end_ref[...] = jnp.zeros_like(end_ref)
    half = q_ref.shape[0] // 2
    for i in range(o_ref.shape[1] // HEAD_DIM):
        q, k, v = head(q_ref, i), head(k_ref, i), head(v_ref, i)
        here = slice(i * HEAD_DIM, (i + 1) * HEAD_DIM)
        top = lower(dot(q[:half], k[:half], ((1,), (1,))))
        o_ref[:half, here] = dot(top, v[:half], ((1,), (0,)))
        left = dot(q[half:], k[:half], ((1,), (1,))).astype(BF16)
        right = lower(dot(q[half:], k[half:], ((1,), (1,))))
        o_ref[half:, here] = dot(left, v[:half], ((1,), (0,))) + dot(right, v[half:], ((1,), (0,)))


def intra_outputs(queries, keys, values, pair):
    tokens, channels = keys.shape
    spec = pl.BlockSpec((tokens, pair * HEAD_DIM), lambda b: (0, b))
    return pl.pallas_call(
        intra_kernel,
        grid=(channels // (pair * HEAD_DIM),),
        in_specs=[spec] * 3,
        out_specs=[spec, pl.BlockSpec(END, lambda b: (0, 0))],
        out_shape=[jax.ShapeDtypeStruct((tokens, channels), F32), jax.ShapeDtypeStruct(END, F32)],
        compiler_params=params(56),
        cost_estimate=pl.CostEstimate(
            flops=4 * tokens * tokens * channels, bytes_accessed=10 * tokens * channels, transcendentals=0
        ),
        name="intra_outputs",
    )(queries, keys, values)


def rms_inverse(x):
    return lax.rsqrt(jnp.mean(x * x, axis=-1, keepdims=True) + norm_eps)


def unit_kernel(begun, pos_ref, q_ref, s_ref, intra_ref, gain_ref, *refs):
    if begun:
        og_ref, _, out_ref, part_ref = refs
    else:
        *og_refs, out_ref, part_ref, og_ref = refs

        @pl.when(pl.program_id(0) == 0)
        def _():
            start = 0
            for ref in og_refs:
                og_ref[start : start + ref.shape[0]] = ref[...]
                start = start + ref.shape[0]

    units = []
    for i in range(s_ref.shape[0]):
        x = head(intra_ref, i) + dot(head(q_ref, i), s_ref[i], ((1,), (0,)))
        out_ref[:, i * HEAD_DIM : (i + 1) * HEAD_DIM] = x
        units.append((x * rms_inverse(x) * head(gain_ref, i)).astype(BF16))
    unit = jnp.concatenate(units, axis=1) if len(units) > 1 else units[0]
    part_ref[0] = dot(unit, og_ref[...], ((0,), (0,))).astype(BF16)


def weight_parts(pos, side, queries, state, intra, gain, out_grad, pair, begun=()):
    tokens, channels = queries.shape
    width = pair * HEAD_DIM
    count = channels // width // 2
    wide = out_grad.shape[1]

    def block(y, pos_ref):
        return 2 * y + lax.rem(pos_ref[0] + side, 2)

    cols = pl.BlockSpec((tokens, width), lambda y, p: (0, block(y, p)))
    whole = pl.BlockSpec((tokens, wide), lambda y, p: (0, 0))
    more = [] if begun else [(whole, jax.ShapeDtypeStruct((tokens, wide), BF16))]
    return pl.pallas_call(
        functools.partial(unit_kernel, len(begun)),
        grid_spec=pltpu.PrefetchScalarGridSpec(
            num_scalar_prefetch=1,
            grid=(count,),
            in_specs=[
                cols,
                pl.BlockSpec((pair, HEAD_DIM, HEAD_DIM), lambda y, p: (block(y, p), 0, 0)),
                cols,
                pl.BlockSpec((1, width), lambda y, p: (0, block(y, p))),
            ]
            + ([whole, pl.BlockSpec(memory_space=pl.ANY)] if begun else row_blocks(tokens, wide)),
            out_specs=[cols, pl.BlockSpec((1, width, wide), lambda y, p: (y, 0, 0))] + [m[0] for m in more],
        ),
        out_shape=[
            jax.ShapeDtypeStruct((tokens, channels), F32),
            jax.ShapeDtypeStruct((count, width, wide), BF16),
        ]
        + [m[1] for m in more],
        input_output_aliases={6: 0} if begun else {},
        compiler_params=params(30 if begun else 44),
        cost_estimate=pl.CostEstimate(
            flops=tokens * channels * wide,
            bytes_accessed=5 * tokens * channels + 2 * tokens * wide + channels * wide,
            transcendentals=0,
        ),
        name="weight_parts",
    )(pos, queries, state, intra, gain, *[out_grad] * (1 if begun else ROW_BLOCKS), *begun)


def attn_grad_kernel(after, q_ref, o_ref, gain_ref, og_ref, w_ref, *refs):
    ag_ref, gg_ref, qg_ref, ug_ref = refs[after:]
    ug_ref[...] = dot(og_ref[...], w_ref[...], ((1,), (1,)))
    for i in range(qg_ref.shape[0]):
        here = slice(i * HEAD_DIM, (i + 1) * HEAD_DIM)
        x = head(o_ref, i)
        inverse = rms_inverse(x)
        normed = x * inverse
        ug = head(ug_ref, i)
        gg_ref[:, here] = jnp.sum(ug * normed, axis=0, keepdims=True)
        scaled = ug * head(gain_ref, i)
        middle = jnp.mean(scaled * normed, axis=-1, keepdims=True)
        ag = ((scaled - normed * middle) * inverse).astype(BF16)
        ag_ref[:, here] = ag
        qg_ref[i] = dot(head(q_ref, i), ag, ((0,), (0,))).astype(BF16)


def attn_grads(queries, outputs, gain, out_grad, weight, pair, after=()):
    tokens, channels = queries.shape
    width = pair * HEAD_DIM
    wide = out_grad.shape[1]
    heads = channels // HEAD_DIM
    cols = pl.BlockSpec((tokens, width), lambda b: (0, b))
    row = pl.BlockSpec((1, width), lambda b: (0, b))
    return pl.pallas_call(
        functools.partial(attn_grad_kernel, len(after)),
        grid=(channels // width,),
        in_specs=[
            cols,
            cols,
            row,
            pl.BlockSpec((tokens, wide), lambda b: (0, 0)),
            pl.BlockSpec((width, wide), lambda b: (b, 0)),
        ]
        + [pl.BlockSpec(memory_space=pl.ANY)] * len(after),
        out_specs=[cols, row, pl.BlockSpec((pair, HEAD_DIM, HEAD_DIM), lambda b: (b, 0, 0))],
        scratch_shapes=[pltpu.VMEM((tokens, width), F32)],
        out_shape=[
            jax.ShapeDtypeStruct((tokens, channels), BF16),
            jax.ShapeDtypeStruct((1, channels), F32),
            jax.ShapeDtypeStruct((heads, HEAD_DIM, HEAD_DIM), BF16),
        ],
        compiler_params=params(54),
        cost_estimate=pl.CostEstimate(
            flops=2 * tokens * channels * wide,
            bytes_accessed=8 * tokens * channels + 2 * tokens * wide + 2 * channels * wide,
            transcendentals=0,
        ),
        name="attn_grads",
    )(queries, outputs, gain, out_grad, weight, *after)


NT, NN, TN = ((1,), (1,)), ((1,), (0,)), ((0,), (0,))


def query_grad_kernel(q_ref, k_ref, v_ref, ag_ref, s_ref, *refs):
    qg_ref, kg_ref, end_ref = refs[-3:]
    end_ref[...] = jnp.zeros_like(end_ref)
    half = q_ref.shape[0] // 2
    top, low = slice(0, half), slice(half, 2 * half)
    for i in range(s_ref.shape[0]):
        q, k, v, ag = head(q_ref, i), head(k_ref, i), head(v_ref, i), head(ag_ref, i)
        here = slice(i * HEAD_DIM, (i + 1) * HEAD_DIM)
        from_state = dot(ag, s_ref[i], NT)
        g00 = lower(dot(ag[top], v[top], NT))
        g10 = dot(ag[low], v[top], NT).astype(BF16)
        g11 = lower(dot(ag[low], v[low], NT))
        qg_ref[top, here] = (dot(g00, k[top], NN) + from_state[top]).astype(BF16)
        qg_ref[low, here] = (dot(g10, k[top], NN) + dot(g11, k[low], NN) + from_state[low]).astype(BF16)
        kg_ref[top, here] = dot(g00, q[top], TN) + dot(g10, q[low], TN)
        kg_ref[low, here] = dot(g11, q[low], TN)


def query_grads(queries, keys, values, attn_grad, state, pair, after=()):
    tokens, channels = queries.shape
    spec = pl.BlockSpec((tokens, pair * HEAD_DIM), lambda b: (0, b))
    return pl.pallas_call(
        query_grad_kernel,
        grid=(channels // (pair * HEAD_DIM),),
        in_specs=[spec] * 4
        + [pl.BlockSpec((pair, HEAD_DIM, HEAD_DIM), lambda b: (b, 0, 0))]
        + [pl.BlockSpec(memory_space=pl.ANY)] * len(after),
        out_specs=[spec, spec, pl.BlockSpec(END, lambda b: (0, 0))],
        out_shape=[jax.ShapeDtypeStruct((tokens, channels), t) for t in (BF16, F32)]
        + [jax.ShapeDtypeStruct(END, F32)],
        compiler_params=params(56),
        cost_estimate=pl.CostEstimate(
            flops=6 * tokens * tokens * channels, bytes_accessed=14 * tokens * channels, transcendentals=0
        ),
        name="query_grads",
    )(queries, keys, values, attn_grad, state, *after)


def key_value_grad_kernel(q_ref, k_ref, v_ref, ag_ref, r_ref, kin_ref, *refs):
    kg_ref, vg_ref = refs[-2:]
    half = q_ref.shape[0] // 2
    top, low = slice(0, half), slice(half, 2 * half)
    for i in range(r_ref.shape[0]):
        q, k, v, ag = head(q_ref, i), head(k_ref, i), head(v_ref, i), head(ag_ref, i)
        here = slice(i * HEAD_DIM, (i + 1) * HEAD_DIM)
        rev = r_ref[i]
        kg_ref[:, here] = (head(kin_ref, i) + dot(v, rev, NT)).astype(BF16)
        a00 = lower(dot(q[top], k[top], NT))
        a10 = dot(q[low], k[top], NT).astype(BF16)
        a11 = lower(dot(q[low], k[low], NT))
        from_rev = dot(k, rev, NN)
        vg_ref[top, here] = (dot(a00, ag[top], TN) + dot(a10, ag[low], TN) + from_rev[top]).astype(BF16)
        vg_ref[low, here] = (dot(a11, ag[low], TN) + from_rev[low]).astype(BF16)


def key_value_grads(queries, keys, values, attn_grad, rev, key_in, pair, after=()):
    tokens, channels = keys.shape
    spec = pl.BlockSpec((tokens, pair * HEAD_DIM), lambda b: (0, b))
    return pl.pallas_call(
        key_value_grad_kernel,
        grid=(channels // (pair * HEAD_DIM),),
        in_specs=[spec] * 4
        + [pl.BlockSpec((pair, HEAD_DIM, HEAD_DIM), lambda b: (b, 0, 0)), spec]
        + [pl.BlockSpec(memory_space=pl.ANY)] * len(after),
        out_specs=[spec] * 2,
        out_shape=[jax.ShapeDtypeStruct((tokens, channels), BF16)] * 2,
        compiler_params=params(56),
        cost_estimate=pl.CostEstimate(
            flops=5 * tokens * tokens * channels, bytes_accessed=16 * tokens * channels, transcendentals=0
        ),
        name="key_value_grads",
    )(queries, keys, values, attn_grad, rev, key_in, *after)


def running_kernel(reverse, after, x_ref, *refs):
    refs = refs[after:]
    o_ref = refs[-1]
    count, rows = x_ref.shape[:2]
    total = jnp.zeros(x_ref.shape[1:], F32)
    for place in range(count)[:: -1 if reverse else 1]:
        o_ref[place, :rows] = total.astype(BF16)
        total = total + x_ref[place].astype(F32)
    if len(refs) > 1:
        parts = in_parts(refs[0][...])
        width = x_ref.shape[-1]
        extra = [part[:, i : i + width] for part in parts for i in range(0, part.shape[1], width)]
        extra = extra + [jnp.zeros((1, width), F32)] * (o_ref.shape[1] - rows - len(extra))
        extra = jnp.concatenate(extra, axis=0).astype(BF16)
        for place in range(count):
            o_ref[place, rows:] = extra


def in_parts(x):
    high = x.astype(BF16).astype(F32)
    middle = (x - high).astype(BF16).astype(F32)
    return high, middle, (x - high - middle).astype(BF16).astype(F32)


def running(rows, reverse, row=None, after=()):
    count, height, width = rows.shape
    more = 0 if row is None else -(-3 * row.shape[1] // width // 16) * 16
    args = [rows, *after] + ([] if row is None else [row])
    return pl.pallas_call(
        functools.partial(running_kernel, reverse, len(after)),
        in_specs=[pl.BlockSpec()]
        + [pl.BlockSpec(memory_space=pl.ANY)] * len(after)
        + ([] if row is None else [pl.BlockSpec()]),
        out_shape=jax.ShapeDtypeStruct((count, height + more, width), BF16),
        compiler_params=pltpu.CompilerParams(vmem_limit_bytes=8 * MIB),
        name="running_sums",
    )(*args)


def row_total(arrived, height, channels):
    count, _, width = arrived.shape
    parts = arrived[:, height : height + 3 * channels // width].astype(F32)
    return jnp.sum(parts.reshape(count, 3, channels // width, width), axis=(0, 1)).reshape(channels)


ALL = ("y", "core", "z", "x")
SEQ = ("z", "x")
PLANE = ("y", "x")


def exchange(x, axis):
    rows = x.reshape((lax.axis_size(axis), -1) + x.shape[-1:])
    return lax.all_to_all(rows, axis, 0, 0, tiled=True)


def everyones(x, axis):
    return lax.all_to_all(jnp.broadcast_to(x[None], (lax.axis_size(axis),) + x.shape), axis, 0, 0, tiled=True)


def flipped(x, axis, bit=1):
    return lax.ppermute(x, axis, [(i, i ^ bit) for i in range(lax.axis_size(axis))])


def added(*terms):
    total = terms[0].astype(F32)
    for term in terms[1:]:
        total = total + term.astype(F32)
    return total


def together(*xs):
    return lax.optimization_barrier(xs)


def small_call(kernel, out_shapes, *args, after=(), mib=56):
    def call(*refs):
        kernel(*refs[: len(args)], *refs[len(args) + len(after) :])

    return pl.pallas_call(
        call,
        in_specs=[pl.BlockSpec()] * len(args)
        + [pl.BlockSpec(memory_space=pl.ANY)] * len(after),
        out_shape=[jax.ShapeDtypeStruct(shape, F32 if shape == END else BF16) for shape in out_shapes],
        compiler_params=pltpu.CompilerParams(vmem_limit_bytes=mib * MIB),
        cost_estimate=pl.CostEstimate(
            flops=0, bytes_accessed=4 * sum(x.size for x in args), transcendentals=0
        ),
        name=kernel.__name__,
    )(*args, *after)


def one(i):
    return pl.ds(i, 1)


def place(axis, bit=1):
    here = (lax.axis_index(axis) // bit) % 2
    return here, 1 - here


def total(a_ref, b_ref, *index):
    return (a_ref[index].astype(F32) + b_ref[index].astype(F32)).astype(BF16)


def split_first(keep_ref, got_ref, left_ref, right_ref, left_keep_ref, right_keep_ref):
    half = left_ref.shape[-1]
    here, there = place("y")
    every = slice(None)
    for at, ref in ((there, left_ref), (here, left_keep_ref)):
        ref[...] = total(keep_ref, got_ref, one(at), every, every, every, slice(0, half))[0]
    here, there = place("x")
    for at, ref in ((there, right_ref), (here, right_keep_ref)):
        ref[...] = total(keep_ref, got_ref, every, every, one(at), every, slice(half, 2 * half))[:, :, 0]


def split_second(
    left_ref, left_got_ref, right_ref, right_got_ref, left_out, right_out, left_keep, right_keep, end_ref
):
    end_ref[...] = jnp.zeros_like(end_ref)
    here, there = place("x")
    for at, ref in ((there, left_out), (here, left_keep)):
        ref[...] = total(left_ref, left_got_ref, slice(None), one(at))[:, 0]
    here, there = place("y")
    for at, ref in ((there, right_out), (here, right_keep)):
        ref[...] = total(right_ref, right_got_ref, one(at))[0]


def join_sides(left_ref, left_got_ref, right_ref, right_got_ref, out_ref, end_ref):
    end_ref[...] = jnp.zeros_like(end_ref)
    half = left_ref.shape[-1]
    out_ref[:, :, :half] = total(left_ref, left_got_ref, slice(None))
    out_ref[:, :, half:] = total(right_ref, right_got_ref, slice(None))


def by_halves(sizes, rows, q, k, v, og, out_weight, gain_row, pos, pair):
    tokens, channels = q.shape
    wide = out_weight.shape[1]
    y, z, x, half = sizes["y"], sizes["z"], sizes["x"], wide // 2

    weight = lax.all_gather(out_weight, ALL, axis=0, tiled=True)
    kv = key_value_sums(k, v, pair)
    sent = exchange(kv, SEQ)
    intra, end = intra_outputs(q, k, v, pair)
    state = exchange(running(sent, False, after=(end,)), SEQ).reshape(kv.shape)
    outputs, send, og = weight_parts(pos, 1, q, state, intra, gain_row, og, pair)
    got = flipped(send, "core")
    outputs, keep = weight_parts(pos, 0, q, state, intra, gain_row, og, pair, (outputs,))

    split = (y, z, x, rows, wide)
    left, right, left_keep, right_keep = small_call(
        split_first,
        [(z, x, rows, half), (y, z, rows, half)] * 2,
        keep.reshape(split),
        got.reshape(split),
        mib=20,
    )
    left_got, right_got = flipped(left, "y"), flipped(right, "x")
    left, right, left_keep, right_keep, end = small_call(
        split_second, [(z, rows, half)] * 4 + [END], left_keep, left_got, right_keep, right_got, mib=20
    )
    left_got, right_got = flipped(left, "x"), flipped(right, "y")
    attn_grad, gain_part, qg = attn_grads(q, outputs, gain_row, og, weight, pair, after=(end,))

    sent = exchange(qg, SEQ)
    gain_part = gain_part + flipped(gain_part, "core")
    sums = running(sent, True, gain_part)
    arrived = exchange(sums, SEQ)
    part, end = small_call(
        join_sides, [(z, rows, wide), END], left_keep, left_got, right_keep, right_got, after=(sums,)
    )
    part = lax.all_to_all(part, "z", 0, 0, tiled=True)
    query_g, key_in, end = query_grads(q, k, v, attn_grad, state, pair, after=(sums, end))
    key_g, value_g = key_value_grads(q, k, v, attn_grad, arrived, key_in, pair, after=(end,))
    gain_sum = row_total(arrived, sent.shape[1], channels)
    return query_g, key_g, value_g, part, gain_sum + flipped(gain_sum, "y")


def by_planes(sizes, rows, q, k, v, og, out_weight, gain_row, pos, pair):
    tokens, channels = q.shape
    wide = out_weight.shape[1]
    y, z, x = sizes["y"], sizes["z"], sizes["x"]
    weight = lax.all_gather(out_weight, ALL, axis=0, tiled=True)
    kv = key_value_sums(k, v, pair)
    intra, _ = intra_outputs(q, k, v, pair)
    state = exchange(running(exchange(kv, SEQ), False), SEQ).reshape(kv.shape)
    outputs, send, og = weight_parts(pos, 1, q, state, intra, gain_row, og, pair)
    outputs, keep = weight_parts(pos, 0, q, state, intra, gain_row, og, pair, (outputs,))
    part = added(keep, flipped(send, "core")).astype(BF16)
    part = part.reshape(y, z, x, rows, wide).transpose(0, 2, 1, 3, 4).reshape(y * x, z, rows, wide)
    part = lax.all_to_all(part, PLANE, 0, 0, tiled=True)
    part = added(*[part[i] for i in range(y * x)]).astype(BF16)
    part = lax.all_to_all(part, "z", 0, 0, tiled=True)
    attn_grad, gain_part, qg = attn_grads(q, outputs, gain_row, og, weight, pair)
    rev = exchange(running(exchange(qg, SEQ), True), SEQ).reshape(kv.shape)
    query_g, key_in, _ = query_grads(q, k, v, attn_grad, state, pair)
    key_g, value_g = key_value_grads(q, k, v, attn_grad, rev, key_in, pair)
    gain_sum = jnp.sum(everyones(gain_part.reshape(channels), ALL), axis=0)
    return query_g, key_g, value_g, part, gain_sum


def shards(queries, keys, values, out_grad, out_weight, gain):
    tokens, channels = queries.shape[1:]
    assert tokens == BLOCK
    sizes = {name: lax.axis_size(name) for name in ALL}
    devices = lax.axis_size(ALL)
    rows = out_weight.shape[0]
    pair = channels // (sizes["y"] * sizes["core"]) // HEAD_DIM
    pos = lax.axis_index(("y", "core")).reshape(1).astype(jnp.int32)
    halves = (sizes["y"], sizes["z"], sizes["x"]) == (2, 4, 2) and rows % 16 == 0
    query_g, key_g, value_g, part, gain_sum = (by_halves if halves else by_planes)(
        sizes,
        rows,
        queries[0],
        keys[0],
        values[0],
        out_grad[0],
        out_weight,
        gain.reshape(1, channels),
        pos,
        pair,
    )
    factor = 1.0 / jnp.sqrt(jnp.float32(tokens * devices))
    out_shape = (1, tokens, channels)
    return (
        query_g.reshape(out_shape),
        key_g.reshape(out_shape),
        value_g.reshape(out_shape),
        added(*[part[i] for i in range(part.shape[0])]) * factor,
        gain_sum * factor,
    )


def solution(mesh):
    dp_count, seq_count = mesh.shape["dp"], mesh.shape["seq"]
    finer = Mesh(mesh.devices.reshape(dp_count // 2, 2, seq_count // 2, 2), ALL)
    tokens = P(("y", "core"), ("z", "x"), None)
    rows = P(ALL, None)
    return jax.shard_map(
        shards,
        mesh=finer,
        in_specs=(tokens, tokens, tokens, tokens, rows, P()),
        out_specs=(tokens, tokens, tokens, rows, P()),
        check_vma=False,
    )
```

```python
import functools

import jax
import jax.numpy as jnp
from jax import lax
from jax.experimental import pallas as pl
from jax.experimental.pallas import tpu as pltpu
from jax.sharding import Mesh
from jax.sharding import PartitionSpec as P

HEAD_DIM = 128
BLOCK = 512
MIB = 1 << 20

norm_eps = 1e-06

END = (8, 128)

F32 = jnp.float32
BF16 = jnp.bfloat16


def dot(a, b, contract):
    return lax.dot_general(a, b, (contract, ((), ())), preferred_element_type=F32)


def params(mib, dims=1):
    return pltpu.CompilerParams(
        vmem_limit_bytes=mib * MIB, dimension_semantics=("arbitrary",) * dims
    )


ROW_BLOCKS = 4


def row_blocks(tokens, wide):
    return [
        pl.BlockSpec((tokens // ROW_BLOCKS, wide), lambda y, p, r=r: (r, 0)) for r in range(ROW_BLOCKS)
    ]


def head(ref, i):
    return ref[:, i * HEAD_DIM : (i + 1) * HEAD_DIM]


def kv_kernel(k_ref, v_ref, o_ref):
    for i in range(o_ref.shape[0]):
        o_ref[i] = dot(head(k_ref, i), head(v_ref, i), ((0,), (0,))).astype(BF16)


def key_value_sums(keys, values, pair):
    tokens, channels = keys.shape
    width = pair * HEAD_DIM
    heads = channels // HEAD_DIM
    spec = pl.BlockSpec((tokens, width), lambda b: (0, b))
    return pl.pallas_call(
        kv_kernel,
        grid=(heads // pair,),
        in_specs=[spec, spec],
        out_specs=pl.BlockSpec((pair, HEAD_DIM, HEAD_DIM), lambda b: (b, 0, 0)),
        out_shape=jax.ShapeDtypeStruct((heads, HEAD_DIM, HEAD_DIM), BF16),
        compiler_params=params(56),
        cost_estimate=pl.CostEstimate(
            flops=2 * tokens * channels * HEAD_DIM, bytes_accessed=4 * tokens * channels, transcendentals=0
        ),
        name="key_value_sums",
    )(keys, values)


def lower(x):
    rows = lax.broadcasted_iota(jnp.int32, x.shape, 0)
    cols = lax.broadcasted_iota(jnp.int32, x.shape, 1)
    return jnp.where(cols <= rows, x, 0.0).astype(BF16)


def intra_kernel(q_ref, k_ref, v_ref, o_ref, end_ref):
    end_ref[...] = jnp.zeros_like(end_ref)
    half = q_ref.shape[0] // 2
    for i in range(o_ref.shape[1] // HEAD_DIM):
        q, k, v = head(q_ref, i), head(k_ref, i), head(v_ref, i)
        here = slice(i * HEAD_DIM, (i + 1) * HEAD_DIM)
        top = lower(dot(q[:half], k[:half], ((1,), (1,))))
        o_ref[:half, here] = dot(top, v[:half], ((1,), (0,)))
        left = dot(q[half:], k[:half], ((1,), (1,))).astype(BF16)
        right = lower(dot(q[half:], k[half:], ((1,), (1,))))
        o_ref[half:, here] = dot(left, v[:half], ((1,), (0,))) + dot(right, v[half:], ((1,), (0,)))


def intra_outputs(queries, keys, values, pair):
    tokens, channels = keys.shape
    spec = pl.BlockSpec((tokens, pair * HEAD_DIM), lambda b: (0, b))
    return pl.pallas_call(
        intra_kernel,
        grid=(channels // (pair * HEAD_DIM),),
        in_specs=[spec] * 3,
        out_specs=[spec, pl.BlockSpec(END, lambda b: (0, 0))],
        out_shape=[jax.ShapeDtypeStruct((tokens, channels), F32), jax.ShapeDtypeStruct(END, F32)],
        compiler_params=params(56),
        cost_estimate=pl.CostEstimate(
            flops=4 * tokens * tokens * channels, bytes_accessed=10 * tokens * channels, transcendentals=0
        ),
        name="intra_outputs",
    )(queries, keys, values)


def rms_inverse(x):
    return lax.rsqrt(jnp.mean(x * x, axis=-1, keepdims=True) + norm_eps)


def unit_kernel(begun, pos_ref, q_ref, s_ref, intra_ref, gain_ref, *refs):
    if begun:
        og_ref, _, out_ref, part_ref = refs
    else:
        *og_refs, out_ref, part_ref, og_ref = refs

        @pl.when(pl.program_id(0) == 0)
        def _():
            start = 0
            for ref in og_refs:
                og_ref[start : start + ref.shape[0]] = ref[...]
                start = start + ref.shape[0]

    units = []
    for i in range(s_ref.shape[0]):
        x = head(intra_ref, i) + dot(head(q_ref, i), s_ref[i], ((1,), (0,)))
        out_ref[:, i * HEAD_DIM : (i + 1) * HEAD_DIM] = x
        units.append((x * rms_inverse(x) * head(gain_ref, i)).astype(BF16))
    unit = jnp.concatenate(units, axis=1) if len(units) > 1 else units[0]
    part_ref[0] = dot(unit, og_ref[...], ((0,), (0,))).astype(BF16)


def weight_parts(pos, side, queries, state, intra, gain, out_grad, pair, begun=()):
    tokens, channels = queries.shape
    width = pair * HEAD_DIM
    count = channels // width // 2
    wide = out_grad.shape[1]

    def block(y, pos_ref):
        return 2 * y + lax.rem(pos_ref[0] + side, 2)

    cols = pl.BlockSpec((tokens, width), lambda y, p: (0, block(y, p)))
    whole = pl.BlockSpec((tokens, wide), lambda y, p: (0, 0))
    more = [] if begun else [(whole, jax.ShapeDtypeStruct((tokens, wide), BF16))]
    return pl.pallas_call(
        functools.partial(unit_kernel, len(begun)),
        grid_spec=pltpu.PrefetchScalarGridSpec(
            num_scalar_prefetch=1,
            grid=(count,),
            in_specs=[
                cols,
                pl.BlockSpec((pair, HEAD_DIM, HEAD_DIM), lambda y, p: (block(y, p), 0, 0)),
                cols,
                pl.BlockSpec((1, width), lambda y, p: (0, block(y, p))),
            ]
            + ([whole, pl.BlockSpec(memory_space=pl.ANY)] if begun else row_blocks(tokens, wide)),
            out_specs=[cols, pl.BlockSpec((1, width, wide), lambda y, p: (y, 0, 0))] + [m[0] for m in more],
        ),
        out_shape=[
            jax.ShapeDtypeStruct((tokens, channels), F32),
            jax.ShapeDtypeStruct((count, width, wide), BF16),
        ]
        + [m[1] for m in more],
        input_output_aliases={6: 0} if begun else {},
        compiler_params=params(30 if begun else 44),
        cost_estimate=pl.CostEstimate(
            flops=tokens * channels * wide,
            bytes_accessed=5 * tokens * channels + 2 * tokens * wide + channels * wide,
            transcendentals=0,
        ),
        name="weight_parts",
    )(pos, queries, state, intra, gain, *[out_grad] * (1 if begun else ROW_BLOCKS), *begun)


def attn_grad_kernel(pos_ref, q_ref, o_ref, gain_ref, og_ref, mine_ref, other_ref, ag_ref, gg_ref, qg_ref, ug_ref):
    count = pl.num_programs(0) // 2

    @pl.when(pl.program_id(0) < count)
    def _():
        ug_ref[...] = dot(og_ref[...], mine_ref[0], ((1,), (1,)))

    @pl.when(pl.program_id(0) >= count)
    def _():
        ug_ref[...] = dot(og_ref[...], other_ref[0], ((1,), (1,)))

    for i in range(qg_ref.shape[0]):
        here = slice(i * HEAD_DIM, (i + 1) * HEAD_DIM)
        x = head(o_ref, i)
        inverse = rms_inverse(x)
        normed = x * inverse
        ug = head(ug_ref, i)
        gg_ref[:, here] = jnp.sum(ug * normed, axis=0, keepdims=True)
        scaled = ug * head(gain_ref, i)
        middle = jnp.mean(scaled * normed, axis=-1, keepdims=True)
        ag = ((scaled - normed * middle) * inverse).astype(BF16)
        ag_ref[:, here] = ag
        qg_ref[i] = dot(head(q_ref, i), ag, ((0,), (0,))).astype(BF16)


def attn_grads(pos, queries, outputs, gain, out_grad, mine, other, pair):
    tokens, channels = queries.shape
    width = pair * HEAD_DIM
    count = channels // width // 2
    wide = out_grad.shape[1]
    heads = channels // HEAD_DIM

    def block(s, pos_ref):
        return 2 * lax.rem(s, count) + lax.rem(pos_ref[0] + s // count, 2)

    cols = pl.BlockSpec((tokens, width), lambda s, p: (0, block(s, p)))
    row = pl.BlockSpec((1, width), lambda s, p: (0, block(s, p)))
    states = pl.BlockSpec((pair, HEAD_DIM, HEAD_DIM), lambda s, p: (block(s, p), 0, 0))
    piece = (1,) + mine.shape[1:]
    return pl.pallas_call(
        attn_grad_kernel,
        grid_spec=pltpu.PrefetchScalarGridSpec(
            num_scalar_prefetch=1,
            grid=(2 * count,),
            in_specs=[
                cols,
                cols,
                row,
                pl.BlockSpec((tokens, wide), lambda s, p: (0, 0)),
                pl.BlockSpec(piece, lambda s, p: (jnp.minimum(s, count - 1), 0, 0)),
                pl.BlockSpec(piece, lambda s, p: (jnp.maximum(s - count, 0), 0, 0)),
            ],
            out_specs=[cols, row, states],
            scratch_shapes=[pltpu.VMEM((tokens, width), F32)],
        ),
        out_shape=[
            jax.ShapeDtypeStruct((tokens, channels), BF16),
            jax.ShapeDtypeStruct((1, channels), F32),
            jax.ShapeDtypeStruct((heads, HEAD_DIM, HEAD_DIM), BF16),
        ],
        compiler_params=params(30),
        cost_estimate=pl.CostEstimate(
            flops=2 * tokens * channels * wide,
            bytes_accessed=8 * tokens * channels + 2 * tokens * wide + 2 * channels * wide,
            transcendentals=0,
        ),
        name="attn_grads",
    )(pos, queries, outputs, gain, out_grad, mine, other)


NT, NN, TN = ((1,), (1,)), ((1,), (0,)), ((0,), (0,))


def query_grad_kernel(q_ref, k_ref, v_ref, ag_ref, s_ref, *refs):
    qg_ref, kg_ref, end_ref = refs[-3:]
    end_ref[...] = jnp.zeros_like(end_ref)
    half = q_ref.shape[0] // 2
    top, low = slice(0, half), slice(half, 2 * half)
    for i in range(s_ref.shape[0]):
        q, k, v, ag = head(q_ref, i), head(k_ref, i), head(v_ref, i), head(ag_ref, i)
        here = slice(i * HEAD_DIM, (i + 1) * HEAD_DIM)
        from_state = dot(ag, s_ref[i], NT)
        g00 = lower(dot(ag[top], v[top], NT))
        g10 = dot(ag[low], v[top], NT).astype(BF16)
        g11 = lower(dot(ag[low], v[low], NT))
        qg_ref[top, here] = (dot(g00, k[top], NN) + from_state[top]).astype(BF16)
        qg_ref[low, here] = (dot(g10, k[top], NN) + dot(g11, k[low], NN) + from_state[low]).astype(BF16)
        kg_ref[top, here] = dot(g00, q[top], TN) + dot(g10, q[low], TN)
        kg_ref[low, here] = dot(g11, q[low], TN)


def query_grads(queries, keys, values, attn_grad, state, pair, after=()):
    tokens, channels = queries.shape
    spec = pl.BlockSpec((tokens, pair * HEAD_DIM), lambda b: (0, b))
    return pl.pallas_call(
        query_grad_kernel,
        grid=(channels // (pair * HEAD_DIM),),
        in_specs=[spec] * 4
        + [pl.BlockSpec((pair, HEAD_DIM, HEAD_DIM), lambda b: (b, 0, 0))]
        + [pl.BlockSpec(memory_space=pl.ANY)] * len(after),
        out_specs=[spec, spec, pl.BlockSpec(END, lambda b: (0, 0))],
        out_shape=[jax.ShapeDtypeStruct((tokens, channels), t) for t in (BF16, F32)]
        + [jax.ShapeDtypeStruct(END, F32)],
        compiler_params=params(56),
        cost_estimate=pl.CostEstimate(
            flops=6 * tokens * tokens * channels, bytes_accessed=14 * tokens * channels, transcendentals=0
        ),
        name="query_grads",
    )(queries, keys, values, attn_grad, state, *after)


def key_value_grad_kernel(q_ref, k_ref, v_ref, ag_ref, r_ref, kin_ref, *refs):
    kg_ref, vg_ref = refs[-2:]
    half = q_ref.shape[0] // 2
    top, low = slice(0, half), slice(half, 2 * half)
    for i in range(r_ref.shape[0]):
        q, k, v, ag = head(q_ref, i), head(k_ref, i), head(v_ref, i), head(ag_ref, i)
        here = slice(i * HEAD_DIM, (i + 1) * HEAD_DIM)
        rev = r_ref[i]
        kg_ref[:, here] = (head(kin_ref, i) + dot(v, rev, NT)).astype(BF16)
        a00 = lower(dot(q[top], k[top], NT))
        a10 = dot(q[low], k[top], NT).astype(BF16)
        a11 = lower(dot(q[low], k[low], NT))
        from_rev = dot(k, rev, NN)
        vg_ref[top, here] = (dot(a00, ag[top], TN) + dot(a10, ag[low], TN) + from_rev[top]).astype(BF16)
        vg_ref[low, here] = (dot(a11, ag[low], TN) + from_rev[low]).astype(BF16)


def key_value_grads(queries, keys, values, attn_grad, rev, key_in, pair, after=()):
    tokens, channels = keys.shape
    spec = pl.BlockSpec((tokens, pair * HEAD_DIM), lambda b: (0, b))
    return pl.pallas_call(
        key_value_grad_kernel,
        grid=(channels // (pair * HEAD_DIM),),
        in_specs=[spec] * 4
        + [pl.BlockSpec((pair, HEAD_DIM, HEAD_DIM), lambda b: (b, 0, 0)), spec]
        + [pl.BlockSpec(memory_space=pl.ANY)] * len(after),
        out_specs=[spec] * 2,
        out_shape=[jax.ShapeDtypeStruct((tokens, channels), BF16)] * 2,
        compiler_params=params(56),
        cost_estimate=pl.CostEstimate(
            flops=5 * tokens * tokens * channels, bytes_accessed=16 * tokens * channels, transcendentals=0
        ),
        name="key_value_grads",
    )(queries, keys, values, attn_grad, rev, key_in, *after)


def running_kernel(reverse, after, x_ref, *refs):
    refs = refs[after:]
    o_ref = refs[-1]
    count, rows = x_ref.shape[:2]
    total = jnp.zeros(x_ref.shape[1:], F32)
    for place in range(count)[:: -1 if reverse else 1]:
        o_ref[place, :rows] = total.astype(BF16)
        total = total + x_ref[place].astype(F32)
    if len(refs) > 1:
        parts = in_parts(refs[0][...])
        width = x_ref.shape[-1]
        extra = [part[:, i : i + width] for part in parts for i in range(0, part.shape[1], width)]
        extra = extra + [jnp.zeros((1, width), F32)] * (o_ref.shape[1] - rows - len(extra))
        extra = jnp.concatenate(extra, axis=0).astype(BF16)
        for place in range(count):
            o_ref[place, rows:] = extra


def in_parts(x):
    high = x.astype(BF16).astype(F32)
    middle = (x - high).astype(BF16).astype(F32)
    return high, middle, (x - high - middle).astype(BF16).astype(F32)


def running(rows, reverse, row=None, after=()):
    count, height, width = rows.shape
    more = 0 if row is None else -(-3 * row.shape[1] // width // 16) * 16
    args = [rows, *after] + ([] if row is None else [row])
    return pl.pallas_call(
        functools.partial(running_kernel, reverse, len(after)),
        in_specs=[pl.BlockSpec()]
        + [pl.BlockSpec(memory_space=pl.ANY)] * len(after)
        + ([] if row is None else [pl.BlockSpec()]),
        out_shape=jax.ShapeDtypeStruct((count, height + more, width), BF16),
        compiler_params=pltpu.CompilerParams(vmem_limit_bytes=8 * MIB),
        name="running_sums",
    )(*args)


def row_total(arrived, height, channels):
    count, _, width = arrived.shape
    parts = arrived[:, height : height + 3 * channels // width].astype(F32)
    return jnp.sum(parts.reshape(count, 3, channels // width, width), axis=(0, 1)).reshape(channels)


ALL = ("y", "core", "z", "x")
SEQ = ("z", "x")
PLANE = ("y", "x")


def exchange(x, axis):
    rows = x.reshape((lax.axis_size(axis), -1) + x.shape[-1:])
    return lax.all_to_all(rows, axis, 0, 0, tiled=True)


def everyones(x, axis):
    return lax.all_to_all(jnp.broadcast_to(x[None], (lax.axis_size(axis),) + x.shape), axis, 0, 0, tiled=True)


def flipped(x, axis, bit=1):
    return lax.ppermute(x, axis, [(i, i ^ bit) for i in range(lax.axis_size(axis))])


def added(*terms):
    total = terms[0].astype(F32)
    for term in terms[1:]:
        total = total + term.astype(F32)
    return total


def together(*xs):
    return lax.optimization_barrier(xs)


def small_call(kernel, out_shapes, *args, after=(), mib=56):
    def call(*refs):
        kernel(*refs[: len(args)], *refs[len(args) + len(after) :])

    return pl.pallas_call(
        call,
        in_specs=[pl.BlockSpec()] * len(args)
        + [pl.BlockSpec(memory_space=pl.ANY)] * len(after),
        out_shape=[jax.ShapeDtypeStruct(shape, F32 if shape == END else BF16) for shape in out_shapes],
        compiler_params=pltpu.CompilerParams(vmem_limit_bytes=mib * MIB),
        cost_estimate=pl.CostEstimate(
            flops=0, bytes_accessed=4 * sum(x.size for x in args), transcendentals=0
        ),
        name=kernel.__name__,
    )(*args, *after)


def one(i):
    return pl.ds(i, 1)


def place(axis, bit=1):
    here = (lax.axis_index(axis) // bit) % 2
    return here, 1 - here


def merge_all(own_ref, x_ref, y_ref, low_ref, high_ref, out_ref):
    y, other_y = place("y")
    x, other_x = place("x")
    half = low_ref.shape[0]
    out_ref[one(y), :, one(x)] = own_ref[...][None, :, None]
    out_ref[one(y), :, one(other_x)] = x_ref[...][None, :, None]
    out_ref[one(other_y), :, one(x)] = y_ref[...][None, :, None]
    out_ref[one(other_y), :half, one(other_x)] = low_ref[...][None, :, None]
    out_ref[one(other_y), half:, one(other_x)] = high_ref[...][None, :, None]


def total(a_ref, b_ref, *index):
    return (a_ref[index].astype(F32) + b_ref[index].astype(F32)).astype(BF16)


def split_first(keep_ref, got_ref, left_ref, right_ref, left_keep_ref, right_keep_ref):
    half = left_ref.shape[-1]
    here, there = place("y")
    every = slice(None)
    for at, ref in ((there, left_ref), (here, left_keep_ref)):
        ref[...] = total(keep_ref, got_ref, one(at), every, every, every, slice(0, half))[0]
    here, there = place("x")
    for at, ref in ((there, right_ref), (here, right_keep_ref)):
        ref[...] = total(keep_ref, got_ref, every, every, one(at), every, slice(half, 2 * half))[:, :, 0]


def split_second(
    left_ref, left_got_ref, right_ref, right_got_ref, left_out, right_out, left_keep, right_keep
):
    here, there = place("x")
    for at, ref in ((there, left_out), (here, left_keep)):
        ref[...] = total(left_ref, left_got_ref, slice(None), one(at))[:, 0]
    here, there = place("y")
    for at, ref in ((there, right_out), (here, right_keep)):
        ref[...] = total(right_ref, right_got_ref, one(at))[0]


def join_sides(left_ref, left_got_ref, right_ref, right_got_ref, out_ref, end_ref):
    end_ref[...] = jnp.zeros_like(end_ref)
    half = left_ref.shape[-1]
    out_ref[:, :, :half] = total(left_ref, left_got_ref, slice(None))
    out_ref[:, :, half:] = total(right_ref, right_got_ref, slice(None))


def by_halves(sizes, rows, q, k, v, og, out_weight, gain_row, pos, pair):
    tokens, channels = q.shape
    wide = out_weight.shape[1]
    y, z, x, half = sizes["y"], sizes["z"], sizes["x"], wide // 2

    own = everyones(out_weight, "z")
    kv = key_value_sums(k, v, pair)
    kv, own = together(kv, own)
    x_got, y_got = flipped(own, "x"), flipped(own, "y")
    sent = exchange(kv, SEQ)
    intra, end = intra_outputs(q, k, v, pair)
    sent, x_got, y_got = together(sent, x_got, y_got)
    low, high = flipped(x_got[: z // 2], "y"), flipped(y_got[z // 2 :], "x")
    state = exchange(running(sent, False, after=(end,)), SEQ).reshape(kv.shape)
    outputs, send, og = weight_parts(pos, 1, q, state, intra, gain_row, og, pair)
    send, low, high = together(send, low, high)
    got = flipped(send, "core")
    (mine,) = small_call(merge_all, [(y, z, x, rows, wide)], own, x_got, y_got, low, high, mib=20)
    mine = mine.reshape(y, -1, wide)
    other = flipped(mine, "core")
    outputs, keep = weight_parts(pos, 0, q, state, intra, gain_row, og, pair, (outputs,))

    split = (y, z, x, rows, wide)
    left, right, left_keep, right_keep = small_call(
        split_first,
        [(z, x, rows, half), (y, z, rows, half)] * 2,
        keep.reshape(split),
        got.reshape(split),
        mib=20,
    )
    other, left, right = together(other, left, right)
    left_got, right_got = flipped(left, "y"), flipped(right, "x")
    attn_grad, gain_part, qg = attn_grads(pos, q, outputs, gain_row, og, mine, other, pair)
    qg, left_got, right_got = together(qg, left_got, right_got)

    sent = exchange(qg, SEQ)
    gain_part = gain_part + flipped(gain_part, "core")
    left, right, left_keep, right_keep = small_call(
        split_second, [(z, rows, half)] * 4, left_keep, left_got, right_keep, right_got
    )
    left_got, right_got = flipped(left, "x"), flipped(right, "y")
    part, end = small_call(join_sides, [(z, rows, wide), END], left_keep, left_got, right_keep, right_got)
    sums = running(sent, True, gain_part, after=(end,))
    arrived = exchange(sums, SEQ)
    part = lax.all_to_all(part, "z", 0, 0, tiled=True)
    query_g, key_in, end = query_grads(q, k, v, attn_grad, state, pair, after=(sums,))
    key_g, value_g = key_value_grads(q, k, v, attn_grad, arrived, key_in, pair, after=(end,))
    gain_sum = row_total(arrived, sent.shape[1], channels)
    return query_g, key_g, value_g, part, gain_sum + flipped(gain_sum, "y")


def by_planes(sizes, rows, q, k, v, og, out_weight, gain_row, pos, pair):
    tokens, channels = q.shape
    wide = out_weight.shape[1]
    y, z, x = sizes["y"], sizes["z"], sizes["x"]
    weight = lax.all_gather(out_weight, ALL, axis=0, tiled=True)
    kv = key_value_sums(k, v, pair)
    intra, _ = intra_outputs(q, k, v, pair)
    state = exchange(running(exchange(kv, SEQ), False), SEQ).reshape(kv.shape)
    outputs, send, og = weight_parts(pos, 1, q, state, intra, gain_row, og, pair)
    outputs, keep = weight_parts(pos, 0, q, state, intra, gain_row, og, pair, (outputs,))
    part = added(keep, flipped(send, "core")).astype(BF16)
    part = part.reshape(y, z, x, rows, wide).transpose(0, 2, 1, 3, 4).reshape(y * x, z, rows, wide)
    part = lax.all_to_all(part, PLANE, 0, 0, tiled=True)
    part = added(*[part[i] for i in range(y * x)]).astype(BF16)
    part = lax.all_to_all(part, "z", 0, 0, tiled=True)
    weight = weight.reshape(y, 2, z * x * rows, wide)
    mine, other = [
        lax.dynamic_index_in_dim(weight, i, 1, keepdims=False) for i in place("core")
    ]
    attn_grad, gain_part, qg = attn_grads(pos, q, outputs, gain_row, og, mine, other, pair)
    rev = exchange(running(exchange(qg, SEQ), True), SEQ).reshape(kv.shape)
    query_g, key_in, _ = query_grads(q, k, v, attn_grad, state, pair)
    key_g, value_g = key_value_grads(q, k, v, attn_grad, rev, key_in, pair)
    gain_sum = jnp.sum(everyones(gain_part.reshape(channels), ALL), axis=0)
    return query_g, key_g, value_g, part, gain_sum


def shards(queries, keys, values, out_grad, out_weight, gain):
    tokens, channels = queries.shape[1:]
    assert tokens == BLOCK
    sizes = {name: lax.axis_size(name) for name in ALL}
    devices = lax.axis_size(ALL)
    rows = out_weight.shape[0]
    pair = channels // (sizes["y"] * sizes["core"]) // HEAD_DIM
    pos = lax.axis_index(("y", "core")).reshape(1).astype(jnp.int32)
    halves = (sizes["y"], sizes["z"], sizes["x"]) == (2, 4, 2) and rows % 16 == 0
    query_g, key_g, value_g, part, gain_sum = (by_halves if halves else by_planes)(
        sizes,
        rows,
        queries[0],
        keys[0],
        values[0],
        out_grad[0],
        out_weight,
        gain.reshape(1, channels),
        pos,
        pair,
    )
    factor = 1.0 / jnp.sqrt(jnp.float32(tokens * devices))
    out_shape = (1, tokens, channels)
    return (
        query_g.reshape(out_shape),
        key_g.reshape(out_shape),
        value_g.reshape(out_shape),
        added(*[part[i] for i in range(part.shape[0])]) * factor,
        gain_sum * factor,
    )


def solution(mesh):
    dp_count, seq_count = mesh.shape["dp"], mesh.shape["seq"]
    finer = Mesh(mesh.devices.reshape(dp_count // 2, 2, seq_count // 2, 2), ALL)
    tokens = P(("y", "core"), ("z", "x"), None)
    rows = P(ALL, None)
    return jax.shard_map(
        shards,
        mesh=finer,
        in_specs=(tokens, tokens, tokens, tokens, rows, P()),
        out_specs=(tokens, tokens, tokens, rows, P()),
        check_vma=False,
    )
```

```python
import functools

import jax
import jax.numpy as jnp
from jax import lax
from jax.experimental import pallas as pl
from jax.experimental.pallas import tpu as pltpu
from jax.sharding import Mesh
from jax.sharding import PartitionSpec as P

HEAD_DIM = 128
BLOCK = 512
MIB = 1 << 20

norm_eps = 1e-06

END = (8, 128)

F32 = jnp.float32
BF16 = jnp.bfloat16


def dot(a, b, contract):
    return lax.dot_general(a, b, (contract, ((), ())), preferred_element_type=F32)


def params(mib, dims=1):
    return pltpu.CompilerParams(
        vmem_limit_bytes=mib * MIB, dimension_semantics=("arbitrary",) * dims
    )


ROW_BLOCKS = 4


def row_blocks(tokens, wide):
    return [
        pl.BlockSpec((tokens // ROW_BLOCKS, wide), lambda y, p, r=r: (r, 0)) for r in range(ROW_BLOCKS)
    ]


def head(ref, i):
    return ref[:, i * HEAD_DIM : (i + 1) * HEAD_DIM]


def kv_kernel(k_ref, v_ref, o_ref):
    for i in range(o_ref.shape[0]):
        o_ref[i] = dot(head(k_ref, i), head(v_ref, i), ((0,), (0,))).astype(BF16)


def key_value_sums(keys, values, pair):
    tokens, channels = keys.shape
    width = pair * HEAD_DIM
    heads = channels // HEAD_DIM
    spec = pl.BlockSpec((tokens, width), lambda b: (0, b))
    return pl.pallas_call(
        kv_kernel,
        grid=(heads // pair,),
        in_specs=[spec, spec],
        out_specs=pl.BlockSpec((pair, HEAD_DIM, HEAD_DIM), lambda b: (b, 0, 0)),
        out_shape=jax.ShapeDtypeStruct((heads, HEAD_DIM, HEAD_DIM), BF16),
        compiler_params=params(56),
        cost_estimate=pl.CostEstimate(
            flops=2 * tokens * channels * HEAD_DIM, bytes_accessed=4 * tokens * channels, transcendentals=0
        ),
        name="key_value_sums",
    )(keys, values)


def lower(x):
    rows = lax.broadcasted_iota(jnp.int32, x.shape, 0)
    cols = lax.broadcasted_iota(jnp.int32, x.shape, 1)
    return jnp.where(cols <= rows, x, 0.0).astype(BF16)


def intra_kernel(q_ref, k_ref, v_ref, o_ref, end_ref):
    end_ref[...] = jnp.zeros_like(end_ref)
    half = q_ref.shape[0] // 2
    for i in range(o_ref.shape[1] // HEAD_DIM):
        q, k, v = head(q_ref, i), head(k_ref, i), head(v_ref, i)
        here = slice(i * HEAD_DIM, (i + 1) * HEAD_DIM)
        top = lower(dot(q[:half], k[:half], ((1,), (1,))))
        o_ref[:half, here] = dot(top, v[:half], ((1,), (0,)))
        left = dot(q[half:], k[:half], ((1,), (1,))).astype(BF16)
        right = lower(dot(q[half:], k[half:], ((1,), (1,))))
        o_ref[half:, here] = dot(left, v[:half], ((1,), (0,))) + dot(right, v[half:], ((1,), (0,)))


def intra_outputs(queries, keys, values, pair):
    tokens, channels = keys.shape
    spec = pl.BlockSpec((tokens, pair * HEAD_DIM), lambda b: (0, b))
    return pl.pallas_call(
        intra_kernel,
        grid=(channels // (pair * HEAD_DIM),),
        in_specs=[spec] * 3,
        out_specs=[spec, pl.BlockSpec(END, lambda b: (0, 0))],
        out_shape=[jax.ShapeDtypeStruct((tokens, channels), F32), jax.ShapeDtypeStruct(END, F32)],
        compiler_params=params(56),
        cost_estimate=pl.CostEstimate(
            flops=4 * tokens * tokens * channels, bytes_accessed=10 * tokens * channels, transcendentals=0
        ),
        name="intra_outputs",
    )(queries, keys, values)


def rms_inverse(x):
    return lax.rsqrt(jnp.mean(x * x, axis=-1, keepdims=True) + norm_eps)


def unit_kernel(begun, pos_ref, q_ref, s_ref, intra_ref, gain_ref, *refs):
    if begun:
        og_ref, _, out_ref, part_ref = refs
    else:
        *og_refs, out_ref, part_ref, og_ref = refs

        @pl.when(pl.program_id(0) == 0)
        def _():
            start = 0
            for ref in og_refs:
                og_ref[start : start + ref.shape[0]] = ref[...]
                start = start + ref.shape[0]

    units = []
    for i in range(s_ref.shape[0]):
        x = head(intra_ref, i) + dot(head(q_ref, i), s_ref[i], ((1,), (0,)))
        out_ref[:, i * HEAD_DIM : (i + 1) * HEAD_DIM] = x
        units.append((x * rms_inverse(x) * head(gain_ref, i)).astype(BF16))
    unit = jnp.concatenate(units, axis=1) if len(units) > 1 else units[0]
    part_ref[0] = dot(unit, og_ref[...], ((0,), (0,))).astype(BF16)


def weight_parts(pos, side, queries, state, intra, gain, out_grad, pair, begun=()):
    tokens, channels = queries.shape
    width = pair * HEAD_DIM
    count = channels // width // 2
    wide = out_grad.shape[1]

    def block(y, pos_ref):
        return 2 * y + lax.rem(pos_ref[0] + side, 2)

    cols = pl.BlockSpec((tokens, width), lambda y, p: (0, block(y, p)))
    whole = pl.BlockSpec((tokens, wide), lambda y, p: (0, 0))
    more = [] if begun else [(whole, jax.ShapeDtypeStruct((tokens, wide), BF16))]
    return pl.pallas_call(
        functools.partial(unit_kernel, len(begun)),
        grid_spec=pltpu.PrefetchScalarGridSpec(
            num_scalar_prefetch=1,
            grid=(count,),
            in_specs=[
                cols,
                pl.BlockSpec((pair, HEAD_DIM, HEAD_DIM), lambda y, p: (block(y, p), 0, 0)),
                cols,
                pl.BlockSpec((1, width), lambda y, p: (0, block(y, p))),
            ]
            + ([whole, pl.BlockSpec(memory_space=pl.ANY)] if begun else row_blocks(tokens, wide)),
            out_specs=[cols, pl.BlockSpec((1, width, wide), lambda y, p: (y, 0, 0))] + [m[0] for m in more],
        ),
        out_shape=[
            jax.ShapeDtypeStruct((tokens, channels), F32),
            jax.ShapeDtypeStruct((count, width, wide), BF16),
        ]
        + [m[1] for m in more],
        input_output_aliases={6: 0} if begun else {},
        compiler_params=params(30 if begun else 44),
        cost_estimate=pl.CostEstimate(
            flops=tokens * channels * wide,
            bytes_accessed=5 * tokens * channels + 2 * tokens * wide + channels * wide,
            transcendentals=0,
        ),
        name="weight_parts",
    )(pos, queries, state, intra, gain, *[out_grad] * (1 if begun else ROW_BLOCKS), *begun)


def attn_grad_kernel(pos_ref, q_ref, o_ref, gain_ref, og_ref, mine_ref, other_ref, ag_ref, gg_ref, qg_ref, ug_ref):
    count = pl.num_programs(0) // 2

    @pl.when(pl.program_id(0) < count)
    def _():
        ug_ref[...] = dot(og_ref[...], mine_ref[0], ((1,), (1,)))

    @pl.when(pl.program_id(0) >= count)
    def _():
        ug_ref[...] = dot(og_ref[...], other_ref[0], ((1,), (1,)))

    for i in range(qg_ref.shape[0]):
        here = slice(i * HEAD_DIM, (i + 1) * HEAD_DIM)
        x = head(o_ref, i)
        inverse = rms_inverse(x)
        normed = x * inverse
        ug = head(ug_ref, i)
        gg_ref[:, here] = jnp.sum(ug * normed, axis=0, keepdims=True)
        scaled = ug * head(gain_ref, i)
        middle = jnp.mean(scaled * normed, axis=-1, keepdims=True)
        ag = ((scaled - normed * middle) * inverse).astype(BF16)
        ag_ref[:, here] = ag
        qg_ref[i] = dot(head(q_ref, i), ag, ((0,), (0,))).astype(BF16)


def attn_grads(pos, queries, outputs, gain, out_grad, mine, other, pair):
    tokens, channels = queries.shape
    width = pair * HEAD_DIM
    count = channels // width // 2
    wide = out_grad.shape[1]
    heads = channels // HEAD_DIM

    def block(s, pos_ref):
        return 2 * lax.rem(s, count) + lax.rem(pos_ref[0] + s // count, 2)

    cols = pl.BlockSpec((tokens, width), lambda s, p: (0, block(s, p)))
    row = pl.BlockSpec((1, width), lambda s, p: (0, block(s, p)))
    states = pl.BlockSpec((pair, HEAD_DIM, HEAD_DIM), lambda s, p: (block(s, p), 0, 0))
    piece = (1,) + mine.shape[1:]
    return pl.pallas_call(
        attn_grad_kernel,
        grid_spec=pltpu.PrefetchScalarGridSpec(
            num_scalar_prefetch=1,
            grid=(2 * count,),
            in_specs=[
                cols,
                cols,
                row,
                pl.BlockSpec((tokens, wide), lambda s, p: (0, 0)),
                pl.BlockSpec(piece, lambda s, p: (jnp.minimum(s, count - 1), 0, 0)),
                pl.BlockSpec(piece, lambda s, p: (jnp.maximum(s - count, 0), 0, 0)),
            ],
            out_specs=[cols, row, states],
            scratch_shapes=[pltpu.VMEM((tokens, width), F32)],
        ),
        out_shape=[
            jax.ShapeDtypeStruct((tokens, channels), BF16),
            jax.ShapeDtypeStruct((1, channels), F32),
            jax.ShapeDtypeStruct((heads, HEAD_DIM, HEAD_DIM), BF16),
        ],
        compiler_params=params(30),
        cost_estimate=pl.CostEstimate(
            flops=2 * tokens * channels * wide,
            bytes_accessed=8 * tokens * channels + 2 * tokens * wide + 2 * channels * wide,
            transcendentals=0,
        ),
        name="attn_grads",
    )(pos, queries, outputs, gain, out_grad, mine, other)


NT, NN, TN = ((1,), (1,)), ((1,), (0,)), ((0,), (0,))


def query_grad_kernel(q_ref, k_ref, v_ref, ag_ref, s_ref, *refs):
    qg_ref, kg_ref, end_ref = refs[-3:]
    end_ref[...] = jnp.zeros_like(end_ref)
    half = q_ref.shape[0] // 2
    top, low = slice(0, half), slice(half, 2 * half)
    for i in range(s_ref.shape[0]):
        q, k, v, ag = head(q_ref, i), head(k_ref, i), head(v_ref, i), head(ag_ref, i)
        here = slice(i * HEAD_DIM, (i + 1) * HEAD_DIM)
        from_state = dot(ag, s_ref[i], NT)
        g00 = lower(dot(ag[top], v[top], NT))
        g10 = dot(ag[low], v[top], NT).astype(BF16)
        g11 = lower(dot(ag[low], v[low], NT))
        qg_ref[top, here] = (dot(g00, k[top], NN) + from_state[top]).astype(BF16)
        qg_ref[low, here] = (dot(g10, k[top], NN) + dot(g11, k[low], NN) + from_state[low]).astype(BF16)
        kg_ref[top, here] = dot(g00, q[top], TN) + dot(g10, q[low], TN)
        kg_ref[low, here] = dot(g11, q[low], TN)


def query_grads(queries, keys, values, attn_grad, state, pair, after=()):
    tokens, channels = queries.shape
    spec = pl.BlockSpec((tokens, pair * HEAD_DIM), lambda b: (0, b))
    return pl.pallas_call(
        query_grad_kernel,
        grid=(channels // (pair * HEAD_DIM),),
        in_specs=[spec] * 4
        + [pl.BlockSpec((pair, HEAD_DIM, HEAD_DIM), lambda b: (b, 0, 0))]
        + [pl.BlockSpec(memory_space=pl.ANY)] * len(after),
        out_specs=[spec, spec, pl.BlockSpec(END, lambda b: (0, 0))],
        out_shape=[jax.ShapeDtypeStruct((tokens, channels), t) for t in (BF16, F32)]
        + [jax.ShapeDtypeStruct(END, F32)],
        compiler_params=params(56),
        cost_estimate=pl.CostEstimate(
            flops=6 * tokens * tokens * channels, bytes_accessed=14 * tokens * channels, transcendentals=0
        ),
        name="query_grads",
    )(queries, keys, values, attn_grad, state, *after)


def key_value_grad_kernel(q_ref, k_ref, v_ref, ag_ref, r_ref, kin_ref, *refs):
    kg_ref, vg_ref = refs[-2:]
    half = q_ref.shape[0] // 2
    top, low = slice(0, half), slice(half, 2 * half)
    for i in range(r_ref.shape[0]):
        q, k, v, ag = head(q_ref, i), head(k_ref, i), head(v_ref, i), head(ag_ref, i)
        here = slice(i * HEAD_DIM, (i + 1) * HEAD_DIM)
        rev = r_ref[i]
        kg_ref[:, here] = (head(kin_ref, i) + dot(v, rev, NT)).astype(BF16)
        a00 = lower(dot(q[top], k[top], NT))
        a10 = dot(q[low], k[top], NT).astype(BF16)
        a11 = lower(dot(q[low], k[low], NT))
        from_rev = dot(k, rev, NN)
        vg_ref[top, here] = (dot(a00, ag[top], TN) + dot(a10, ag[low], TN) + from_rev[top]).astype(BF16)
        vg_ref[low, here] = (dot(a11, ag[low], TN) + from_rev[low]).astype(BF16)


def key_value_grads(queries, keys, values, attn_grad, rev, key_in, pair, after=()):
    tokens, channels = keys.shape
    spec = pl.BlockSpec((tokens, pair * HEAD_DIM), lambda b: (0, b))
    return pl.pallas_call(
        key_value_grad_kernel,
        grid=(channels // (pair * HEAD_DIM),),
        in_specs=[spec] * 4
        + [pl.BlockSpec((pair, HEAD_DIM, HEAD_DIM), lambda b: (b, 0, 0)), spec]
        + [pl.BlockSpec(memory_space=pl.ANY)] * len(after),
        out_specs=[spec] * 2,
        out_shape=[jax.ShapeDtypeStruct((tokens, channels), BF16)] * 2,
        compiler_params=params(56),
        cost_estimate=pl.CostEstimate(
            flops=5 * tokens * tokens * channels, bytes_accessed=16 * tokens * channels, transcendentals=0
        ),
        name="key_value_grads",
    )(queries, keys, values, attn_grad, rev, key_in, *after)


def running_kernel(reverse, after, x_ref, *refs):
    refs = refs[after:]
    o_ref = refs[-1]
    count, rows = x_ref.shape[:2]
    total = jnp.zeros(x_ref.shape[1:], F32)
    for place in range(count)[:: -1 if reverse else 1]:
        o_ref[place, :rows] = total.astype(BF16)
        total = total + x_ref[place].astype(F32)
    if len(refs) > 1:
        parts = in_parts(refs[0][...])
        width = x_ref.shape[-1]
        extra = [part[:, i : i + width] for part in parts for i in range(0, part.shape[1], width)]
        extra = extra + [jnp.zeros((1, width), F32)] * (o_ref.shape[1] - rows - len(extra))
        extra = jnp.concatenate(extra, axis=0).astype(BF16)
        for place in range(count):
            o_ref[place, rows:] = extra


def in_parts(x):
    high = x.astype(BF16).astype(F32)
    middle = (x - high).astype(BF16).astype(F32)
    return high, middle, (x - high - middle).astype(BF16).astype(F32)


def running(rows, reverse, row=None, after=()):
    count, height, width = rows.shape
    more = 0 if row is None else -(-3 * row.shape[1] // width // 16) * 16
    args = [rows, *after] + ([] if row is None else [row])
    return pl.pallas_call(
        functools.partial(running_kernel, reverse, len(after)),
        in_specs=[pl.BlockSpec()]
        + [pl.BlockSpec(memory_space=pl.ANY)] * len(after)
        + ([] if row is None else [pl.BlockSpec()]),
        out_shape=jax.ShapeDtypeStruct((count, height + more, width), BF16),
        compiler_params=pltpu.CompilerParams(vmem_limit_bytes=8 * MIB),
        name="running_sums",
    )(*args)


def row_total(arrived, height, channels):
    count, _, width = arrived.shape
    parts = arrived[:, height : height + 3 * channels // width].astype(F32)
    return jnp.sum(parts.reshape(count, 3, channels // width, width), axis=(0, 1)).reshape(channels)


ALL = ("y", "core", "z", "x")
SEQ = ("z", "x")
PLANE = ("y", "x")


def exchange(x, axis):
    rows = x.reshape((lax.axis_size(axis), -1) + x.shape[-1:])
    return lax.all_to_all(rows, axis, 0, 0, tiled=True)


def everyones(x, axis):
    return lax.all_to_all(jnp.broadcast_to(x[None], (lax.axis_size(axis),) + x.shape), axis, 0, 0, tiled=True)


def flipped(x, axis, bit=1):
    return lax.ppermute(x, axis, [(i, i ^ bit) for i in range(lax.axis_size(axis))])


def added(*terms):
    total = terms[0].astype(F32)
    for term in terms[1:]:
        total = total + term.astype(F32)
    return total


def together(*xs):
    return lax.optimization_barrier(xs)


def small_call(kernel, out_shapes, *args, after=(), mib=56):
    def call(*refs):
        kernel(*refs[: len(args)], *refs[len(args) + len(after) :])

    return pl.pallas_call(
        call,
        in_specs=[pl.BlockSpec()] * len(args)
        + [pl.BlockSpec(memory_space=pl.ANY)] * len(after),
        out_shape=[jax.ShapeDtypeStruct(shape, F32 if shape == END else BF16) for shape in out_shapes],
        compiler_params=pltpu.CompilerParams(vmem_limit_bytes=mib * MIB),
        cost_estimate=pl.CostEstimate(
            flops=0, bytes_accessed=4 * sum(x.size for x in args), transcendentals=0
        ),
        name=kernel.__name__,
    )(*args, *after)


def one(i):
    return pl.ds(i, 1)


def place(axis, bit=1):
    here = (lax.axis_index(axis) // bit) % 2
    return here, 1 - here


def merge_all(own_ref, x_ref, y_ref, low_ref, high_ref, out_ref):
    y, other_y = place("y")
    x, other_x = place("x")
    half = low_ref.shape[0]
    out_ref[one(y), :, one(x)] = own_ref[...][None, :, None]
    out_ref[one(y), :, one(other_x)] = x_ref[...][None, :, None]
    out_ref[one(other_y), :, one(x)] = y_ref[...][None, :, None]
    out_ref[one(other_y), :half, one(other_x)] = low_ref[...][None, :, None]
    out_ref[one(other_y), half:, one(other_x)] = high_ref[...][None, :, None]


def cut_kernel(x_ref, y_ref, low_ref, high_ref, end_ref):
    low_ref[...] = x_ref[...]
    high_ref[...] = y_ref[...]
    end_ref[...] = jnp.zeros_like(end_ref)


def cut(x_got, y_got):
    half = (x_got.shape[0] // 2,) + x_got.shape[1:]
    return pl.pallas_call(
        cut_kernel,
        grid=(1,),
        in_specs=[pl.BlockSpec(half, lambda i: (0, 0, 0)), pl.BlockSpec(half, lambda i: (1, 0, 0))],
        out_specs=[pl.BlockSpec(half, lambda i: (0, 0, 0))] * 2 + [pl.BlockSpec(END, lambda i: (0, 0))],
        out_shape=[jax.ShapeDtypeStruct(half, BF16)] * 2 + [jax.ShapeDtypeStruct(END, F32)],
        compiler_params=params(20),
        name="cut",
    )(x_got, y_got)


def total(a_ref, b_ref, *index):
    return (a_ref[index].astype(F32) + b_ref[index].astype(F32)).astype(BF16)


def split_first(keep_ref, got_ref, left_ref, right_ref, left_keep_ref, right_keep_ref):
    half = left_ref.shape[-1]
    here, there = place("y")
    every = slice(None)
    for at, ref in ((there, left_ref), (here, left_keep_ref)):
        ref[...] = total(keep_ref, got_ref, one(at), every, every, every, slice(0, half))[0]
    here, there = place("x")
    for at, ref in ((there, right_ref), (here, right_keep_ref)):
        ref[...] = total(keep_ref, got_ref, every, every, one(at), every, slice(half, 2 * half))[:, :, 0]


def split_second(
    left_ref, left_got_ref, right_ref, right_got_ref, left_out, right_out, left_keep, right_keep
):
    here, there = place("x")
    for at, ref in ((there, left_out), (here, left_keep)):
        ref[...] = total(left_ref, left_got_ref, slice(None), one(at))[:, 0]
    here, there = place("y")
    for at, ref in ((there, right_out), (here, right_keep)):
        ref[...] = total(right_ref, right_got_ref, one(at))[0]


def join_sides(left_ref, left_got_ref, right_ref, right_got_ref, send_ref, keep_ref, end_ref):
    here, there = place("z")
    half = left_ref.shape[-1]
    for far in range(send_ref.shape[0]):
        for at, ref in ((there, send_ref), (here, keep_ref)):
            ref[far, :, :half] = total(left_ref, left_got_ref, one(2 * far + at))[0]
            ref[far, :, half:] = total(right_ref, right_got_ref, one(2 * far + at))[0]
    end_ref[...] = jnp.zeros_like(end_ref)


def split_far(keep_ref, got_ref, send_ref, rest_ref, end_ref):
    here, there = place("z", 2)
    send_ref[...] = total(keep_ref, got_ref, one(there))[0]
    rest_ref[...] = total(keep_ref, got_ref, one(here))[0]
    end_ref[...] = jnp.zeros_like(end_ref)


def by_halves(sizes, rows, q, k, v, og, out_weight, gain_row, pos, pair):
    tokens, channels = q.shape
    wide = out_weight.shape[1]
    y, z, x, half = sizes["y"], sizes["z"], sizes["x"], wide // 2

    own = everyones(out_weight, "z")
    kv = key_value_sums(k, v, pair)
    kv, own = together(kv, own)
    x_got, y_got = flipped(own, "x"), flipped(own, "y")
    sent = exchange(kv, SEQ)
    intra, end = intra_outputs(q, k, v, pair)
    low, high, cut_end = cut(x_got, y_got)
    low, high = flipped(low, "y"), flipped(high, "x")
    state = exchange(running(sent, False, after=(end, cut_end)), SEQ).reshape(kv.shape)
    outputs, send, og = weight_parts(pos, 1, q, state, intra, gain_row, og, pair)
    got = flipped(send, "core")
    (mine,) = small_call(merge_all, [(y, z, x, rows, wide)], own, x_got, y_got, low, high, mib=20)
    mine = mine.reshape(y, -1, wide)
    other = flipped(mine, "core")
    outputs, mine = together(outputs, mine)
    outputs, keep = weight_parts(pos, 0, q, state, intra, gain_row, og, pair, (outputs,))

    split = (y, z, x, rows, wide)
    left, right, left_keep, right_keep = small_call(
        split_first,
        [(z, x, rows, half), (y, z, rows, half)] * 2,
        keep.reshape(split),
        got.reshape(split),
        mib=20,
    )
    outputs, left, right = together(outputs, left, right)
    left_got, right_got = flipped(left, "y"), flipped(right, "x")
    attn_grad, gain_part, qg = attn_grads(pos, q, outputs, gain_row, og, mine, other, pair)
    qg, left_got, right_got = together(qg, left_got, right_got)

    sent = exchange(qg, SEQ)
    gain_part = gain_part + flipped(gain_part, "core")
    left, right, left_keep, right_keep = small_call(
        split_second, [(z, rows, half)] * 4, left_keep, left_got, right_keep, right_got
    )
    left_got, right_got = flipped(left, "x"), flipped(right, "y")
    send, keep, end = small_call(
        join_sides, [(2, rows, wide)] * 2 + [END], left_keep, left_got, right_keep, right_got
    )
    got = flipped(send, "z", 1)
    sums = running(sent, True, gain_part, after=(end,))
    arrived = exchange(sums, SEQ)
    query_g, key_in, end = query_grads(q, k, v, attn_grad, state, pair, after=(sums,))
    keep, got, end = together(keep, got, end)
    send, keep, end = small_call(split_far, [(rows, wide)] * 2 + [END], keep, got, after=(end,))
    got = flipped(send, "z", 2)
    key_g, value_g = key_value_grads(q, k, v, attn_grad, arrived, key_in, pair, after=(end,))
    gain_sum = row_total(arrived, sent.shape[1], channels)
    return query_g, key_g, value_g, (keep, got), gain_sum + flipped(gain_sum, "y")


def by_planes(sizes, rows, q, k, v, og, out_weight, gain_row, pos, pair):
    tokens, channels = q.shape
    wide = out_weight.shape[1]
    y, z, x = sizes["y"], sizes["z"], sizes["x"]
    weight = lax.all_gather(out_weight, ALL, axis=0, tiled=True)
    kv = key_value_sums(k, v, pair)
    intra, _ = intra_outputs(q, k, v, pair)
    state = exchange(running(exchange(kv, SEQ), False), SEQ).reshape(kv.shape)
    outputs, send, og = weight_parts(pos, 1, q, state, intra, gain_row, og, pair)
    outputs, keep = weight_parts(pos, 0, q, state, intra, gain_row, og, pair, (outputs,))
    part = added(keep, flipped(send, "core")).astype(BF16)
    part = part.reshape(y, z, x, rows, wide).transpose(0, 2, 1, 3, 4).reshape(y * x, z, rows, wide)
    part = lax.all_to_all(part, PLANE, 0, 0, tiled=True)
    part = added(*[part[i] for i in range(y * x)]).astype(BF16)
    part = lax.all_to_all(part, "z", 0, 0, tiled=True)
    weight = weight.reshape(y, 2, z * x * rows, wide)
    mine, other = [
        lax.dynamic_index_in_dim(weight, i, 1, keepdims=False) for i in place("core")
    ]
    attn_grad, gain_part, qg = attn_grads(pos, q, outputs, gain_row, og, mine, other, pair)
    rev = exchange(running(exchange(qg, SEQ), True), SEQ).reshape(kv.shape)
    query_g, key_in, _ = query_grads(q, k, v, attn_grad, state, pair)
    key_g, value_g = key_value_grads(q, k, v, attn_grad, rev, key_in, pair)
    gain_sum = jnp.sum(everyones(gain_part.reshape(channels), ALL), axis=0)
    return query_g, key_g, value_g, [part[i] for i in range(z)], gain_sum


def shards(queries, keys, values, out_grad, out_weight, gain):
    tokens, channels = queries.shape[1:]
    assert tokens == BLOCK
    sizes = {name: lax.axis_size(name) for name in ALL}
    devices = lax.axis_size(ALL)
    rows = out_weight.shape[0]
    pair = channels // (sizes["y"] * sizes["core"]) // HEAD_DIM
    pos = lax.axis_index(("y", "core")).reshape(1).astype(jnp.int32)
    halves = (sizes["y"], sizes["z"], sizes["x"]) == (2, 4, 2) and rows % 16 == 0
    query_g, key_g, value_g, parts, gain_sum = (by_halves if halves else by_planes)(
        sizes,
        rows,
        queries[0],
        keys[0],
        values[0],
        out_grad[0],
        out_weight,
        gain.reshape(1, channels),
        pos,
        pair,
    )
    factor = 1.0 / jnp.sqrt(jnp.float32(tokens * devices))
    out_shape = (1, tokens, channels)
    return (
        query_g.reshape(out_shape),
        key_g.reshape(out_shape),
        value_g.reshape(out_shape),
        added(*parts) * factor,
        gain_sum * factor,
    )


def solution(mesh):
    dp_count, seq_count = mesh.shape["dp"], mesh.shape["seq"]
    finer = Mesh(mesh.devices.reshape(dp_count // 2, 2, seq_count // 2, 2), ALL)
    tokens = P(("y", "core"), ("z", "x"), None)
    rows = P(ALL, None)
    return jax.shard_map(
        shards,
        mesh=finer,
        in_specs=(tokens, tokens, tokens, tokens, rows, P()),
        out_specs=(tokens, tokens, tokens, rows, P()),
        check_vma=False,
    )
```

```python
import functools

import jax
import jax.numpy as jnp
from jax import lax
from jax.experimental import pallas as pl
from jax.experimental.pallas import tpu as pltpu
from jax.sharding import Mesh
from jax.sharding import PartitionSpec as P

HEAD_DIM = 128
BLOCK = 512
MIB = 1 << 20

norm_eps = 1e-06

END = (8, 128)

F32 = jnp.float32
BF16 = jnp.bfloat16


def dot(a, b, contract):
    return lax.dot_general(a, b, (contract, ((), ())), preferred_element_type=F32)


def params(mib, dims=1):
    return pltpu.CompilerParams(
        vmem_limit_bytes=mib * MIB, dimension_semantics=("arbitrary",) * dims
    )


ROW_BLOCKS = 4


def row_blocks(tokens, wide):
    return [
        pl.BlockSpec((tokens // ROW_BLOCKS, wide), lambda y, p, r=r: (r, 0)) for r in range(ROW_BLOCKS)
    ]


def head(ref, i):
    return ref[:, i * HEAD_DIM : (i + 1) * HEAD_DIM]


def kv_kernel(k_ref, v_ref, o_ref):
    for i in range(o_ref.shape[0]):
        o_ref[i] = dot(head(k_ref, i), head(v_ref, i), ((0,), (0,))).astype(BF16)


def key_value_sums(keys, values, pair):
    tokens, channels = keys.shape
    width = pair * HEAD_DIM
    heads = channels // HEAD_DIM
    spec = pl.BlockSpec((tokens, width), lambda b: (0, b))
    return pl.pallas_call(
        kv_kernel,
        grid=(heads // pair,),
        in_specs=[spec, spec],
        out_specs=pl.BlockSpec((pair, HEAD_DIM, HEAD_DIM), lambda b: (b, 0, 0)),
        out_shape=jax.ShapeDtypeStruct((heads, HEAD_DIM, HEAD_DIM), BF16),
        compiler_params=params(56),
        cost_estimate=pl.CostEstimate(
            flops=2 * tokens * channels * HEAD_DIM, bytes_accessed=4 * tokens * channels, transcendentals=0
        ),
        name="key_value_sums",
    )(keys, values)


def lower(x):
    rows = lax.broadcasted_iota(jnp.int32, x.shape, 0)
    cols = lax.broadcasted_iota(jnp.int32, x.shape, 1)
    return jnp.where(cols <= rows, x, 0.0).astype(BF16)


def intra_kernel(q_ref, k_ref, v_ref, o_ref, end_ref):
    end_ref[...] = jnp.zeros_like(end_ref)
    half = q_ref.shape[0] // 2
    for i in range(o_ref.shape[1] // HEAD_DIM):
        q, k, v = head(q_ref, i), head(k_ref, i), head(v_ref, i)
        here = slice(i * HEAD_DIM, (i + 1) * HEAD_DIM)
        top = lower(dot(q[:half], k[:half], ((1,), (1,))))
        o_ref[:half, here] = dot(top, v[:half], ((1,), (0,)))
        left = dot(q[half:], k[:half], ((1,), (1,))).astype(BF16)
        right = lower(dot(q[half:], k[half:], ((1,), (1,))))
        o_ref[half:, here] = dot(left, v[:half], ((1,), (0,))) + dot(right, v[half:], ((1,), (0,)))


def intra_outputs(queries, keys, values, pair):
    tokens, channels = keys.shape
    spec = pl.BlockSpec((tokens, pair * HEAD_DIM), lambda b: (0, b))
    return pl.pallas_call(
        intra_kernel,
        grid=(channels // (pair * HEAD_DIM),),
        in_specs=[spec] * 3,
        out_specs=[spec, pl.BlockSpec(END, lambda b: (0, 0))],
        out_shape=[jax.ShapeDtypeStruct((tokens, channels), F32), jax.ShapeDtypeStruct(END, F32)],
        compiler_params=params(56),
        cost_estimate=pl.CostEstimate(
            flops=4 * tokens * tokens * channels, bytes_accessed=10 * tokens * channels, transcendentals=0
        ),
        name="intra_outputs",
    )(queries, keys, values)


def rms_inverse(x):
    return lax.rsqrt(jnp.mean(x * x, axis=-1, keepdims=True) + norm_eps)


def unit_kernel(begun, pos_ref, q_ref, s_ref, intra_ref, gain_ref, *refs):
    if begun:
        og_ref, _, out_ref, part_ref = refs
    else:
        *og_refs, out_ref, part_ref, og_ref = refs

        @pl.when(pl.program_id(0) == 0)
        def _():
            start = 0
            for ref in og_refs:
                og_ref[start : start + ref.shape[0]] = ref[...]
                start = start + ref.shape[0]

    units = []
    for i in range(s_ref.shape[0]):
        x = head(intra_ref, i) + dot(head(q_ref, i), s_ref[i], ((1,), (0,)))
        out_ref[:, i * HEAD_DIM : (i + 1) * HEAD_DIM] = x
        units.append((x * rms_inverse(x) * head(gain_ref, i)).astype(BF16))
    unit = jnp.concatenate(units, axis=1) if len(units) > 1 else units[0]
    part_ref[0] = dot(unit, og_ref[...], ((0,), (0,))).astype(BF16)


def weight_parts(pos, side, queries, state, intra, gain, out_grad, pair, begun=()):
    tokens, channels = queries.shape
    width = pair * HEAD_DIM
    count = channels // width // 2
    wide = out_grad.shape[1]

    def block(y, pos_ref):
        return 2 * y + lax.rem(pos_ref[0] + side, 2)

    cols = pl.BlockSpec((tokens, width), lambda y, p: (0, block(y, p)))
    whole = pl.BlockSpec((tokens, wide), lambda y, p: (0, 0))
    more = [] if begun else [(whole, jax.ShapeDtypeStruct((tokens, wide), BF16))]
    return pl.pallas_call(
        functools.partial(unit_kernel, len(begun)),
        grid_spec=pltpu.PrefetchScalarGridSpec(
            num_scalar_prefetch=1,
            grid=(count,),
            in_specs=[
                cols,
                pl.BlockSpec((pair, HEAD_DIM, HEAD_DIM), lambda y, p: (block(y, p), 0, 0)),
                cols,
                pl.BlockSpec((1, width), lambda y, p: (0, block(y, p))),
            ]
            + ([whole, pl.BlockSpec(memory_space=pl.ANY)] if begun else row_blocks(tokens, wide)),
            out_specs=[cols, pl.BlockSpec((1, width, wide), lambda y, p: (y, 0, 0))] + [m[0] for m in more],
        ),
        out_shape=[
            jax.ShapeDtypeStruct((tokens, channels), F32),
            jax.ShapeDtypeStruct((count, width, wide), BF16),
        ]
        + [m[1] for m in more],
        input_output_aliases={6: 0} if begun else {},
        compiler_params=params(30 if begun else 44),
        cost_estimate=pl.CostEstimate(
            flops=tokens * channels * wide,
            bytes_accessed=5 * tokens * channels + 2 * tokens * wide + channels * wide,
            transcendentals=0,
        ),
        name="weight_parts",
    )(pos, queries, state, intra, gain, *[out_grad] * (1 if begun else ROW_BLOCKS), *begun)


def attn_grad_kernel(pos_ref, q_ref, o_ref, gain_ref, og_ref, mine_ref, other_ref, ag_ref, gg_ref, qg_ref, ug_ref):
    count = pl.num_programs(0) // 2

    @pl.when(pl.program_id(0) < count)
    def _():
        ug_ref[...] = dot(og_ref[...], mine_ref[0], ((1,), (1,)))

    @pl.when(pl.program_id(0) >= count)
    def _():
        ug_ref[...] = dot(og_ref[...], other_ref[0], ((1,), (1,)))

    for i in range(qg_ref.shape[0]):
        here = slice(i * HEAD_DIM, (i + 1) * HEAD_DIM)
        x = head(o_ref, i)
        inverse = rms_inverse(x)
        normed = x * inverse
        ug = head(ug_ref, i)
        gg_ref[:, here] = jnp.sum(ug * normed, axis=0, keepdims=True)
        scaled = ug * head(gain_ref, i)
        middle = jnp.mean(scaled * normed, axis=-1, keepdims=True)
        ag = ((scaled - normed * middle) * inverse).astype(BF16)
        ag_ref[:, here] = ag
        qg_ref[i] = dot(head(q_ref, i), ag, ((0,), (0,))).astype(BF16)


def attn_grads(pos, queries, outputs, gain, out_grad, mine, other, pair):
    tokens, channels = queries.shape
    width = pair * HEAD_DIM
    count = channels // width // 2
    wide = out_grad.shape[1]
    heads = channels // HEAD_DIM

    def block(s, pos_ref):
        return 2 * lax.rem(s, count) + lax.rem(pos_ref[0] + s // count, 2)

    cols = pl.BlockSpec((tokens, width), lambda s, p: (0, block(s, p)))
    row = pl.BlockSpec((1, width), lambda s, p: (0, block(s, p)))
    states = pl.BlockSpec((pair, HEAD_DIM, HEAD_DIM), lambda s, p: (block(s, p), 0, 0))
    piece = (1,) + mine.shape[1:]
    return pl.pallas_call(
        attn_grad_kernel,
        grid_spec=pltpu.PrefetchScalarGridSpec(
            num_scalar_prefetch=1,
            grid=(2 * count,),
            in_specs=[
                cols,
                cols,
                row,
                pl.BlockSpec((tokens, wide), lambda s, p: (0, 0)),
                pl.BlockSpec(piece, lambda s, p: (jnp.minimum(s, count - 1), 0, 0)),
                pl.BlockSpec(piece, lambda s, p: (jnp.maximum(s - count, 0), 0, 0)),
            ],
            out_specs=[cols, row, states],
            scratch_shapes=[pltpu.VMEM((tokens, width), F32)],
        ),
        out_shape=[
            jax.ShapeDtypeStruct((tokens, channels), BF16),
            jax.ShapeDtypeStruct((1, channels), F32),
            jax.ShapeDtypeStruct((heads, HEAD_DIM, HEAD_DIM), BF16),
        ],
        compiler_params=params(30),
        cost_estimate=pl.CostEstimate(
            flops=2 * tokens * channels * wide,
            bytes_accessed=8 * tokens * channels + 2 * tokens * wide + 2 * channels * wide,
            transcendentals=0,
        ),
        name="attn_grads",
    )(pos, queries, outputs, gain, out_grad, mine, other)


NT, NN, TN = ((1,), (1,)), ((1,), (0,)), ((0,), (0,))


def query_grad_kernel(q_ref, k_ref, v_ref, ag_ref, s_ref, *refs):
    qg_ref, kg_ref, end_ref = refs[-3:]
    end_ref[...] = jnp.zeros_like(end_ref)
    half = q_ref.shape[0] // 2
    top, low = slice(0, half), slice(half, 2 * half)
    for i in range(s_ref.shape[0]):
        q, k, v, ag = head(q_ref, i), head(k_ref, i), head(v_ref, i), head(ag_ref, i)
        here = slice(i * HEAD_DIM, (i + 1) * HEAD_DIM)
        from_state = dot(ag, s_ref[i], NT)
        g00 = lower(dot(ag[top], v[top], NT))
        g10 = dot(ag[low], v[top], NT).astype(BF16)
        g11 = lower(dot(ag[low], v[low], NT))
        qg_ref[top, here] = (dot(g00, k[top], NN) + from_state[top]).astype(BF16)
        qg_ref[low, here] = (dot(g10, k[top], NN) + dot(g11, k[low], NN) + from_state[low]).astype(BF16)
        kg_ref[top, here] = dot(g00, q[top], TN) + dot(g10, q[low], TN)
        kg_ref[low, here] = dot(g11, q[low], TN)


def query_grads(queries, keys, values, attn_grad, state, pair, after=()):
    tokens, channels = queries.shape
    spec = pl.BlockSpec((tokens, pair * HEAD_DIM), lambda b: (0, b))
    return pl.pallas_call(
        query_grad_kernel,
        grid=(channels // (pair * HEAD_DIM),),
        in_specs=[spec] * 4
        + [pl.BlockSpec((pair, HEAD_DIM, HEAD_DIM), lambda b: (b, 0, 0))]
        + [pl.BlockSpec(memory_space=pl.ANY)] * len(after),
        out_specs=[spec, spec, pl.BlockSpec(END, lambda b: (0, 0))],
        out_shape=[jax.ShapeDtypeStruct((tokens, channels), t) for t in (BF16, F32)]
        + [jax.ShapeDtypeStruct(END, F32)],
        compiler_params=params(56),
        cost_estimate=pl.CostEstimate(
            flops=6 * tokens * tokens * channels, bytes_accessed=14 * tokens * channels, transcendentals=0
        ),
        name="query_grads",
    )(queries, keys, values, attn_grad, state, *after)


def key_value_grad_kernel(q_ref, k_ref, v_ref, ag_ref, r_ref, kin_ref, *refs):
    kg_ref, vg_ref = refs[-2:]
    half = q_ref.shape[0] // 2
    top, low = slice(0, half), slice(half, 2 * half)
    for i in range(r_ref.shape[0]):
        q, k, v, ag = head(q_ref, i), head(k_ref, i), head(v_ref, i), head(ag_ref, i)
        here = slice(i * HEAD_DIM, (i + 1) * HEAD_DIM)
        rev = r_ref[i]
        kg_ref[:, here] = (head(kin_ref, i) + dot(v, rev, NT)).astype(BF16)
        a00 = lower(dot(q[top], k[top], NT))
        a10 = dot(q[low], k[top], NT).astype(BF16)
        a11 = lower(dot(q[low], k[low], NT))
        from_rev = dot(k, rev, NN)
        vg_ref[top, here] = (dot(a00, ag[top], TN) + dot(a10, ag[low], TN) + from_rev[top]).astype(BF16)
        vg_ref[low, here] = (dot(a11, ag[low], TN) + from_rev[low]).astype(BF16)


def key_value_grads(queries, keys, values, attn_grad, rev, key_in, pair, after=()):
    tokens, channels = keys.shape
    spec = pl.BlockSpec((tokens, pair * HEAD_DIM), lambda b: (0, b))
    return pl.pallas_call(
        key_value_grad_kernel,
        grid=(channels // (pair * HEAD_DIM),),
        in_specs=[spec] * 4
        + [pl.BlockSpec((pair, HEAD_DIM, HEAD_DIM), lambda b: (b, 0, 0)), spec]
        + [pl.BlockSpec(memory_space=pl.ANY)] * len(after),
        out_specs=[spec] * 2,
        out_shape=[jax.ShapeDtypeStruct((tokens, channels), BF16)] * 2,
        compiler_params=params(56),
        cost_estimate=pl.CostEstimate(
            flops=5 * tokens * tokens * channels, bytes_accessed=16 * tokens * channels, transcendentals=0
        ),
        name="key_value_grads",
    )(queries, keys, values, attn_grad, rev, key_in, *after)


def running_kernel(reverse, after, x_ref, *refs):
    refs = refs[after:]
    o_ref = refs[-1]
    count, rows = x_ref.shape[:2]
    total = jnp.zeros(x_ref.shape[1:], F32)
    for place in range(count)[:: -1 if reverse else 1]:
        o_ref[place, :rows] = total.astype(BF16)
        total = total + x_ref[place].astype(F32)
    if len(refs) > 1:
        parts = in_parts(refs[0][...])
        width = x_ref.shape[-1]
        extra = [part[:, i : i + width] for part in parts for i in range(0, part.shape[1], width)]
        extra = extra + [jnp.zeros((1, width), F32)] * (o_ref.shape[1] - rows - len(extra))
        extra = jnp.concatenate(extra, axis=0).astype(BF16)
        for place in range(count):
            o_ref[place, rows:] = extra


def in_parts(x):
    high = x.astype(BF16).astype(F32)
    middle = (x - high).astype(BF16).astype(F32)
    return high, middle, (x - high - middle).astype(BF16).astype(F32)


def running(rows, reverse, row=None, after=()):
    count, height, width = rows.shape
    more = 0 if row is None else -(-3 * row.shape[1] // width // 16) * 16
    args = [rows, *after] + ([] if row is None else [row])
    return pl.pallas_call(
        functools.partial(running_kernel, reverse, len(after)),
        in_specs=[pl.BlockSpec()]
        + [pl.BlockSpec(memory_space=pl.ANY)] * len(after)
        + ([] if row is None else [pl.BlockSpec()]),
        out_shape=jax.ShapeDtypeStruct((count, height + more, width), BF16),
        compiler_params=pltpu.CompilerParams(vmem_limit_bytes=8 * MIB),
        name="running_sums",
    )(*args)


def row_total(arrived, height, channels):
    count, _, width = arrived.shape
    parts = arrived[:, height : height + 3 * channels // width].astype(F32)
    return jnp.sum(parts.reshape(count, 3, channels // width, width), axis=(0, 1)).reshape(channels)


ALL = ("y", "core", "z", "x")
SEQ = ("z", "x")
PLANE = ("y", "x")


def exchange(x, axis):
    rows = x.reshape((lax.axis_size(axis), -1) + x.shape[-1:])
    return lax.all_to_all(rows, axis, 0, 0, tiled=True)


def everyones(x, axis):
    return lax.all_to_all(jnp.broadcast_to(x[None], (lax.axis_size(axis),) + x.shape), axis, 0, 0, tiled=True)


def flipped(x, axis, bit=1):
    return lax.ppermute(x, axis, [(i, i ^ bit) for i in range(lax.axis_size(axis))])


def added(*terms):
    total = terms[0].astype(F32)
    for term in terms[1:]:
        total = total + term.astype(F32)
    return total


def together(*xs):
    return lax.optimization_barrier(xs)


def small_call(kernel, out_shapes, *args, after=(), mib=56):
    def call(*refs):
        kernel(*refs[: len(args)], *refs[len(args) + len(after) :])

    return pl.pallas_call(
        call,
        in_specs=[pl.BlockSpec()] * len(args)
        + [pl.BlockSpec(memory_space=pl.ANY)] * len(after),
        out_shape=[jax.ShapeDtypeStruct(shape, F32 if shape == END else BF16) for shape in out_shapes],
        compiler_params=pltpu.CompilerParams(vmem_limit_bytes=mib * MIB),
        cost_estimate=pl.CostEstimate(
            flops=0, bytes_accessed=4 * sum(x.size for x in args), transcendentals=0
        ),
        name=kernel.__name__,
    )(*args, *after)


def one(i):
    return pl.ds(i, 1)


def place(axis, bit=1):
    here = (lax.axis_index(axis) // bit) % 2
    return here, 1 - here


def merge_far(mine_ref, theirs_ref, out_ref, end_ref):
    here, there = place("z", 2)
    out_ref[one(here)] = mine_ref[...][None]
    out_ref[one(there)] = theirs_ref[...][None]
    end_ref[...] = jnp.zeros_like(end_ref)


def merge_near(mine_ref, theirs_ref, out_ref):
    here, there = place("z")
    out_ref[:, one(here)] = mine_ref[...][:, None]
    out_ref[:, one(there)] = theirs_ref[...][:, None]


def merge_all(own_ref, x_ref, y_ref, low_ref, high_ref, out_ref):
    y, other_y = place("y")
    x, other_x = place("x")
    half = low_ref.shape[0]
    out_ref[one(y), :, one(x)] = own_ref[...][None, :, None]
    out_ref[one(y), :, one(other_x)] = x_ref[...][None, :, None]
    out_ref[one(other_y), :, one(x)] = y_ref[...][None, :, None]
    out_ref[one(other_y), :half, one(other_x)] = low_ref[...][None, :, None]
    out_ref[one(other_y), half:, one(other_x)] = high_ref[...][None, :, None]


def cut_kernel(x_ref, y_ref, low_ref, high_ref):
    low_ref[...] = x_ref[...]
    high_ref[...] = y_ref[...]


def cut(x_got, y_got):
    half = (x_got.shape[0] // 2,) + x_got.shape[1:]
    return pl.pallas_call(
        cut_kernel,
        grid=(1,),
        in_specs=[pl.BlockSpec(half, lambda i: (0, 0, 0)), pl.BlockSpec(half, lambda i: (1, 0, 0))],
        out_specs=[pl.BlockSpec(half, lambda i: (0, 0, 0))] * 2,
        out_shape=[jax.ShapeDtypeStruct(half, BF16)] * 2,
        compiler_params=params(20),
        name="cut",
    )(x_got, y_got)


def total(a_ref, b_ref, *index):
    return (a_ref[index].astype(F32) + b_ref[index].astype(F32)).astype(BF16)


def split_first(keep_ref, got_ref, left_ref, right_ref, left_keep_ref, right_keep_ref):
    half = left_ref.shape[-1]
    here, there = place("y")
    every = slice(None)
    for at, ref in ((there, left_ref), (here, left_keep_ref)):
        ref[...] = total(keep_ref, got_ref, one(at), every, every, every, slice(0, half))[0]
    here, there = place("x")
    for at, ref in ((there, right_ref), (here, right_keep_ref)):
        ref[...] = total(keep_ref, got_ref, every, every, one(at), every, slice(half, 2 * half))[:, :, 0]


def split_second(
    left_ref, left_got_ref, right_ref, right_got_ref, left_out, right_out, left_keep, right_keep, end_ref
):
    end_ref[...] = jnp.zeros_like(end_ref)
    here, there = place("x")
    for at, ref in ((there, left_out), (here, left_keep)):
        ref[...] = total(left_ref, left_got_ref, slice(None), one(at))[:, 0]
    here, there = place("y")
    for at, ref in ((there, right_out), (here, right_keep)):
        ref[...] = total(right_ref, right_got_ref, one(at))[0]


def join_sides(left_ref, left_got_ref, right_ref, right_got_ref, send_ref, keep_ref, end_ref):
    here, there = place("z")
    half = left_ref.shape[-1]
    for far in range(send_ref.shape[0]):
        for at, ref in ((there, send_ref), (here, keep_ref)):
            ref[far, :, :half] = total(left_ref, left_got_ref, one(2 * far + at))[0]
            ref[far, :, half:] = total(right_ref, right_got_ref, one(2 * far + at))[0]
    end_ref[...] = jnp.zeros_like(end_ref)


def split_far(keep_ref, got_ref, send_ref, rest_ref, end_ref):
    here, there = place("z", 2)
    send_ref[...] = total(keep_ref, got_ref, one(there))[0]
    rest_ref[...] = total(keep_ref, got_ref, one(here))[0]
    end_ref[...] = jnp.zeros_like(end_ref)


def by_halves(sizes, rows, q, k, v, og, out_weight, gain_row, pos, pair):
    tokens, channels = q.shape
    wide = out_weight.shape[1]
    y, z, x, half = sizes["y"], sizes["z"], sizes["x"], wide // 2

    got = flipped(out_weight, "z", 2)
    kv = key_value_sums(k, v, pair)
    sent = exchange(kv, SEQ)
    intra, end = intra_outputs(q, k, v, pair)
    own, end = small_call(merge_far, [(2, rows, wide), END], out_weight, got, after=(end,))
    got = flipped(own, "z", 1)
    sums = running(sent, False, after=(end,))
    state = exchange(sums, SEQ).reshape(kv.shape)
    (own,) = small_call(merge_near, [(2, 2, rows, wide)], own, got, after=(sums,))
    own = own.reshape(z, rows, wide)

    state, own = together(state, own)
    x_got, y_got = flipped(own, "x"), flipped(own, "y")
    outputs, send, og = weight_parts(pos, 1, q, state, intra, gain_row, og, pair)
    got = flipped(send, "core")
    outputs, x_got, y_got = together(outputs, x_got, y_got)

    low, high = cut(x_got, y_got)
    outputs, low, high = together(outputs, low, high)
    low, high = flipped(low, "y"), flipped(high, "x")
    outputs, keep = weight_parts(pos, 0, q, state, intra, gain_row, og, pair, (outputs,))
    keep, low, high = together(keep, low, high)

    (mine,) = small_call(merge_all, [(y, z, x, rows, wide)], own, x_got, y_got, low, high, mib=20)
    mine = mine.reshape(y, -1, wide)
    other = flipped(mine, "core")
    split = (y, z, x, rows, wide)
    left, right, left_keep, right_keep = small_call(
        split_first,
        [(z, x, rows, half), (y, z, rows, half)] * 2,
        keep.reshape(split),
        got.reshape(split),
        mib=20,
    )
    outputs, left, right = together(outputs, left, right)
    left_got, right_got = flipped(left, "y"), flipped(right, "x")
    attn_grad, gain_part, qg = attn_grads(pos, q, outputs, gain_row, og, mine, other, pair)
    qg, left_got, right_got = together(qg, left_got, right_got)

    sent = exchange(qg, SEQ)
    gain_part = gain_part + flipped(gain_part, "core")
    left, right, left_keep, right_keep, end = small_call(
        split_second, [(z, rows, half)] * 4 + [END], left_keep, left_got, right_keep, right_got
    )
    left_got, right_got = flipped(left, "x"), flipped(right, "y")
    query_g, key_in, end = query_grads(q, k, v, attn_grad, state, pair, after=(end,))
    left_got, right_got, end = together(left_got, right_got, end)

    send, keep, end = small_call(
        join_sides, [(2, rows, wide)] * 2 + [END], left_keep, left_got, right_keep, right_got, after=(end,)
    )
    got = flipped(send, "z", 1)
    sums = running(sent, True, gain_part, after=(end,))
    arrived = exchange(sums, SEQ)
    send, keep, end = small_call(split_far, [(rows, wide)] * 2 + [END], keep, got, after=(sums,))
    got = flipped(send, "z", 2)
    key_g, value_g = key_value_grads(q, k, v, attn_grad, arrived, key_in, pair, after=(end,))
    gain_sum = row_total(arrived, sent.shape[1], channels)
    return query_g, key_g, value_g, (keep, got), gain_sum + flipped(gain_sum, "y")


def by_planes(sizes, rows, q, k, v, og, out_weight, gain_row, pos, pair):
    tokens, channels = q.shape
    wide = out_weight.shape[1]
    y, z, x = sizes["y"], sizes["z"], sizes["x"]
    weight = lax.all_gather(out_weight, ALL, axis=0, tiled=True)
    kv = key_value_sums(k, v, pair)
    intra, _ = intra_outputs(q, k, v, pair)
    state = exchange(running(exchange(kv, SEQ), False), SEQ).reshape(kv.shape)
    outputs, send, og = weight_parts(pos, 1, q, state, intra, gain_row, og, pair)
    outputs, keep = weight_parts(pos, 0, q, state, intra, gain_row, og, pair, (outputs,))
    part = added(keep, flipped(send, "core")).astype(BF16)
    part = part.reshape(y, z, x, rows, wide).transpose(0, 2, 1, 3, 4).reshape(y * x, z, rows, wide)
    part = lax.all_to_all(part, PLANE, 0, 0, tiled=True)
    part = added(*[part[i] for i in range(y * x)]).astype(BF16)
    part = lax.all_to_all(part, "z", 0, 0, tiled=True)
    weight = weight.reshape(y, 2, z * x * rows, wide)
    mine, other = [
        lax.dynamic_index_in_dim(weight, i, 1, keepdims=False) for i in place("core")
    ]
    attn_grad, gain_part, qg = attn_grads(pos, q, outputs, gain_row, og, mine, other, pair)
    rev = exchange(running(exchange(qg, SEQ), True), SEQ).reshape(kv.shape)
    query_g, key_in, _ = query_grads(q, k, v, attn_grad, state, pair)
    key_g, value_g = key_value_grads(q, k, v, attn_grad, rev, key_in, pair)
    gain_sum = jnp.sum(everyones(gain_part.reshape(channels), ALL), axis=0)
    return query_g, key_g, value_g, [part[i] for i in range(z)], gain_sum


def shards(queries, keys, values, out_grad, out_weight, gain):
    tokens, channels = queries.shape[1:]
    assert tokens == BLOCK
    sizes = {name: lax.axis_size(name) for name in ALL}
    devices = lax.axis_size(ALL)
    rows = out_weight.shape[0]
    pair = channels // (sizes["y"] * sizes["core"]) // HEAD_DIM
    pos = lax.axis_index(("y", "core")).reshape(1).astype(jnp.int32)
    halves = (sizes["y"], sizes["z"], sizes["x"]) == (2, 4, 2) and rows % 16 == 0
    query_g, key_g, value_g, parts, gain_sum = (by_halves if halves else by_planes)(
        sizes,
        rows,
        queries[0],
        keys[0],
        values[0],
        out_grad[0],
        out_weight,
        gain.reshape(1, channels),
        pos,
        pair,
    )
    factor = 1.0 / jnp.sqrt(jnp.float32(tokens * devices))
    out_shape = (1, tokens, channels)
    return (
        query_g.reshape(out_shape),
        key_g.reshape(out_shape),
        value_g.reshape(out_shape),
        added(*parts) * factor,
        gain_sum * factor,
    )


def solution(mesh):
    dp_count, seq_count = mesh.shape["dp"], mesh.shape["seq"]
    finer = Mesh(mesh.devices.reshape(dp_count // 2, 2, seq_count // 2, 2), ALL)
    tokens = P(("y", "core"), ("z", "x"), None)
    rows = P(ALL, None)
    return jax.shard_map(
        shards,
        mesh=finer,
        in_specs=(tokens, tokens, tokens, tokens, rows, P()),
        out_specs=(tokens, tokens, tokens, rows, P()),
        check_vma=False,
    )
```

```python
import functools

import jax
import jax.numpy as jnp
from jax import lax
from jax.experimental import pallas as pl
from jax.experimental.pallas import tpu as pltpu
from jax.sharding import Mesh
from jax.sharding import PartitionSpec as P

HEAD_DIM = 128
BLOCK = 512
MIB = 1 << 20

norm_eps = 1e-06

END = (8, 128)

F32 = jnp.float32
BF16 = jnp.bfloat16


def dot(a, b, contract):
    return lax.dot_general(a, b, (contract, ((), ())), preferred_element_type=F32)


def params(mib, dims=1):
    return pltpu.CompilerParams(
        vmem_limit_bytes=mib * MIB, dimension_semantics=("arbitrary",) * dims
    )


ROW_BLOCKS = 4


def row_blocks(tokens, wide):
    return [
        pl.BlockSpec((tokens // ROW_BLOCKS, wide), lambda y, p, r=r: (r, 0)) for r in range(ROW_BLOCKS)
    ]


def head(ref, i):
    return ref[:, i * HEAD_DIM : (i + 1) * HEAD_DIM]


def kv_kernel(k_ref, v_ref, o_ref):
    for i in range(o_ref.shape[0]):
        o_ref[i] = dot(head(k_ref, i), head(v_ref, i), ((0,), (0,))).astype(BF16)


def key_value_sums(keys, values, pair):
    tokens, channels = keys.shape
    width = pair * HEAD_DIM
    heads = channels // HEAD_DIM
    spec = pl.BlockSpec((tokens, width), lambda b: (0, b))
    return pl.pallas_call(
        kv_kernel,
        grid=(heads // pair,),
        in_specs=[spec, spec],
        out_specs=pl.BlockSpec((pair, HEAD_DIM, HEAD_DIM), lambda b: (b, 0, 0)),
        out_shape=jax.ShapeDtypeStruct((heads, HEAD_DIM, HEAD_DIM), BF16),
        compiler_params=params(56),
        cost_estimate=pl.CostEstimate(
            flops=2 * tokens * channels * HEAD_DIM, bytes_accessed=4 * tokens * channels, transcendentals=0
        ),
        name="key_value_sums",
    )(keys, values)


def lower(x):
    rows = lax.broadcasted_iota(jnp.int32, x.shape, 0)
    cols = lax.broadcasted_iota(jnp.int32, x.shape, 1)
    return jnp.where(cols <= rows, x, 0.0).astype(BF16)


def intra_kernel(q_ref, k_ref, v_ref, o_ref, end_ref):
    end_ref[...] = jnp.zeros_like(end_ref)
    half = q_ref.shape[0] // 2
    for i in range(o_ref.shape[1] // HEAD_DIM):
        q, k, v = head(q_ref, i), head(k_ref, i), head(v_ref, i)
        here = slice(i * HEAD_DIM, (i + 1) * HEAD_DIM)
        top = lower(dot(q[:half], k[:half], ((1,), (1,))))
        o_ref[:half, here] = dot(top, v[:half], ((1,), (0,)))
        left = dot(q[half:], k[:half], ((1,), (1,))).astype(BF16)
        right = lower(dot(q[half:], k[half:], ((1,), (1,))))
        o_ref[half:, here] = dot(left, v[:half], ((1,), (0,))) + dot(right, v[half:], ((1,), (0,)))


def intra_outputs(queries, keys, values, pair):
    tokens, channels = keys.shape
    spec = pl.BlockSpec((tokens, pair * HEAD_DIM), lambda b: (0, b))
    return pl.pallas_call(
        intra_kernel,
        grid=(channels // (pair * HEAD_DIM),),
        in_specs=[spec] * 3,
        out_specs=[spec, pl.BlockSpec(END, lambda b: (0, 0))],
        out_shape=[jax.ShapeDtypeStruct((tokens, channels), F32), jax.ShapeDtypeStruct(END, F32)],
        compiler_params=params(56),
        cost_estimate=pl.CostEstimate(
            flops=4 * tokens * tokens * channels, bytes_accessed=10 * tokens * channels, transcendentals=0
        ),
        name="intra_outputs",
    )(queries, keys, values)


def rms_inverse(x):
    return lax.rsqrt(jnp.mean(x * x, axis=-1, keepdims=True) + norm_eps)


def unit_kernel(begun, pos_ref, q_ref, s_ref, intra_ref, gain_ref, *refs):
    if begun:
        og_ref, _, out_ref, part_ref = refs
    else:
        *og_refs, out_ref, part_ref, og_ref = refs

        @pl.when(pl.program_id(0) == 0)
        def _():
            start = 0
            for ref in og_refs:
                og_ref[start : start + ref.shape[0]] = ref[...]
                start = start + ref.shape[0]

    units = []
    for i in range(s_ref.shape[0]):
        x = head(intra_ref, i) + dot(head(q_ref, i), s_ref[i], ((1,), (0,)))
        out_ref[:, i * HEAD_DIM : (i + 1) * HEAD_DIM] = x
        units.append((x * rms_inverse(x) * head(gain_ref, i)).astype(BF16))
    unit = jnp.concatenate(units, axis=1) if len(units) > 1 else units[0]
    part_ref[0] = dot(unit, og_ref[...], ((0,), (0,))).astype(BF16)


def weight_parts(pos, side, queries, state, intra, gain, out_grad, pair, begun=()):
    tokens, channels = queries.shape
    width = pair * HEAD_DIM
    count = channels // width // 2
    wide = out_grad.shape[1]

    def block(y, pos_ref):
        return 2 * y + lax.rem(pos_ref[0] + side, 2)

    cols = pl.BlockSpec((tokens, width), lambda y, p: (0, block(y, p)))
    whole = pl.BlockSpec((tokens, wide), lambda y, p: (0, 0))
    more = [] if begun else [(whole, jax.ShapeDtypeStruct((tokens, wide), BF16))]
    return pl.pallas_call(
        functools.partial(unit_kernel, len(begun)),
        grid_spec=pltpu.PrefetchScalarGridSpec(
            num_scalar_prefetch=1,
            grid=(count,),
            in_specs=[
                cols,
                pl.BlockSpec((pair, HEAD_DIM, HEAD_DIM), lambda y, p: (block(y, p), 0, 0)),
                cols,
                pl.BlockSpec((1, width), lambda y, p: (0, block(y, p))),
            ]
            + ([whole, pl.BlockSpec(memory_space=pl.ANY)] if begun else row_blocks(tokens, wide)),
            out_specs=[cols, pl.BlockSpec((1, width, wide), lambda y, p: (y, 0, 0))] + [m[0] for m in more],
        ),
        out_shape=[
            jax.ShapeDtypeStruct((tokens, channels), F32),
            jax.ShapeDtypeStruct((count, width, wide), BF16),
        ]
        + [m[1] for m in more],
        input_output_aliases={6: 0} if begun else {},
        compiler_params=params(30 if begun else 44),
        cost_estimate=pl.CostEstimate(
            flops=tokens * channels * wide,
            bytes_accessed=5 * tokens * channels + 2 * tokens * wide + channels * wide,
            transcendentals=0,
        ),
        name="weight_parts",
    )(pos, queries, state, intra, gain, *[out_grad] * (1 if begun else ROW_BLOCKS), *begun)


def attn_grad_kernel(pos_ref, q_ref, o_ref, gain_ref, og_ref, mine_ref, other_ref, ag_ref, gg_ref, qg_ref, ug_ref):
    count = pl.num_programs(0) // 2

    @pl.when(pl.program_id(0) < count)
    def _():
        ug_ref[...] = dot(og_ref[...], mine_ref[0], ((1,), (1,)))

    @pl.when(pl.program_id(0) >= count)
    def _():
        ug_ref[...] = dot(og_ref[...], other_ref[0], ((1,), (1,)))

    for i in range(qg_ref.shape[0]):
        here = slice(i * HEAD_DIM, (i + 1) * HEAD_DIM)
        x = head(o_ref, i)
        inverse = rms_inverse(x)
        normed = x * inverse
        ug = head(ug_ref, i)
        gg_ref[:, here] = jnp.sum(ug * normed, axis=0, keepdims=True)
        scaled = ug * head(gain_ref, i)
        middle = jnp.mean(scaled * normed, axis=-1, keepdims=True)
        ag = ((scaled - normed * middle) * inverse).astype(BF16)
        ag_ref[:, here] = ag
        qg_ref[i] = dot(head(q_ref, i), ag, ((0,), (0,))).astype(BF16)


def attn_grads(pos, queries, outputs, gain, out_grad, mine, other, pair):
    tokens, channels = queries.shape
    width = pair * HEAD_DIM
    count = channels // width // 2
    wide = out_grad.shape[1]
    heads = channels // HEAD_DIM

    def block(s, pos_ref):
        return 2 * lax.rem(s, count) + lax.rem(pos_ref[0] + s // count, 2)

    cols = pl.BlockSpec((tokens, width), lambda s, p: (0, block(s, p)))
    row = pl.BlockSpec((1, width), lambda s, p: (0, block(s, p)))
    states = pl.BlockSpec((pair, HEAD_DIM, HEAD_DIM), lambda s, p: (block(s, p), 0, 0))
    piece = (1,) + mine.shape[1:]
    return pl.pallas_call(
        attn_grad_kernel,
        grid_spec=pltpu.PrefetchScalarGridSpec(
            num_scalar_prefetch=1,
            grid=(2 * count,),
            in_specs=[
                cols,
                cols,
                row,
                pl.BlockSpec((tokens, wide), lambda s, p: (0, 0)),
                pl.BlockSpec(piece, lambda s, p: (jnp.minimum(s, count - 1), 0, 0)),
                pl.BlockSpec(piece, lambda s, p: (jnp.maximum(s - count, 0), 0, 0)),
            ],
            out_specs=[cols, row, states],
            scratch_shapes=[pltpu.VMEM((tokens, width), F32)],
        ),
        out_shape=[
            jax.ShapeDtypeStruct((tokens, channels), BF16),
            jax.ShapeDtypeStruct((1, channels), F32),
            jax.ShapeDtypeStruct((heads, HEAD_DIM, HEAD_DIM), BF16),
        ],
        compiler_params=params(30),
        cost_estimate=pl.CostEstimate(
            flops=2 * tokens * channels * wide,
            bytes_accessed=8 * tokens * channels + 2 * tokens * wide + 2 * channels * wide,
            transcendentals=0,
        ),
        name="attn_grads",
    )(pos, queries, outputs, gain, out_grad, mine, other)


NT, NN, TN = ((1,), (1,)), ((1,), (0,)), ((0,), (0,))


def query_grad_kernel(q_ref, k_ref, v_ref, ag_ref, s_ref, *refs):
    qg_ref, kg_ref, end_ref = refs[-3:]
    end_ref[...] = jnp.zeros_like(end_ref)
    half = q_ref.shape[0] // 2
    top, low = slice(0, half), slice(half, 2 * half)
    for i in range(s_ref.shape[0]):
        q, k, v, ag = head(q_ref, i), head(k_ref, i), head(v_ref, i), head(ag_ref, i)
        here = slice(i * HEAD_DIM, (i + 1) * HEAD_DIM)
        from_state = dot(ag, s_ref[i], NT)
        g00 = lower(dot(ag[top], v[top], NT))
        g10 = dot(ag[low], v[top], NT).astype(BF16)
        g11 = lower(dot(ag[low], v[low], NT))
        qg_ref[top, here] = (dot(g00, k[top], NN) + from_state[top]).astype(BF16)
        qg_ref[low, here] = (dot(g10, k[top], NN) + dot(g11, k[low], NN) + from_state[low]).astype(BF16)
        kg_ref[top, here] = dot(g00, q[top], TN) + dot(g10, q[low], TN)
        kg_ref[low, here] = dot(g11, q[low], TN)


def query_grads(queries, keys, values, attn_grad, state, pair, after=()):
    tokens, channels = queries.shape
    spec = pl.BlockSpec((tokens, pair * HEAD_DIM), lambda b: (0, b))
    return pl.pallas_call(
        query_grad_kernel,
        grid=(channels // (pair * HEAD_DIM),),
        in_specs=[spec] * 4
        + [pl.BlockSpec((pair, HEAD_DIM, HEAD_DIM), lambda b: (b, 0, 0))]
        + [pl.BlockSpec(memory_space=pl.ANY)] * len(after),
        out_specs=[spec, spec, pl.BlockSpec(END, lambda b: (0, 0))],
        out_shape=[jax.ShapeDtypeStruct((tokens, channels), t) for t in (BF16, F32)]
        + [jax.ShapeDtypeStruct(END, F32)],
        compiler_params=params(56),
        cost_estimate=pl.CostEstimate(
            flops=6 * tokens * tokens * channels, bytes_accessed=14 * tokens * channels, transcendentals=0
        ),
        name="query_grads",
    )(queries, keys, values, attn_grad, state, *after)


def key_value_grad_kernel(q_ref, k_ref, v_ref, ag_ref, r_ref, kin_ref, *refs):
    kg_ref, vg_ref = refs[-2:]
    half = q_ref.shape[0] // 2
    top, low = slice(0, half), slice(half, 2 * half)
    for i in range(r_ref.shape[0]):
        q, k, v, ag = head(q_ref, i), head(k_ref, i), head(v_ref, i), head(ag_ref, i)
        here = slice(i * HEAD_DIM, (i + 1) * HEAD_DIM)
        rev = r_ref[i]
        kg_ref[:, here] = (head(kin_ref, i) + dot(v, rev, NT)).astype(BF16)
        a00 = lower(dot(q[top], k[top], NT))
        a10 = dot(q[low], k[top], NT).astype(BF16)
        a11 = lower(dot(q[low], k[low], NT))
        from_rev = dot(k, rev, NN)
        vg_ref[top, here] = (dot(a00, ag[top], TN) + dot(a10, ag[low], TN) + from_rev[top]).astype(BF16)
        vg_ref[low, here] = (dot(a11, ag[low], TN) + from_rev[low]).astype(BF16)


def key_value_grads(queries, keys, values, attn_grad, rev, key_in, pair, after=()):
    tokens, channels = keys.shape
    spec = pl.BlockSpec((tokens, pair * HEAD_DIM), lambda b: (0, b))
    return pl.pallas_call(
        key_value_grad_kernel,
        grid=(channels // (pair * HEAD_DIM),),
        in_specs=[spec] * 4
        + [pl.BlockSpec((pair, HEAD_DIM, HEAD_DIM), lambda b: (b, 0, 0)), spec]
        + [pl.BlockSpec(memory_space=pl.ANY)] * len(after),
        out_specs=[spec] * 2,
        out_shape=[jax.ShapeDtypeStruct((tokens, channels), BF16)] * 2,
        compiler_params=params(56),
        cost_estimate=pl.CostEstimate(
            flops=5 * tokens * tokens * channels, bytes_accessed=16 * tokens * channels, transcendentals=0
        ),
        name="key_value_grads",
    )(queries, keys, values, attn_grad, rev, key_in, *after)


def running_kernel(reverse, after, x_ref, *refs):
    refs = refs[after:]
    o_ref = refs[-1]
    count, rows = x_ref.shape[:2]
    total = jnp.zeros(x_ref.shape[1:], F32)
    for place in range(count)[:: -1 if reverse else 1]:
        o_ref[place, :rows] = total.astype(BF16)
        total = total + x_ref[place].astype(F32)
    if len(refs) > 1:
        parts = in_parts(refs[0][...])
        width = x_ref.shape[-1]
        extra = [part[:, i : i + width] for part in parts for i in range(0, part.shape[1], width)]
        extra = extra + [jnp.zeros((1, width), F32)] * (o_ref.shape[1] - rows - len(extra))
        extra = jnp.concatenate(extra, axis=0).astype(BF16)
        for place in range(count):
            o_ref[place, rows:] = extra


def in_parts(x):
    high = x.astype(BF16).astype(F32)
    middle = (x - high).astype(BF16).astype(F32)
    return high, middle, (x - high - middle).astype(BF16).astype(F32)


def running(rows, reverse, row=None, after=()):
    count, height, width = rows.shape
    more = 0 if row is None else -(-3 * row.shape[1] // width // 16) * 16
    args = [rows, *after] + ([] if row is None else [row])
    return pl.pallas_call(
        functools.partial(running_kernel, reverse, len(after)),
        in_specs=[pl.BlockSpec()]
        + [pl.BlockSpec(memory_space=pl.ANY)] * len(after)
        + ([] if row is None else [pl.BlockSpec()]),
        out_shape=jax.ShapeDtypeStruct((count, height + more, width), BF16),
        compiler_params=pltpu.CompilerParams(vmem_limit_bytes=8 * MIB),
        name="running_sums",
    )(*args)


def row_total(arrived, height, channels):
    count, _, width = arrived.shape
    parts = arrived[:, height : height + 3 * channels // width].astype(F32)
    return jnp.sum(parts.reshape(count, 3, channels // width, width), axis=(0, 1)).reshape(channels)


ALL = ("y", "core", "z", "x")
SEQ = ("z", "x")
PLANE = ("y", "x")


def exchange(x, axis):
    rows = x.reshape((lax.axis_size(axis), -1) + x.shape[-1:])
    return lax.all_to_all(rows, axis, 0, 0, tiled=True)


def everyones(x, axis):
    return lax.all_to_all(jnp.broadcast_to(x[None], (lax.axis_size(axis),) + x.shape), axis, 0, 0, tiled=True)


def flipped(x, axis, bit=1):
    return lax.ppermute(x, axis, [(i, i ^ bit) for i in range(lax.axis_size(axis))])


def added(*terms):
    total = terms[0].astype(F32)
    for term in terms[1:]:
        total = total + term.astype(F32)
    return total


def together(*xs):
    return lax.optimization_barrier(xs)


def small_call(kernel, out_shapes, *args, after=(), mib=56):
    def call(*refs):
        kernel(*refs[: len(args)], *refs[len(args) + len(after) :])

    return pl.pallas_call(
        call,
        in_specs=[pl.BlockSpec()] * len(args)
        + [pl.BlockSpec(memory_space=pl.ANY)] * len(after),
        out_shape=[jax.ShapeDtypeStruct(shape, F32 if shape == END else BF16) for shape in out_shapes],
        compiler_params=pltpu.CompilerParams(vmem_limit_bytes=mib * MIB),
        cost_estimate=pl.CostEstimate(
            flops=0, bytes_accessed=4 * sum(x.size for x in args), transcendentals=0
        ),
        name=kernel.__name__,
    )(*args, *after)


def one(i):
    return pl.ds(i, 1)


def place(axis, bit=1):
    here = (lax.axis_index(axis) // bit) % 2
    return here, 1 - here


def merge_all(own_ref, x_ref, y_ref, low_ref, high_ref, out_ref):
    y, other_y = place("y")
    x, other_x = place("x")
    half = low_ref.shape[0]
    out_ref[one(y), :, one(x)] = own_ref[...][None, :, None]
    out_ref[one(y), :, one(other_x)] = x_ref[...][None, :, None]
    out_ref[one(other_y), :, one(x)] = y_ref[...][None, :, None]
    out_ref[one(other_y), :half, one(other_x)] = low_ref[...][None, :, None]
    out_ref[one(other_y), half:, one(other_x)] = high_ref[...][None, :, None]


def cut_kernel(x_ref, y_ref, low_ref, high_ref):
    low_ref[...] = x_ref[...]
    high_ref[...] = y_ref[...]


def cut(x_got, y_got):
    half = (x_got.shape[0] // 2,) + x_got.shape[1:]
    return pl.pallas_call(
        cut_kernel,
        grid=(1,),
        in_specs=[pl.BlockSpec(half, lambda i: (0, 0, 0)), pl.BlockSpec(half, lambda i: (1, 0, 0))],
        out_specs=[pl.BlockSpec(half, lambda i: (0, 0, 0))] * 2,
        out_shape=[jax.ShapeDtypeStruct(half, BF16)] * 2,
        compiler_params=params(20),
        name="cut",
    )(x_got, y_got)


def total(a_ref, b_ref, *index):
    return (a_ref[index].astype(F32) + b_ref[index].astype(F32)).astype(BF16)


def split_first(keep_ref, got_ref, left_ref, right_ref, left_keep_ref, right_keep_ref):
    half = left_ref.shape[-1]
    here, there = place("y")
    every = slice(None)
    for at, ref in ((there, left_ref), (here, left_keep_ref)):
        ref[...] = total(keep_ref, got_ref, one(at), every, every, every, slice(0, half))[0]
    here, there = place("x")
    for at, ref in ((there, right_ref), (here, right_keep_ref)):
        ref[...] = total(keep_ref, got_ref, every, every, one(at), every, slice(half, 2 * half))[:, :, 0]


def split_second(
    left_ref, left_got_ref, right_ref, right_got_ref, left_out, right_out, left_keep, right_keep
):
    here, there = place("x")
    for at, ref in ((there, left_out), (here, left_keep)):
        ref[...] = total(left_ref, left_got_ref, slice(None), one(at))[:, 0]
    here, there = place("y")
    for at, ref in ((there, right_out), (here, right_keep)):
        ref[...] = total(right_ref, right_got_ref, one(at))[0]


def join_sides(left_ref, left_got_ref, right_ref, right_got_ref, send_ref, keep_ref, end_ref):
    here, there = place("z")
    half = left_ref.shape[-1]
    for far in range(send_ref.shape[0]):
        for at, ref in ((there, send_ref), (here, keep_ref)):
            ref[far, :, :half] = total(left_ref, left_got_ref, one(2 * far + at))[0]
            ref[far, :, half:] = total(right_ref, right_got_ref, one(2 * far + at))[0]
    end_ref[...] = jnp.zeros_like(end_ref)


def split_far(keep_ref, got_ref, send_ref, rest_ref, end_ref):
    here, there = place("z", 2)
    send_ref[...] = total(keep_ref, got_ref, one(there))[0]
    rest_ref[...] = total(keep_ref, got_ref, one(here))[0]
    end_ref[...] = jnp.zeros_like(end_ref)


def by_halves(sizes, rows, q, k, v, og, out_weight, gain_row, pos, pair):
    tokens, channels = q.shape
    wide = out_weight.shape[1]
    y, z, x, half = sizes["y"], sizes["z"], sizes["x"], wide // 2

    own = everyones(out_weight, "z")
    kv = key_value_sums(k, v, pair)
    kv, own = together(kv, own)
    x_got, y_got = flipped(own, "x"), flipped(own, "y")
    sent = exchange(kv, SEQ)
    intra, end = intra_outputs(q, k, v, pair)
    sent, x_got, y_got = together(sent, x_got, y_got)
    low, high = cut(x_got, y_got)
    low, high = flipped(low, "y"), flipped(high, "x")
    state = exchange(running(sent, False, after=(end,)), SEQ).reshape(kv.shape)
    outputs, send, og = weight_parts(pos, 1, q, state, intra, gain_row, og, pair)
    send, low, high = together(send, low, high)
    got = flipped(send, "core")
    (mine,) = small_call(merge_all, [(y, z, x, rows, wide)], own, x_got, y_got, low, high, mib=20)
    mine = mine.reshape(y, -1, wide)
    other = flipped(mine, "core")
    outputs, keep = weight_parts(pos, 0, q, state, intra, gain_row, og, pair, (outputs,))

    split = (y, z, x, rows, wide)
    left, right, left_keep, right_keep = small_call(
        split_first,
        [(z, x, rows, half), (y, z, rows, half)] * 2,
        keep.reshape(split),
        got.reshape(split),
        mib=20,
    )
    outputs, left, right = together(outputs, left, right)
    left_got, right_got = flipped(left, "y"), flipped(right, "x")
    attn_grad, gain_part, qg = attn_grads(pos, q, outputs, gain_row, og, mine, other, pair)
    gain_part, left_got, right_got = together(gain_part, left_got, right_got)

    sent = exchange(qg, SEQ)
    gain_part = gain_part + flipped(gain_part, "core")
    left, right, left_keep, right_keep = small_call(
        split_second, [(z, rows, half)] * 4, left_keep, left_got, right_keep, right_got
    )
    left_got, right_got = flipped(left, "x"), flipped(right, "y")
    send, keep, end = small_call(
        join_sides, [(2, rows, wide)] * 2 + [END], left_keep, left_got, right_keep, right_got
    )
    got = flipped(send, "z", 1)
    sums = running(sent, True, gain_part, after=(end,))
    arrived = exchange(sums, SEQ)
    query_g, key_in, end = query_grads(q, k, v, attn_grad, state, pair, after=(sums,))
    end, got, arrived = together(end, got, arrived)
    send, keep, end = small_call(split_far, [(rows, wide)] * 2 + [END], keep, got, after=(end,))
    got = flipped(send, "z", 2)
    key_g, value_g = key_value_grads(q, k, v, attn_grad, arrived, key_in, pair, after=(end,))
    gain_sum = row_total(arrived, sent.shape[1], channels)
    return query_g, key_g, value_g, (keep, got), gain_sum + flipped(gain_sum, "y")


def by_planes(sizes, rows, q, k, v, og, out_weight, gain_row, pos, pair):
    tokens, channels = q.shape
    wide = out_weight.shape[1]
    y, z, x = sizes["y"], sizes["z"], sizes["x"]
    weight = lax.all_gather(out_weight, ALL, axis=0, tiled=True)
    kv = key_value_sums(k, v, pair)
    intra, _ = intra_outputs(q, k, v, pair)
    state = exchange(running(exchange(kv, SEQ), False), SEQ).reshape(kv.shape)
    outputs, send, og = weight_parts(pos, 1, q, state, intra, gain_row, og, pair)
    outputs, keep = weight_parts(pos, 0, q, state, intra, gain_row, og, pair, (outputs,))
    part = added(keep, flipped(send, "core")).astype(BF16)
    part = part.reshape(y, z, x, rows, wide).transpose(0, 2, 1, 3, 4).reshape(y * x, z, rows, wide)
    part = lax.all_to_all(part, PLANE, 0, 0, tiled=True)
    part = added(*[part[i] for i in range(y * x)]).astype(BF16)
    part = lax.all_to_all(part, "z", 0, 0, tiled=True)
    weight = weight.reshape(y, 2, z * x * rows, wide)
    mine, other = [
        lax.dynamic_index_in_dim(weight, i, 1, keepdims=False) for i in place("core")
    ]
    attn_grad, gain_part, qg = attn_grads(pos, q, outputs, gain_row, og, mine, other, pair)
    rev = exchange(running(exchange(qg, SEQ), True), SEQ).reshape(kv.shape)
    query_g, key_in, _ = query_grads(q, k, v, attn_grad, state, pair)
    key_g, value_g = key_value_grads(q, k, v, attn_grad, rev, key_in, pair)
    gain_sum = jnp.sum(everyones(gain_part.reshape(channels), ALL), axis=0)
    return query_g, key_g, value_g, [part[i] for i in range(z)], gain_sum


def shards(queries, keys, values, out_grad, out_weight, gain):
    tokens, channels = queries.shape[1:]
    assert tokens == BLOCK
    sizes = {name: lax.axis_size(name) for name in ALL}
    devices = lax.axis_size(ALL)
    rows = out_weight.shape[0]
    pair = channels // (sizes["y"] * sizes["core"]) // HEAD_DIM
    pos = lax.axis_index(("y", "core")).reshape(1).astype(jnp.int32)
    halves = (sizes["y"], sizes["z"], sizes["x"]) == (2, 4, 2) and rows % 16 == 0
    query_g, key_g, value_g, parts, gain_sum = (by_halves if halves else by_planes)(
        sizes,
        rows,
        queries[0],
        keys[0],
        values[0],
        out_grad[0],
        out_weight,
        gain.reshape(1, channels),
        pos,
        pair,
    )
    factor = 1.0 / jnp.sqrt(jnp.float32(tokens * devices))
    out_shape = (1, tokens, channels)
    return (
        query_g.reshape(out_shape),
        key_g.reshape(out_shape),
        value_g.reshape(out_shape),
        added(*parts) * factor,
        gain_sum * factor,
    )


def solution(mesh):
    dp_count, seq_count = mesh.shape["dp"], mesh.shape["seq"]
    finer = Mesh(mesh.devices.reshape(dp_count // 2, 2, seq_count // 2, 2), ALL)
    tokens = P(("y", "core"), ("z", "x"), None)
    rows = P(ALL, None)
    return jax.shard_map(
        shards,
        mesh=finer,
        in_specs=(tokens, tokens, tokens, tokens, rows, P()),
        out_specs=(tokens, tokens, tokens, rows, P()),
        check_vma=False,
    )
```

```python
import functools

import jax
import jax.numpy as jnp
from jax import lax
from jax.experimental import pallas as pl
from jax.experimental.pallas import tpu as pltpu
from jax.sharding import Mesh
from jax.sharding import PartitionSpec as P

HEAD_DIM = 128
BLOCK = 512
MIB = 1 << 20

norm_eps = 1e-06

END = (8, 128)

F32 = jnp.float32
BF16 = jnp.bfloat16


def dot(a, b, contract):
    return lax.dot_general(a, b, (contract, ((), ())), preferred_element_type=F32)


def params(mib, dims=1):
    return pltpu.CompilerParams(
        vmem_limit_bytes=mib * MIB, dimension_semantics=("arbitrary",) * dims
    )


ROW_BLOCKS = 4


def row_blocks(tokens, wide):
    return [
        pl.BlockSpec((tokens // ROW_BLOCKS, wide), lambda y, p, r=r: (r, 0)) for r in range(ROW_BLOCKS)
    ]


def head(ref, i):
    return ref[:, i * HEAD_DIM : (i + 1) * HEAD_DIM]


def kv_kernel(k_ref, v_ref, o_ref):
    for i in range(o_ref.shape[0]):
        o_ref[i] = dot(head(k_ref, i), head(v_ref, i), ((0,), (0,))).astype(BF16)


def key_value_sums(keys, values, pair):
    tokens, channels = keys.shape
    width = pair * HEAD_DIM
    heads = channels // HEAD_DIM
    spec = pl.BlockSpec((tokens, width), lambda b: (0, b))
    return pl.pallas_call(
        kv_kernel,
        grid=(heads // pair,),
        in_specs=[spec, spec],
        out_specs=pl.BlockSpec((pair, HEAD_DIM, HEAD_DIM), lambda b: (b, 0, 0)),
        out_shape=jax.ShapeDtypeStruct((heads, HEAD_DIM, HEAD_DIM), BF16),
        compiler_params=params(56),
        cost_estimate=pl.CostEstimate(
            flops=2 * tokens * channels * HEAD_DIM, bytes_accessed=4 * tokens * channels, transcendentals=0
        ),
        name="key_value_sums",
    )(keys, values)


def lower(x):
    rows = lax.broadcasted_iota(jnp.int32, x.shape, 0)
    cols = lax.broadcasted_iota(jnp.int32, x.shape, 1)
    return jnp.where(cols <= rows, x, 0.0).astype(BF16)


def intra_kernel(q_ref, k_ref, v_ref, o_ref, end_ref):
    end_ref[...] = jnp.zeros_like(end_ref)
    half = q_ref.shape[0] // 2
    for i in range(o_ref.shape[1] // HEAD_DIM):
        q, k, v = head(q_ref, i), head(k_ref, i), head(v_ref, i)
        here = slice(i * HEAD_DIM, (i + 1) * HEAD_DIM)
        top = lower(dot(q[:half], k[:half], ((1,), (1,))))
        o_ref[:half, here] = dot(top, v[:half], ((1,), (0,)))
        left = dot(q[half:], k[:half], ((1,), (1,))).astype(BF16)
        right = lower(dot(q[half:], k[half:], ((1,), (1,))))
        low = dot(left, v[:half], ((1,), (0,))) + dot(right, v[half:], ((1,), (0,)))
        o_ref[half:, here] = low


def intra_outputs(queries, keys, values, pair):
    tokens, channels = keys.shape
    spec = pl.BlockSpec((tokens, pair * HEAD_DIM), lambda b: (0, b))
    return pl.pallas_call(
        intra_kernel,
        grid=(channels // (pair * HEAD_DIM),),
        in_specs=[spec] * 3,
        out_specs=[spec, pl.BlockSpec(END, lambda b: (0, 0))],
        out_shape=[jax.ShapeDtypeStruct((tokens, channels), F32), pltpu.HBM(END, F32)],
        compiler_params=params(56),
        cost_estimate=pl.CostEstimate(
            flops=4 * tokens * tokens * channels, bytes_accessed=10 * tokens * channels, transcendentals=0
        ),
        name="intra_outputs",
    )(queries, keys, values)


def rms_inverse(x):
    return lax.rsqrt(jnp.mean(x * x, axis=-1, keepdims=True) + norm_eps)


def unit_kernel(begun, pos_ref, q_ref, s_ref, intra_ref, gain_ref, *refs):
    if begun:
        og_ref, _, out_ref, part_ref = refs
    else:
        *og_refs, out_ref, part_ref, og_ref = refs

        @pl.when(pl.program_id(0) == 0)
        def _():
            start = 0
            for ref in og_refs:
                og_ref[start : start + ref.shape[0]] = ref[...]
                start = start + ref.shape[0]

    units = []
    for i in range(s_ref.shape[0]):
        x = head(intra_ref, i) + dot(head(q_ref, i), s_ref[i], ((1,), (0,)))
        out_ref[:, i * HEAD_DIM : (i + 1) * HEAD_DIM] = x
        units.append((x * rms_inverse(x) * head(gain_ref, i)).astype(BF16))
    unit = jnp.concatenate(units, axis=1) if len(units) > 1 else units[0]
    part_ref[0] = dot(unit, og_ref[...], ((0,), (0,))).astype(BF16)


def weight_parts(pos, side, queries, state, intra, gain, out_grad, pair, begun=()):
    tokens, channels = queries.shape
    width = pair * HEAD_DIM
    count = channels // width // 2
    wide = out_grad.shape[1]

    def block(y, pos_ref):
        return 2 * y + lax.rem(pos_ref[0] + side, 2)

    cols = pl.BlockSpec((tokens, width), lambda y, p: (0, block(y, p)))
    whole = pl.BlockSpec((tokens, wide), lambda y, p: (0, 0))
    more = [] if begun else [(whole, jax.ShapeDtypeStruct((tokens, wide), BF16))]
    return pl.pallas_call(
        functools.partial(unit_kernel, len(begun)),
        grid_spec=pltpu.PrefetchScalarGridSpec(
            num_scalar_prefetch=1,
            grid=(count,),
            in_specs=[
                cols,
                pl.BlockSpec((pair, HEAD_DIM, HEAD_DIM), lambda y, p: (block(y, p), 0, 0)),
                cols,
                pl.BlockSpec((1, width), lambda y, p: (0, block(y, p))),
            ]
            + ([whole, pl.BlockSpec(memory_space=pl.ANY)] if begun else row_blocks(tokens, wide)),
            out_specs=[cols, pl.BlockSpec((1, width, wide), lambda y, p: (y, 0, 0))] + [m[0] for m in more],
        ),
        out_shape=[
            jax.ShapeDtypeStruct((tokens, channels), F32),
            jax.ShapeDtypeStruct((count, width, wide), BF16),
        ]
        + [m[1] for m in more],
        input_output_aliases={6: 0} if begun else {},
        compiler_params=params(30 if begun else 44),
        cost_estimate=pl.CostEstimate(
            flops=tokens * channels * wide,
            bytes_accessed=5 * tokens * channels + 2 * tokens * wide + channels * wide,
            transcendentals=0,
        ),
        name="weight_parts",
    )(pos, queries, state, intra, gain, *[out_grad] * (1 if begun else ROW_BLOCKS), *begun)


def attn_grad_kernel(pos_ref, q_ref, o_ref, gain_ref, og_ref, mine_ref, other_ref, ag_ref, gg_ref, qg_ref, ug_ref):
    count = pl.num_programs(0) // 2

    @pl.when(pl.program_id(0) < count)
    def _():
        ug_ref[...] = dot(og_ref[...], mine_ref[0], ((1,), (1,)))

    @pl.when(pl.program_id(0) >= count)
    def _():
        ug_ref[...] = dot(og_ref[...], other_ref[0], ((1,), (1,)))

    for i in range(qg_ref.shape[0]):
        here = slice(i * HEAD_DIM, (i + 1) * HEAD_DIM)
        x = head(o_ref, i)
        inverse = rms_inverse(x)
        normed = x * inverse
        ug = head(ug_ref, i)
        gg_ref[:, here] = jnp.sum(ug * normed, axis=0, keepdims=True)
        scaled = ug * head(gain_ref, i)
        middle = jnp.mean(scaled * normed, axis=-1, keepdims=True)
        ag = ((scaled - normed * middle) * inverse).astype(BF16)
        ag_ref[:, here] = ag
        qg_ref[i] = dot(head(q_ref, i), ag, ((0,), (0,))).astype(BF16)


def attn_grads(pos, queries, outputs, gain, out_grad, mine, other, pair):
    tokens, channels = queries.shape
    width = pair * HEAD_DIM
    count = channels // width // 2
    wide = out_grad.shape[1]
    heads = channels // HEAD_DIM

    def block(s, pos_ref):
        return 2 * lax.rem(s, count) + lax.rem(pos_ref[0] + s // count, 2)

    cols = pl.BlockSpec((tokens, width), lambda s, p: (0, block(s, p)))
    row = pl.BlockSpec((1, width), lambda s, p: (0, block(s, p)))
    states = pl.BlockSpec((pair, HEAD_DIM, HEAD_DIM), lambda s, p: (block(s, p), 0, 0))
    piece = (1,) + mine.shape[1:]
    return pl.pallas_call(
        attn_grad_kernel,
        grid_spec=pltpu.PrefetchScalarGridSpec(
            num_scalar_prefetch=1,
            grid=(2 * count,),
            in_specs=[
                cols,
                cols,
                row,
                pl.BlockSpec((tokens, wide), lambda s, p: (0, 0)),
                pl.BlockSpec(piece, lambda s, p: (jnp.minimum(s, count - 1), 0, 0)),
                pl.BlockSpec(piece, lambda s, p: (jnp.maximum(s - count, 0), 0, 0)),
            ],
            out_specs=[cols, row, states],
            scratch_shapes=[pltpu.VMEM((tokens, width), F32)],
        ),
        out_shape=[
            pltpu.HBM((tokens, channels), BF16),
            jax.ShapeDtypeStruct((1, channels), F32),
            pltpu.HBM((heads, HEAD_DIM, HEAD_DIM), BF16),
        ],
        compiler_params=params(30),
        cost_estimate=pl.CostEstimate(
            flops=2 * tokens * channels * wide,
            bytes_accessed=8 * tokens * channels + 2 * tokens * wide + 2 * channels * wide,
            transcendentals=0,
        ),
        name="attn_grads",
    )(pos, queries, outputs, gain, out_grad, mine, other)


NT, NN, TN = ((1,), (1,)), ((1,), (0,)), ((0,), (0,))


def query_grad_kernel(q_ref, k_ref, v_ref, ag_ref, s_ref, *refs):
    qg_ref, kg_ref, end_ref = refs[-3:]
    end_ref[...] = jnp.zeros_like(end_ref)
    half = q_ref.shape[0] // 2
    top, low = slice(0, half), slice(half, 2 * half)
    for i in range(s_ref.shape[0]):
        q, k, v, ag = head(q_ref, i), head(k_ref, i), head(v_ref, i), head(ag_ref, i)
        here = slice(i * HEAD_DIM, (i + 1) * HEAD_DIM)
        from_state = dot(ag, s_ref[i], NT)
        g00 = lower(dot(ag[top], v[top], NT))
        g10 = dot(ag[low], v[top], NT).astype(BF16)
        g11 = lower(dot(ag[low], v[low], NT))
        qg_ref[top, here] = (dot(g00, k[top], NN) + from_state[top]).astype(BF16)
        qg_ref[low, here] = (dot(g10, k[top], NN) + dot(g11, k[low], NN) + from_state[low]).astype(BF16)
        kg_ref[top, here] = (dot(g00, q[top], TN) + dot(g10, q[low], TN)).astype(BF16)
        kg_ref[low, here] = dot(g11, q[low], TN).astype(BF16)


def query_grads(queries, keys, values, attn_grad, state, pair, after=()):
    tokens, channels = queries.shape
    spec = pl.BlockSpec((tokens, pair * HEAD_DIM), lambda b: (0, b))
    return pl.pallas_call(
        query_grad_kernel,
        grid=(channels // (pair * HEAD_DIM),),
        in_specs=[spec] * 4
        + [pl.BlockSpec((pair, HEAD_DIM, HEAD_DIM), lambda b: (b, 0, 0))]
        + [pl.BlockSpec(memory_space=pl.ANY)] * len(after),
        out_specs=[spec, spec, pl.BlockSpec(END, lambda b: (0, 0))],
        out_shape=[jax.ShapeDtypeStruct((tokens, channels), BF16)] * 2 + [pltpu.HBM(END, F32)],
        compiler_params=params(56),
        cost_estimate=pl.CostEstimate(
            flops=6 * tokens * tokens * channels, bytes_accessed=14 * tokens * channels, transcendentals=0
        ),
        name="query_grads",
    )(queries, keys, values, attn_grad, state, *after)


def value_grad_kernel(q_ref, k_ref, ag_ref, *refs):
    vg_ref, end_ref = refs[-2:]
    end_ref[...] = jnp.zeros_like(end_ref)
    half = q_ref.shape[0] // 2
    top, low = slice(0, half), slice(half, 2 * half)
    for i in range(q_ref.shape[1] // HEAD_DIM):
        q, k, ag = head(q_ref, i), head(k_ref, i), head(ag_ref, i)
        here = slice(i * HEAD_DIM, (i + 1) * HEAD_DIM)
        a00 = lower(dot(q[top], k[top], NT))
        a10 = dot(q[low], k[top], NT).astype(BF16)
        a11 = lower(dot(q[low], k[low], NT))
        vg_ref[top, here] = (dot(a00, ag[top], TN) + dot(a10, ag[low], TN)).astype(BF16)
        vg_ref[low, here] = dot(a11, ag[low], TN).astype(BF16)


def value_grads(queries, keys, attn_grad, pair, after=()):
    tokens, channels = queries.shape
    spec = pl.BlockSpec((tokens, pair * HEAD_DIM), lambda b: (0, b))
    return pl.pallas_call(
        value_grad_kernel,
        grid=(channels // (pair * HEAD_DIM),),
        in_specs=[spec] * 3 + [pl.BlockSpec(memory_space=pl.ANY)] * len(after),
        out_specs=[spec, pl.BlockSpec(END, lambda b: (0, 0))],
        out_shape=[jax.ShapeDtypeStruct((tokens, channels), BF16), pltpu.HBM(END, F32)],
        compiler_params=params(56),
        cost_estimate=pl.CostEstimate(
            flops=4 * tokens * tokens * channels, bytes_accessed=8 * tokens * channels, transcendentals=0
        ),
        name="value_grads",
    )(queries, keys, attn_grad, *after)


def rev_grad_kernel(k_ref, v_ref, r_ref, kin_ref, vin_ref, *refs):
    kg_ref, vg_ref = refs[-2:]
    for i in range(r_ref.shape[0]):
        here = slice(i * HEAD_DIM, (i + 1) * HEAD_DIM)
        rev = r_ref[i]
        kg_ref[:, here] = (head(kin_ref, i).astype(F32) + dot(head(v_ref, i), rev, NT)).astype(BF16)
        vg_ref[:, here] = (head(vin_ref, i).astype(F32) + dot(head(k_ref, i), rev, NN)).astype(BF16)


def rev_grads(keys, values, rev, key_in, value_in, pair, after=()):
    tokens, channels = keys.shape
    spec = pl.BlockSpec((tokens, pair * HEAD_DIM), lambda b: (0, b))
    return pl.pallas_call(
        rev_grad_kernel,
        grid=(channels // (pair * HEAD_DIM),),
        in_specs=[spec] * 2
        + [pl.BlockSpec((pair, HEAD_DIM, HEAD_DIM), lambda b: (b, 0, 0)), spec, spec]
        + [pl.BlockSpec(memory_space=pl.ANY)] * len(after),
        out_specs=[spec] * 2,
        out_shape=[jax.ShapeDtypeStruct((tokens, channels), BF16)] * 2,
        compiler_params=params(56),
        cost_estimate=pl.CostEstimate(
            flops=4 * tokens * channels * HEAD_DIM, bytes_accessed=12 * tokens * channels, transcendentals=0
        ),
        name="rev_grads",
    )(keys, values, rev, key_in, value_in, *after)


def running_kernel(reverse, after, x_ref, *refs):
    refs = refs[after:]
    o_ref = refs[-1]
    count, rows = x_ref.shape[:2]
    total = jnp.zeros(x_ref.shape[1:], F32)
    for place in range(count)[:: -1 if reverse else 1]:
        o_ref[place, :rows] = total.astype(BF16)
        total = total + x_ref[place].astype(F32)
    if len(refs) > 1:
        parts = in_parts(refs[0][...])
        width = x_ref.shape[-1]
        extra = [part[:, i : i + width] for part in parts for i in range(0, part.shape[1], width)]
        extra = extra + [jnp.zeros((1, width), F32)] * (o_ref.shape[1] - rows - len(extra))
        extra = jnp.concatenate(extra, axis=0).astype(BF16)
        for place in range(count):
            o_ref[place, rows:] = extra


def in_parts(x):
    high = x.astype(BF16).astype(F32)
    middle = (x - high).astype(BF16).astype(F32)
    return high, middle, (x - high - middle).astype(BF16).astype(F32)


def running(rows, reverse, row=None, after=()):
    count, height, width = rows.shape
    more = 0 if row is None else -(-3 * row.shape[1] // width // 16) * 16
    args = [rows, *after] + ([] if row is None else [row])
    return pl.pallas_call(
        functools.partial(running_kernel, reverse, len(after)),
        in_specs=[pl.BlockSpec()]
        + [pl.BlockSpec(memory_space=pl.ANY)] * len(after)
        + ([] if row is None else [pl.BlockSpec()]),
        out_shape=pltpu.HBM((count, height + more, width), BF16),
        compiler_params=pltpu.CompilerParams(vmem_limit_bytes=8 * MIB),
        name="running_sums",
    )(*args)


def row_total(arrived, height, channels):
    count, _, width = arrived.shape
    parts = arrived[:, height : height + 3 * channels // width].astype(F32)
    return jnp.sum(parts.reshape(count, 3, channels // width, width), axis=(0, 1)).reshape(channels)


ALL = ("y", "core", "z", "x")
SEQ = ("z", "x")
PLANE = ("y", "x")


def exchange(x, axis):
    rows = x.reshape((lax.axis_size(axis), -1) + x.shape[-1:])
    return lax.all_to_all(rows, axis, 0, 0, tiled=True)


def everyones(x, axis):
    return lax.all_to_all(jnp.broadcast_to(x[None], (lax.axis_size(axis),) + x.shape), axis, 0, 0, tiled=True)


def flipped(x, axis, bit=1):
    return lax.ppermute(x, axis, [(i, i ^ bit) for i in range(lax.axis_size(axis))])


def added(*terms):
    total = terms[0].astype(F32)
    for term in terms[1:]:
        total = total + term.astype(F32)
    return total


def together(*xs):
    return lax.optimization_barrier(xs)


def small_call(kernel, out_shapes, *args, after=(), kept=(), mib=56):
    def call(*refs):
        kernel(*refs[: len(args)], *refs[len(args) + len(after) :])

    return pl.pallas_call(
        call,
        in_specs=[pl.BlockSpec()] * len(args)
        + [pl.BlockSpec(memory_space=pl.ANY)] * len(after),
        out_shape=[
            pltpu.HBM(shape, F32 if shape == END else BF16)
            if shape == END or at in kept
            else jax.ShapeDtypeStruct(shape, BF16)
            for at, shape in enumerate(out_shapes)
        ],
        compiler_params=pltpu.CompilerParams(vmem_limit_bytes=mib * MIB),
        cost_estimate=pl.CostEstimate(
            flops=0, bytes_accessed=4 * sum(x.size for x in args), transcendentals=0
        ),
        name=kernel.__name__,
    )(*args, *after)


def one(i):
    return pl.ds(i, 1)


def place(axis, bit=1):
    here = (lax.axis_index(axis) // bit) % 2
    return here, 1 - here


def merge_all(own_ref, x_ref, y_ref, low_ref, high_ref, out_ref):
    y, other_y = place("y")
    x, other_x = place("x")
    half = low_ref.shape[0]
    out_ref[one(y), :, one(x)] = own_ref[...][None, :, None]
    out_ref[one(y), :, one(other_x)] = x_ref[...][None, :, None]
    out_ref[one(other_y), :, one(x)] = y_ref[...][None, :, None]
    out_ref[one(other_y), :half, one(other_x)] = low_ref[...][None, :, None]
    out_ref[one(other_y), half:, one(other_x)] = high_ref[...][None, :, None]


def cut_kernel(x_ref, y_ref, low_ref, high_ref):
    low_ref[...] = x_ref[...]
    high_ref[...] = y_ref[...]


def cut(x_got, y_got):
    half = (x_got.shape[0] // 2,) + x_got.shape[1:]
    return pl.pallas_call(
        cut_kernel,
        grid=(1,),
        in_specs=[pl.BlockSpec(half, lambda i: (0, 0, 0)), pl.BlockSpec(half, lambda i: (1, 0, 0))],
        out_specs=[pl.BlockSpec(half, lambda i: (0, 0, 0))] * 2,
        out_shape=[jax.ShapeDtypeStruct(half, BF16)] * 2,
        compiler_params=params(20),
        name="cut",
    )(x_got, y_got)


def total(a_ref, b_ref, *index):
    return (a_ref[index].astype(F32) + b_ref[index].astype(F32)).astype(BF16)


def split_first(keep_ref, got_ref, left_ref, right_ref, left_keep_ref, right_keep_ref):
    half = left_ref.shape[-1]
    here, there = place("y")
    every = slice(None)
    for at, ref in ((there, left_ref), (here, left_keep_ref)):
        ref[...] = total(keep_ref, got_ref, one(at), every, every, every, slice(0, half))[0]
    here, there = place("x")
    for at, ref in ((there, right_ref), (here, right_keep_ref)):
        ref[...] = total(keep_ref, got_ref, every, every, one(at), every, slice(half, 2 * half))[:, :, 0]


def split_second(
    left_ref, left_got_ref, right_ref, right_got_ref, left_out, right_out, left_keep, right_keep, end_ref
):
    end_ref[...] = jnp.zeros_like(end_ref)
    here, there = place("x")
    for at, ref in ((there, left_out), (here, left_keep)):
        ref[...] = total(left_ref, left_got_ref, slice(None), one(at))[:, 0]
    here, there = place("y")
    for at, ref in ((there, right_out), (here, right_keep)):
        ref[...] = total(right_ref, right_got_ref, one(at))[0]


def join_sides(left_ref, left_got_ref, right_ref, right_got_ref, send_ref, keep_ref, end_ref):
    here, there = place("z")
    half = left_ref.shape[-1]
    for far in range(send_ref.shape[0]):
        for at, ref in ((there, send_ref), (here, keep_ref)):
            ref[far, :, :half] = total(left_ref, left_got_ref, one(2 * far + at))[0]
            ref[far, :, half:] = total(right_ref, right_got_ref, one(2 * far + at))[0]
    end_ref[...] = jnp.zeros_like(end_ref)


def split_far(keep_ref, got_ref, send_ref, rest_ref, end_ref):
    here, there = place("z", 2)
    send_ref[...] = total(keep_ref, got_ref, one(there))[0]
    rest_ref[...] = total(keep_ref, got_ref, one(here))[0]
    end_ref[...] = jnp.zeros_like(end_ref)


def repeat(x_ref, out_ref):
    for i in range(out_ref.shape[0]):
        out_ref[i] = x_ref[...]


def by_halves(sizes, rows, q, k, v, og, out_weight, gain_row, pos, pair):
    tokens, channels = q.shape
    wide = out_weight.shape[1]
    y, z, x, half = sizes["y"], sizes["z"], sizes["x"], wide // 2

    (own,) = small_call(repeat, [(z, rows, wide)], out_weight, kept=(0,))
    own = lax.all_to_all(own, "z", 0, 0, tiled=True)
    kv = key_value_sums(k, v, pair)
    kv, own = together(kv, own)
    x_got, y_got = flipped(own, "x"), flipped(own, "y")
    sent = exchange(kv, SEQ)
    intra, end = intra_outputs(q, k, v, pair)
    sent, x_got, y_got = together(sent, x_got, y_got)
    low, high = cut(x_got, y_got)
    low, high = flipped(low, "y"), flipped(high, "x")
    state = exchange(running(sent, False, after=(end,)), SEQ).reshape(kv.shape)
    outputs, send, og = weight_parts(pos, 1, q, state, intra, gain_row, og, pair)
    send, low, high = together(send, low, high)
    got = flipped(send, "core")
    (mine,) = small_call(merge_all, [(y, z, x, rows, wide)], own, x_got, y_got, low, high, mib=20)
    mine = mine.reshape(y, -1, wide)
    other = flipped(mine, "core")
    outputs, keep = weight_parts(pos, 0, q, state, intra, gain_row, og, pair, (outputs,))

    split = (y, z, x, rows, wide)
    left, right, left_keep, right_keep = small_call(
        split_first,
        [(z, x, rows, half), (y, z, rows, half)] * 2,
        keep.reshape(split),
        got.reshape(split),
        kept=(2, 3),
        mib=20,
    )
    outputs, left, right = together(outputs, left, right)
    left_got, right_got = flipped(left, "y"), flipped(right, "x")
    attn_grad, gain_part, qg = attn_grads(pos, q, outputs, gain_row, og, mine, other, pair)
    gain_part, left_got, right_got = together(gain_part, left_got, right_got)

    sent = exchange(qg, SEQ)
    gain_part = gain_part + flipped(gain_part, "core")
    left, right, left_keep, right_keep, end = small_call(
        split_second, [(z, rows, half)] * 4 + [END], left_keep, left_got, right_keep, right_got
    )
    left_got, right_got = flipped(left, "x"), flipped(right, "y")
    value_in, end = value_grads(q, k, attn_grad, pair, after=(end,))
    end, left_got, right_got = together(end, left_got, right_got)
    sums = running(sent, True, gain_part, after=(end,))
    arrived = exchange(sums, SEQ)
    send, keep, end = small_call(
        join_sides, [(2, rows, wide)] * 2 + [END], left_keep, left_got, right_keep, right_got, after=(sums,)
    )
    got = flipped(send, "z", 1)
    query_g, key_in, end = query_grads(q, k, v, attn_grad, state, pair, after=(end,))
    end, got, arrived = together(end, got, arrived)
    send, keep, end = small_call(split_far, [(rows, wide)] * 2 + [END], keep, got, after=(end,))
    got = flipped(send, "z", 2)
    key_g, value_g = rev_grads(k, v, arrived, key_in, value_in, pair, after=(end,))
    gain_sum = row_total(arrived, sent.shape[1], channels)
    return query_g, key_g, value_g, (keep, got), gain_sum + flipped(gain_sum, "y")


def by_planes(sizes, rows, q, k, v, og, out_weight, gain_row, pos, pair):
    tokens, channels = q.shape
    wide = out_weight.shape[1]
    y, z, x = sizes["y"], sizes["z"], sizes["x"]
    weight = lax.all_gather(out_weight, ALL, axis=0, tiled=True)
    kv = key_value_sums(k, v, pair)
    intra, _ = intra_outputs(q, k, v, pair)
    state = exchange(running(exchange(kv, SEQ), False), SEQ).reshape(kv.shape)
    outputs, send, og = weight_parts(pos, 1, q, state, intra, gain_row, og, pair)
    outputs, keep = weight_parts(pos, 0, q, state, intra, gain_row, og, pair, (outputs,))
    part = added(keep, flipped(send, "core")).astype(BF16)
    part = part.reshape(y, z, x, rows, wide).transpose(0, 2, 1, 3, 4).reshape(y * x, z, rows, wide)
    part = lax.all_to_all(part, PLANE, 0, 0, tiled=True)
    part = added(*[part[i] for i in range(y * x)]).astype(BF16)
    part = lax.all_to_all(part, "z", 0, 0, tiled=True)
    weight = weight.reshape(y, 2, z * x * rows, wide)
    mine, other = [
        lax.dynamic_index_in_dim(weight, i, 1, keepdims=False) for i in place("core")
    ]
    attn_grad, gain_part, qg = attn_grads(pos, q, outputs, gain_row, og, mine, other, pair)
    rev = exchange(running(exchange(qg, SEQ), True), SEQ).reshape(kv.shape)
    query_g, key_in, _ = query_grads(q, k, v, attn_grad, state, pair)
    value_in, _ = value_grads(q, k, attn_grad, pair)
    key_g, value_g = rev_grads(k, v, rev, key_in, value_in, pair)
    gain_sum = jnp.sum(everyones(gain_part.reshape(channels), ALL), axis=0)
    return query_g, key_g, value_g, [part[i] for i in range(z)], gain_sum


def shards(queries, keys, values, out_grad, out_weight, gain):
    tokens, channels = queries.shape[1:]
    assert tokens == BLOCK
    sizes = {name: lax.axis_size(name) for name in ALL}
    devices = lax.axis_size(ALL)
    rows = out_weight.shape[0]
    pair = channels // (sizes["y"] * sizes["core"]) // HEAD_DIM
    pos = lax.axis_index(("y", "core")).reshape(1).astype(jnp.int32)
    halves = (sizes["y"], sizes["z"], sizes["x"]) == (2, 4, 2) and rows % 16 == 0
    query_g, key_g, value_g, parts, gain_sum = (by_halves if halves else by_planes)(
        sizes,
        rows,
        queries[0],
        keys[0],
        values[0],
        out_grad[0],
        out_weight,
        gain.reshape(1, channels),
        pos,
        pair,
    )
    factor = 1.0 / jnp.sqrt(jnp.float32(tokens * devices))
    out_shape = (1, tokens, channels)
    return (
        query_g.reshape(out_shape),
        key_g.reshape(out_shape),
        value_g.reshape(out_shape),
        added(*parts) * factor,
        gain_sum * factor,
    )


def solution(mesh):
    dp_count, seq_count = mesh.shape["dp"], mesh.shape["seq"]
    finer = Mesh(mesh.devices.reshape(dp_count // 2, 2, seq_count // 2, 2), ALL)
    tokens = P(("y", "core"), ("z", "x"), None)
    rows = P(ALL, None)
    return jax.shard_map(
        shards,
        mesh=finer,
        in_specs=(tokens, tokens, tokens, tokens, rows, P()),
        out_specs=(tokens, tokens, tokens, rows, P()),
        check_vma=False,
    )
```

```python
import functools

import jax
import jax.numpy as jnp
from jax import lax
from jax.experimental import pallas as pl
from jax.experimental.pallas import tpu as pltpu
from jax.sharding import Mesh
from jax.sharding import PartitionSpec as P

HEAD_DIM = 128
BLOCK = 512
MIB = 1 << 20

norm_eps = 1e-06

END = (8, 128)

F32 = jnp.float32
BF16 = jnp.bfloat16


def dot(a, b, contract):
    return lax.dot_general(a, b, (contract, ((), ())), preferred_element_type=F32)


def params(mib, dims=1):
    return pltpu.CompilerParams(
        vmem_limit_bytes=mib * MIB, dimension_semantics=("arbitrary",) * dims
    )


ROW_BLOCKS = 4


def row_blocks(tokens, wide):
    return [
        pl.BlockSpec((tokens // ROW_BLOCKS, wide), lambda y, p, r=r: (r, 0)) for r in range(ROW_BLOCKS)
    ]


def head(ref, i):
    return ref[:, i * HEAD_DIM : (i + 1) * HEAD_DIM]


def kv_kernel(k_ref, v_ref, o_ref):
    for i in range(o_ref.shape[0]):
        o_ref[i] = dot(head(k_ref, i), head(v_ref, i), ((0,), (0,))).astype(BF16)


def key_value_sums(keys, values, pair):
    tokens, channels = keys.shape
    width = pair * HEAD_DIM
    heads = channels // HEAD_DIM
    spec = pl.BlockSpec((tokens, width), lambda b: (0, b))
    return pl.pallas_call(
        kv_kernel,
        grid=(heads // pair,),
        in_specs=[spec, spec],
        out_specs=pl.BlockSpec((pair, HEAD_DIM, HEAD_DIM), lambda b: (b, 0, 0)),
        out_shape=jax.ShapeDtypeStruct((heads, HEAD_DIM, HEAD_DIM), BF16),
        compiler_params=params(56),
        cost_estimate=pl.CostEstimate(
            flops=2 * tokens * channels * HEAD_DIM, bytes_accessed=4 * tokens * channels, transcendentals=0
        ),
        name="key_value_sums",
    )(keys, values)


def lower(x):
    rows = lax.broadcasted_iota(jnp.int32, x.shape, 0)
    cols = lax.broadcasted_iota(jnp.int32, x.shape, 1)
    return jnp.where(cols <= rows, x, 0.0).astype(BF16)


def intra_kernel(q_ref, k_ref, v_ref, o_ref, end_ref):
    end_ref[...] = jnp.zeros_like(end_ref)
    half = q_ref.shape[0] // 2
    for i in range(o_ref.shape[1] // HEAD_DIM):
        q, k, v = head(q_ref, i), head(k_ref, i), head(v_ref, i)
        here = slice(i * HEAD_DIM, (i + 1) * HEAD_DIM)
        top = lower(dot(q[:half], k[:half], ((1,), (1,))))
        o_ref[:half, here] = dot(top, v[:half], ((1,), (0,)))
        left = dot(q[half:], k[:half], ((1,), (1,))).astype(BF16)
        right = lower(dot(q[half:], k[half:], ((1,), (1,))))
        low = dot(left, v[:half], ((1,), (0,))) + dot(right, v[half:], ((1,), (0,)))
        o_ref[half:, here] = low


def intra_outputs(queries, keys, values, pair):
    tokens, channels = keys.shape
    spec = pl.BlockSpec((tokens, pair * HEAD_DIM), lambda b: (0, b))
    return pl.pallas_call(
        intra_kernel,
        grid=(channels // (pair * HEAD_DIM),),
        in_specs=[spec] * 3,
        out_specs=[spec, pl.BlockSpec(END, lambda b: (0, 0))],
        out_shape=[jax.ShapeDtypeStruct((tokens, channels), F32), pltpu.HBM(END, F32)],
        compiler_params=params(56),
        cost_estimate=pl.CostEstimate(
            flops=4 * tokens * tokens * channels, bytes_accessed=10 * tokens * channels, transcendentals=0
        ),
        name="intra_outputs",
    )(queries, keys, values)


def rms_inverse(x):
    return lax.rsqrt(jnp.mean(x * x, axis=-1, keepdims=True) + norm_eps)


def unit_kernel(begun, pos_ref, q_ref, s_ref, intra_ref, gain_ref, *refs):
    if begun:
        og_ref, _, out_ref, part_ref = refs
    else:
        *og_refs, out_ref, part_ref, og_ref = refs

        @pl.when(pl.program_id(0) == 0)
        def _():
            start = 0
            for ref in og_refs:
                og_ref[start : start + ref.shape[0]] = ref[...]
                start = start + ref.shape[0]

    units = []
    for i in range(s_ref.shape[0]):
        x = head(intra_ref, i) + dot(head(q_ref, i), s_ref[i], ((1,), (0,)))
        out_ref[:, i * HEAD_DIM : (i + 1) * HEAD_DIM] = x
        units.append((x * rms_inverse(x) * head(gain_ref, i)).astype(BF16))
    unit = jnp.concatenate(units, axis=1) if len(units) > 1 else units[0]
    part_ref[0] = dot(unit, og_ref[...], ((0,), (0,))).astype(BF16)


def weight_parts(pos, side, queries, state, intra, gain, out_grad, pair, begun=()):
    tokens, channels = queries.shape
    width = pair * HEAD_DIM
    count = channels // width // 2
    wide = out_grad.shape[1]

    def block(y, pos_ref):
        return 2 * y + lax.rem(pos_ref[0] + side, 2)

    cols = pl.BlockSpec((tokens, width), lambda y, p: (0, block(y, p)))
    whole = pl.BlockSpec((tokens, wide), lambda y, p: (0, 0))
    more = [] if begun else [(whole, jax.ShapeDtypeStruct((tokens, wide), BF16))]
    return pl.pallas_call(
        functools.partial(unit_kernel, len(begun)),
        grid_spec=pltpu.PrefetchScalarGridSpec(
            num_scalar_prefetch=1,
            grid=(count,),
            in_specs=[
                cols,
                pl.BlockSpec((pair, HEAD_DIM, HEAD_DIM), lambda y, p: (block(y, p), 0, 0)),
                cols,
                pl.BlockSpec((1, width), lambda y, p: (0, block(y, p))),
            ]
            + ([whole, pl.BlockSpec(memory_space=pl.ANY)] if begun else row_blocks(tokens, wide)),
            out_specs=[cols, pl.BlockSpec((1, width, wide), lambda y, p: (y, 0, 0))] + [m[0] for m in more],
        ),
        out_shape=[
            jax.ShapeDtypeStruct((tokens, channels), F32),
            jax.ShapeDtypeStruct((count, width, wide), BF16),
        ]
        + [m[1] for m in more],
        input_output_aliases={6: 0} if begun else {},
        compiler_params=params(30 if begun else 44),
        cost_estimate=pl.CostEstimate(
            flops=tokens * channels * wide,
            bytes_accessed=5 * tokens * channels + 2 * tokens * wide + channels * wide,
            transcendentals=0,
        ),
        name="weight_parts",
    )(pos, queries, state, intra, gain, *[out_grad] * (1 if begun else ROW_BLOCKS), *begun)


def attn_grad_kernel(pos_ref, q_ref, o_ref, gain_ref, og_ref, mine_ref, other_ref, ag_ref, gg_ref, qg_ref, ug_ref):
    count = pl.num_programs(0) // 2

    @pl.when(pl.program_id(0) < count)
    def _():
        ug_ref[...] = dot(og_ref[...], mine_ref[0], ((1,), (1,)))

    @pl.when(pl.program_id(0) >= count)
    def _():
        ug_ref[...] = dot(og_ref[...], other_ref[0], ((1,), (1,)))

    for i in range(qg_ref.shape[0]):
        here = slice(i * HEAD_DIM, (i + 1) * HEAD_DIM)
        x = head(o_ref, i)
        inverse = rms_inverse(x)
        normed = x * inverse
        ug = head(ug_ref, i)
        gg_ref[:, here] = jnp.sum(ug * normed, axis=0, keepdims=True)
        scaled = ug * head(gain_ref, i)
        middle = jnp.mean(scaled * normed, axis=-1, keepdims=True)
        ag = ((scaled - normed * middle) * inverse).astype(BF16)
        ag_ref[:, here] = ag
        qg_ref[i] = dot(head(q_ref, i), ag, ((0,), (0,))).astype(BF16)


def attn_grads(pos, queries, outputs, gain, out_grad, mine, other, pair):
    tokens, channels = queries.shape
    width = pair * HEAD_DIM
    count = channels // width // 2
    wide = out_grad.shape[1]
    heads = channels // HEAD_DIM

    def block(s, pos_ref):
        return 2 * lax.rem(s, count) + lax.rem(pos_ref[0] + s // count, 2)

    cols = pl.BlockSpec((tokens, width), lambda s, p: (0, block(s, p)))
    row = pl.BlockSpec((1, width), lambda s, p: (0, block(s, p)))
    states = pl.BlockSpec((pair, HEAD_DIM, HEAD_DIM), lambda s, p: (block(s, p), 0, 0))
    piece = (1,) + mine.shape[1:]
    return pl.pallas_call(
        attn_grad_kernel,
        grid_spec=pltpu.PrefetchScalarGridSpec(
            num_scalar_prefetch=1,
            grid=(2 * count,),
            in_specs=[
                cols,
                cols,
                row,
                pl.BlockSpec((tokens, wide), lambda s, p: (0, 0)),
                pl.BlockSpec(piece, lambda s, p: (jnp.minimum(s, count - 1), 0, 0)),
                pl.BlockSpec(piece, lambda s, p: (jnp.maximum(s - count, 0), 0, 0)),
            ],
            out_specs=[cols, row, states],
            scratch_shapes=[pltpu.VMEM((tokens, width), F32)],
        ),
        out_shape=[
            pltpu.HBM((tokens, channels), BF16),
            jax.ShapeDtypeStruct((1, channels), F32),
            pltpu.HBM((heads, HEAD_DIM, HEAD_DIM), BF16),
        ],
        compiler_params=params(30),
        cost_estimate=pl.CostEstimate(
            flops=2 * tokens * channels * wide,
            bytes_accessed=8 * tokens * channels + 2 * tokens * wide + 2 * channels * wide,
            transcendentals=0,
        ),
        name="attn_grads",
    )(pos, queries, outputs, gain, out_grad, mine, other)


NT, NN, TN = ((1,), (1,)), ((1,), (0,)), ((0,), (0,))


def query_grad_kernel(q_ref, k_ref, v_ref, ag_ref, s_ref, *refs):
    qg_ref, kg_ref, end_ref = refs[-3:]
    end_ref[...] = jnp.zeros_like(end_ref)
    half = q_ref.shape[0] // 2
    top, low = slice(0, half), slice(half, 2 * half)
    for i in range(s_ref.shape[0]):
        q, k, v, ag = head(q_ref, i), head(k_ref, i), head(v_ref, i), head(ag_ref, i)
        here = slice(i * HEAD_DIM, (i + 1) * HEAD_DIM)
        from_state = dot(ag, s_ref[i], NT)
        g00 = lower(dot(ag[top], v[top], NT))
        g10 = dot(ag[low], v[top], NT).astype(BF16)
        g11 = lower(dot(ag[low], v[low], NT))
        qg_ref[top, here] = (dot(g00, k[top], NN) + from_state[top]).astype(BF16)
        qg_ref[low, here] = (dot(g10, k[top], NN) + dot(g11, k[low], NN) + from_state[low]).astype(BF16)
        kg_ref[top, here] = (dot(g00, q[top], TN) + dot(g10, q[low], TN)).astype(BF16)
        kg_ref[low, here] = dot(g11, q[low], TN).astype(BF16)


def query_grads(queries, keys, values, attn_grad, state, pair, after=()):
    tokens, channels = queries.shape
    spec = pl.BlockSpec((tokens, pair * HEAD_DIM), lambda b: (0, b))
    return pl.pallas_call(
        query_grad_kernel,
        grid=(channels // (pair * HEAD_DIM),),
        in_specs=[spec] * 4
        + [pl.BlockSpec((pair, HEAD_DIM, HEAD_DIM), lambda b: (b, 0, 0))]
        + [pl.BlockSpec(memory_space=pl.ANY)] * len(after),
        out_specs=[spec, spec, pl.BlockSpec(END, lambda b: (0, 0))],
        out_shape=[jax.ShapeDtypeStruct((tokens, channels), BF16)] * 2 + [pltpu.HBM(END, F32)],
        compiler_params=params(56),
        cost_estimate=pl.CostEstimate(
            flops=6 * tokens * tokens * channels, bytes_accessed=14 * tokens * channels, transcendentals=0
        ),
        name="query_grads",
    )(queries, keys, values, attn_grad, state, *after)


def value_grad_kernel(q_ref, k_ref, ag_ref, *refs):
    vg_ref, end_ref = refs[-2:]
    end_ref[...] = jnp.zeros_like(end_ref)
    half = q_ref.shape[0] // 2
    top, low = slice(0, half), slice(half, 2 * half)
    for i in range(q_ref.shape[1] // HEAD_DIM):
        q, k, ag = head(q_ref, i), head(k_ref, i), head(ag_ref, i)
        here = slice(i * HEAD_DIM, (i + 1) * HEAD_DIM)
        a00 = lower(dot(q[top], k[top], NT))
        a10 = dot(q[low], k[top], NT).astype(BF16)
        a11 = lower(dot(q[low], k[low], NT))
        vg_ref[top, here] = (dot(a00, ag[top], TN) + dot(a10, ag[low], TN)).astype(BF16)
        vg_ref[low, here] = dot(a11, ag[low], TN).astype(BF16)


def value_grads(queries, keys, attn_grad, pair, after=()):
    tokens, channels = queries.shape
    spec = pl.BlockSpec((tokens, pair * HEAD_DIM), lambda b: (0, b))
    return pl.pallas_call(
        value_grad_kernel,
        grid=(channels // (pair * HEAD_DIM),),
        in_specs=[spec] * 3 + [pl.BlockSpec(memory_space=pl.ANY)] * len(after),
        out_specs=[spec, pl.BlockSpec(END, lambda b: (0, 0))],
        out_shape=[jax.ShapeDtypeStruct((tokens, channels), BF16), pltpu.HBM(END, F32)],
        compiler_params=params(56),
        cost_estimate=pl.CostEstimate(
            flops=4 * tokens * tokens * channels, bytes_accessed=8 * tokens * channels, transcendentals=0
        ),
        name="value_grads",
    )(queries, keys, attn_grad, *after)


def rev_grad_kernel(k_ref, v_ref, r_ref, kin_ref, vin_ref, *refs):
    kg_ref, vg_ref = refs[-2:]
    for i in range(r_ref.shape[0]):
        here = slice(i * HEAD_DIM, (i + 1) * HEAD_DIM)
        rev = r_ref[i]
        kg_ref[:, here] = (head(kin_ref, i).astype(F32) + dot(head(v_ref, i), rev, NT)).astype(BF16)
        vg_ref[:, here] = (head(vin_ref, i).astype(F32) + dot(head(k_ref, i), rev, NN)).astype(BF16)


def rev_grads(keys, values, rev, key_in, value_in, pair, after=()):
    tokens, channels = keys.shape
    spec = pl.BlockSpec((tokens, pair * HEAD_DIM), lambda b: (0, b))
    return pl.pallas_call(
        rev_grad_kernel,
        grid=(channels // (pair * HEAD_DIM),),
        in_specs=[spec] * 2
        + [pl.BlockSpec((pair, HEAD_DIM, HEAD_DIM), lambda b: (b, 0, 0)), spec, spec]
        + [pl.BlockSpec(memory_space=pl.ANY)] * len(after),
        out_specs=[spec] * 2,
        out_shape=[jax.ShapeDtypeStruct((tokens, channels), BF16)] * 2,
        compiler_params=params(56),
        cost_estimate=pl.CostEstimate(
            flops=4 * tokens * channels * HEAD_DIM, bytes_accessed=12 * tokens * channels, transcendentals=0
        ),
        name="rev_grads",
    )(keys, values, rev, key_in, value_in, *after)


def running_kernel(reverse, after, x_ref, *refs):
    refs = refs[after:]
    o_ref = refs[-1]
    count, rows = x_ref.shape[:2]
    total = jnp.zeros(x_ref.shape[1:], F32)
    for place in range(count)[:: -1 if reverse else 1]:
        o_ref[place, :rows] = total.astype(BF16)
        total = total + x_ref[place].astype(F32)
    if len(refs) > 1:
        parts = in_parts(refs[0][...])
        width = x_ref.shape[-1]
        extra = [part[:, i : i + width] for part in parts for i in range(0, part.shape[1], width)]
        extra = extra + [jnp.zeros((1, width), F32)] * (o_ref.shape[1] - rows - len(extra))
        extra = jnp.concatenate(extra, axis=0).astype(BF16)
        for place in range(count):
            o_ref[place, rows:] = extra


def in_parts(x):
    high = x.astype(BF16).astype(F32)
    middle = (x - high).astype(BF16).astype(F32)
    return high, middle, (x - high - middle).astype(BF16).astype(F32)


def running(rows, reverse, row=None, after=()):
    count, height, width = rows.shape
    more = 0 if row is None else -(-3 * row.shape[1] // width // 16) * 16
    args = [rows, *after] + ([] if row is None else [row])
    return pl.pallas_call(
        functools.partial(running_kernel, reverse, len(after)),
        in_specs=[pl.BlockSpec()]
        + [pl.BlockSpec(memory_space=pl.ANY)] * len(after)
        + ([] if row is None else [pl.BlockSpec()]),
        out_shape=pltpu.HBM((count, height + more, width), BF16),
        compiler_params=pltpu.CompilerParams(vmem_limit_bytes=8 * MIB),
        name="running_sums",
    )(*args)


def row_total(arrived, height, channels):
    count, _, width = arrived.shape
    parts = arrived[:, height : height + 3 * channels // width].astype(F32)
    return jnp.sum(parts.reshape(count, 3, channels // width, width), axis=(0, 1)).reshape(channels)


ALL = ("y", "core", "z", "x")
SEQ = ("z", "x")
PLANE = ("y", "x")


def exchange(x, axis):
    rows = x.reshape((lax.axis_size(axis), -1) + x.shape[-1:])
    return lax.all_to_all(rows, axis, 0, 0, tiled=True)


def everyones(x, axis):
    return lax.all_to_all(jnp.broadcast_to(x[None], (lax.axis_size(axis),) + x.shape), axis, 0, 0, tiled=True)


def flipped(x, axis, bit=1):
    return lax.ppermute(x, axis, [(i, i ^ bit) for i in range(lax.axis_size(axis))])


def added(*terms):
    total = terms[0].astype(F32)
    for term in terms[1:]:
        total = total + term.astype(F32)
    return total


def together(*xs):
    return lax.optimization_barrier(xs)


def small_call(kernel, out_shapes, *args, after=(), kept=(), mib=56):
    def call(*refs):
        kernel(*refs[: len(args)], *refs[len(args) + len(after) :])

    return pl.pallas_call(
        call,
        in_specs=[pl.BlockSpec()] * len(args)
        + [pl.BlockSpec(memory_space=pl.ANY)] * len(after),
        out_shape=[
            pltpu.HBM(shape, F32 if shape == END else BF16)
            if shape == END or at in kept
            else jax.ShapeDtypeStruct(shape, BF16)
            for at, shape in enumerate(out_shapes)
        ],
        compiler_params=pltpu.CompilerParams(vmem_limit_bytes=mib * MIB),
        cost_estimate=pl.CostEstimate(
            flops=0, bytes_accessed=4 * sum(x.size for x in args), transcendentals=0
        ),
        name=kernel.__name__,
    )(*args, *after)


def one(i):
    return pl.ds(i, 1)


def place(axis, bit=1):
    here = (lax.axis_index(axis) // bit) % 2
    return here, 1 - here


def merge_all(own_ref, x_ref, y_ref, low_ref, high_ref, out_ref):
    y, other_y = place("y")
    x, other_x = place("x")
    half = low_ref.shape[0]
    out_ref[one(y), :, one(x)] = own_ref[...][None, :, None]
    out_ref[one(y), :, one(other_x)] = x_ref[...][None, :, None]
    out_ref[one(other_y), :, one(x)] = y_ref[...][None, :, None]
    out_ref[one(other_y), :half, one(other_x)] = low_ref[...][None, :, None]
    out_ref[one(other_y), half:, one(other_x)] = high_ref[...][None, :, None]


def cut_kernel(x_ref, y_ref, low_ref, high_ref):
    low_ref[...] = x_ref[...]
    high_ref[...] = y_ref[...]


def cut(x_got, y_got):
    half = (x_got.shape[0] // 2,) + x_got.shape[1:]
    return pl.pallas_call(
        cut_kernel,
        grid=(1,),
        in_specs=[pl.BlockSpec(half, lambda i: (0, 0, 0)), pl.BlockSpec(half, lambda i: (1, 0, 0))],
        out_specs=[pl.BlockSpec(half, lambda i: (0, 0, 0))] * 2,
        out_shape=[jax.ShapeDtypeStruct(half, BF16)] * 2,
        compiler_params=params(20),
        name="cut",
    )(x_got, y_got)


def total(a_ref, b_ref, *index):
    return (a_ref[index].astype(F32) + b_ref[index].astype(F32)).astype(BF16)


def split_first(keep_ref, got_ref, left_ref, right_ref, left_keep_ref, right_keep_ref):
    half = left_ref.shape[-1]
    here, there = place("y")
    every = slice(None)
    for at, ref in ((there, left_ref), (here, left_keep_ref)):
        ref[...] = total(keep_ref, got_ref, one(at), every, every, every, slice(0, half))[0]
    here, there = place("x")
    for at, ref in ((there, right_ref), (here, right_keep_ref)):
        ref[...] = total(keep_ref, got_ref, every, every, one(at), every, slice(half, 2 * half))[:, :, 0]


def split_second(
    left_ref, left_got_ref, right_ref, right_got_ref, left_out, right_out, left_keep, right_keep, end_ref
):
    end_ref[...] = jnp.zeros_like(end_ref)
    here, there = place("x")
    for at, ref in ((there, left_out), (here, left_keep)):
        ref[...] = total(left_ref, left_got_ref, slice(None), one(at))[:, 0]
    here, there = place("y")
    for at, ref in ((there, right_out), (here, right_keep)):
        ref[...] = total(right_ref, right_got_ref, one(at))[0]


def join_sides(left_ref, left_got_ref, right_ref, right_got_ref, send_ref, keep_ref, end_ref):
    here, there = place("z")
    half = left_ref.shape[-1]
    for far in range(send_ref.shape[0]):
        for at, ref in ((there, send_ref), (here, keep_ref)):
            ref[far, :, :half] = total(left_ref, left_got_ref, one(2 * far + at))[0]
            ref[far, :, half:] = total(right_ref, right_got_ref, one(2 * far + at))[0]
    end_ref[...] = jnp.zeros_like(end_ref)


def split_far(keep_ref, got_ref, send_ref, rest_ref, end_ref):
    here, there = place("z", 2)
    send_ref[...] = total(keep_ref, got_ref, one(there))[0]
    rest_ref[...] = total(keep_ref, got_ref, one(here))[0]
    end_ref[...] = jnp.zeros_like(end_ref)


def repeat(x_ref, out_ref):
    for i in range(out_ref.shape[0]):
        out_ref[i] = x_ref[...]


def by_halves(sizes, rows, q, k, v, og, out_weight, gain_row, pos, pair):
    tokens, channels = q.shape
    wide = out_weight.shape[1]
    y, z, x, half = sizes["y"], sizes["z"], sizes["x"], wide // 2

    (own,) = small_call(repeat, [(z, rows, wide)], out_weight, kept=(0,))
    own = lax.all_to_all(own, "z", 0, 0, tiled=True)
    kv = key_value_sums(k, v, pair)
    kv, own = together(kv, own)
    x_got, y_got = flipped(own, "x"), flipped(own, "y")
    sent = exchange(kv, SEQ)
    intra, end = intra_outputs(q, k, v, pair)
    sent, x_got, y_got = together(sent, x_got, y_got)
    low, high = cut(x_got, y_got)
    low, high = flipped(low, "y"), flipped(high, "x")
    state = exchange(running(sent, False, after=(end,)), SEQ).reshape(kv.shape)
    outputs, send, og = weight_parts(pos, 1, q, state, intra, gain_row, og, pair)
    send, low, high = together(send, low, high)
    got = flipped(send, "core")
    (mine,) = small_call(merge_all, [(y, z, x, rows, wide)], own, x_got, y_got, low, high, mib=20)
    mine = mine.reshape(y, -1, wide)
    other = flipped(mine, "core")
    outputs, keep = weight_parts(pos, 0, q, state, intra, gain_row, og, pair, (outputs,))

    split = (y, z, x, rows, wide)
    left, right, left_keep, right_keep = small_call(
        split_first,
        [(z, x, rows, half), (y, z, rows, half)] * 2,
        keep.reshape(split),
        got.reshape(split),
        kept=(2, 3),
        mib=20,
    )
    outputs, left, right = together(outputs, left, right)
    left_got, right_got = flipped(left, "y"), flipped(right, "x")
    attn_grad, gain_part, qg = attn_grads(pos, q, outputs, gain_row, og, mine, other, pair)
    gain_part, left_got, right_got = together(gain_part, left_got, right_got)

    sent = exchange(qg, SEQ)
    gain_part = gain_part + flipped(gain_part, "core")
    left, right, left_keep, right_keep, end = small_call(
        split_second, [(z, rows, half)] * 4 + [END], left_keep, left_got, right_keep, right_got
    )
    left_got, right_got = flipped(left, "x"), flipped(right, "y")
    value_in, end = value_grads(q, k, attn_grad, pair, after=(end,))
    end, left_got, right_got, gain_got = together(end, left_got, right_got, flipped(gain_part, "y"))
    sums = running(sent, True, gain_part + gain_got, after=(end,))
    arrived = exchange(sums, SEQ)
    send, keep, end = small_call(
        join_sides, [(2, rows, wide)] * 2 + [END], left_keep, left_got, right_keep, right_got, after=(sums,)
    )
    got = flipped(send, "z", 1)
    query_g, key_in, end = query_grads(q, k, v, attn_grad, state, pair, after=(end,))
    end, got, arrived = together(end, got, arrived)
    send, keep, end = small_call(split_far, [(rows, wide)] * 2 + [END], keep, got, after=(end,))
    got = flipped(send, "z", 2)
    key_g, value_g = rev_grads(k, v, arrived, key_in, value_in, pair, after=(end,))
    gain_sum = row_total(arrived, sent.shape[1], channels)
    return query_g, key_g, value_g, (keep, got), gain_sum


def by_planes(sizes, rows, q, k, v, og, out_weight, gain_row, pos, pair):
    tokens, channels = q.shape
    wide = out_weight.shape[1]
    y, z, x = sizes["y"], sizes["z"], sizes["x"]
    weight = lax.all_gather(out_weight, ALL, axis=0, tiled=True)
    kv = key_value_sums(k, v, pair)
    intra, _ = intra_outputs(q, k, v, pair)
    state = exchange(running(exchange(kv, SEQ), False), SEQ).reshape(kv.shape)
    outputs, send, og = weight_parts(pos, 1, q, state, intra, gain_row, og, pair)
    outputs, keep = weight_parts(pos, 0, q, state, intra, gain_row, og, pair, (outputs,))
    part = added(keep, flipped(send, "core")).astype(BF16)
    part = part.reshape(y, z, x, rows, wide).transpose(0, 2, 1, 3, 4).reshape(y * x, z, rows, wide)
    part = lax.all_to_all(part, PLANE, 0, 0, tiled=True)
    part = added(*[part[i] for i in range(y * x)]).astype(BF16)
    part = lax.all_to_all(part, "z", 0, 0, tiled=True)
    weight = weight.reshape(y, 2, z * x * rows, wide)
    mine, other = [
        lax.dynamic_index_in_dim(weight, i, 1, keepdims=False) for i in place("core")
    ]
    attn_grad, gain_part, qg = attn_grads(pos, q, outputs, gain_row, og, mine, other, pair)
    rev = exchange(running(exchange(qg, SEQ), True), SEQ).reshape(kv.shape)
    query_g, key_in, _ = query_grads(q, k, v, attn_grad, state, pair)
    value_in, _ = value_grads(q, k, attn_grad, pair)
    key_g, value_g = rev_grads(k, v, rev, key_in, value_in, pair)
    gain_sum = jnp.sum(everyones(gain_part.reshape(channels), ALL), axis=0)
    return query_g, key_g, value_g, [part[i] for i in range(z)], gain_sum


def shards(queries, keys, values, out_grad, out_weight, gain):
    tokens, channels = queries.shape[1:]
    assert tokens == BLOCK
    sizes = {name: lax.axis_size(name) for name in ALL}
    devices = lax.axis_size(ALL)
    rows = out_weight.shape[0]
    pair = channels // (sizes["y"] * sizes["core"]) // HEAD_DIM
    pos = lax.axis_index(("y", "core")).reshape(1).astype(jnp.int32)
    halves = (sizes["y"], sizes["z"], sizes["x"]) == (2, 4, 2) and rows % 16 == 0
    query_g, key_g, value_g, parts, gain_sum = (by_halves if halves else by_planes)(
        sizes,
        rows,
        queries[0],
        keys[0],
        values[0],
        out_grad[0],
        out_weight,
        gain.reshape(1, channels),
        pos,
        pair,
    )
    factor = 1.0 / jnp.sqrt(jnp.float32(tokens * devices))
    out_shape = (1, tokens, channels)
    return (
        query_g.reshape(out_shape),
        key_g.reshape(out_shape),
        value_g.reshape(out_shape),
        added(*parts) * factor,
        gain_sum * factor,
    )


def solution(mesh):
    dp_count, seq_count = mesh.shape["dp"], mesh.shape["seq"]
    finer = Mesh(mesh.devices.reshape(dp_count // 2, 2, seq_count // 2, 2), ALL)
    tokens = P(("y", "core"), ("z", "x"), None)
    rows = P(ALL, None)
    return jax.shard_map(
        shards,
        mesh=finer,
        in_specs=(tokens, tokens, tokens, tokens, rows, P()),
        out_specs=(tokens, tokens, tokens, rows, P()),
        check_vma=False,
    )
```

```python
import functools

import jax
import jax.numpy as jnp
from jax import lax
from jax.experimental import pallas as pl
from jax.experimental.pallas import tpu as pltpu
from jax.sharding import Mesh
from jax.sharding import PartitionSpec as P

HEAD_DIM = 128
BLOCK = 512
MIB = 1 << 20

norm_eps = 1e-06

END = (8, 128)

F32 = jnp.float32
BF16 = jnp.bfloat16


def dot(a, b, contract):
    return lax.dot_general(a, b, (contract, ((), ())), preferred_element_type=F32)


def params(mib, dims=1):
    return pltpu.CompilerParams(
        vmem_limit_bytes=mib * MIB, dimension_semantics=("arbitrary",) * dims
    )


ROW_BLOCKS = 4


def row_blocks(tokens, wide):
    return [
        pl.BlockSpec((tokens // ROW_BLOCKS, wide), lambda y, p, r=r: (r, 0)) for r in range(ROW_BLOCKS)
    ]


def head(ref, i):
    return ref[:, i * HEAD_DIM : (i + 1) * HEAD_DIM]


def kv_kernel(k_ref, v_ref, o_ref):
    for i in range(o_ref.shape[0]):
        o_ref[i] = dot(head(k_ref, i), head(v_ref, i), ((0,), (0,))).astype(BF16)


def key_value_sums(keys, values, pair):
    tokens, channels = keys.shape
    width = pair * HEAD_DIM
    heads = channels // HEAD_DIM
    spec = pl.BlockSpec((tokens, width), lambda b: (0, b))
    return pl.pallas_call(
        kv_kernel,
        grid=(heads // pair,),
        in_specs=[spec, spec],
        out_specs=pl.BlockSpec((pair, HEAD_DIM, HEAD_DIM), lambda b: (b, 0, 0)),
        out_shape=jax.ShapeDtypeStruct((heads, HEAD_DIM, HEAD_DIM), BF16),
        compiler_params=params(56),
        cost_estimate=pl.CostEstimate(
            flops=2 * tokens * channels * HEAD_DIM, bytes_accessed=4 * tokens * channels, transcendentals=0
        ),
        name="key_value_sums",
    )(keys, values)


def lower(x):
    rows = lax.broadcasted_iota(jnp.int32, x.shape, 0)
    cols = lax.broadcasted_iota(jnp.int32, x.shape, 1)
    return jnp.where(cols <= rows, x, 0.0).astype(BF16)


def intra_kernel(q_ref, k_ref, v_ref, o_ref, end_ref):
    end_ref[...] = jnp.zeros_like(end_ref)
    half = q_ref.shape[0] // 2
    for i in range(o_ref.shape[1] // HEAD_DIM):
        q, k, v = head(q_ref, i), head(k_ref, i), head(v_ref, i)
        here = slice(i * HEAD_DIM, (i + 1) * HEAD_DIM)
        top = lower(dot(q[:half], k[:half], ((1,), (1,))))
        o_ref[:half, here] = dot(top, v[:half], ((1,), (0,)))
        left = dot(q[half:], k[:half], ((1,), (1,))).astype(BF16)
        right = lower(dot(q[half:], k[half:], ((1,), (1,))))
        low = dot(left, v[:half], ((1,), (0,))) + dot(right, v[half:], ((1,), (0,)))
        o_ref[half:, here] = low


def intra_outputs(queries, keys, values, pair):
    tokens, channels = keys.shape
    spec = pl.BlockSpec((tokens, pair * HEAD_DIM), lambda b: (0, b))
    return pl.pallas_call(
        intra_kernel,
        grid=(channels // (pair * HEAD_DIM),),
        in_specs=[spec] * 3,
        out_specs=[spec, pl.BlockSpec(END, lambda b: (0, 0))],
        out_shape=[jax.ShapeDtypeStruct((tokens, channels), F32), pltpu.HBM(END, F32)],
        compiler_params=params(56),
        cost_estimate=pl.CostEstimate(
            flops=4 * tokens * tokens * channels, bytes_accessed=10 * tokens * channels, transcendentals=0
        ),
        name="intra_outputs",
    )(queries, keys, values)


def rms_inverse(x):
    return lax.rsqrt(jnp.mean(x * x, axis=-1, keepdims=True) + norm_eps)


def unit_kernel(begun, pos_ref, q_ref, s_ref, intra_ref, gain_ref, *refs):
    if begun:
        og_ref, _, out_ref, part_ref = refs
    else:
        *og_refs, out_ref, part_ref, og_ref = refs

        @pl.when(pl.program_id(0) == 0)
        def _():
            start = 0
            for ref in og_refs:
                og_ref[start : start + ref.shape[0]] = ref[...]
                start = start + ref.shape[0]

    units = []
    for i in range(s_ref.shape[0]):
        x = head(intra_ref, i) + dot(head(q_ref, i), s_ref[i], ((1,), (0,)))
        out_ref[:, i * HEAD_DIM : (i + 1) * HEAD_DIM] = x
        units.append((x * rms_inverse(x) * head(gain_ref, i)).astype(BF16))
    unit = jnp.concatenate(units, axis=1) if len(units) > 1 else units[0]
    part_ref[0] = dot(unit, og_ref[...], ((0,), (0,))).astype(BF16)


def weight_parts(pos, side, queries, state, intra, gain, out_grad, pair, begun=()):
    tokens, channels = queries.shape
    width = pair * HEAD_DIM
    count = channels // width // 2
    wide = out_grad.shape[1]

    def block(y, pos_ref):
        return 2 * y + lax.rem(pos_ref[0] + side, 2)

    cols = pl.BlockSpec((tokens, width), lambda y, p: (0, block(y, p)))
    whole = pl.BlockSpec((tokens, wide), lambda y, p: (0, 0))
    more = [] if begun else [(whole, jax.ShapeDtypeStruct((tokens, wide), BF16))]
    return pl.pallas_call(
        functools.partial(unit_kernel, len(begun)),
        grid_spec=pltpu.PrefetchScalarGridSpec(
            num_scalar_prefetch=1,
            grid=(count,),
            in_specs=[
                cols,
                pl.BlockSpec((pair, HEAD_DIM, HEAD_DIM), lambda y, p: (block(y, p), 0, 0)),
                cols,
                pl.BlockSpec((1, width), lambda y, p: (0, block(y, p))),
            ]
            + ([whole, pl.BlockSpec(memory_space=pl.ANY)] if begun else row_blocks(tokens, wide)),
            out_specs=[cols, pl.BlockSpec((1, width, wide), lambda y, p: (y, 0, 0))] + [m[0] for m in more],
        ),
        out_shape=[
            jax.ShapeDtypeStruct((tokens, channels), F32),
            jax.ShapeDtypeStruct((count, width, wide), BF16),
        ]
        + [m[1] for m in more],
        input_output_aliases={6: 0} if begun else {},
        compiler_params=params(30 if begun else 44),
        cost_estimate=pl.CostEstimate(
            flops=tokens * channels * wide,
            bytes_accessed=5 * tokens * channels + 2 * tokens * wide + channels * wide,
            transcendentals=0,
        ),
        name="weight_parts",
    )(pos, queries, state, intra, gain, *[out_grad] * (1 if begun else ROW_BLOCKS), *begun)


def attn_grad_kernel(pos_ref, q_ref, o_ref, gain_ref, og_ref, mine_ref, other_ref, ag_ref, gg_ref, qg_ref, ug_ref):
    count = pl.num_programs(0) // 2

    @pl.when(pl.program_id(0) < count)
    def _():
        ug_ref[...] = dot(og_ref[...], mine_ref[0], ((1,), (1,)))

    @pl.when(pl.program_id(0) >= count)
    def _():
        ug_ref[...] = dot(og_ref[...], other_ref[0], ((1,), (1,)))

    for i in range(qg_ref.shape[0]):
        here = slice(i * HEAD_DIM, (i + 1) * HEAD_DIM)
        x = head(o_ref, i)
        inverse = rms_inverse(x)
        normed = x * inverse
        ug = head(ug_ref, i)
        gg_ref[:, here] = jnp.sum(ug * normed, axis=0, keepdims=True)
        scaled = ug * head(gain_ref, i)
        middle = jnp.mean(scaled * normed, axis=-1, keepdims=True)
        ag = ((scaled - normed * middle) * inverse).astype(BF16)
        ag_ref[:, here] = ag
        qg_ref[i] = dot(head(q_ref, i), ag, ((0,), (0,))).astype(BF16)


def attn_grads(pos, queries, outputs, gain, out_grad, mine, other, pair):
    tokens, channels = queries.shape
    width = pair * HEAD_DIM
    count = channels // width // 2
    wide = out_grad.shape[1]
    heads = channels // HEAD_DIM

    def block(s, pos_ref):
        return 2 * lax.rem(s, count) + lax.rem(pos_ref[0] + s // count, 2)

    cols = pl.BlockSpec((tokens, width), lambda s, p: (0, block(s, p)))
    row = pl.BlockSpec((1, width), lambda s, p: (0, block(s, p)))
    states = pl.BlockSpec((pair, HEAD_DIM, HEAD_DIM), lambda s, p: (block(s, p), 0, 0))
    piece = (1,) + mine.shape[1:]
    return pl.pallas_call(
        attn_grad_kernel,
        grid_spec=pltpu.PrefetchScalarGridSpec(
            num_scalar_prefetch=1,
            grid=(2 * count,),
            in_specs=[
                cols,
                cols,
                row,
                pl.BlockSpec((tokens, wide), lambda s, p: (0, 0)),
                pl.BlockSpec(piece, lambda s, p: (jnp.minimum(s, count - 1), 0, 0)),
                pl.BlockSpec(piece, lambda s, p: (jnp.maximum(s - count, 0), 0, 0)),
            ],
            out_specs=[cols, row, states],
            scratch_shapes=[pltpu.VMEM((tokens, width), F32)],
        ),
        out_shape=[
            pltpu.HBM((tokens, channels), BF16),
            jax.ShapeDtypeStruct((1, channels), F32),
            pltpu.HBM((heads, HEAD_DIM, HEAD_DIM), BF16),
        ],
        compiler_params=params(30),
        cost_estimate=pl.CostEstimate(
            flops=2 * tokens * channels * wide,
            bytes_accessed=8 * tokens * channels + 2 * tokens * wide + 2 * channels * wide,
            transcendentals=0,
        ),
        name="attn_grads",
    )(pos, queries, outputs, gain, out_grad, mine, other)


NT, NN, TN = ((1,), (1,)), ((1,), (0,)), ((0,), (0,))


def query_grad_kernel(q_ref, k_ref, v_ref, ag_ref, s_ref, *refs):
    qg_ref, kg_ref, end_ref = refs[-3:]
    end_ref[...] = jnp.zeros_like(end_ref)
    half = q_ref.shape[0] // 2
    top, low = slice(0, half), slice(half, 2 * half)
    for i in range(s_ref.shape[0]):
        q, k, v, ag = head(q_ref, i), head(k_ref, i), head(v_ref, i), head(ag_ref, i)
        here = slice(i * HEAD_DIM, (i + 1) * HEAD_DIM)
        from_state = dot(ag, s_ref[i], NT)
        g00 = lower(dot(ag[top], v[top], NT))
        g10 = dot(ag[low], v[top], NT).astype(BF16)
        g11 = lower(dot(ag[low], v[low], NT))
        qg_ref[top, here] = (dot(g00, k[top], NN) + from_state[top]).astype(BF16)
        qg_ref[low, here] = (dot(g10, k[top], NN) + dot(g11, k[low], NN) + from_state[low]).astype(BF16)
        kg_ref[top, here] = (dot(g00, q[top], TN) + dot(g10, q[low], TN)).astype(BF16)
        kg_ref[low, here] = dot(g11, q[low], TN).astype(BF16)


def query_grads(queries, keys, values, attn_grad, state, pair, after=()):
    tokens, channels = queries.shape
    spec = pl.BlockSpec((tokens, pair * HEAD_DIM), lambda b: (0, b))
    return pl.pallas_call(
        query_grad_kernel,
        grid=(channels // (pair * HEAD_DIM),),
        in_specs=[spec] * 4
        + [pl.BlockSpec((pair, HEAD_DIM, HEAD_DIM), lambda b: (b, 0, 0))]
        + [pl.BlockSpec(memory_space=pl.ANY)] * len(after),
        out_specs=[spec, spec, pl.BlockSpec(END, lambda b: (0, 0))],
        out_shape=[jax.ShapeDtypeStruct((tokens, channels), BF16)] * 2 + [pltpu.HBM(END, F32)],
        compiler_params=params(56),
        cost_estimate=pl.CostEstimate(
            flops=6 * tokens * tokens * channels, bytes_accessed=14 * tokens * channels, transcendentals=0
        ),
        name="query_grads",
    )(queries, keys, values, attn_grad, state, *after)


def value_grad_kernel(q_ref, k_ref, ag_ref, *refs):
    vg_ref, end_ref = refs[-2:]
    end_ref[...] = jnp.zeros_like(end_ref)
    half = q_ref.shape[0] // 2
    top, low = slice(0, half), slice(half, 2 * half)
    for i in range(q_ref.shape[1] // HEAD_DIM):
        q, k, ag = head(q_ref, i), head(k_ref, i), head(ag_ref, i)
        here = slice(i * HEAD_DIM, (i + 1) * HEAD_DIM)
        a00 = lower(dot(q[top], k[top], NT))
        a10 = dot(q[low], k[top], NT).astype(BF16)
        a11 = lower(dot(q[low], k[low], NT))
        vg_ref[top, here] = (dot(a00, ag[top], TN) + dot(a10, ag[low], TN)).astype(BF16)
        vg_ref[low, here] = dot(a11, ag[low], TN).astype(BF16)


def value_grads(queries, keys, attn_grad, pair, after=()):
    tokens, channels = queries.shape
    spec = pl.BlockSpec((tokens, pair * HEAD_DIM), lambda b: (0, b))
    return pl.pallas_call(
        value_grad_kernel,
        grid=(channels // (pair * HEAD_DIM),),
        in_specs=[spec] * 3 + [pl.BlockSpec(memory_space=pl.ANY)] * len(after),
        out_specs=[spec, pl.BlockSpec(END, lambda b: (0, 0))],
        out_shape=[jax.ShapeDtypeStruct((tokens, channels), BF16), pltpu.HBM(END, F32)],
        compiler_params=params(56),
        cost_estimate=pl.CostEstimate(
            flops=4 * tokens * tokens * channels, bytes_accessed=8 * tokens * channels, transcendentals=0
        ),
        name="value_grads",
    )(queries, keys, attn_grad, *after)


def rev_grad_kernel(k_ref, v_ref, r_ref, kin_ref, vin_ref, *refs):
    kg_ref, vg_ref = refs[-2:]
    for i in range(r_ref.shape[0]):
        here = slice(i * HEAD_DIM, (i + 1) * HEAD_DIM)
        rev = r_ref[i]
        kg_ref[:, here] = (head(kin_ref, i).astype(F32) + dot(head(v_ref, i), rev, NT)).astype(BF16)
        vg_ref[:, here] = (head(vin_ref, i).astype(F32) + dot(head(k_ref, i), rev, NN)).astype(BF16)


def rev_grads(keys, values, rev, key_in, value_in, pair, after=()):
    tokens, channels = keys.shape
    spec = pl.BlockSpec((tokens, pair * HEAD_DIM), lambda b: (0, b))
    return pl.pallas_call(
        rev_grad_kernel,
        grid=(channels // (pair * HEAD_DIM),),
        in_specs=[spec] * 2
        + [pl.BlockSpec((pair, HEAD_DIM, HEAD_DIM), lambda b: (b, 0, 0)), spec, spec]
        + [pl.BlockSpec(memory_space=pl.ANY)] * len(after),
        out_specs=[spec] * 2,
        out_shape=[jax.ShapeDtypeStruct((tokens, channels), BF16)] * 2,
        compiler_params=params(56),
        cost_estimate=pl.CostEstimate(
            flops=4 * tokens * channels * HEAD_DIM, bytes_accessed=12 * tokens * channels, transcendentals=0
        ),
        name="rev_grads",
    )(keys, values, rev, key_in, value_in, *after)


def running_kernel(reverse, after, x_ref, *refs):
    refs = refs[after:]
    o_ref = refs[-1]
    count, rows = x_ref.shape[:2]
    total = jnp.zeros(x_ref.shape[1:], F32)
    for place in range(count)[:: -1 if reverse else 1]:
        o_ref[place, :rows] = total.astype(BF16)
        total = total + x_ref[place].astype(F32)
    if len(refs) > 1:
        parts = in_parts(refs[0][...])
        width = x_ref.shape[-1]
        extra = [part[:, i : i + width] for part in parts for i in range(0, part.shape[1], width)]
        extra = extra + [jnp.zeros((1, width), F32)] * (o_ref.shape[1] - rows - len(extra))
        extra = jnp.concatenate(extra, axis=0).astype(BF16)
        for place in range(count):
            o_ref[place, rows:] = extra


def in_parts(x):
    high = x.astype(BF16).astype(F32)
    middle = (x - high).astype(BF16).astype(F32)
    return high, middle, (x - high - middle).astype(BF16).astype(F32)


def running(rows, reverse, row=None, after=()):
    count, height, width = rows.shape
    more = 0 if row is None else -(-3 * row.shape[1] // width // 16) * 16
    args = [rows, *after] + ([] if row is None else [row])
    return pl.pallas_call(
        functools.partial(running_kernel, reverse, len(after)),
        in_specs=[pl.BlockSpec()]
        + [pl.BlockSpec(memory_space=pl.ANY)] * len(after)
        + ([] if row is None else [pl.BlockSpec()]),
        out_shape=pltpu.HBM((count, height + more, width), BF16),
        compiler_params=pltpu.CompilerParams(vmem_limit_bytes=8 * MIB),
        name="running_sums",
    )(*args)


def row_total(arrived, height, channels):
    count, _, width = arrived.shape
    parts = arrived[:, height : height + 3 * channels // width].astype(F32)
    return jnp.sum(parts.reshape(count, 3, channels // width, width), axis=(0, 1)).reshape(channels)


ALL = ("y", "core", "z", "x")
SEQ = ("z", "x")
PLANE = ("y", "x")


def exchange(x, axis):
    rows = x.reshape((lax.axis_size(axis), -1) + x.shape[-1:])
    return lax.all_to_all(rows, axis, 0, 0, tiled=True)


def everyones(x, axis):
    return lax.all_to_all(jnp.broadcast_to(x[None], (lax.axis_size(axis),) + x.shape), axis, 0, 0, tiled=True)


def flipped(x, axis, bit=1):
    return lax.ppermute(x, axis, [(i, i ^ bit) for i in range(lax.axis_size(axis))])


def added(*terms):
    total = terms[0].astype(F32)
    for term in terms[1:]:
        total = total + term.astype(F32)
    return total


def together(*xs):
    return lax.optimization_barrier(xs)


def small_call(kernel, out_shapes, *args, after=(), kept=(), mib=56):
    def call(*refs):
        kernel(*refs[: len(args)], *refs[len(args) + len(after) :])

    return pl.pallas_call(
        call,
        in_specs=[pl.BlockSpec()] * len(args)
        + [pl.BlockSpec(memory_space=pl.ANY)] * len(after),
        out_shape=[
            pltpu.HBM(shape, F32 if shape == END else BF16)
            if shape == END or at in kept
            else jax.ShapeDtypeStruct(shape, BF16)
            for at, shape in enumerate(out_shapes)
        ],
        compiler_params=pltpu.CompilerParams(vmem_limit_bytes=mib * MIB),
        cost_estimate=pl.CostEstimate(
            flops=0, bytes_accessed=4 * sum(x.size for x in args), transcendentals=0
        ),
        name=kernel.__name__,
    )(*args, *after)


def one(i):
    return pl.ds(i, 1)


def place(axis, bit=1):
    here = (lax.axis_index(axis) // bit) % 2
    return here, 1 - here


def merge_all(own_ref, x_ref, y_ref, low_ref, high_ref, out_ref):
    y, other_y = place("y")
    x, other_x = place("x")
    half = low_ref.shape[0]
    out_ref[one(y), :, one(x)] = own_ref[...][None, :, None]
    out_ref[one(y), :, one(other_x)] = x_ref[...][None, :, None]
    out_ref[one(other_y), :, one(x)] = y_ref[...][None, :, None]
    out_ref[one(other_y), :half, one(other_x)] = low_ref[...][None, :, None]
    out_ref[one(other_y), half:, one(other_x)] = high_ref[...][None, :, None]


def cut_kernel(x_ref, y_ref, low_ref, high_ref):
    low_ref[...] = x_ref[...]
    high_ref[...] = y_ref[...]


def cut(x_got, y_got):
    half = (x_got.shape[0] // 2,) + x_got.shape[1:]
    return pl.pallas_call(
        cut_kernel,
        grid=(1,),
        in_specs=[pl.BlockSpec(half, lambda i: (0, 0, 0)), pl.BlockSpec(half, lambda i: (1, 0, 0))],
        out_specs=[pl.BlockSpec(half, lambda i: (0, 0, 0))] * 2,
        out_shape=[jax.ShapeDtypeStruct(half, BF16)] * 2,
        compiler_params=params(20),
        name="cut",
    )(x_got, y_got)


def total(a_ref, b_ref, *index):
    return (a_ref[index].astype(F32) + b_ref[index].astype(F32)).astype(BF16)


def split_first(keep_ref, got_ref, left_ref, right_ref, left_keep_ref, right_keep_ref):
    half = left_ref.shape[-1]
    here, there = place("y")
    every = slice(None)
    for at, ref in ((there, left_ref), (here, left_keep_ref)):
        ref[...] = total(keep_ref, got_ref, one(at), every, every, every, slice(0, half))[0]
    here, there = place("x")
    for at, ref in ((there, right_ref), (here, right_keep_ref)):
        ref[...] = total(keep_ref, got_ref, every, every, one(at), every, slice(half, 2 * half))[:, :, 0]


def split_second(
    left_ref, left_got_ref, right_ref, right_got_ref, left_out, right_out, left_keep, right_keep, end_ref
):
    end_ref[...] = jnp.zeros_like(end_ref)
    here, there = place("x")
    for at, ref in ((there, left_out), (here, left_keep)):
        ref[...] = total(left_ref, left_got_ref, slice(None), one(at))[:, 0]
    here, there = place("y")
    for at, ref in ((there, right_out), (here, right_keep)):
        ref[...] = total(right_ref, right_got_ref, one(at))[0]


def join_sides(left_ref, left_got_ref, right_ref, right_got_ref, send_ref, keep_ref, end_ref):
    here, there = place("z")
    half = left_ref.shape[-1]
    for far in range(send_ref.shape[0]):
        for at, ref in ((there, send_ref), (here, keep_ref)):
            ref[far, :, :half] = total(left_ref, left_got_ref, one(2 * far + at))[0]
            ref[far, :, half:] = total(right_ref, right_got_ref, one(2 * far + at))[0]
    end_ref[...] = jnp.zeros_like(end_ref)


def split_far(keep_ref, got_ref, send_ref, rest_ref, end_ref):
    here, there = place("z", 2)
    send_ref[...] = total(keep_ref, got_ref, one(there))[0]
    rest_ref[...] = total(keep_ref, got_ref, one(here))[0]
    end_ref[...] = jnp.zeros_like(end_ref)


def repeat(x_ref, out_ref):
    for i in range(out_ref.shape[0]):
        out_ref[i] = x_ref[...]


def by_halves(sizes, rows, q, k, v, og, out_weight, gain_row, pos, pair):
    tokens, channels = q.shape
    wide = out_weight.shape[1]
    y, z, x, half = sizes["y"], sizes["z"], sizes["x"], wide // 2

    (own,) = small_call(repeat, [(z, rows, wide)], out_weight, kept=(0,))
    own = lax.all_to_all(own, "z", 0, 0, tiled=True)
    kv = key_value_sums(k, v, pair)
    kv, own = together(kv, own)
    x_got, y_got = flipped(own, "x"), flipped(own, "y")
    sent = exchange(kv, SEQ)
    intra, end = intra_outputs(q, k, v, pair)
    sent, x_got, y_got = together(sent, x_got, y_got)
    low, high = cut(x_got, y_got)
    low, high = flipped(low, "y"), flipped(high, "x")
    state = exchange(running(sent, False, after=(end,)), SEQ).reshape(kv.shape)
    outputs, send, og = weight_parts(pos, 1, q, state, intra, gain_row, og, pair)
    send, low, high = together(send, low, high)
    got = flipped(send, "core")
    (mine,) = small_call(merge_all, [(y, z, x, rows, wide)], own, x_got, y_got, low, high, mib=20)
    mine = mine.reshape(y, -1, wide)
    other = flipped(mine, "core")
    outputs, keep = weight_parts(pos, 0, q, state, intra, gain_row, og, pair, (outputs,))

    split = (y, z, x, rows, wide)
    left, right, left_keep, right_keep = small_call(
        split_first,
        [(z, x, rows, half), (y, z, rows, half)] * 2,
        keep.reshape(split),
        got.reshape(split),
        kept=(2, 3),
        mib=20,
    )
    outputs, left, right = together(outputs, left, right)
    left_got, right_got = flipped(left, "y"), flipped(right, "x")
    attn_grad, gain_part, qg = attn_grads(pos, q, outputs, gain_row, og, mine, other, pair)
    gain_part, left_got, right_got = together(gain_part, left_got, right_got)

    sent = exchange(qg, SEQ)
    gain_part = gain_part + flipped(gain_part, "core")
    left, right, left_keep, right_keep, end = small_call(
        split_second, [(z, rows, half)] * 4 + [END], left_keep, left_got, right_keep, right_got
    )
    left_got, right_got = flipped(left, "x"), flipped(right, "y")
    value_in, end = value_grads(q, k, attn_grad, pair, after=(end,))
    end, left_got, right_got = together(end, left_got, right_got)
    sums = running(sent, True, gain_part, after=(end,))
    arrived = exchange(sums, SEQ)
    send, keep, end = small_call(
        join_sides, [(2, rows, wide)] * 2 + [END], left_keep, left_got, right_keep, right_got, after=(sums,)
    )
    got = flipped(send, "z", 1)
    query_g, key_in, end = query_grads(q, k, v, attn_grad, state, pair, after=(end,))
    gain_sum = row_total(arrived, sent.shape[1], channels)
    end, got, arrived, gain_got = together(end, got, arrived, flipped(gain_sum, "y"))
    send, keep, end = small_call(split_far, [(rows, wide)] * 2 + [END], keep, got, after=(end,))
    got = flipped(send, "z", 2)
    key_g, value_g = rev_grads(k, v, arrived, key_in, value_in, pair, after=(end,))
    return query_g, key_g, value_g, (keep, got), gain_sum + gain_got


def by_planes(sizes, rows, q, k, v, og, out_weight, gain_row, pos, pair):
    tokens, channels = q.shape
    wide = out_weight.shape[1]
    y, z, x = sizes["y"], sizes["z"], sizes["x"]
    weight = lax.all_gather(out_weight, ALL, axis=0, tiled=True)
    kv = key_value_sums(k, v, pair)
    intra, _ = intra_outputs(q, k, v, pair)
    state = exchange(running(exchange(kv, SEQ), False), SEQ).reshape(kv.shape)
    outputs, send, og = weight_parts(pos, 1, q, state, intra, gain_row, og, pair)
    outputs, keep = weight_parts(pos, 0, q, state, intra, gain_row, og, pair, (outputs,))
    part = added(keep, flipped(send, "core")).astype(BF16)
    part = part.reshape(y, z, x, rows, wide).transpose(0, 2, 1, 3, 4).reshape(y * x, z, rows, wide)
    part = lax.all_to_all(part, PLANE, 0, 0, tiled=True)
    part = added(*[part[i] for i in range(y * x)]).astype(BF16)
    part = lax.all_to_all(part, "z", 0, 0, tiled=True)
    weight = weight.reshape(y, 2, z * x * rows, wide)
    mine, other = [
        lax.dynamic_index_in_dim(weight, i, 1, keepdims=False) for i in place("core")
    ]
    attn_grad, gain_part, qg = attn_grads(pos, q, outputs, gain_row, og, mine, other, pair)
    rev = exchange(running(exchange(qg, SEQ), True), SEQ).reshape(kv.shape)
    query_g, key_in, _ = query_grads(q, k, v, attn_grad, state, pair)
    value_in, _ = value_grads(q, k, attn_grad, pair)
    key_g, value_g = rev_grads(k, v, rev, key_in, value_in, pair)
    gain_sum = jnp.sum(everyones(gain_part.reshape(channels), ALL), axis=0)
    return query_g, key_g, value_g, [part[i] for i in range(z)], gain_sum


def shards(queries, keys, values, out_grad, out_weight, gain):
    tokens, channels = queries.shape[1:]
    assert tokens == BLOCK
    sizes = {name: lax.axis_size(name) for name in ALL}
    devices = lax.axis_size(ALL)
    rows = out_weight.shape[0]
    pair = channels // (sizes["y"] * sizes["core"]) // HEAD_DIM
    pos = lax.axis_index(("y", "core")).reshape(1).astype(jnp.int32)
    halves = (sizes["y"], sizes["z"], sizes["x"]) == (2, 4, 2) and rows % 16 == 0
    query_g, key_g, value_g, parts, gain_sum = (by_halves if halves else by_planes)(
        sizes,
        rows,
        queries[0],
        keys[0],
        values[0],
        out_grad[0],
        out_weight,
        gain.reshape(1, channels),
        pos,
        pair,
    )
    factor = 1.0 / jnp.sqrt(jnp.float32(tokens * devices))
    out_shape = (1, tokens, channels)
    return (
        query_g.reshape(out_shape),
        key_g.reshape(out_shape),
        value_g.reshape(out_shape),
        added(*parts) * factor,
        gain_sum * factor,
    )


def solution(mesh):
    dp_count, seq_count = mesh.shape["dp"], mesh.shape["seq"]
    finer = Mesh(mesh.devices.reshape(dp_count // 2, 2, seq_count // 2, 2), ALL)
    tokens = P(("y", "core"), ("z", "x"), None)
    rows = P(ALL, None)
    return jax.shard_map(
        shards,
        mesh=finer,
        in_specs=(tokens, tokens, tokens, tokens, rows, P()),
        out_specs=(tokens, tokens, tokens, rows, P()),
        check_vma=False,
    )
```
